32 devices in a mesh: groups: 2 (over y), dp: 4 (over z), tile: 4 (over x, core).
Axes of the slice: x: 2, y: 2, z: 4, core: 2. Of those that a mesh axis runs over, the one named last changes fastest.
Arguments:
- left_outputs: bfloat16 [4096, 2048], P(('groups', 'dp'), 'tile'), parts along dimension 0, may hold values from -48 to 48, as said below
- right_outputs: bfloat16 [4096, 2048], P(('groups', 'dp'), 'tile'), parts along dimension 0, may hold values from -48 to 48, as said below
Outputs:
- left_gradient: bfloat16 [4096, 2048], P(('groups', 'dp'), 'tile'), parts along dimension 0
- right_gradient: bfloat16 [4096, 2048], P(('groups', 'dp'), 'tile'), parts along dimension 0
- corr_tiles: float32 [8, 1024, 1024], P(('groups', 'tile'), 'dp'), parts along dimension 0
- loss: float32 [2], P('groups'), parts along dimension 0
The draws below stay inside these ranges and needn't reach their ends.
There are 2 independent parts, one for each index of `groups`. The reference program is written for one: setup_inputs(seed, part) draws one part's arguments, and reference() takes and returns one part's arrays. A program takes and returns all parts, laid end to end along the dimension named above; each array names one. Nothing has to cross between parts.
Inputs may be any that keep to these rules, and one draw needn't show every extreme that they name: `left_outputs`: projector outputs; each feature has its own offset and scale, and the two views share a part. `right_outputs`: projector outputs; each feature has its own offset and scale, and the two views share a part.
All inputs are finite; a program needn't handle non-finite values.
Results may differ from the reference program's by a relative error of at most 0.0061.
Values may be sent and summed in bfloat16 or wider, within the bound.
No kernel may reach another device: no remote copies, remote signals or barrier semaphores. Data moves between devices by JAX's collectives and lax.ppermute only.
A program may use at most 64 MiB of HBM per device.

```python
import math
import jax
import jax.numpy as jnp
from jax import lax

FEATURE_COUNT = 2048
IMAGE_TOTAL = 2048


def shared_part(key):
    first_moment, second_moment = jax.random.split(key)
    latent = jnp.clip(jax.random.normal(first_moment, (IMAGE_TOTAL, FEATURE_COUNT), jnp.float32), -4.0, 4.0)
    mixing = jax.random.uniform(second_moment, (FEATURE_COUNT,), jnp.float32, 0.5, 0.97)
    return (latent, mixing)


def noise_part(key):
    return jnp.clip(jax.random.normal(key, (IMAGE_TOTAL, FEATURE_COUNT), jnp.float32), -4.0, 4.0)


def finish(key, signal, wide_offset):
    scale_seed, offset_seed = jax.random.split(key)
    loss_scale = jnp.exp(jax.random.uniform(scale_seed, (FEATURE_COUNT,), jnp.float32, 0.0, math.log(8.0)))
    offset = jax.random.uniform(offset_seed, (FEATURE_COUNT,), jnp.float32, -wide_offset, wide_offset)
    return (offset + loss_scale * signal).astype(jnp.bfloat16)


def draw_left_outputs(key, part):
    latent, mixing = shared_part(key)
    key = jax.random.fold_in(key, 11)
    knoise, krest = jax.random.split(key)
    noise = noise_part(knoise)
    signal = 0.9 * latent + 0.3 * noise
    return finish(krest, signal, 3.0)


def draw_right_outputs(key, part):
    latent, mixing = shared_part(key)
    key = jax.random.fold_in(key, 23)
    knoise, krest = jax.random.split(key)
    noise = noise_part(knoise)
    signal = 0.9 * (mixing * latent + jnp.sqrt(1.0 - mixing * mixing) * noise)
    return finish(krest, signal, 3.0)


def setup_inputs(seed: int = 0, part: int = 0) -> dict:
    splits = jax.random.split(jax.random.key(seed), 3)
    part_splits = jax.random.split(jax.random.fold_in(splits[2], part), 3)
    left_outputs = draw_left_outputs(jax.random.fold_in(jax.random.fold_in(splits[2], part), 71), part)
    right_outputs = draw_right_outputs(jax.random.fold_in(jax.random.fold_in(splits[2], part), 71), part)
    return {"left_outputs": left_outputs, "right_outputs": right_outputs}


off_weight = 0.0051

def moment_pair(view):
    value_list = view.astype(jnp.float32)
    column_mean = lax.optimization_barrier(jnp.sum(value_list, axis=0)) / IMAGE_TOTAL
    var = lax.optimization_barrier(jnp.sum(value_list * value_list, axis=0)) / IMAGE_TOTAL - column_mean * column_mean
    inverse_deviation = lax.rsqrt(var + 1e-05)
    standardized_input = (value_list - column_mean) * inverse_deviation
    return (inverse_deviation, standardized_input)

def normalize_backward(incoming_gradient, standardized_input, inverse_deviation):
    first_moment = lax.optimization_barrier(jnp.sum(incoming_gradient, axis=0)) / IMAGE_TOTAL
    second_moment = lax.optimization_barrier(jnp.sum(incoming_gradient * standardized_input, axis=0)) / IMAGE_TOTAL
    return (inverse_deviation * (incoming_gradient - first_moment - standardized_input * second_moment)).astype(jnp.bfloat16)

def reference(left_outputs, right_outputs):
    left_inverse_deviation, standardized_left = moment_pair(left_outputs)
    right_inverse_deviation, standardized_right = moment_pair(right_outputs)
    left_norm = standardized_left.astype(jnp.bfloat16)
    right_norm = standardized_right.astype(jnp.bfloat16)
    corr = jnp.dot(left_norm.T, right_norm, preferred_element_type=jnp.float32) / IMAGE_TOTAL
    quart = FEATURE_COUNT // 4
    half = FEATURE_COUNT // 2
    tiles = []
    for tpos in range(4):
        r = tpos // 2
        s = tpos % 2
        rows_part = corr[half * r:half * (r + 1)]
        tiles.append(jnp.concatenate([rows_part[:, quart * s:quart * (s + 1)], rows_part[:, quart * (s + 2):quart * (s + 3)]], axis=1))
    corr_tiles = jnp.stack(tiles)
    eye = jnp.arange(FEATURE_COUNT)[:, None] == jnp.arange(FEATURE_COUNT)[None, :]
    loss = jnp.sum(jnp.where(eye, (1.0 - corr) ** 2, off_weight * corr * corr)) / FEATURE_COUNT
    dcorr = jnp.where(eye, corr - 1.0, off_weight * corr).astype(jnp.bfloat16)
    normed_grad_left = jnp.dot(right_norm, dcorr.T, preferred_element_type=jnp.float32)
    normed_grad_right = jnp.dot(left_norm, dcorr, preferred_element_type=jnp.float32)
    left_gradient = normalize_backward(normed_grad_left, standardized_left, left_inverse_deviation)
    right_gradient = normalize_backward(normed_grad_right, standardized_right, right_inverse_deviation)
    return (left_gradient, right_gradient, corr_tiles, jnp.reshape(loss, (1,)))
```

```python
import jax
import jax.numpy as jnp
from jax import lax
from jax.sharding import PartitionSpec as P

off_weight = 0.0051


def swapped(block, axis, bit):
    count = lax.axis_size(axis)
    route = []
    for low in range(count):
        high = low | 1 << bit
        if high != low and high < count:
            route += [(low, high), (high, low)]
    return lax.ppermute(block, axis, route)


def pair_views(first_moment, second_moment, row_halves, column_halves):
    other_a = swapped(first_moment, "tile", 0)
    other_b = swapped(second_moment, "tile", 1)
    joined_a = jnp.where(
        column_halves == 0,
        jnp.concatenate([first_moment, other_a], axis=1),
        jnp.concatenate([other_a, first_moment], axis=1),
    )
    joined_b = jnp.where(
        row_halves == 0,
        jnp.concatenate([second_moment, other_b], axis=1),
        jnp.concatenate([other_b, second_moment], axis=1),
    )
    return (joined_a, joined_b)


def moment_pair(total, squares, batch_images):
    column_mean = total / batch_images
    var = squares / batch_images - column_mean * column_mean
    return (column_mean, lax.rsqrt(var + 1e-05))


def col_sums(values):
    as_float = values.astype(jnp.float32)
    return (jnp.sum(as_float, axis=0), jnp.sum(as_float * as_float, axis=0))


def reduced_device(left_outputs, right_outputs):
    rows, quart = left_outputs.shape
    half = 2 * quart
    feats = 4 * quart
    dp_count = lax.axis_size("dp")
    batch_images = rows * dp_count
    tpos = lax.axis_index("tile")
    row_halves = tpos // 2
    column_halves = tpos % 2
    sum_a, sq_a = col_sums(left_outputs)
    sum_b, sq_b = col_sums(right_outputs)
    sum_a, sq_a, sum_b, sq_b = lax.psum((sum_a, sq_a, sum_b, sq_b), "dp")
    left_mean, left_inverse_deviation = moment_pair(sum_a, sq_a, batch_images)
    right_mean, right_inverse_deviation = moment_pair(sum_b, sq_b, batch_images)
    standardized_left = (left_outputs.astype(jnp.float32) - left_mean) * left_inverse_deviation
    standardized_right = (right_outputs.astype(jnp.float32) - right_mean) * right_inverse_deviation
    half_a, cols_b = pair_views(
        standardized_left.astype(jnp.bfloat16),
        standardized_right.astype(jnp.bfloat16),
        row_halves,
        column_halves,
    )
    col_local = jnp.arange(half, dtype=jnp.int32)
    col_ids = quart * column_halves + col_local + jnp.where(col_local >= quart, quart, 0)
    owned = half // dp_count
    picked = half_a
    corr_rows = (
        lax.psum_scatter(
            lax.dot_general(
                picked, cols_b, (((0,), (0,)), ((), ())), preferred_element_type=jnp.float32
            ),
            "dp",
            scatter_dimension=0,
            tiled=True,
        )
        / batch_images
    )
    row_ids = half * row_halves + lax.axis_index("dp") * owned + jnp.arange(owned, dtype=jnp.int32)
    diagonal = row_ids[:, None] == col_ids[None, :]
    part_loss = jnp.sum(
        jnp.where(diagonal, (1.0 - corr_rows) ** 2, off_weight * corr_rows * corr_rows)
    )
    loss = lax.psum(part_loss, ("dp", "tile")) / feats
    dcorr_part = jnp.where(diagonal, corr_rows - 1.0, off_weight * corr_rows).astype(jnp.bfloat16)
    piece = lax.all_gather(dcorr_part, "dp", axis=0, tiled=True)
    block_a = lax.dot_general(
        cols_b, piece, (((1,), (1,)), ((), ())), preferred_element_type=jnp.float32
    )
    picked = half_a
    into_b = jnp.dot(picked, piece, preferred_element_type=jnp.float32)
    other_a = swapped(block_a.astype(jnp.bfloat16), "tile", 0).astype(block_a.dtype)
    other_b = swapped(into_b.astype(jnp.bfloat16), "tile", 1).astype(into_b.dtype)
    normed_grad_left = lax.dynamic_slice_in_dim(block_a + other_a, column_halves * quart, quart, 1)
    normed_grad_right = lax.dynamic_slice_in_dim(into_b + other_b, row_halves * quart, quart, 1)
    first_moment_left, second_moment_left, first_moment_right, second_moment_right = lax.psum(
        (
            jnp.sum(normed_grad_left, axis=0),
            jnp.sum(normed_grad_left * standardized_left, axis=0),
            jnp.sum(normed_grad_right, axis=0),
            jnp.sum(normed_grad_right * standardized_right, axis=0),
        ),
        "dp",
    )
    left_gradient = (
        left_inverse_deviation
        * (
            normed_grad_left
            - first_moment_left / batch_images
            - standardized_left * (second_moment_left / batch_images)
        )
    ).astype(jnp.bfloat16)
    right_gradient = (
        right_inverse_deviation
        * (
            normed_grad_right
            - first_moment_right / batch_images
            - standardized_right * (second_moment_right / batch_images)
        )
    ).astype(jnp.bfloat16)
    return (left_gradient, right_gradient, corr_rows[None, :, :], jnp.reshape(loss, (1,)))


def gathered_device(left_outputs, right_outputs):
    rows, quart = left_outputs.shape
    half = 2 * quart
    feats = 4 * quart
    batch_images = rows * 4
    tpos = lax.axis_index("tile")
    dpos = lax.axis_index("dp")
    row_halves = tpos // 2
    column_halves = tpos % 2
    at_end = (dpos == 0) | (dpos == 3)

    pairs = [(0, 1), (1, 0), (2, 3), (3, 2)]
    middle = [(1, 2), (2, 1)]
    outward = [(1, 0), (2, 3)]

    def chain(block):
        first = lax.ppermute(block, "dp", pairs)
        second_inner = lax.ppermute(block, "dp", middle)
        second_outer = lax.ppermute(second_inner, "dp", outward)
        third_inner = lax.ppermute(first, "dp", middle)
        third_outer = lax.ppermute(third_inner, "dp", outward)
        return [
            block,
            first,
            jnp.where(at_end, second_outer, second_inner),
            jnp.where(at_end, third_outer, third_inner),
        ]

    own_b = chain(right_outputs)
    own_a = chain(left_outputs)

    sum_a, sq_a = col_sums(left_outputs)
    sum_b, sq_b = col_sums(right_outputs)
    sum_a, sq_a, sum_b, sq_b = lax.psum((sum_a, sq_a, sum_b, sq_b), "dp")
    mean_a, rstd_a = moment_pair(sum_a, sq_a, batch_images)
    mean_b, rstd_b = moment_pair(sum_b, sq_b, batch_images)
    stats_a = jnp.stack([mean_a, rstd_a])
    stats_b = jnp.stack([mean_b, rstd_b])
    stats_a = jnp.concatenate([stats_a, swapped(stats_a, "tile", 0)], axis=1)
    stats_b = jnp.concatenate([stats_b, swapped(stats_b, "tile", 1)], axis=1)

    def normalized(own, bit, stats):
        pair = jnp.concatenate([own, swapped(own, "tile", bit)], axis=1)
        return (pair.astype(jnp.float32) - stats[0]) * stats[1]

    total = None
    colsum_a = colsum_b = 0.0
    for step in range(4):
        x_a = normalized(own_a[step], 0, stats_a)
        x_b = normalized(own_b[step], 1, stats_b)
        n_a = x_a.astype(jnp.bfloat16)
        n_b = x_b.astype(jnp.bfloat16)
        if step == 0:
            xhat_a, xhat_b, norm_a, norm_b = x_a, x_b, n_a, n_b
        part = lax.dot_general(
            n_a, n_b, (((0,), (0,)), ((), ())), preferred_element_type=jnp.float32
        )
        total = part if total is None else total + part
        colsum_a = colsum_a + jnp.sum(n_a.astype(jnp.float32), axis=0)
        colsum_b = colsum_b + jnp.sum(n_b.astype(jnp.float32), axis=0)
    corr = total / batch_images

    local = jnp.arange(half, dtype=jnp.int32)
    diagonal = (local[:, None] == local[None, :]) & (local < quart)[:, None]
    part_loss = jnp.sum(jnp.where(diagonal, (1.0 - corr) ** 2, off_weight * corr * corr))
    part_loss = part_loss + swapped(part_loss, "tile", 0)
    part_loss = part_loss + swapped(part_loss, "tile", 1)
    loss = part_loss / feats
    dcorr = jnp.where(diagonal, corr - 1.0, off_weight * corr).astype(jnp.bfloat16)

    wide = dcorr.astype(jnp.float32)
    first_a = jnp.sum(wide * (colsum_b / batch_images)[None, :], axis=1)
    first_b = jnp.sum(wide * (colsum_a / batch_images)[:, None], axis=0)
    product = wide * corr
    second_a = jnp.sum(product, axis=1)
    second_b = jnp.sum(product, axis=0)
    grad_a = lax.dot_general(
        norm_b, dcorr, (((1,), (1,)), ((), ())), preferred_element_type=jnp.float32
    )
    grad_b = jnp.dot(norm_a, dcorr, preferred_element_type=jnp.float32)
    grad_a = grad_a - first_a - xhat_a * second_a
    grad_b = grad_b - first_b - xhat_b * second_b
    other_b = swapped(grad_b[:, quart:].astype(jnp.bfloat16), "tile", 1)
    other_a = swapped(grad_a[:, quart:].astype(jnp.bfloat16), "tile", 0)
    left_gradient = (rstd_a * (grad_a[:, :quart] + other_a.astype(jnp.float32))).astype(
        jnp.bfloat16
    )
    right_gradient = (rstd_b * (grad_b[:, :quart] + other_b.astype(jnp.float32))).astype(
        jnp.bfloat16
    )

    owned = half // 4
    row_quarter = jnp.where(dpos // 2 == column_halves, 0, quart)
    mine = lax.dynamic_slice_in_dim(corr, row_quarter + (dpos % 2) * owned, owned, 0)
    mine = jnp.where(
        row_halves == 0, mine, jnp.concatenate([mine[:, quart:], mine[:, :quart]], axis=1)
    )
    return (left_gradient, right_gradient, mine[None, :, :], jnp.reshape(loss, (1,)))


def solution(mesh):
    per_device = gathered_device if mesh.shape["dp"] == 4 else reduced_device
    return jax.shard_map(
        per_device,
        mesh=mesh,
        in_specs=(P(("groups", "dp"), "tile"), P(("groups", "dp"), "tile")),
        out_specs=(
            P(("groups", "dp"), "tile"),
            P(("groups", "dp"), "tile"),
            P(("groups", "tile"), "dp", None),
            P("groups"),
        ),
        check_vma=False,
    )
```

```python
import jax
import jax.numpy as jnp
from jax import lax
from jax.sharding import PartitionSpec as P

off_weight = 0.0051


def swapped(block, axis, bit):
    count = lax.axis_size(axis)
    route = []
    for low in range(count):
        high = low | 1 << bit
        if high != low and high < count:
            route += [(low, high), (high, low)]
    return lax.ppermute(block, axis, route)


def pair_views(first_moment, second_moment, row_halves, column_halves):
    other_a = swapped(first_moment, "tile", 0)
    other_b = swapped(second_moment, "tile", 1)
    joined_a = jnp.where(
        column_halves == 0,
        jnp.concatenate([first_moment, other_a], axis=1),
        jnp.concatenate([other_a, first_moment], axis=1),
    )
    joined_b = jnp.where(
        row_halves == 0,
        jnp.concatenate([second_moment, other_b], axis=1),
        jnp.concatenate([other_b, second_moment], axis=1),
    )
    return (joined_a, joined_b)


def moment_pair(total, squares, batch_images):
    column_mean = total / batch_images
    var = squares / batch_images - column_mean * column_mean
    return (column_mean, lax.rsqrt(var + 1e-05))


def col_sums(values):
    as_float = values.astype(jnp.float32)
    return (jnp.sum(as_float, axis=0), jnp.sum(as_float * as_float, axis=0))


def reduced_device(left_outputs, right_outputs):
    rows, quart = left_outputs.shape
    half = 2 * quart
    feats = 4 * quart
    dp_count = lax.axis_size("dp")
    batch_images = rows * dp_count
    tpos = lax.axis_index("tile")
    row_halves = tpos // 2
    column_halves = tpos % 2
    sum_a, sq_a = col_sums(left_outputs)
    sum_b, sq_b = col_sums(right_outputs)
    sum_a, sq_a, sum_b, sq_b = lax.psum((sum_a, sq_a, sum_b, sq_b), "dp")
    left_mean, left_inverse_deviation = moment_pair(sum_a, sq_a, batch_images)
    right_mean, right_inverse_deviation = moment_pair(sum_b, sq_b, batch_images)
    standardized_left = (left_outputs.astype(jnp.float32) - left_mean) * left_inverse_deviation
    standardized_right = (right_outputs.astype(jnp.float32) - right_mean) * right_inverse_deviation
    half_a, cols_b = pair_views(
        standardized_left.astype(jnp.bfloat16),
        standardized_right.astype(jnp.bfloat16),
        row_halves,
        column_halves,
    )
    col_local = jnp.arange(half, dtype=jnp.int32)
    col_ids = quart * column_halves + col_local + jnp.where(col_local >= quart, quart, 0)
    owned = half // dp_count
    picked = half_a
    corr_rows = (
        lax.psum_scatter(
            lax.dot_general(
                picked, cols_b, (((0,), (0,)), ((), ())), preferred_element_type=jnp.float32
            ),
            "dp",
            scatter_dimension=0,
            tiled=True,
        )
        / batch_images
    )
    row_ids = half * row_halves + lax.axis_index("dp") * owned + jnp.arange(owned, dtype=jnp.int32)
    diagonal = row_ids[:, None] == col_ids[None, :]
    part_loss = jnp.sum(
        jnp.where(diagonal, (1.0 - corr_rows) ** 2, off_weight * corr_rows * corr_rows)
    )
    loss = lax.psum(part_loss, ("dp", "tile")) / feats
    dcorr_part = jnp.where(diagonal, corr_rows - 1.0, off_weight * corr_rows).astype(jnp.bfloat16)
    piece = lax.all_gather(dcorr_part, "dp", axis=0, tiled=True)
    block_a = lax.dot_general(
        cols_b, piece, (((1,), (1,)), ((), ())), preferred_element_type=jnp.float32
    )
    picked = half_a
    into_b = jnp.dot(picked, piece, preferred_element_type=jnp.float32)
    other_a = swapped(block_a.astype(jnp.bfloat16), "tile", 0).astype(block_a.dtype)
    other_b = swapped(into_b.astype(jnp.bfloat16), "tile", 1).astype(into_b.dtype)
    normed_grad_left = lax.dynamic_slice_in_dim(block_a + other_a, column_halves * quart, quart, 1)
    normed_grad_right = lax.dynamic_slice_in_dim(into_b + other_b, row_halves * quart, quart, 1)
    first_moment_left, second_moment_left, first_moment_right, second_moment_right = lax.psum(
        (
            jnp.sum(normed_grad_left, axis=0),
            jnp.sum(normed_grad_left * standardized_left, axis=0),
            jnp.sum(normed_grad_right, axis=0),
            jnp.sum(normed_grad_right * standardized_right, axis=0),
        ),
        "dp",
    )
    left_gradient = (
        left_inverse_deviation
        * (
            normed_grad_left
            - first_moment_left / batch_images
            - standardized_left * (second_moment_left / batch_images)
        )
    ).astype(jnp.bfloat16)
    right_gradient = (
        right_inverse_deviation
        * (
            normed_grad_right
            - first_moment_right / batch_images
            - standardized_right * (second_moment_right / batch_images)
        )
    ).astype(jnp.bfloat16)
    return (left_gradient, right_gradient, corr_rows[None, :, :], jnp.reshape(loss, (1,)))


def gathered_device(left_outputs, right_outputs):
    rows, quart = left_outputs.shape
    half = 2 * quart
    feats = 4 * quart
    batch_images = rows * 4
    tpos = lax.axis_index("tile")
    dpos = lax.axis_index("dp")
    row_halves = tpos // 2
    column_halves = tpos % 2
    at_end = (dpos == 0) | (dpos == 3)

    pairs = [(0, 1), (1, 0), (2, 3), (3, 2)]
    middle = [(1, 2), (2, 1)]
    outward = [(1, 0), (2, 3)]

    def along(block, route):
        return lax.ppermute(block, "dp", route)

    def chain(block):
        first = along(block, pairs)
        second_inner = along(block, middle)
        second_outer = along(second_inner, outward)
        third_inner = along(first, middle)
        third_outer = along(third_inner, outward)
        return [
            block,
            first,
            jnp.where(at_end, second_outer, second_inner),
            jnp.where(at_end, third_outer, third_inner),
        ]

    def paired(own, bit):
        return jnp.concatenate([own, swapped(own, "tile", bit)], axis=1).astype(jnp.float32)

    partner_a = swapped(left_outputs, "tile", 0)
    left_behind, partner_a = lax.optimization_barrier((left_outputs, partner_a))
    own_b = chain(right_outputs)
    own_a = chain(left_behind)
    raw_a = jnp.concatenate([left_outputs, partner_a], axis=1).astype(jnp.float32)
    raw_b = paired(own_b[0], 1)
    shift_a = jnp.sum(raw_a, axis=0) / rows
    shift_b = jnp.sum(raw_b, axis=0) / rows

    products = None
    sums_a = sums_b = (0.0, 0.0, 0.0)

    def add_sums(sums, centred, rounded):
        return (
            sums[0] + jnp.sum(centred, axis=0),
            sums[1] + jnp.sum(centred * centred, axis=0),
            sums[2] + jnp.sum(rounded.astype(jnp.float32), axis=0),
        )

    for step in range(4):
        c_a = (raw_a if step == 0 else paired(own_a[step], 0)) - shift_a
        c_b = (raw_b if step == 0 else paired(own_b[step], 1)) - shift_b
        u_a = c_a.astype(jnp.bfloat16)
        u_b = c_b.astype(jnp.bfloat16)
        part = lax.dot_general(
            u_a, u_b, (((0,), (0,)), ((), ())), preferred_element_type=jnp.float32
        )
        products = part if products is None else products + part
        sums_a = add_sums(sums_a, c_a, u_a)
        sums_b = add_sums(sums_b, c_b, u_b)

    def moments(sums):
        delta = sums[0] / batch_images
        rstd = lax.rsqrt(sums[1] / batch_images - delta * delta + 1e-05)
        return delta, rstd, (sums[2] / batch_images - delta) * rstd

    delta_a, rstd_a, rest_a = moments(sums_a)
    delta_b, rstd_b, rest_b = moments(sums_b)
    corr = (products / batch_images - delta_a[:, None] * delta_b[None, :]) * (
        rstd_a[:, None] * rstd_b[None, :]
    )
    xhat_a = (raw_a - shift_a - delta_a) * rstd_a
    xhat_b = (raw_b - shift_b - delta_b) * rstd_b
    norm_a = xhat_a.astype(jnp.bfloat16)
    norm_b = xhat_b.astype(jnp.bfloat16)

    local = jnp.arange(half, dtype=jnp.int32)
    diagonal = (local[:, None] == local[None, :]) & (local < quart)[:, None]
    part_loss = jnp.sum(jnp.where(diagonal, (1.0 - corr) ** 2, off_weight * corr * corr))
    part_loss = part_loss + swapped(part_loss, "tile", 0)
    part_loss = part_loss + swapped(part_loss, "tile", 1)
    loss = part_loss / feats
    dcorr = jnp.where(diagonal, corr - 1.0, off_weight * corr).astype(jnp.bfloat16)

    wide = dcorr.astype(jnp.float32)
    first_a = jnp.sum(wide * rest_b[None, :], axis=1)
    first_b = jnp.sum(wide * rest_a[:, None], axis=0)
    product = wide * corr
    second_a = jnp.sum(product, axis=1)
    second_b = jnp.sum(product, axis=0)
    grad_a = lax.dot_general(
        norm_b, dcorr, (((1,), (1,)), ((), ())), preferred_element_type=jnp.float32
    )
    grad_b = jnp.dot(norm_a, dcorr, preferred_element_type=jnp.float32)
    grad_a = grad_a - first_a - xhat_a * second_a
    grad_b = grad_b - first_b - xhat_b * second_b
    other_b = swapped(grad_b[:, quart:].astype(jnp.bfloat16), "tile", 1)
    other_a = swapped(grad_a[:, quart:].astype(jnp.bfloat16), "tile", 0)
    left_gradient = (
        rstd_a[:quart] * (grad_a[:, :quart] + other_a.astype(jnp.float32))
    ).astype(jnp.bfloat16)
    right_gradient = (
        rstd_b[:quart] * (grad_b[:, :quart] + other_b.astype(jnp.float32))
    ).astype(jnp.bfloat16)

    owned = half // 4
    row_quarter = jnp.where(dpos // 2 == column_halves, 0, quart)
    mine = lax.dynamic_slice_in_dim(corr, row_quarter + (dpos % 2) * owned, owned, 0)
    mine = jnp.where(
        row_halves == 0, mine, jnp.concatenate([mine[:, quart:], mine[:, :quart]], axis=1)
    )
    return (left_gradient, right_gradient, mine[None, :, :], jnp.reshape(loss, (1,)))


def solution(mesh):
    per_device = gathered_device if mesh.shape["dp"] == 4 else reduced_device
    return jax.shard_map(
        per_device,
        mesh=mesh,
        in_specs=(P(("groups", "dp"), "tile"), P(("groups", "dp"), "tile")),
        out_specs=(
            P(("groups", "dp"), "tile"),
            P(("groups", "dp"), "tile"),
            P(("groups", "tile"), "dp", None),
            P("groups"),
        ),
        check_vma=False,
    )
```

```python
import functools
import jax
import jax.numpy as jnp
from jax import lax
from jax.experimental import pallas as pl
from jax.experimental.pallas import tpu as pltpu
from jax.sharding import PartitionSpec as P

off_weight = 0.0051


def swapped(block, axis, bit):
    count = lax.axis_size(axis)
    route = []
    for low in range(count):
        high = low | 1 << bit
        if high != low and high < count:
            route += [(low, high), (high, low)]
    return lax.ppermute(block, axis, route)


def pair_views(first_moment, second_moment, row_halves, column_halves):
    other_a = swapped(first_moment, "tile", 0)
    other_b = swapped(second_moment, "tile", 1)
    joined_a = jnp.where(
        column_halves == 0,
        jnp.concatenate([first_moment, other_a], axis=1),
        jnp.concatenate([other_a, first_moment], axis=1),
    )
    joined_b = jnp.where(
        row_halves == 0,
        jnp.concatenate([second_moment, other_b], axis=1),
        jnp.concatenate([other_b, second_moment], axis=1),
    )
    return (joined_a, joined_b)


def moment_pair(total, squares, batch_images):
    column_mean = total / batch_images
    var = squares / batch_images - column_mean * column_mean
    return (column_mean, lax.rsqrt(var + 1e-05))


def col_sums(values):
    as_float = values.astype(jnp.float32)
    return (jnp.sum(as_float, axis=0), jnp.sum(as_float * as_float, axis=0))


def reduced_device(left_outputs, right_outputs):
    rows, quart = left_outputs.shape
    half = 2 * quart
    feats = 4 * quart
    dp_count = lax.axis_size("dp")
    batch_images = rows * dp_count
    tpos = lax.axis_index("tile")
    row_halves = tpos // 2
    column_halves = tpos % 2
    sum_a, sq_a = col_sums(left_outputs)
    sum_b, sq_b = col_sums(right_outputs)
    sum_a, sq_a, sum_b, sq_b = lax.psum((sum_a, sq_a, sum_b, sq_b), "dp")
    left_mean, left_inverse_deviation = moment_pair(sum_a, sq_a, batch_images)
    right_mean, right_inverse_deviation = moment_pair(sum_b, sq_b, batch_images)
    standardized_left = (left_outputs.astype(jnp.float32) - left_mean) * left_inverse_deviation
    standardized_right = (right_outputs.astype(jnp.float32) - right_mean) * right_inverse_deviation
    half_a, cols_b = pair_views(
        standardized_left.astype(jnp.bfloat16),
        standardized_right.astype(jnp.bfloat16),
        row_halves,
        column_halves,
    )
    col_local = jnp.arange(half, dtype=jnp.int32)
    col_ids = quart * column_halves + col_local + jnp.where(col_local >= quart, quart, 0)
    owned = half // dp_count
    picked = half_a
    corr_rows = (
        lax.psum_scatter(
            lax.dot_general(
                picked, cols_b, (((0,), (0,)), ((), ())), preferred_element_type=jnp.float32
            ),
            "dp",
            scatter_dimension=0,
            tiled=True,
        )
        / batch_images
    )
    row_ids = half * row_halves + lax.axis_index("dp") * owned + jnp.arange(owned, dtype=jnp.int32)
    diagonal = row_ids[:, None] == col_ids[None, :]
    part_loss = jnp.sum(
        jnp.where(diagonal, (1.0 - corr_rows) ** 2, off_weight * corr_rows * corr_rows)
    )
    loss = lax.psum(part_loss, ("dp", "tile")) / feats
    dcorr_part = jnp.where(diagonal, corr_rows - 1.0, off_weight * corr_rows).astype(jnp.bfloat16)
    piece = lax.all_gather(dcorr_part, "dp", axis=0, tiled=True)
    block_a = lax.dot_general(
        cols_b, piece, (((1,), (1,)), ((), ())), preferred_element_type=jnp.float32
    )
    picked = half_a
    into_b = jnp.dot(picked, piece, preferred_element_type=jnp.float32)
    other_a = swapped(block_a.astype(jnp.bfloat16), "tile", 0).astype(block_a.dtype)
    other_b = swapped(into_b.astype(jnp.bfloat16), "tile", 1).astype(into_b.dtype)
    normed_grad_left = lax.dynamic_slice_in_dim(block_a + other_a, column_halves * quart, quart, 1)
    normed_grad_right = lax.dynamic_slice_in_dim(into_b + other_b, row_halves * quart, quart, 1)
    first_moment_left, second_moment_left, first_moment_right, second_moment_right = lax.psum(
        (
            jnp.sum(normed_grad_left, axis=0),
            jnp.sum(normed_grad_left * standardized_left, axis=0),
            jnp.sum(normed_grad_right, axis=0),
            jnp.sum(normed_grad_right * standardized_right, axis=0),
        ),
        "dp",
    )
    left_gradient = (
        left_inverse_deviation
        * (
            normed_grad_left
            - first_moment_left / batch_images
            - standardized_left * (second_moment_left / batch_images)
        )
    ).astype(jnp.bfloat16)
    right_gradient = (
        right_inverse_deviation
        * (
            normed_grad_right
            - first_moment_right / batch_images
            - standardized_right * (second_moment_right / batch_images)
        )
    ).astype(jnp.bfloat16)
    return (left_gradient, right_gradient, corr_rows[None, :, :], jnp.reshape(loss, (1,)))


def tile_scaled(sums, delta_col, rstd_col, delta_row, rstd_row, inverse_images):
    return (sums * inverse_images - delta_col * delta_row) * rstd_col * rstd_row


def centre_rows(source, shift, target, lanes, chunk):
    rows, width = source.shape
    zero = jnp.zeros((8, width), jnp.float32)

    def body(step, carry):
        total, squares, rounded = carry
        at = pl.ds(pl.multiple_of(step * chunk, chunk), chunk)
        centred = source[at, :].astype(jnp.float32) - shift
        low = centred.astype(jnp.bfloat16)
        target[at, lanes] = low
        fold = lambda v: jnp.sum(v.reshape(chunk // 8, 8, width), axis=0)
        return (
            total + fold(centred),
            squares + fold(centred * centred),
            rounded + fold(low.astype(jnp.float32)),
        )

    sums = lax.fori_loop(0, rows // chunk, body, (zero, zero, zero), unroll=True)
    return [jnp.sum(s, axis=0, keepdims=True) for s in sums]


def normalise_rows(source, offset, rstd, target, lanes, chunk):
    rows = source.shape[0]

    def body(step, carry):
        at = pl.ds(pl.multiple_of(step * chunk, chunk), chunk)
        target[at, lanes] = ((source[at, :].astype(jnp.float32) - offset) * rstd).astype(
            jnp.bfloat16
        )
        return carry

    lax.fori_loop(0, rows // chunk, body, 0, unroll=True)


def lanes_to_row(partial):
    ones = jnp.ones((16, partial.shape[1]), jnp.bfloat16)
    high = partial.astype(jnp.bfloat16)
    low = (partial - high.astype(jnp.float32)).astype(jnp.bfloat16)
    contract = (((1,), (1,)), ((), ()))
    row = lax.dot_general(ones, high, contract, preferred_element_type=jnp.float32)
    row = row + lax.dot_general(ones, low, contract, preferred_element_type=jnp.float32)
    return row[:1, :]


def fold_lanes(values):
    width = values.shape[1]
    return sum(values[:, at : at + 128] for at in range(0, width, 128))


def partner_kernel(
    images,
    own_tile,
    late_a,
    late_other,
    first_a,
    first_other,
    row_a,
    prev,
    late_b,
    col_b,
    norm_b,
    partial_out,
    dcorr_out,
    mine_out,
    vec_out,
    centred,
    norms,
):
    rows, quart = late_a.shape
    half = 2 * quart
    inverse = 1.0 / images
    shift = row_a[0:1, :]
    own = centre_rows(late_a, shift[:, :quart], centred, slice(0, quart), 64)
    other = centre_rows(late_other, shift[:, quart:], centred, slice(quart, half), 64)
    total, squares, rounded = [
        row_a[i + 1 : i + 2, :] + jnp.concatenate([own[i], other[i]], axis=1) for i in range(3)
    ]
    delta = total * inverse
    rstd = lax.rsqrt(squares * inverse - delta * delta + 1e-05)
    rest = (rounded * inverse - delta) * rstd
    offset = shift + delta
    normalise_rows(first_a, offset[:, :quart], rstd[:, :quart], norms, slice(0, quart), 64)
    normalise_rows(first_other, offset[:, quart:], rstd[:, quart:], norms, slice(quart, half), 64)
    norms[rows : rows + 16, :] = jnp.broadcast_to(rest, (16, half)).astype(jnp.bfloat16)

    delta_col = col_b[:, 0:1]
    rstd_col = col_b[:, 1:2]
    width = half // 4
    across = jnp.zeros((quart, 128), jnp.float32)
    down = []
    for tile in range(4):
        at = slice(tile * width, (tile + 1) * width)
        sums = prev[:, at] + jnp.dot(
            late_b[...], centred[:, at], preferred_element_type=jnp.float32
        )
        corr = tile_scaled(sums, delta_col, rstd_col, delta[:, at], rstd[:, at], inverse)
        dcorr = off_weight * corr
        dcorr_out[:, at] = dcorr.astype(jnp.bfloat16)
        product = dcorr * corr
        across = across + fold_lanes(product)
        down.append(jnp.sum(product, axis=0, keepdims=True))

        @pl.when(own_tile[0] == tile)
        def _():
            mine_out[...] = corr

    vec_out[0:1, :] = delta
    vec_out[1:2, :] = rstd
    vec_out[2:3, :] = rest
    vec_out[3:4, :] = jnp.concatenate(down, axis=1)
    vec_out[4:8, :] = jnp.zeros((4, half), jnp.float32)
    second = lanes_to_row(across)
    contract = (((1,), (1,)), ((), ()))
    for tile in range(2):
        at = slice(tile * width, (tile + 1) * width)
        terms = lax.dot_general(
            norms[...], dcorr_out[at, :], contract, preferred_element_type=jnp.float32
        )
        partial_out[:, at] = (
            terms[:rows]
            - terms[rows : rows + 1]
            - norm_b[:, at].astype(jnp.float32) * second[:, at]
        ).astype(jnp.bfloat16)


def own_kernel(
    images,
    own_tile,
    late_a,
    late_other,
    first_a,
    first_other,
    row_a,
    prev,
    late_b,
    col_b,
    norm_b,
    first_b,
    row_b,
    partner_dcorr,
    partner_mine,
    vec_a,
    right_out,
    left_out,
    left_partial_out,
    mine_out,
    loss_out,
    centred,
    norms,
    dcorr_own,
    mine_own,
):
    rows, quart = late_a.shape
    half = 2 * quart
    inverse = 1.0 / images
    shift = row_a[0:1, :]
    delta = vec_a[0:1, :]
    rstd = vec_a[1:2, :]
    rest = vec_a[2:3, :]
    offset = shift + delta
    for source, lanes in ((late_a, slice(0, quart)), (late_other, slice(quart, half))):
        normalise_rows(source, shift[:, lanes], 1.0, centred, lanes, 64)
    for source, lanes in ((first_a, slice(0, quart)), (first_other, slice(quart, half))):
        normalise_rows(source, offset[:, lanes], rstd[:, lanes], norms, lanes, 64)
    norms[rows : rows + 16, :] = jnp.broadcast_to(rest, (16, half)).astype(jnp.bfloat16)

    delta_col = col_b[:, 0:1]
    rstd_col = col_b[:, 1:2]
    width = half // 4
    across = jnp.zeros((quart, 128), jnp.float32)
    losses = jnp.zeros((8, 128), jnp.float32)
    down = []
    for tile in range(4):
        at = slice(tile * width, (tile + 1) * width)
        sums = prev[:, at] + jnp.dot(
            late_b[...], centred[:, at], preferred_element_type=jnp.float32
        )
        corr = tile_scaled(sums, delta_col, rstd_col, delta[:, at], rstd[:, at], inverse)
        dcorr = off_weight * corr
        product = dcorr * corr
        loss = product
        if tile < 2:
            feature = lax.broadcasted_iota(jnp.int32, (quart, width), 0)
            lane = lax.broadcasted_iota(jnp.int32, (quart, width), 1) + tile * width
            diagonal = feature == lane
            dcorr = jnp.where(diagonal, corr - 1.0, dcorr)
            product = dcorr * corr
            loss = jnp.where(diagonal, dcorr * dcorr, product)
        dcorr_own[:, at] = dcorr.astype(jnp.bfloat16)
        across = across + fold_lanes(product)
        folded = fold_lanes(loss)
        losses = losses + jnp.sum(folded.reshape(quart // 8, 8, 128), axis=0)
        down.append(jnp.sum(product, axis=0, keepdims=True))

        @pl.when(own_tile[0] == tile)
        def _():
            mine_own[...] = corr

    second_a = vec_a[3:4, :] + jnp.concatenate(down, axis=1)
    second_b = lanes_to_row(across)
    total_loss = jnp.sum(losses, keepdims=True) + jnp.sum(vec_a[3:4, :], keepdims=True)
    loss_out[...] = jnp.broadcast_to(total_loss, (8, 128))

    for tile in (2, 3, 0, 1):
        at = slice(tile * width, (tile + 1) * width)
        terms = jnp.dot(
            norm_b[:, :quart], dcorr_own[:, at], preferred_element_type=jnp.float32
        ) + jnp.dot(norm_b[:, quart:], partner_dcorr[:, at], preferred_element_type=jnp.float32)
        source = first_a if tile < 2 else first_other
        inner = slice((tile % 2) * width, (tile % 2 + 1) * width)
        xhat = (source[:, inner].astype(jnp.float32) - offset[:, at]) * rstd[:, at]
        value = terms[:rows] - terms[rows : rows + 1] - xhat * second_a[:, at]
        if tile < 2:
            left_out[:, inner] = value
        else:
            left_partial_out[:, inner] = value.astype(jnp.bfloat16)

    contract = (((1,), (1,)), ((), ()))
    for tile in range(2):
        at = slice(tile * width, (tile + 1) * width)
        terms = lax.dot_general(
            norms[...], dcorr_own[at, :], contract, preferred_element_type=jnp.float32
        )
        xhat = (first_b[:, at].astype(jnp.float32) - row_b[0:1, at]) * row_b[1:2, at]
        right_out[:, at] = terms[:rows] - terms[rows : rows + 1] - xhat * second_b[:, at]

    own_columns = jnp.transpose(mine_own[...])
    partner_columns = jnp.transpose(partner_mine[...])

    @pl.when(own_tile[1] == 0)
    def _():
        mine_out[:, :quart] = own_columns
        mine_out[:, quart:] = partner_columns

    @pl.when(own_tile[1] != 0)
    def _():
        mine_out[:, :quart] = partner_columns
        mine_out[:, quart:] = own_columns


vmem = pl.BlockSpec(memory_space=pltpu.VMEM)
smem = pl.BlockSpec(memory_space=pltpu.SMEM)


def local_call(kernel, scalars, operands, outs, scratch, flops):
    moved = sum(x.size * x.dtype.itemsize for x in (*operands, *outs))
    return pl.pallas_call(
        kernel,
        out_shape=outs,
        in_specs=[smem] + [vmem] * len(operands),
        out_specs=[vmem] * len(outs),
        scratch_shapes=scratch,
        compiler_params=pltpu.CompilerParams(vmem_limit_bytes=28 * 2**20),
        cost_estimate=pl.CostEstimate(flops=flops, bytes_accessed=moved, transcendentals=0),
    )(scalars, *operands)


def gathered_device(left_outputs, right_outputs):
    rows, quart = left_outputs.shape
    half = 2 * quart
    feats = 4 * quart
    batch_images = rows * 4
    tpos = lax.axis_index("tile")
    dpos = lax.axis_index("dp")
    row_halves = tpos // 2
    column_halves = tpos % 2
    at_end = (dpos == 0) | (dpos == 3)

    pairs = [(0, 1), (1, 0), (2, 3), (3, 2)]
    middle = [(1, 2), (2, 1)]
    outward = [(1, 0), (2, 3)]

    def along(block, route):
        return lax.ppermute(block, "dp", route)

    def core_swap(block):
        return swapped(block, "tile", 0)

    def x_swap(block):
        return swapped(block, "tile", 1)

    other_a0 = core_swap(left_outputs)
    left_behind, other_a0 = lax.optimization_barrier((left_outputs, other_a0))

    first_b = along(right_outputs, pairs)
    inner_b = along(right_outputs, middle)
    other_b0 = x_swap(right_outputs)
    first_a = along(left_behind, pairs)
    inner_a = along(left_behind, middle)

    outer_b = along(inner_b, outward)
    third_b = along(first_b, middle)
    other_b1 = x_swap(first_b)
    outer_a = along(inner_a, outward)
    third_a = along(first_a, middle)
    other_a1 = core_swap(first_a)

    last_b = along(third_b, outward)
    second_b = jnp.where(at_end, outer_b, inner_b)
    other_b2 = x_swap(second_b)
    third_a, other_b1, other_a1 = lax.optimization_barrier((third_a, other_b1, other_a1))
    last_a = along(third_a, outward)
    second_a = jnp.where(at_end, outer_a, inner_a)
    other_a2 = core_swap(second_a)
    late_b = jnp.where(at_end, last_b, third_b)
    other_b3 = x_swap(late_b)

    def paired(own, other):
        return jnp.concatenate([own, other], axis=1).astype(jnp.float32)

    raw_a = [paired(*p) for p in ((left_outputs, other_a0), (first_a, other_a1), (second_a, other_a2))]
    raw_b = [
        paired(*p)
        for p in (
            (right_outputs, other_b0),
            (first_b, other_b1),
            (second_b, other_b2),
            (late_b, other_b3),
        )
    ]
    shift_a = jnp.sum(raw_a[0], axis=0) / rows
    shift_b = jnp.sum(raw_b[0], axis=0) / rows
    centred_a = [x - shift_a for x in raw_a]
    centred_b = [x - shift_b for x in raw_b]
    low_a = [x.astype(jnp.bfloat16) for x in centred_a]
    low_b = [x.astype(jnp.bfloat16) for x in centred_b]

    def three_sums(centred, low):
        return (
            sum(jnp.sum(x, axis=0) for x in centred),
            sum(jnp.sum(x * x, axis=0) for x in centred),
            sum(jnp.sum(x.astype(jnp.float32), axis=0) for x in low),
        )

    prev = sum(
        lax.dot_general(y, x, (((0,), (0,)), ((), ())), preferred_element_type=jnp.float32)
        for x, y in zip(low_a, low_b)
    )
    sums_a = three_sums(centred_a, low_a)
    sums_b = three_sums(centred_b, low_b)
    delta_b = sums_b[0] / batch_images
    rstd_b = lax.rsqrt(sums_b[1] / batch_images - delta_b * delta_b + 1e-05)
    rest_b = (sums_b[2] / batch_images - delta_b) * rstd_b
    norm_b = ((centred_b[0] - delta_b) * rstd_b).astype(jnp.bfloat16)
    norm_b = jnp.concatenate(
        [norm_b, jnp.broadcast_to(rest_b.astype(jnp.bfloat16), (16, half))], axis=0
    )
    late_low_b = low_b[3].T
    col_b = jnp.stack([delta_b, rstd_b], axis=1)
    row_b = jnp.stack([shift_b + delta_b, rstd_b] + [rest_b] * 6)
    row_a = jnp.stack([shift_a, *sums_a] + [shift_a] * 4)

    late_a = jnp.where(at_end, last_a, third_a)
    (late_a, prev_own, prev_other, late_low_own, late_low_other, col_own, col_other, norm_b, norm_b_other, row_a, row_b) = (
        lax.optimization_barrier(
            (
                late_a,
                prev[:quart],
                prev[quart:],
                late_low_b[:quart],
                late_low_b[quart:],
                col_b[:quart],
                col_b[quart:],
                norm_b,
                norm_b[:rows, quart:],
                row_a,
                row_b,
            )
        )
    )
    other_a3 = core_swap(late_a)

    owned_tile = jnp.where(dpos // 2 == column_halves, 0, 2) + dpos % 2
    scalars = jnp.stack([owned_tile, row_halves]).astype(jnp.int32)
    quarter_f32 = jax.ShapeDtypeStruct((rows, quart), jnp.float32)
    quarter_bf16 = jax.ShapeDtypeStruct((rows, quart), jnp.bfloat16)
    width = half // 4
    wide_low = pltpu.VMEM((rows, half), jnp.bfloat16)
    wide_ext = pltpu.VMEM((rows + 16, half), jnp.bfloat16)
    gemm = 2 * rows * half * quart
    partial_right, dcorr_other, mine_other, vec_a = local_call(
        functools.partial(partner_kernel, batch_images),
        scalars,
        (
            late_a,
            other_a3,
            left_outputs,
            other_a0,
            row_a,
            prev_other,
            late_low_other,
            col_other,
            norm_b_other,
        ),
        (
            quarter_bf16,
            jax.ShapeDtypeStruct((quart, half), jnp.bfloat16),
            jax.ShapeDtypeStruct((quart, width), jnp.float32),
            jax.ShapeDtypeStruct((8, half), jnp.float32),
        ),
        [wide_low, wide_ext],
        2 * gemm,
    )
    from_x = x_swap(partial_right)
    right_own, left_own, partial_left, mine, part_loss = local_call(
        functools.partial(own_kernel, batch_images),
        scalars,
        (
            late_a,
            other_a3,
            left_outputs,
            other_a0,
            row_a,
            prev_own,
            late_low_own,
            col_own,
            norm_b,
            right_outputs,
            row_b,
            dcorr_other,
            mine_other,
            vec_a,
        ),
        (
            quarter_f32,
            quarter_f32,
            quarter_bf16,
            jax.ShapeDtypeStruct((width, half), jnp.float32),
            jax.ShapeDtypeStruct((8, 128), jnp.float32),
        ),
        [
            wide_low,
            wide_ext,
            pltpu.VMEM((quart, half), jnp.bfloat16),
            pltpu.VMEM((quart, width), jnp.float32),
        ],
        4 * gemm,
    )
    from_core = core_swap(partial_left)
    loss = part_loss + core_swap(part_loss)
    left_gradient = (vec_a[1, :quart] * (left_own + from_core.astype(jnp.float32))).astype(
        jnp.bfloat16
    )
    loss, left_gradient, from_x = lax.optimization_barrier((loss, left_gradient, from_x))
    loss = loss + x_swap(loss)
    right_gradient = (row_b[1, :quart] * (right_own + from_x.astype(jnp.float32))).astype(
        jnp.bfloat16
    )
    return (left_gradient, right_gradient, mine[None, :, :], loss[0, :1] / feats)


def solution(mesh):
    per_device = gathered_device if mesh.shape["dp"] == 4 else reduced_device
    return jax.shard_map(
        per_device,
        mesh=mesh,
        in_specs=(P(("groups", "dp"), "tile"), P(("groups", "dp"), "tile")),
        out_specs=(
            P(("groups", "dp"), "tile"),
            P(("groups", "dp"), "tile"),
            P(("groups", "tile"), "dp", None),
            P("groups"),
        ),
        check_vma=False,
    )
```

```python
import functools
import jax
import jax.numpy as jnp
from jax import lax
from jax.experimental import pallas as pl
from jax.experimental.pallas import tpu as pltpu
from jax.sharding import PartitionSpec as P

off_weight = 0.0051


def swapped(block, axis, bit):
    count = lax.axis_size(axis)
    route = []
    for low in range(count):
        high = low | 1 << bit
        if high != low and high < count:
            route += [(low, high), (high, low)]
    return lax.ppermute(block, axis, route)


def pair_views(first_moment, second_moment, row_halves, column_halves):
    other_a = swapped(first_moment, "tile", 0)
    other_b = swapped(second_moment, "tile", 1)
    joined_a = jnp.where(
        column_halves == 0,
        jnp.concatenate([first_moment, other_a], axis=1),
        jnp.concatenate([other_a, first_moment], axis=1),
    )
    joined_b = jnp.where(
        row_halves == 0,
        jnp.concatenate([second_moment, other_b], axis=1),
        jnp.concatenate([other_b, second_moment], axis=1),
    )
    return (joined_a, joined_b)


def moment_pair(total, squares, batch_images):
    column_mean = total / batch_images
    var = squares / batch_images - column_mean * column_mean
    return (column_mean, lax.rsqrt(var + 1e-05))


def col_sums(values):
    as_float = values.astype(jnp.float32)
    return (jnp.sum(as_float, axis=0), jnp.sum(as_float * as_float, axis=0))


def reduced_device(left_outputs, right_outputs):
    rows, quart = left_outputs.shape
    half = 2 * quart
    feats = 4 * quart
    dp_count = lax.axis_size("dp")
    batch_images = rows * dp_count
    tpos = lax.axis_index("tile")
    row_halves = tpos // 2
    column_halves = tpos % 2
    sum_a, sq_a = col_sums(left_outputs)
    sum_b, sq_b = col_sums(right_outputs)
    sum_a, sq_a, sum_b, sq_b = lax.psum((sum_a, sq_a, sum_b, sq_b), "dp")
    left_mean, left_inverse_deviation = moment_pair(sum_a, sq_a, batch_images)
    right_mean, right_inverse_deviation = moment_pair(sum_b, sq_b, batch_images)
    standardized_left = (left_outputs.astype(jnp.float32) - left_mean) * left_inverse_deviation
    standardized_right = (right_outputs.astype(jnp.float32) - right_mean) * right_inverse_deviation
    half_a, cols_b = pair_views(
        standardized_left.astype(jnp.bfloat16),
        standardized_right.astype(jnp.bfloat16),
        row_halves,
        column_halves,
    )
    col_local = jnp.arange(half, dtype=jnp.int32)
    col_ids = quart * column_halves + col_local + jnp.where(col_local >= quart, quart, 0)
    owned = half // dp_count
    picked = half_a
    corr_rows = (
        lax.psum_scatter(
            lax.dot_general(
                picked, cols_b, (((0,), (0,)), ((), ())), preferred_element_type=jnp.float32
            ),
            "dp",
            scatter_dimension=0,
            tiled=True,
        )
        / batch_images
    )
    row_ids = half * row_halves + lax.axis_index("dp") * owned + jnp.arange(owned, dtype=jnp.int32)
    diagonal = row_ids[:, None] == col_ids[None, :]
    part_loss = jnp.sum(
        jnp.where(diagonal, (1.0 - corr_rows) ** 2, off_weight * corr_rows * corr_rows)
    )
    loss = lax.psum(part_loss, ("dp", "tile")) / feats
    dcorr_part = jnp.where(diagonal, corr_rows - 1.0, off_weight * corr_rows).astype(jnp.bfloat16)
    piece = lax.all_gather(dcorr_part, "dp", axis=0, tiled=True)
    block_a = lax.dot_general(
        cols_b, piece, (((1,), (1,)), ((), ())), preferred_element_type=jnp.float32
    )
    picked = half_a
    into_b = jnp.dot(picked, piece, preferred_element_type=jnp.float32)
    other_a = swapped(block_a.astype(jnp.bfloat16), "tile", 0).astype(block_a.dtype)
    other_b = swapped(into_b.astype(jnp.bfloat16), "tile", 1).astype(into_b.dtype)
    normed_grad_left = lax.dynamic_slice_in_dim(block_a + other_a, column_halves * quart, quart, 1)
    normed_grad_right = lax.dynamic_slice_in_dim(into_b + other_b, row_halves * quart, quart, 1)
    first_moment_left, second_moment_left, first_moment_right, second_moment_right = lax.psum(
        (
            jnp.sum(normed_grad_left, axis=0),
            jnp.sum(normed_grad_left * standardized_left, axis=0),
            jnp.sum(normed_grad_right, axis=0),
            jnp.sum(normed_grad_right * standardized_right, axis=0),
        ),
        "dp",
    )
    left_gradient = (
        left_inverse_deviation
        * (
            normed_grad_left
            - first_moment_left / batch_images
            - standardized_left * (second_moment_left / batch_images)
        )
    ).astype(jnp.bfloat16)
    right_gradient = (
        right_inverse_deviation
        * (
            normed_grad_right
            - first_moment_right / batch_images
            - standardized_right * (second_moment_right / batch_images)
        )
    ).astype(jnp.bfloat16)
    return (left_gradient, right_gradient, corr_rows[None, :, :], jnp.reshape(loss, (1,)))


def tile_scaled(sums, delta_col, rstd_col, delta_row, rstd_row, inverse_images):
    return (sums * inverse_images - delta_col * delta_row) * rstd_col * rstd_row


def centre_rows(source, shift, target, lanes, chunk):
    rows, width = source.shape
    zero = jnp.zeros((8, width), jnp.float32)

    def body(step, carry):
        total, squares, rounded = carry
        at = pl.ds(pl.multiple_of(step * chunk, chunk), chunk)
        centred = source[at, :].astype(jnp.float32) - shift
        low = centred.astype(jnp.bfloat16)
        target[at, lanes] = low
        fold = lambda v: jnp.sum(v.reshape(chunk // 8, 8, width), axis=0)
        return (
            total + fold(centred),
            squares + fold(centred * centred),
            rounded + fold(low.astype(jnp.float32)),
        )

    sums = lax.fori_loop(0, rows // chunk, body, (zero, zero, zero), unroll=True)
    return [jnp.sum(s, axis=0, keepdims=True) for s in sums]


def normalise_rows(source, offset, rstd, target, lanes, chunk):
    rows = source.shape[0]

    def body(step, carry):
        at = pl.ds(pl.multiple_of(step * chunk, chunk), chunk)
        target[at, lanes] = ((source[at, :].astype(jnp.float32) - offset) * rstd).astype(
            jnp.bfloat16
        )
        return carry

    lax.fori_loop(0, rows // chunk, body, 0, unroll=True)


def lanes_to_row(partial):
    ones = jnp.ones((16, partial.shape[1]), jnp.bfloat16)
    high = partial.astype(jnp.bfloat16)
    low = (partial - high.astype(jnp.float32)).astype(jnp.bfloat16)
    contract = (((1,), (1,)), ((), ()))
    row = lax.dot_general(ones, high, contract, preferred_element_type=jnp.float32)
    row = row + lax.dot_general(ones, low, contract, preferred_element_type=jnp.float32)
    return row[:1, :]


def three_parts(row):
    high = row.astype(jnp.bfloat16)
    rest = row - high.astype(jnp.float32)
    middle = rest.astype(jnp.bfloat16)
    low = (rest - middle.astype(jnp.float32)).astype(jnp.bfloat16)
    return [high, middle, low]


def joined_parts(ref, at):
    parts = ref[at : at + 16, :].astype(jnp.float32)
    return [parts[3 * i : 3 * i + 1] + parts[3 * i + 1 : 3 * i + 2] + parts[3 * i + 2 : 3 * i + 3] for i in range(4)]


def moments(sums, images):
    total, squares, rounded = sums
    delta = total / images
    rstd = lax.rsqrt(squares / images - delta * delta + 1e-05)
    return delta, rstd, (rounded / images - delta) * rstd


def fold_lanes(values):
    width = values.shape[1]
    return sum(values[:, at : at + 128] for at in range(0, width, 128))


def late_right_kernel(images, late, row, out, stats):
    rows, quart = late.shape
    shift = row[0:1, :]
    zero = jnp.zeros((8, quart), jnp.float32)
    sums = [zero, zero, zero]
    fold = lambda v: jnp.sum(v.reshape(v.shape[0] // 8, 8, quart), axis=0)
    for at in range(0, rows, 128):
        centred = late[at : at + 128, :].astype(jnp.float32) - shift
        low = centred.astype(jnp.bfloat16)
        out[:quart, at : at + 128] = jnp.transpose(low)
        sums = [
            sums[0] + fold(centred),
            sums[1] + fold(centred * centred),
            sums[2] + fold(low.astype(jnp.float32)),
        ]
    sums = [row[i + 1 : i + 2, :] + jnp.sum(s, axis=0, keepdims=True) for i, s in enumerate(sums)]
    delta, rstd, rest = moments(sums, images)
    values = [shift + delta, rstd, rest, delta]
    stats[...] = jnp.concatenate(values + [jnp.zeros((4, quart), jnp.float32)], axis=0)
    parts = sum([three_parts(v) for v in values], [])
    parts = [p.astype(jnp.float32) for p in parts] + [jnp.zeros((4, quart), jnp.float32)]
    out[quart:, :] = jnp.concatenate(parts, axis=0).astype(jnp.bfloat16)


def partner_kernel(images, part, own_tile, late, first, row, sums_all, late_b, first_b, *refs):
    if part:
        (terms_in, across_in, partial_out, dcorr_out, mine_out, vec_out, centred, norms) = refs
    else:
        (terms_out, across_out, dcorr_out, mine_out, vec_out, centred, norms) = refs
    rows, quart = late.shape
    inverse = 1.0 / images
    shift = row[0:1, :]
    everything = slice(0, quart)
    sums = centre_rows(late, shift, centred, everything, 64)
    delta, rstd, rest = moments([row[i + 1 : i + 2, :] + sums[i] for i in range(3)], images)
    normalise_rows(first, shift + delta, rstd, norms, everything, 64)
    norms[rows : rows + 16, :] = jnp.broadcast_to(rest, (16, quart)).astype(jnp.bfloat16)

    offset_b, rstd_b, _, delta_b = joined_parts(late_b, quart)
    columns = jnp.transpose(
        jnp.concatenate([delta_b, rstd_b, jnp.zeros((6, quart), jnp.float32)], axis=0)
    )
    delta_col = columns[:, 0:1]
    rstd_col = columns[:, 1:2]
    width = quart // 2
    across = across_in[...] if part else jnp.zeros((quart, 128), jnp.float32)
    for tile in range(2):
        at = slice(tile * width, (tile + 1) * width)
        wide = slice(part * quart + tile * width, part * quart + (tile + 1) * width)
        sums = sums_all[quart:, wide] + jnp.dot(
            late_b[:quart, :], centred[:, at], preferred_element_type=jnp.float32
        )
        corr = tile_scaled(sums, delta_col, rstd_col, delta[:, at], rstd[:, at], inverse)
        dcorr = off_weight * corr
        dcorr_out[:, at] = dcorr.astype(jnp.bfloat16)
        product = dcorr * corr
        across = across + fold_lanes(product)
        vec_out[3:4, at] = jnp.sum(product, axis=0, keepdims=True)

        @pl.when(own_tile[0] == 2 * part + tile)
        def _():
            mine_out[...] = corr

    vec_out[0:1, :] = delta
    vec_out[1:2, :] = rstd
    vec_out[2:3, :] = rest
    vec_out[4:8, :] = jnp.zeros((4, quart), jnp.float32)
    contract = (((1,), (1,)), ((), ()))
    if part:
        second = lanes_to_row(across)
    else:
        across_out[...] = across
    for tile in range(2):
        at = slice(tile * width, (tile + 1) * width)
        terms = lax.dot_general(
            norms[...], dcorr_out[at, :], contract, preferred_element_type=jnp.float32
        )
        if part:
            terms = terms + terms_in[:, at]
            xhat = (first_b[:, at].astype(jnp.float32) - offset_b[:, at]) * rstd_b[:, at]
            partial_out[:, at] = (
                terms[:rows] - terms[rows : rows + 1] - xhat * second[:, at]
            ).astype(jnp.bfloat16)
        else:
            terms_out[:, at] = terms


def own_kernel(
    images,
    own_tile,
    late_own,
    late_other,
    first_own,
    first_other,
    row_own,
    row_other,
    sums_all,
    late_b,
    late_b_other,
    first_b,
    first_b_other,
    dcorr_left,
    dcorr_right,
    mine_left,
    mine_right,
    vec_own,
    vec_other,
    right_out,
    left_out,
    left_partial_out,
    mine_out,
    loss_out,
    centred,
    norms,
    norm_b,
    dcorr_own,
    mine_own,
):
    rows, quart = late_own.shape
    half = 2 * quart
    inverse = 1.0 / images
    both = lambda i: jnp.concatenate([vec_own[i : i + 1, :], vec_other[i : i + 1, :]], axis=1)
    delta, rstd, rest, second_partner = [both(i) for i in range(4)]
    shift = jnp.concatenate([row_own[0:1, :], row_other[0:1, :]], axis=1)
    offset = shift + delta
    left, right = slice(0, quart), slice(quart, half)
    for source, lanes in ((late_own, left), (late_other, right)):
        normalise_rows(source, shift[:, lanes], 1.0, centred, lanes, 64)
    for source, lanes in ((first_own, left), (first_other, right)):
        normalise_rows(source, offset[:, lanes], rstd[:, lanes], norms, lanes, 64)
    norms[rows : rows + 16, :] = jnp.broadcast_to(rest, (16, half)).astype(jnp.bfloat16)
    own_b = joined_parts(late_b, quart)
    other_b = joined_parts(late_b_other, quart)
    for source, stats, lanes in ((first_b, own_b, left), (first_b_other, other_b, right)):
        normalise_rows(source, stats[0], stats[1], norm_b, lanes, 64)
        norm_b[rows : rows + 16, lanes] = jnp.broadcast_to(stats[2], (16, quart)).astype(
            jnp.bfloat16
        )

    columns = jnp.transpose(
        jnp.concatenate([own_b[3], own_b[1], jnp.zeros((6, quart), jnp.float32)], axis=0)
    )
    delta_col = columns[:, 0:1]
    rstd_col = columns[:, 1:2]
    width = quart // 2
    across = jnp.zeros((quart, 128), jnp.float32)
    losses = jnp.zeros((8, 128), jnp.float32)
    down = []
    for tile in range(4):
        at = slice(tile * width, (tile + 1) * width)
        sums = sums_all[:quart, at] + jnp.dot(
            late_b[:quart, :], centred[:, at], preferred_element_type=jnp.float32
        )
        corr = tile_scaled(sums, delta_col, rstd_col, delta[:, at], rstd[:, at], inverse)
        dcorr = off_weight * corr
        product = dcorr * corr
        loss = product
        if tile < 2:
            feature = lax.broadcasted_iota(jnp.int32, (quart, width), 0)
            lane = lax.broadcasted_iota(jnp.int32, (quart, width), 1) + tile * width
            diagonal = feature == lane
            dcorr = jnp.where(diagonal, corr - 1.0, dcorr)
            product = dcorr * corr
            loss = jnp.where(diagonal, dcorr * dcorr, product)
        dcorr_own[:, at] = dcorr.astype(jnp.bfloat16)
        across = across + fold_lanes(product)
        folded = fold_lanes(loss)
        losses = losses + jnp.sum(folded.reshape(quart // 8, 8, 128), axis=0)
        down.append(jnp.sum(product, axis=0, keepdims=True))

        @pl.when(own_tile[0] == tile)
        def _():
            mine_own[...] = corr

    second_a = second_partner + jnp.concatenate(down, axis=1)
    second_b = lanes_to_row(across)
    loss_out[0, 0] = jnp.sum(losses) + jnp.sum(second_partner)

    for tile in (2, 3, 0, 1):
        at = slice(tile * width, (tile + 1) * width)
        source, partner_dcorr = (
            (first_own, dcorr_left) if tile < 2 else (first_other, dcorr_right)
        )
        inner = slice((tile % 2) * width, (tile % 2 + 1) * width)
        terms = jnp.dot(
            norm_b[:, left], dcorr_own[:, at], preferred_element_type=jnp.float32
        ) + jnp.dot(norm_b[:, right], partner_dcorr[:, inner], preferred_element_type=jnp.float32)
        xhat = (source[:, inner].astype(jnp.float32) - offset[:, at]) * rstd[:, at]
        value = terms[:rows] - terms[rows : rows + 1] - xhat * second_a[:, at]
        if tile < 2:
            left_out[:, inner] = value
        else:
            left_partial_out[:, inner] = value.astype(jnp.bfloat16)

    contract = (((1,), (1,)), ((), ()))
    for tile in range(2):
        at = slice(tile * width, (tile + 1) * width)
        terms = lax.dot_general(
            norms[...], dcorr_own[at, :], contract, preferred_element_type=jnp.float32
        )
        xhat = (first_b[:, at].astype(jnp.float32) - own_b[0][:, at]) * own_b[1][:, at]
        right_out[:, at] = terms[:rows] - terms[rows : rows + 1] - xhat * second_b[:, at]

    own_columns = jnp.transpose(mine_own[...])
    in_left = own_tile[0] < 2
    partner_columns = jnp.transpose(jnp.where(in_left, mine_left[...], mine_right[...]))

    @pl.when(own_tile[1] == 0)
    def _():
        mine_out[:, left] = own_columns
        mine_out[:, right] = partner_columns

    @pl.when(own_tile[1] != 0)
    def _():
        mine_out[:, left] = partner_columns
        mine_out[:, right] = own_columns


vmem = pl.BlockSpec(memory_space=pltpu.VMEM)
smem = pl.BlockSpec(memory_space=pltpu.SMEM)


def local_call(kernel, operands, outs, scratch, flops, specs=None):
    moved = sum(x.size * x.dtype.itemsize for x in (*operands, *outs))
    return pl.pallas_call(
        kernel,
        out_shape=outs,
        in_specs=[smem if x.dtype == jnp.int32 else vmem for x in operands],
        out_specs=[smem if x.shape == (1, 1) else vmem for x in outs],
        scratch_shapes=scratch,
        compiler_params=pltpu.CompilerParams(vmem_limit_bytes=20 * 2**20),
        cost_estimate=pl.CostEstimate(flops=flops, bytes_accessed=moved, transcendentals=0),
    )(*operands)


def gathered_device(left_outputs, right_outputs):
    rows, quart = left_outputs.shape
    half = 2 * quart
    feats = 4 * quart
    batch_images = rows * 4
    tpos = lax.axis_index("tile")
    dpos = lax.axis_index("dp")
    row_halves = tpos // 2
    column_halves = tpos % 2
    at_end = (dpos == 0) | (dpos == 3)

    pairs = [(0, 1), (1, 0), (2, 3), (3, 2)]
    middle = [(1, 2), (2, 1)]
    outward = [(1, 0), (2, 3)]

    def along(block, route):
        return lax.ppermute(block, "dp", route)

    def core_swap(block):
        return swapped(block, "tile", 0)

    def x_swap(block):
        return swapped(block, "tile", 1)

    def after(value, *others):
        return lax.optimization_barrier((value, *others))

    other_a0 = core_swap(left_outputs)
    left_behind, other_a0 = after(left_outputs, other_a0)

    first_b = along(right_outputs, pairs)
    inner_b = along(right_outputs, middle)
    other_b0 = x_swap(right_outputs)
    first_a = along(left_behind, pairs)
    inner_a = along(left_behind, middle)

    outer_b = along(inner_b, outward)
    third_b = along(first_b, middle)
    other_b1 = x_swap(first_b)
    outer_a = along(inner_a, outward)
    third_a = along(first_a, middle)
    other_a1 = core_swap(first_a)

    last_b = along(third_b, outward)
    second_b = jnp.where(at_end, outer_b, inner_b)
    second_b, other_b1 = after(second_b, other_b1)
    other_b2 = x_swap(second_b)
    last_a = along(third_a, outward)
    second_a = jnp.where(at_end, outer_a, inner_a)
    second_a, other_a1 = after(second_a, other_a1)
    other_a2 = core_swap(second_a)

    def centred(blocks, shift):
        wide = [
            jnp.concatenate([own, other], axis=1).astype(jnp.float32) - shift
            for own, other in blocks
        ]
        return wide, [x.astype(jnp.bfloat16) for x in wide]

    def three_sums(wide, low):
        return (
            sum(jnp.sum(x, axis=0) for x in wide),
            sum(jnp.sum(x * x, axis=0) for x in wide),
            sum(jnp.sum(x.astype(jnp.float32), axis=0) for x in low),
        )

    def column_mean(own, other):
        return jnp.sum(jnp.concatenate([own, other], axis=1).astype(jnp.float32), axis=0) / rows

    def products(lows_a, lows_b):
        return sum(
            lax.dot_general(y, x, (((0,), (0,)), ((), ())), preferred_element_type=jnp.float32)
            for x, y in zip(lows_a, lows_b)
        )

    shift_a = column_mean(left_outputs, other_a0)
    shift_b = column_mean(right_outputs, other_b0)
    wide_a, low_a = centred(((left_outputs, other_a0), (first_a, other_a1)), shift_a)
    wide_b, low_b = centred(((right_outputs, other_b0), (first_b, other_b1)), shift_b)
    total = products(low_a, low_b)
    sums_a = three_sums(wide_a, low_a)
    sums_b = three_sums(wide_b, low_b)

    late_b = jnp.where(at_end, last_b, third_b)
    late_b, total, sums_a, sums_b = after(late_b, total, sums_a, sums_b)
    wide_b, low_b = centred(((second_b, other_b2),), shift_b)
    sums_b = [x + y for x, y in zip(sums_b, three_sums(wide_b, low_b))]
    row_b = jnp.stack([shift_b, *sums_b] + [shift_b] * 4)[:, :quart]
    gemm = 2 * rows * quart * quart
    extended = jax.ShapeDtypeStruct((quart + 16, rows), jnp.bfloat16)
    row_out = jax.ShapeDtypeStruct((8, quart), jnp.float32)
    late_low_b, stats_b = local_call(
        functools.partial(late_right_kernel, batch_images),
        (late_b, row_b),
        (extended, row_out),
        [],
        gemm,
    )
    late_low_other = x_swap(late_low_b)

    wide_a, low_a = centred(((second_a, other_a2),), shift_a)
    total = total + products(low_a, low_b)
    sums_a = [x + y for x, y in zip(sums_a, three_sums(wide_a, low_a))]
    row_a = jnp.stack([shift_a, *sums_a] + [shift_a] * 4)
    row_own, row_other = row_a[:, :quart], row_a[:, quart:]
    late_a = jnp.where(at_end, last_a, third_a)
    late_a, total, row_own, row_other = after(late_a, total, row_own, row_other)
    late_other = core_swap(late_a)

    owned_tile = jnp.where(dpos // 2 == column_halves, 0, 2) + dpos % 2
    scalars = jnp.stack([owned_tile, row_halves]).astype(jnp.int32)
    quarter_f32 = jax.ShapeDtypeStruct((rows, quart), jnp.float32)
    quarter_bf16 = jax.ShapeDtypeStruct((rows, quart), jnp.bfloat16)
    width = quart // 2
    mine_shape = jax.ShapeDtypeStruct((quart, width), jnp.float32)
    across_shape = jax.ShapeDtypeStruct((quart, 128), jnp.float32)
    low = lambda n, m: pltpu.VMEM((n, m), jnp.bfloat16)
    half_scratch = [low(rows, quart), low(rows + 16, quart)]
    terms, across, dcorr_left, mine_left, vec_own = local_call(
        functools.partial(partner_kernel, batch_images, 0),
        (scalars, late_a, left_outputs, row_own, total, late_low_other, other_b0),
        (
            jax.ShapeDtypeStruct((rows + 16, quart), jnp.float32),
            across_shape,
            quarter_bf16,
            mine_shape,
            row_out,
        ),
        half_scratch,
        2 * gemm,
    )
    partial_right, dcorr_right, mine_right, vec_other = local_call(
        functools.partial(partner_kernel, batch_images, 1),
        (scalars, late_other, other_a0, row_other, total, late_low_other, other_b0, terms, across),
        (quarter_bf16, quarter_bf16, mine_shape, row_out),
        half_scratch,
        2 * gemm,
    )
    from_x = x_swap(partial_right)
    right_own, left_own, partial_left, mine, part_loss = local_call(
        functools.partial(own_kernel, batch_images),
        (
            scalars,
            late_a,
            late_other,
            left_outputs,
            other_a0,
            row_own,
            row_other,
            total,
            late_low_b,
            late_low_other,
            right_outputs,
            other_b0,
            dcorr_left,
            dcorr_right,
            mine_left,
            mine_right,
            vec_own,
            vec_other,
        ),
        (
            quarter_f32,
            quarter_f32,
            quarter_bf16,
            jax.ShapeDtypeStruct((width, half), jnp.float32),
            jax.ShapeDtypeStruct((1, 1), jnp.float32),
        ),
        [
            low(rows, half),
            low(rows + 16, half),
            low(rows + 16, half),
            low(quart, half),
            pltpu.VMEM((quart, width), jnp.float32),
        ],
        8 * gemm,
    )
    from_core = core_swap(partial_left)
    loss = part_loss[0, 0]
    loss = loss + core_swap(loss)
    left_gradient = (vec_own[1] * (left_own + from_core.astype(jnp.float32))).astype(jnp.bfloat16)
    loss, from_x = after(loss, from_x)
    loss = loss + x_swap(loss)
    right_gradient = (stats_b[1] * (right_own + from_x.astype(jnp.float32))).astype(jnp.bfloat16)
    return (left_gradient, right_gradient, mine[None, :, :], jnp.reshape(loss / feats, (1,)))


def solution(mesh):
    per_device = gathered_device if mesh.shape["dp"] == 4 else reduced_device
    return jax.shard_map(
        per_device,
        mesh=mesh,
        in_specs=(P(("groups", "dp"), "tile"), P(("groups", "dp"), "tile")),
        out_specs=(
            P(("groups", "dp"), "tile"),
            P(("groups", "dp"), "tile"),
            P(("groups", "tile"), "dp", None),
            P("groups"),
        ),
        check_vma=False,
    )
```

```python
import functools
import jax
import jax.numpy as jnp
from jax import lax
from jax.experimental import pallas as pl
from jax.experimental.pallas import tpu as pltpu
from jax.sharding import PartitionSpec as P

off_weight = 0.0051


def swapped(block, axis, bit):
    count = lax.axis_size(axis)
    route = []
    for low in range(count):
        high = low | 1 << bit
        if high != low and high < count:
            route += [(low, high), (high, low)]
    return lax.ppermute(block, axis, route)


def pair_views(first_moment, second_moment, row_halves, column_halves):
    other_a = swapped(first_moment, "tile", 0)
    other_b = swapped(second_moment, "tile", 1)
    joined_a = jnp.where(
        column_halves == 0,
        jnp.concatenate([first_moment, other_a], axis=1),
        jnp.concatenate([other_a, first_moment], axis=1),
    )
    joined_b = jnp.where(
        row_halves == 0,
        jnp.concatenate([second_moment, other_b], axis=1),
        jnp.concatenate([other_b, second_moment], axis=1),
    )
    return (joined_a, joined_b)


def moment_pair(total, squares, batch_images):
    column_mean = total / batch_images
    var = squares / batch_images - column_mean * column_mean
    return (column_mean, lax.rsqrt(var + 1e-05))


def col_sums(values):
    as_float = values.astype(jnp.float32)
    return (jnp.sum(as_float, axis=0), jnp.sum(as_float * as_float, axis=0))


def reduced_device(left_outputs, right_outputs):
    rows, quart = left_outputs.shape
    half = 2 * quart
    feats = 4 * quart
    dp_count = lax.axis_size("dp")
    batch_images = rows * dp_count
    tpos = lax.axis_index("tile")
    row_halves = tpos // 2
    column_halves = tpos % 2
    sum_a, sq_a = col_sums(left_outputs)
    sum_b, sq_b = col_sums(right_outputs)
    sum_a, sq_a, sum_b, sq_b = lax.psum((sum_a, sq_a, sum_b, sq_b), "dp")
    left_mean, left_inverse_deviation = moment_pair(sum_a, sq_a, batch_images)
    right_mean, right_inverse_deviation = moment_pair(sum_b, sq_b, batch_images)
    standardized_left = (left_outputs.astype(jnp.float32) - left_mean) * left_inverse_deviation
    standardized_right = (right_outputs.astype(jnp.float32) - right_mean) * right_inverse_deviation
    half_a, cols_b = pair_views(
        standardized_left.astype(jnp.bfloat16),
        standardized_right.astype(jnp.bfloat16),
        row_halves,
        column_halves,
    )
    col_local = jnp.arange(half, dtype=jnp.int32)
    col_ids = quart * column_halves + col_local + jnp.where(col_local >= quart, quart, 0)
    owned = half // dp_count
    picked = half_a
    corr_rows = (
        lax.psum_scatter(
            lax.dot_general(
                picked, cols_b, (((0,), (0,)), ((), ())), preferred_element_type=jnp.float32
            ),
            "dp",
            scatter_dimension=0,
            tiled=True,
        )
        / batch_images
    )
    row_ids = half * row_halves + lax.axis_index("dp") * owned + jnp.arange(owned, dtype=jnp.int32)
    diagonal = row_ids[:, None] == col_ids[None, :]
    part_loss = jnp.sum(
        jnp.where(diagonal, (1.0 - corr_rows) ** 2, off_weight * corr_rows * corr_rows)
    )
    loss = lax.psum(part_loss, ("dp", "tile")) / feats
    dcorr_part = jnp.where(diagonal, corr_rows - 1.0, off_weight * corr_rows).astype(jnp.bfloat16)
    piece = lax.all_gather(dcorr_part, "dp", axis=0, tiled=True)
    block_a = lax.dot_general(
        cols_b, piece, (((1,), (1,)), ((), ())), preferred_element_type=jnp.float32
    )
    picked = half_a
    into_b = jnp.dot(picked, piece, preferred_element_type=jnp.float32)
    other_a = swapped(block_a.astype(jnp.bfloat16), "tile", 0).astype(block_a.dtype)
    other_b = swapped(into_b.astype(jnp.bfloat16), "tile", 1).astype(into_b.dtype)
    normed_grad_left = lax.dynamic_slice_in_dim(block_a + other_a, column_halves * quart, quart, 1)
    normed_grad_right = lax.dynamic_slice_in_dim(into_b + other_b, row_halves * quart, quart, 1)
    first_moment_left, second_moment_left, first_moment_right, second_moment_right = lax.psum(
        (
            jnp.sum(normed_grad_left, axis=0),
            jnp.sum(normed_grad_left * standardized_left, axis=0),
            jnp.sum(normed_grad_right, axis=0),
            jnp.sum(normed_grad_right * standardized_right, axis=0),
        ),
        "dp",
    )
    left_gradient = (
        left_inverse_deviation
        * (
            normed_grad_left
            - first_moment_left / batch_images
            - standardized_left * (second_moment_left / batch_images)
        )
    ).astype(jnp.bfloat16)
    right_gradient = (
        right_inverse_deviation
        * (
            normed_grad_right
            - first_moment_right / batch_images
            - standardized_right * (second_moment_right / batch_images)
        )
    ).astype(jnp.bfloat16)
    return (left_gradient, right_gradient, corr_rows[None, :, :], jnp.reshape(loss, (1,)))


def tile_scaled(sums, delta_col, rstd_col, delta_row, rstd_row, inverse_images):
    return (sums * inverse_images - delta_col * delta_row) * rstd_col * rstd_row


def centre_rows(source, shift, target, lanes, chunk):
    rows, width = source.shape
    zero = jnp.zeros((8, width), jnp.float32)

    def body(step, carry):
        total, squares, rounded = carry
        at = pl.ds(pl.multiple_of(step * chunk, chunk), chunk)
        centred = source[at, :].astype(jnp.float32) - shift
        low = centred.astype(jnp.bfloat16)
        target[at, lanes] = low
        fold = lambda v: jnp.sum(v.reshape(chunk // 8, 8, width), axis=0)
        return (
            total + fold(centred),
            squares + fold(centred * centred),
            rounded + fold(low.astype(jnp.float32)),
        )

    sums = lax.fori_loop(0, rows // chunk, body, (zero, zero, zero), unroll=True)
    return [jnp.sum(s, axis=0, keepdims=True) for s in sums]


def normalise_rows(source, offset, rstd, target, lanes, chunk):
    rows = source.shape[0]

    def body(step, carry):
        at = pl.ds(pl.multiple_of(step * chunk, chunk), chunk)
        target[at, lanes] = ((source[at, :].astype(jnp.float32) - offset) * rstd).astype(
            jnp.bfloat16
        )
        return carry

    lax.fori_loop(0, rows // chunk, body, 0, unroll=True)


def lanes_to_row(partial):
    ones = jnp.ones((16, partial.shape[1]), jnp.bfloat16)
    high = partial.astype(jnp.bfloat16)
    low = (partial - high.astype(jnp.float32)).astype(jnp.bfloat16)
    contract = (((1,), (1,)), ((), ()))
    row = lax.dot_general(ones, high, contract, preferred_element_type=jnp.float32)
    row = row + lax.dot_general(ones, low, contract, preferred_element_type=jnp.float32)
    return row[:1, :]


def three_parts(row):
    high = row.astype(jnp.bfloat16)
    rest = row - high.astype(jnp.float32)
    middle = rest.astype(jnp.bfloat16)
    low = (rest - middle.astype(jnp.float32)).astype(jnp.bfloat16)
    return [high, middle, low]


def joined_parts(ref, at):
    parts = ref[at : at + 16, :].astype(jnp.float32)
    return [parts[3 * i : 3 * i + 1] + parts[3 * i + 1 : 3 * i + 2] + parts[3 * i + 2 : 3 * i + 3] for i in range(4)]


def moments(sums, images):
    total, squares, rounded = sums
    delta = total / images
    rstd = lax.rsqrt(squares / images - delta * delta + 1e-05)
    return delta, rstd, (rounded / images - delta) * rstd


def fold_lanes(values):
    width = values.shape[1]
    return sum(values[:, at : at + 128] for at in range(0, width, 128))


def column_mean(block):
    rows, width = block.shape
    folded = jnp.zeros((8, width), jnp.float32)
    for at in range(0, rows, 64):
        piece = block[at : at + 64, :].astype(jnp.float32)
        folded = folded + jnp.sum(piece.reshape(8, 8, width), axis=0)
    return jnp.sum(folded, axis=0, keepdims=True) / rows


def add_sums(sums, centred, low):
    fold = lambda v: jnp.sum(v.reshape(v.shape[0] // 8, 8, v.shape[1]), axis=0)
    return [
        sums[0] + fold(centred),
        sums[1] + fold(centred * centred),
        sums[2] + fold(low.astype(jnp.float32)),
    ]


def late_right_kernel(images, first, second, third, late, out, stats):
    rows, quart = late.shape
    shift = column_mean(first)
    sums = [jnp.zeros((8, quart), jnp.float32)] * 3
    for block in (first, second, third, late):
        for at in range(0, rows, 128):
            centred = block[at : at + 128, :].astype(jnp.float32) - shift
            low = centred.astype(jnp.bfloat16)
            if block is late:
                out[:quart, at : at + 128] = jnp.transpose(low)
            sums = add_sums(sums, centred, low)
    sums = [jnp.sum(s, axis=0, keepdims=True) for s in sums]
    delta, rstd, rest = moments(sums, images)
    values = [shift + delta, rstd, rest, delta]
    stats[...] = jnp.concatenate(values + [jnp.zeros((4, quart), jnp.float32)], axis=0)
    parts = sum([three_parts(v) for v in values], [])
    parts = [p.astype(jnp.float32) for p in parts] + [jnp.zeros((4, quart), jnp.float32)]
    out[quart:, :] = jnp.concatenate(parts, axis=0).astype(jnp.bfloat16)


def products_kernel(*refs):
    lefts, rights = refs[0:6], refs[6:12]
    partner_own, partner_other, own_all, row_own, low_left, low_right = refs[12:]
    rows, quart = lefts[0].shape
    width = quart // 2
    for half in range(2):
        lanes = slice(half * quart, (half + 1) * quart)
        shift = column_mean(lefts[half])
        sums = [jnp.zeros((8, quart), jnp.float32)] * 3
        for block in range(3):
            source = lefts[2 * block + half]
            for at in range(0, rows, 64):
                centred = source[at : at + 64, :].astype(jnp.float32) - shift
                low = centred.astype(jnp.bfloat16)
                low_left[block * rows + at : block * rows + at + 64, lanes] = low
                if half == 0:
                    sums = add_sums(sums, centred, low)
        if half == 0:
            sums = [jnp.sum(s, axis=0, keepdims=True) for s in sums]
            zeros = jnp.zeros((4, quart), jnp.float32)
            row_own[...] = jnp.concatenate([shift, *sums, zeros], axis=0)
    for half in range(2):
        lanes = slice(half * quart, (half + 1) * quart)
        shift = column_mean(rights[half])
        for block in range(3):
            source = rights[2 * block + half]
            for at in range(0, rows, 128):
                low = (source[at : at + 128, :].astype(jnp.float32) - shift).astype(jnp.bfloat16)
                low_right[lanes, block * rows + at : block * rows + at + 128] = jnp.transpose(low)
    for tile in range(4):
        wide = slice(tile * width, (tile + 1) * width)
        inner = slice((tile % 2) * width, (tile % 2 + 1) * width)
        target = partner_own if tile < 2 else partner_other
        target[:, inner] = jnp.dot(
            low_right[quart:, :], low_left[:, wide], preferred_element_type=jnp.float32
        )
        own_all[:, wide] = jnp.dot(
            low_right[:quart, :], low_left[:, wide], preferred_element_type=jnp.float32
        )


def final_kernel(own, other, stats, out):
    rows = own.shape[0]
    for at in range(0, rows, 64):
        piece = slice(at, at + 64)
        value = stats[1:2, :] * (own[piece, :] + other[piece, :].astype(jnp.float32))
        out[piece, :] = value.astype(jnp.bfloat16)


def partner_kernel(images, part, own_tile, late, first, row, sums_all, late_b, first_b, *refs):
    if part:
        (terms_in, across_in, partial_out, dcorr_out, mine_out, vec_out, centred, norms) = refs
    else:
        (terms_out, across_out, dcorr_out, mine_out, vec_out, centred, norms) = refs
    rows, quart = late.shape
    inverse = 1.0 / images
    shift = row[0:1, :]
    everything = slice(0, quart)
    sums = centre_rows(late, shift, centred, everything, 64)
    delta, rstd, rest = moments([row[i + 1 : i + 2, :] + sums[i] for i in range(3)], images)
    normalise_rows(first, shift + delta, rstd, norms, everything, 64)
    norms[rows : rows + 16, :] = jnp.broadcast_to(rest, (16, quart)).astype(jnp.bfloat16)

    offset_b, rstd_b, _, delta_b = joined_parts(late_b, quart)
    columns = jnp.transpose(
        jnp.concatenate([delta_b, rstd_b, jnp.zeros((6, quart), jnp.float32)], axis=0)
    )
    delta_col = columns[:, 0:1]
    rstd_col = columns[:, 1:2]
    width = quart // 2
    across = across_in[...] if part else jnp.zeros((quart, 128), jnp.float32)
    for tile in range(2):
        at = slice(tile * width, (tile + 1) * width)
        sums = sums_all[:, at] + jnp.dot(
            late_b[:quart, :], centred[:, at], preferred_element_type=jnp.float32
        )
        corr = tile_scaled(sums, delta_col, rstd_col, delta[:, at], rstd[:, at], inverse)
        dcorr = off_weight * corr
        dcorr_out[:, at] = dcorr.astype(jnp.bfloat16)
        product = dcorr * corr
        across = across + fold_lanes(product)
        vec_out[3:4, at] = jnp.sum(product, axis=0, keepdims=True)

        @pl.when(own_tile[0] == 2 * part + tile)
        def _():
            mine_out[...] = corr

    vec_out[0:1, :] = delta
    vec_out[1:2, :] = rstd
    vec_out[2:3, :] = rest
    vec_out[4:8, :] = jnp.zeros((4, quart), jnp.float32)
    contract = (((1,), (1,)), ((), ()))
    if part:
        second = lanes_to_row(across)
    else:
        across_out[...] = across
    for tile in range(2):
        at = slice(tile * width, (tile + 1) * width)
        terms = lax.dot_general(
            norms[...], dcorr_out[at, :], contract, preferred_element_type=jnp.float32
        )
        if part:
            terms = terms + terms_in[:, at]
            xhat = (first_b[:, at].astype(jnp.float32) - offset_b[:, at]) * rstd_b[:, at]
            partial_out[:, at] = (
                terms[:rows] - terms[rows : rows + 1] - xhat * second[:, at]
            ).astype(jnp.bfloat16)
        else:
            terms_out[:, at] = terms


def own_kernel(
    images,
    own_tile,
    late_own,
    late_other,
    first_own,
    first_other,
    row_own,
    row_other,
    sums_all,
    late_b,
    late_b_other,
    first_b,
    first_b_other,
    dcorr_left,
    dcorr_right,
    mine_left,
    mine_right,
    vec_own,
    vec_other,
    right_out,
    left_out,
    left_partial_out,
    mine_out,
    loss_out,
    centred,
    norms,
    norm_b,
    dcorr_own,
    mine_own,
):
    rows, quart = late_own.shape
    half = 2 * quart
    inverse = 1.0 / images
    both = lambda i: jnp.concatenate([vec_own[i : i + 1, :], vec_other[i : i + 1, :]], axis=1)
    delta, rstd, rest, second_partner = [both(i) for i in range(4)]
    shift = jnp.concatenate([row_own[0:1, :], row_other[0:1, :]], axis=1)
    offset = shift + delta
    left, right = slice(0, quart), slice(quart, half)
    for source, lanes in ((late_own, left), (late_other, right)):
        normalise_rows(source, shift[:, lanes], 1.0, centred, lanes, 64)
    for source, lanes in ((first_own, left), (first_other, right)):
        normalise_rows(source, offset[:, lanes], rstd[:, lanes], norms, lanes, 64)
    norms[rows : rows + 16, :] = jnp.broadcast_to(rest, (16, half)).astype(jnp.bfloat16)
    own_b = joined_parts(late_b, quart)
    other_b = joined_parts(late_b_other, quart)
    for source, stats, lanes in ((first_b, own_b, left), (first_b_other, other_b, right)):
        normalise_rows(source, stats[0], stats[1], norm_b, lanes, 64)
        norm_b[rows : rows + 16, lanes] = jnp.broadcast_to(stats[2], (16, quart)).astype(
            jnp.bfloat16
        )

    columns = jnp.transpose(
        jnp.concatenate([own_b[3], own_b[1], jnp.zeros((6, quart), jnp.float32)], axis=0)
    )
    delta_col = columns[:, 0:1]
    rstd_col = columns[:, 1:2]
    width = quart // 2
    across = jnp.zeros((quart, 128), jnp.float32)
    losses = jnp.zeros((8, 128), jnp.float32)
    down = []
    for tile in range(4):
        at = slice(tile * width, (tile + 1) * width)
        sums = sums_all[:, at] + jnp.dot(
            late_b[:quart, :], centred[:, at], preferred_element_type=jnp.float32
        )
        corr = tile_scaled(sums, delta_col, rstd_col, delta[:, at], rstd[:, at], inverse)
        dcorr = off_weight * corr
        product = dcorr * corr
        loss = product
        if tile < 2:
            feature = lax.broadcasted_iota(jnp.int32, (quart, width), 0)
            lane = lax.broadcasted_iota(jnp.int32, (quart, width), 1) + tile * width
            diagonal = feature == lane
            dcorr = jnp.where(diagonal, corr - 1.0, dcorr)
            product = dcorr * corr
            loss = jnp.where(diagonal, dcorr * dcorr, product)
        dcorr_own[:, at] = dcorr.astype(jnp.bfloat16)
        across = across + fold_lanes(product)
        folded = fold_lanes(loss)
        losses = losses + jnp.sum(folded.reshape(quart // 8, 8, 128), axis=0)
        down.append(jnp.sum(product, axis=0, keepdims=True))

        @pl.when(own_tile[0] == tile)
        def _():
            mine_own[...] = corr

    second_a = second_partner + jnp.concatenate(down, axis=1)
    second_b = lanes_to_row(across)
    loss_out[0, 0] = jnp.sum(losses) + jnp.sum(second_partner)

    for tile in (2, 3, 0, 1):
        at = slice(tile * width, (tile + 1) * width)
        source, partner_dcorr = (
            (first_own, dcorr_left) if tile < 2 else (first_other, dcorr_right)
        )
        inner = slice((tile % 2) * width, (tile % 2 + 1) * width)
        terms = jnp.dot(
            norm_b[:, left], dcorr_own[:, at], preferred_element_type=jnp.float32
        ) + jnp.dot(norm_b[:, right], partner_dcorr[:, inner], preferred_element_type=jnp.float32)
        xhat = (source[:, inner].astype(jnp.float32) - offset[:, at]) * rstd[:, at]
        value = terms[:rows] - terms[rows : rows + 1] - xhat * second_a[:, at]
        if tile < 2:
            left_out[:, inner] = value
        else:
            left_partial_out[:, inner] = value.astype(jnp.bfloat16)

    contract = (((1,), (1,)), ((), ()))
    for tile in range(2):
        at = slice(tile * width, (tile + 1) * width)
        terms = lax.dot_general(
            norms[...], dcorr_own[at, :], contract, preferred_element_type=jnp.float32
        )
        xhat = (first_b[:, at].astype(jnp.float32) - own_b[0][:, at]) * own_b[1][:, at]
        right_out[:, at] = terms[:rows] - terms[rows : rows + 1] - xhat * second_b[:, at]

    own_columns = jnp.transpose(mine_own[...])
    in_left = own_tile[0] < 2
    partner_columns = jnp.transpose(jnp.where(in_left, mine_left[...], mine_right[...]))

    @pl.when(own_tile[1] == 0)
    def _():
        mine_out[:, left] = own_columns
        mine_out[:, right] = partner_columns

    @pl.when(own_tile[1] != 0)
    def _():
        mine_out[:, left] = partner_columns
        mine_out[:, right] = own_columns


vmem = pl.BlockSpec(memory_space=pltpu.VMEM)
smem = pl.BlockSpec(memory_space=pltpu.SMEM)


def local_call(kernel, operands, outs, scratch, flops, specs=None):
    moved = sum(x.size * x.dtype.itemsize for x in (*operands, *outs))
    return pl.pallas_call(
        kernel,
        out_shape=outs,
        in_specs=[smem if x.dtype == jnp.int32 else vmem for x in operands],
        out_specs=[smem if x.shape == (1, 1) else vmem for x in outs],
        scratch_shapes=scratch,
        compiler_params=pltpu.CompilerParams(vmem_limit_bytes=24 * 2**20),
        cost_estimate=pl.CostEstimate(flops=flops, bytes_accessed=moved, transcendentals=0),
    )(*operands)


def gathered_device(left_outputs, right_outputs):
    rows, quart = left_outputs.shape
    half = 2 * quart
    feats = 4 * quart
    batch_images = rows * 4
    tpos = lax.axis_index("tile")
    dpos = lax.axis_index("dp")
    row_halves = tpos // 2
    column_halves = tpos % 2
    at_end = (dpos == 0) | (dpos == 3)

    pairs = [(0, 1), (1, 0), (2, 3), (3, 2)]
    middle = [(1, 2), (2, 1)]
    outward = [(1, 0), (2, 3)]

    def along(block, route):
        return lax.ppermute(block, "dp", route)

    def core_swap(block):
        return swapped(block, "tile", 0)

    def x_swap(block):
        return swapped(block, "tile", 1)

    def after(value, *others):
        return lax.optimization_barrier((value, *others))

    first_b = along(right_outputs, pairs)
    inner_b = along(right_outputs, middle)
    first_a = along(left_outputs, pairs)
    other_b0 = x_swap(right_outputs)
    other_a0 = core_swap(left_outputs)
    left_behind, other_a0 = after(left_outputs, other_a0)
    inner_a = along(left_behind, middle)

    outer_b = along(inner_b, outward)
    third_b = along(first_b, middle)
    ready_b, other_b0 = after(first_b, other_b0)
    other_b1 = x_swap(ready_b)
    outer_a = along(inner_a, outward)
    third_a = along(first_a, middle)
    other_a1 = core_swap(first_a)

    last_b = along(third_b, outward)
    second_b = jnp.where(at_end, outer_b, inner_b)
    second_b, other_b1 = after(second_b, other_b1)
    other_b2 = x_swap(second_b)
    last_a = along(third_a, outward)
    second_a = jnp.where(at_end, outer_a, inner_a)
    second_a, other_a1 = after(second_a, other_a1)
    other_a2 = core_swap(second_a)

    gemm = 2 * rows * quart * quart
    quarter_f32 = jax.ShapeDtypeStruct((rows, quart), jnp.float32)
    quarter_bf16 = jax.ShapeDtypeStruct((rows, quart), jnp.bfloat16)
    extended = jax.ShapeDtypeStruct((quart + 16, rows), jnp.bfloat16)
    row_out = jax.ShapeDtypeStruct((8, quart), jnp.float32)
    low = lambda n, m: pltpu.VMEM((n, m), jnp.bfloat16)
    late_b = jnp.where(at_end, last_b, third_b)
    late_low_b, stats_b = local_call(
        functools.partial(late_right_kernel, batch_images),
        (right_outputs, first_b, second_b, late_b),
        (extended, row_out),
        [],
        gemm,
    )
    late_low_other = x_swap(late_low_b)
    partner_own, partner_other, own_all, row_own = local_call(
        products_kernel,
        (left_outputs, other_a0, first_a, other_a1, second_a, other_a2)
        + (right_outputs, other_b0, first_b, other_b1, second_b, other_b2),
        (
            quarter_f32,
            quarter_f32,
            jax.ShapeDtypeStruct((quart, half), jnp.float32),
            row_out,
        ),
        [low(3 * rows, half), low(half, 3 * rows)],
        12 * gemm,
    )
    late_a = jnp.where(at_end, last_a, third_a)
    row_other = core_swap(row_own)
    late_a, row_other = after(late_a, row_other)
    late_other = core_swap(late_a)

    owned_tile = jnp.where(dpos // 2 == column_halves, 0, 2) + dpos % 2
    scalars = jnp.stack([owned_tile, row_halves]).astype(jnp.int32)
    width = quart // 2
    mine_shape = jax.ShapeDtypeStruct((quart, width), jnp.float32)
    across_shape = jax.ShapeDtypeStruct((quart, 128), jnp.float32)
    half_scratch = [low(rows, quart), low(rows + 16, quart)]
    terms, across, dcorr_left, mine_left, vec_own = local_call(
        functools.partial(partner_kernel, batch_images, 0),
        (scalars, late_a, left_outputs, row_own, partner_own, late_low_other, other_b0),
        (
            jax.ShapeDtypeStruct((rows + 16, quart), jnp.float32),
            across_shape,
            quarter_bf16,
            mine_shape,
            row_out,
        ),
        half_scratch,
        2 * gemm,
    )
    partial_right, dcorr_right, mine_right, vec_other = local_call(
        functools.partial(partner_kernel, batch_images, 1),
        (scalars, late_other, other_a0, row_other, partner_other, late_low_other, other_b0)
        + (terms, across),
        (quarter_bf16, quarter_bf16, mine_shape, row_out),
        half_scratch,
        2 * gemm,
    )
    from_x = x_swap(partial_right)
    right_own, left_own, partial_left, mine, part_loss = local_call(
        functools.partial(own_kernel, batch_images),
        (
            scalars,
            late_a,
            late_other,
            left_outputs,
            other_a0,
            row_own,
            row_other,
            own_all,
            late_low_b,
            late_low_other,
            right_outputs,
            other_b0,
            dcorr_left,
            dcorr_right,
            mine_left,
            mine_right,
            vec_own,
            vec_other,
        ),
        (
            quarter_f32,
            quarter_f32,
            quarter_bf16,
            jax.ShapeDtypeStruct((width, half), jnp.float32),
            jax.ShapeDtypeStruct((1, 1), jnp.float32),
        ),
        [
            low(rows, half),
            low(rows + 16, half),
            low(rows + 16, half),
            low(quart, half),
            pltpu.VMEM((quart, width), jnp.float32),
        ],
        8 * gemm,
    )
    from_core = core_swap(partial_left)
    loss = part_loss[0, 0]
    loss = loss + core_swap(loss)
    (left_gradient,) = local_call(
        final_kernel, (left_own, from_core, vec_own), (quarter_bf16,), [], gemm // 16
    )
    loss, from_x = after(loss, from_x)
    loss = loss + x_swap(loss)
    (right_gradient,) = local_call(
        final_kernel, (right_own, from_x, stats_b), (quarter_bf16,), [], gemm // 16
    )
    return (left_gradient, right_gradient, mine[None, :, :], jnp.reshape(loss / feats, (1,)))


def solution(mesh):
    per_device = gathered_device if mesh.shape["dp"] == 4 else reduced_device
    return jax.shard_map(
        per_device,
        mesh=mesh,
        in_specs=(P(("groups", "dp"), "tile"), P(("groups", "dp"), "tile")),
        out_specs=(
            P(("groups", "dp"), "tile"),
            P(("groups", "dp"), "tile"),
            P(("groups", "tile"), "dp", None),
            P("groups"),
        ),
        check_vma=False,
    )
```

```python
import functools
import jax
import jax.numpy as jnp
from jax import lax
from jax.experimental import pallas as pl
from jax.experimental.pallas import tpu as pltpu
from jax.sharding import PartitionSpec as P

off_weight = 0.0051


def swapped(block, axis, bit):
    count = lax.axis_size(axis)
    route = []
    for low in range(count):
        high = low | 1 << bit
        if high != low and high < count:
            route += [(low, high), (high, low)]
    return lax.ppermute(block, axis, route)


def pair_views(first_moment, second_moment, row_halves, column_halves):
    other_a = swapped(first_moment, "tile", 0)
    other_b = swapped(second_moment, "tile", 1)
    joined_a = jnp.where(
        column_halves == 0,
        jnp.concatenate([first_moment, other_a], axis=1),
        jnp.concatenate([other_a, first_moment], axis=1),
    )
    joined_b = jnp.where(
        row_halves == 0,
        jnp.concatenate([second_moment, other_b], axis=1),
        jnp.concatenate([other_b, second_moment], axis=1),
    )
    return (joined_a, joined_b)


def moment_pair(total, squares, batch_images):
    column_mean = total / batch_images
    var = squares / batch_images - column_mean * column_mean
    return (column_mean, lax.rsqrt(var + 1e-05))


def col_sums(values):
    as_float = values.astype(jnp.float32)
    return (jnp.sum(as_float, axis=0), jnp.sum(as_float * as_float, axis=0))


def reduced_device(left_outputs, right_outputs):
    rows, quart = left_outputs.shape
    half = 2 * quart
    feats = 4 * quart
    dp_count = lax.axis_size("dp")
    batch_images = rows * dp_count
    tpos = lax.axis_index("tile")
    row_halves = tpos // 2
    column_halves = tpos % 2
    sum_a, sq_a = col_sums(left_outputs)
    sum_b, sq_b = col_sums(right_outputs)
    sum_a, sq_a, sum_b, sq_b = lax.psum((sum_a, sq_a, sum_b, sq_b), "dp")
    left_mean, left_inverse_deviation = moment_pair(sum_a, sq_a, batch_images)
    right_mean, right_inverse_deviation = moment_pair(sum_b, sq_b, batch_images)
    standardized_left = (left_outputs.astype(jnp.float32) - left_mean) * left_inverse_deviation
    standardized_right = (right_outputs.astype(jnp.float32) - right_mean) * right_inverse_deviation
    half_a, cols_b = pair_views(
        standardized_left.astype(jnp.bfloat16),
        standardized_right.astype(jnp.bfloat16),
        row_halves,
        column_halves,
    )
    col_local = jnp.arange(half, dtype=jnp.int32)
    col_ids = quart * column_halves + col_local + jnp.where(col_local >= quart, quart, 0)
    owned = half // dp_count
    picked = half_a
    corr_rows = (
        lax.psum_scatter(
            lax.dot_general(
                picked, cols_b, (((0,), (0,)), ((), ())), preferred_element_type=jnp.float32
            ),
            "dp",
            scatter_dimension=0,
            tiled=True,
        )
        / batch_images
    )
    row_ids = half * row_halves + lax.axis_index("dp") * owned + jnp.arange(owned, dtype=jnp.int32)
    diagonal = row_ids[:, None] == col_ids[None, :]
    part_loss = jnp.sum(
        jnp.where(diagonal, (1.0 - corr_rows) ** 2, off_weight * corr_rows * corr_rows)
    )
    loss = lax.psum(part_loss, ("dp", "tile")) / feats
    dcorr_part = jnp.where(diagonal, corr_rows - 1.0, off_weight * corr_rows).astype(jnp.bfloat16)
    piece = lax.all_gather(dcorr_part, "dp", axis=0, tiled=True)
    block_a = lax.dot_general(
        cols_b, piece, (((1,), (1,)), ((), ())), preferred_element_type=jnp.float32
    )
    picked = half_a
    into_b = jnp.dot(picked, piece, preferred_element_type=jnp.float32)
    other_a = swapped(block_a.astype(jnp.bfloat16), "tile", 0).astype(block_a.dtype)
    other_b = swapped(into_b.astype(jnp.bfloat16), "tile", 1).astype(into_b.dtype)
    normed_grad_left = lax.dynamic_slice_in_dim(block_a + other_a, column_halves * quart, quart, 1)
    normed_grad_right = lax.dynamic_slice_in_dim(into_b + other_b, row_halves * quart, quart, 1)
    first_moment_left, second_moment_left, first_moment_right, second_moment_right = lax.psum(
        (
            jnp.sum(normed_grad_left, axis=0),
            jnp.sum(normed_grad_left * standardized_left, axis=0),
            jnp.sum(normed_grad_right, axis=0),
            jnp.sum(normed_grad_right * standardized_right, axis=0),
        ),
        "dp",
    )
    left_gradient = (
        left_inverse_deviation
        * (
            normed_grad_left
            - first_moment_left / batch_images
            - standardized_left * (second_moment_left / batch_images)
        )
    ).astype(jnp.bfloat16)
    right_gradient = (
        right_inverse_deviation
        * (
            normed_grad_right
            - first_moment_right / batch_images
            - standardized_right * (second_moment_right / batch_images)
        )
    ).astype(jnp.bfloat16)
    return (left_gradient, right_gradient, corr_rows[None, :, :], jnp.reshape(loss, (1,)))


def tile_scaled(sums, delta_col, rstd_col, delta_row, rstd_row, inverse_images):
    return (sums * inverse_images - delta_col * delta_row) * rstd_col * rstd_row


def centre_rows(source, shift, target, lanes, chunk):
    rows, width = source.shape
    zero = jnp.zeros((8, width), jnp.float32)

    def body(step, carry):
        total, squares, rounded = carry
        at = pl.ds(pl.multiple_of(step * chunk, chunk), chunk)
        centred = source[at, :].astype(jnp.float32) - shift
        low = centred.astype(jnp.bfloat16)
        target[at, lanes] = low
        fold = lambda v: jnp.sum(v.reshape(chunk // 8, 8, width), axis=0)
        return (
            total + fold(centred),
            squares + fold(centred * centred),
            rounded + fold(low.astype(jnp.float32)),
        )

    sums = lax.fori_loop(0, rows // chunk, body, (zero, zero, zero), unroll=True)
    return [jnp.sum(s, axis=0, keepdims=True) for s in sums]


def normalise_rows(source, offset, rstd, target, lanes, chunk):
    rows = source.shape[0]

    def body(step, carry):
        at = pl.ds(pl.multiple_of(step * chunk, chunk), chunk)
        target[at, lanes] = ((source[at, :].astype(jnp.float32) - offset) * rstd).astype(
            jnp.bfloat16
        )
        return carry

    lax.fori_loop(0, rows // chunk, body, 0, unroll=True)


def lanes_to_row(partial):
    ones = jnp.ones((16, partial.shape[1]), jnp.bfloat16)
    high = partial.astype(jnp.bfloat16)
    low = (partial - high.astype(jnp.float32)).astype(jnp.bfloat16)
    contract = (((1,), (1,)), ((), ()))
    row = lax.dot_general(ones, high, contract, preferred_element_type=jnp.float32)
    row = row + lax.dot_general(ones, low, contract, preferred_element_type=jnp.float32)
    return row[:1, :]


def three_parts(row):
    high = row.astype(jnp.bfloat16)
    rest = row - high.astype(jnp.float32)
    middle = rest.astype(jnp.bfloat16)
    low = (rest - middle.astype(jnp.float32)).astype(jnp.bfloat16)
    return [high, middle, low]


def joined_parts(ref, at):
    parts = ref[at : at + 16, :].astype(jnp.float32)
    return [parts[3 * i : 3 * i + 1] + parts[3 * i + 1 : 3 * i + 2] + parts[3 * i + 2 : 3 * i + 3] for i in range(4)]


def moments(sums, images):
    total, squares, rounded = sums
    delta = total / images
    rstd = lax.rsqrt(squares / images - delta * delta + 1e-05)
    return delta, rstd, (rounded / images - delta) * rstd


def fold_lanes(values):
    width = values.shape[1]
    return sum(values[:, at : at + 128] for at in range(0, width, 128))


def column_mean(block):
    rows, width = block.shape
    folded = jnp.zeros((8, width), jnp.float32)
    for at in range(0, rows, 64):
        piece = block[at : at + 64, :].astype(jnp.float32)
        folded = folded + jnp.sum(piece.reshape(8, 8, width), axis=0)
    return jnp.sum(folded, axis=0, keepdims=True) / rows


def add_sums(sums, centred, low):
    fold = lambda v: jnp.sum(v.reshape(v.shape[0] // 8, 8, v.shape[1]), axis=0)
    return [
        sums[0] + fold(centred),
        sums[1] + fold(centred * centred),
        sums[2] + fold(low.astype(jnp.float32)),
    ]


def late_right_kernel(images, first, second, third, late, out, stats):
    rows, quart = late.shape
    first = first()
    shift = column_mean(first)
    sums = [jnp.zeros((8, quart), jnp.float32)] * 3
    for block in (first, second, third, late):
        block = block() if callable(block) else block
        for at in range(0, rows, 128):
            centred = block[at : at + 128, :].astype(jnp.float32) - shift
            low = centred.astype(jnp.bfloat16)
            if block is late:
                out[:quart, at : at + 128] = jnp.transpose(low)
            sums = add_sums(sums, centred, low)
    sums = [jnp.sum(s, axis=0, keepdims=True) for s in sums]
    delta, rstd, rest = moments(sums, images)
    values = [shift + delta, rstd, rest, delta]
    stats[...] = jnp.concatenate(values + [jnp.zeros((4, quart), jnp.float32)], axis=0)
    parts = sum([three_parts(v) for v in values], [])
    parts = [p.astype(jnp.float32) for p in parts] + [jnp.zeros((4, quart), jnp.float32)]
    out[quart:, :] = jnp.concatenate(parts, axis=0).astype(jnp.bfloat16)


def products_kernel(*refs):
    lefts, rights = refs[0:6], refs[6:12]
    partner_own, partner_other, own_all, row_own, low_left, low_right = refs[12:]
    lefts, rights = [[x if callable(x) else (lambda x=x: x) for x in xs] for xs in (lefts, rights)]
    rows, quart = lefts[0]().shape
    width = quart // 2
    for half in range(2):
        lanes = slice(half * quart, (half + 1) * quart)
        shift = column_mean(lefts[half]())
        sums = [jnp.zeros((8, quart), jnp.float32)] * 3
        for block in range(3):
            source = lefts[2 * block + half]()
            for at in range(0, rows, 64):
                centred = source[at : at + 64, :].astype(jnp.float32) - shift
                low = centred.astype(jnp.bfloat16)
                low_left[block * rows + at : block * rows + at + 64, lanes] = low
                if half == 0:
                    sums = add_sums(sums, centred, low)
        if half == 0:
            sums = [jnp.sum(s, axis=0, keepdims=True) for s in sums]
            zeros = jnp.zeros((4, quart), jnp.float32)
            row_own[...] = jnp.concatenate([shift, *sums, zeros], axis=0)
    for half in range(2):
        lanes = slice(half * quart, (half + 1) * quart)
        shift = column_mean(rights[half]())
        for block in range(3):
            source = rights[2 * block + half]()
            for at in range(0, rows, 128):
                low = (source[at : at + 128, :].astype(jnp.float32) - shift).astype(jnp.bfloat16)
                low_right[lanes, block * rows + at : block * rows + at + 128] = jnp.transpose(low)
    for tile in range(4):
        wide = slice(tile * width, (tile + 1) * width)
        inner = slice((tile % 2) * width, (tile % 2 + 1) * width)
        target = partner_own if tile < 2 else partner_other
        target.buffer[:, inner] = jnp.dot(
            low_right[quart:, :], low_left[:, wide], preferred_element_type=jnp.float32
        )
        if tile % 2:
            target.send()
    for tile in range(4):
        wide = slice(tile * width, (tile + 1) * width)
        own_all.buffer[:, wide] = jnp.dot(
            low_right[:quart, :], low_left[:, wide], preferred_element_type=jnp.float32
        )
    own_all.send()


def final_kernel(own, other, stats, out):
    rows = other.shape[0]
    own = own()
    for at in range(0, rows, 64):
        piece = slice(at, at + 64)
        value = stats[1:2, :] * (own[piece, :] + other[piece, :].astype(jnp.float32))
        out[piece, :] = value.astype(jnp.bfloat16)


def partner_kernel(images, part, own_tile, late, first, row, sums_all, late_b, *refs):
    if part:
        (first_b, terms_in, across_in, *refs) = refs
        (partial_out, dcorr_out, mine_out, vec_out, centred, norms) = refs
    else:
        (terms_out, across_out, dcorr_out, mine_out, vec_out, centred, norms) = refs
    rows, quart = late.shape
    inverse = 1.0 / images
    shift = row[0:1, :]
    everything = slice(0, quart)
    sums = centre_rows(late, shift, centred, everything, 64)
    delta, rstd, rest = moments([row[i + 1 : i + 2, :] + sums[i] for i in range(3)], images)
    normalise_rows(first(), shift + delta, rstd, norms, everything, 64)
    norms[rows : rows + 16, :] = jnp.broadcast_to(rest, (16, quart)).astype(jnp.bfloat16)

    sums_all = sums_all()
    offset_b, rstd_b, _, delta_b = joined_parts(late_b, quart)
    columns = jnp.transpose(
        jnp.concatenate([delta_b, rstd_b, jnp.zeros((6, quart), jnp.float32)], axis=0)
    )
    delta_col = columns[:, 0:1]
    rstd_col = columns[:, 1:2]
    width = quart // 2
    across = across_in[...] if part else jnp.zeros((quart, 128), jnp.float32)
    for tile in range(2):
        at = slice(tile * width, (tile + 1) * width)
        sums = sums_all[:, at] + jnp.dot(
            late_b[:quart, :], centred[:, at], preferred_element_type=jnp.float32
        )
        corr = tile_scaled(sums, delta_col, rstd_col, delta[:, at], rstd[:, at], inverse)
        dcorr = off_weight * corr
        dcorr_out[:, at] = dcorr.astype(jnp.bfloat16)
        product = dcorr * corr
        across = across + fold_lanes(product)
        vec_out[3:4, at] = jnp.sum(product, axis=0, keepdims=True)

        @pl.when(own_tile[0] == 2 * part + tile)
        def _():
            mine_out[...] = corr

    vec_out[0:1, :] = delta
    vec_out[1:2, :] = rstd
    vec_out[2:3, :] = rest
    vec_out[4:8, :] = jnp.zeros((4, quart), jnp.float32)
    contract = (((1,), (1,)), ((), ()))
    if part:
        second = lanes_to_row(across)
    else:
        across_out[...] = across
    for tile in range(2):
        at = slice(tile * width, (tile + 1) * width)
        terms = lax.dot_general(
            norms[...], dcorr_out[at, :], contract, preferred_element_type=jnp.float32
        )
        if part:
            terms = terms + terms_in[:, at]
            xhat = (first_b()[:, at].astype(jnp.float32) - offset_b[:, at]) * rstd_b[:, at]
            partial_out[:, at] = (
                terms[:rows] - terms[rows : rows + 1] - xhat * second[:, at]
            ).astype(jnp.bfloat16)
        else:
            terms_out[:, at] = terms


def own_kernel(
    images,
    own_tile,
    late_own,
    late_other,
    first_own,
    first_other,
    row_own,
    row_other,
    sums_all,
    late_b,
    late_b_other,
    first_b,
    first_b_other,
    dcorr_left,
    dcorr_right,
    mine_left,
    mine_right,
    vec_own,
    vec_other,
    right_out,
    left_out,
    left_partial_out,
    mine_out,
    loss_out,
    centred,
    norms,
    norm_b,
    dcorr_own,
    mine_own,
):
    rows, quart = late_own.shape
    half = 2 * quart
    inverse = 1.0 / images
    first_own, first_other, late_b, first_b, first_b_other, sums_all = [
        x() for x in (first_own, first_other, late_b, first_b, first_b_other, sums_all)
    ]
    both = lambda i: jnp.concatenate([vec_own[i : i + 1, :], vec_other[i : i + 1, :]], axis=1)
    delta, rstd, rest, second_partner = [both(i) for i in range(4)]
    shift = jnp.concatenate([row_own[0:1, :], row_other[0:1, :]], axis=1)
    offset = shift + delta
    left, right = slice(0, quart), slice(quart, half)
    for source, lanes in ((late_own, left), (late_other, right)):
        normalise_rows(source, shift[:, lanes], 1.0, centred, lanes, 64)
    for source, lanes in ((first_own, left), (first_other, right)):
        normalise_rows(source, offset[:, lanes], rstd[:, lanes], norms, lanes, 64)
    norms[rows : rows + 16, :] = jnp.broadcast_to(rest, (16, half)).astype(jnp.bfloat16)
    own_b = joined_parts(late_b, quart)
    other_b = joined_parts(late_b_other, quart)
    for source, stats, lanes in ((first_b, own_b, left), (first_b_other, other_b, right)):
        normalise_rows(source, stats[0], stats[1], norm_b, lanes, 64)
        norm_b[rows : rows + 16, lanes] = jnp.broadcast_to(stats[2], (16, quart)).astype(
            jnp.bfloat16
        )

    columns = jnp.transpose(
        jnp.concatenate([own_b[3], own_b[1], jnp.zeros((6, quart), jnp.float32)], axis=0)
    )
    delta_col = columns[:, 0:1]
    rstd_col = columns[:, 1:2]
    width = quart // 2
    across = jnp.zeros((quart, 128), jnp.float32)
    losses = jnp.zeros((8, 128), jnp.float32)
    down = []
    for tile in range(4):
        at = slice(tile * width, (tile + 1) * width)
        sums = sums_all[:, at] + jnp.dot(
            late_b[:quart, :], centred[:, at], preferred_element_type=jnp.float32
        )
        corr = tile_scaled(sums, delta_col, rstd_col, delta[:, at], rstd[:, at], inverse)
        dcorr = off_weight * corr
        product = dcorr * corr
        loss = product
        if tile < 2:
            feature = lax.broadcasted_iota(jnp.int32, (quart, width), 0)
            lane = lax.broadcasted_iota(jnp.int32, (quart, width), 1) + tile * width
            diagonal = feature == lane
            dcorr = jnp.where(diagonal, corr - 1.0, dcorr)
            product = dcorr * corr
            loss = jnp.where(diagonal, dcorr * dcorr, product)
        dcorr_own[:, at] = dcorr.astype(jnp.bfloat16)
        across = across + fold_lanes(product)
        folded = fold_lanes(loss)
        losses = losses + jnp.sum(folded.reshape(quart // 8, 8, 128), axis=0)
        down.append(jnp.sum(product, axis=0, keepdims=True))

        @pl.when(own_tile[0] == tile)
        def _():
            mine_own[...] = corr

    second_a = second_partner + jnp.concatenate(down, axis=1)
    second_b = lanes_to_row(across)
    loss_out[0, 0] = jnp.sum(losses) + jnp.sum(second_partner)

    for tile in (2, 3, 0, 1):
        at = slice(tile * width, (tile + 1) * width)
        source, partner_dcorr = (
            (first_own, dcorr_left) if tile < 2 else (first_other, dcorr_right)
        )
        inner = slice((tile % 2) * width, (tile % 2 + 1) * width)
        terms = jnp.dot(
            norm_b[:, left], dcorr_own[:, at], preferred_element_type=jnp.float32
        ) + jnp.dot(norm_b[:, right], partner_dcorr[:, inner], preferred_element_type=jnp.float32)
        xhat = (source[:, inner].astype(jnp.float32) - offset[:, at]) * rstd[:, at]
        value = terms[:rows] - terms[rows : rows + 1] - xhat * second_a[:, at]
        if tile < 2:
            left_out.buffer[:, inner] = value
        else:
            left_partial_out[:, inner] = value.astype(jnp.bfloat16)

    contract = (((1,), (1,)), ((), ()))
    for tile in range(2):
        at = slice(tile * width, (tile + 1) * width)
        terms = lax.dot_general(
            norms[...], dcorr_own[at, :], contract, preferred_element_type=jnp.float32
        )
        xhat = (first_b[:, at].astype(jnp.float32) - own_b[0][:, at]) * own_b[1][:, at]
        right_out.buffer[:, at] = terms[:rows] - terms[rows : rows + 1] - xhat * second_b[:, at]
    left_out.send()
    right_out.send()

    own_columns = jnp.transpose(mine_own[...])
    in_left = own_tile[0] < 2
    partner_columns = jnp.transpose(jnp.where(in_left, mine_left[...], mine_right[...]))

    @pl.when(own_tile[1] == 0)
    def _():
        mine_out[:, left] = own_columns
        mine_out[:, right] = partner_columns

    @pl.when(own_tile[1] != 0)
    def _():
        mine_out[:, left] = partner_columns
        mine_out[:, right] = own_columns


vmem = pl.BlockSpec(memory_space=pltpu.VMEM)
smem = pl.BlockSpec(memory_space=pltpu.SMEM)


class Result:
    def __init__(self, buffer, copy):
        self.buffer = buffer
        self.send = copy.start
        self.wait = copy.wait


def local_call(kernel, operands, outs, scratch, flops, fetched=(), sent=()):
    moved = sum(x.size * x.dtype.itemsize for x in (*operands, *outs))
    hbm = pl.BlockSpec(memory_space=pltpu.HBM)

    def in_space(i, x):
        return smem if x.dtype == jnp.int32 else hbm if i in fetched else vmem

    def out_space(i, x):
        return smem if x.shape == (1, 1) else hbm if i in sent else vmem

    def body(*refs):
        count, total = len(operands), len(operands) + len(outs)
        ins, results = list(refs[:count]), list(refs[count:total])
        staging, sems = refs[total + len(scratch) : -1], refs[-1]
        for slot, i in enumerate(fetched):
            copy = pltpu.make_async_copy(ins[i], staging[slot], sems.at[slot])
            copy.start()

            def arrived(waiting=[copy], buffer=staging[slot]):
                if waiting:
                    waiting.pop().wait()
                return buffer

            ins[i] = arrived
        for slot, i in enumerate(sent, len(fetched)):
            results[i] = Result(
                staging[slot], pltpu.make_async_copy(staging[slot], results[i], sems.at[slot])
            )
        kernel(*ins, *results, *refs[total : total + len(scratch)])
        for i in fetched:
            ins[i]()
        for i in sent:
            results[i].wait()

    buffers = [operands[i] for i in fetched] + [outs[i] for i in sent]
    return pl.pallas_call(
        body,
        out_shape=[pltpu.HBM(x.shape, x.dtype) if i in sent else x for i, x in enumerate(outs)],
        in_specs=[in_space(i, x) for i, x in enumerate(operands)],
        out_specs=[out_space(i, x) for i, x in enumerate(outs)],
        scratch_shapes=[
            *scratch,
            *(pltpu.VMEM(x.shape, x.dtype) for x in buffers),
            pltpu.SemaphoreType.DMA((max(len(buffers), 1),)),
        ],
        compiler_params=pltpu.CompilerParams(vmem_limit_bytes=28 * 2**20),
        cost_estimate=pl.CostEstimate(flops=flops, bytes_accessed=moved, transcendentals=0),
    )(
        *(
            pltpu.with_memory_space_constraint(x, pltpu.HBM) if i in fetched else x
            for i, x in enumerate(operands)
        )
    )


def gathered_device(left_outputs, right_outputs):
    rows, quart = left_outputs.shape
    half = 2 * quart
    feats = 4 * quart
    batch_images = rows * 4
    tpos = lax.axis_index("tile")
    dpos = lax.axis_index("dp")
    row_halves = tpos // 2
    column_halves = tpos % 2
    at_end = (dpos == 0) | (dpos == 3)

    pairs = [(0, 1), (1, 0), (2, 3), (3, 2)]
    middle = [(1, 2), (2, 1)]
    outward = [(1, 0), (2, 3)]

    def along(block, route):
        return lax.ppermute(block, "dp", route)

    def core_swap(block):
        return swapped(block, "tile", 0)

    def x_swap(block):
        return swapped(block, "tile", 1)

    def after(value, *others):
        return lax.optimization_barrier((value, *others))

    first_b = along(right_outputs, pairs)
    inner_b = along(right_outputs, middle)
    first_a = along(left_outputs, pairs)
    other_b0 = x_swap(right_outputs)
    other_a0 = core_swap(left_outputs)
    left_behind, first_a = after(left_outputs, first_a)
    inner_a = along(left_behind, middle)

    outer_b = along(inner_b, outward)
    third_b = along(first_b, middle)
    ready_b, other_b0 = after(first_b, other_b0)
    other_b1 = x_swap(ready_b)
    outer_a = along(inner_a, outward)
    third_a = along(first_a, middle)
    other_a1 = core_swap(first_a)

    last_b = along(third_b, outward)
    second_b = jnp.where(at_end, outer_b, inner_b)
    second_b, other_b1 = after(second_b, other_b1)
    other_b2 = x_swap(second_b)
    last_a = along(third_a, outward)
    second_a = jnp.where(at_end, outer_a, inner_a)
    second_a, other_a1 = after(second_a, other_a1)
    other_a2 = core_swap(second_a)

    gemm = 2 * rows * quart * quart
    quarter_f32 = jax.ShapeDtypeStruct((rows, quart), jnp.float32)
    quarter_bf16 = jax.ShapeDtypeStruct((rows, quart), jnp.bfloat16)
    extended = jax.ShapeDtypeStruct((quart + 16, rows), jnp.bfloat16)
    row_out = jax.ShapeDtypeStruct((8, quart), jnp.float32)
    low = lambda n, m: pltpu.VMEM((n, m), jnp.bfloat16)
    late_b = jnp.where(at_end, last_b, third_b)
    late_low_b, stats_b = local_call(
        functools.partial(late_right_kernel, batch_images),
        (right_outputs, first_b, second_b, late_b),
        (extended, row_out),
        [],
        gemm,
        fetched=(0, 1, 2),
    )
    late_low_other = x_swap(late_low_b)
    partner_own, partner_other, own_all, row_own = local_call(
        products_kernel,
        (left_outputs, other_a0, first_a, other_a1, second_a, other_a2)
        + (right_outputs, other_b0, first_b, other_b1, second_b, other_b2),
        (
            quarter_f32,
            quarter_f32,
            jax.ShapeDtypeStruct((quart, half), jnp.float32),
            row_out,
        ),
        [low(3 * rows, half), low(half, 3 * rows)],
        12 * gemm,
        fetched=(0, 1, 2, 3, 6, 7, 8, 9, 10),
        sent=(0, 1, 2),
    )
    late_a = jnp.where(at_end, last_a, third_a)
    row_other = core_swap(row_own)
    late_a, row_other = after(late_a, row_other)
    late_other = core_swap(late_a)

    owned_tile = jnp.where(dpos // 2 == column_halves, 0, 2) + dpos % 2
    scalars = jnp.stack([owned_tile, row_halves]).astype(jnp.int32)
    width = quart // 2
    mine_shape = jax.ShapeDtypeStruct((quart, width), jnp.float32)
    across_shape = jax.ShapeDtypeStruct((quart, 128), jnp.float32)
    half_scratch = [low(rows, quart), low(rows + 16, quart)]
    terms, across, dcorr_left, mine_left, vec_own = local_call(
        functools.partial(partner_kernel, batch_images, 0),
        (scalars, late_a, left_outputs, row_own, partner_own, late_low_other),
        (
            jax.ShapeDtypeStruct((rows + 16, quart), jnp.float32),
            across_shape,
            quarter_bf16,
            mine_shape,
            row_out,
        ),
        half_scratch,
        2 * gemm,
        fetched=(2, 4),
    )
    partial_right, dcorr_right, mine_right, vec_other = local_call(
        functools.partial(partner_kernel, batch_images, 1),
        (scalars, late_other, other_a0, row_other, partner_other, late_low_other, other_b0)
        + (terms, across),
        (quarter_bf16, quarter_bf16, mine_shape, row_out),
        half_scratch,
        2 * gemm,
        fetched=(2, 4, 6),
    )
    from_x = x_swap(partial_right)
    right_own, left_own, partial_left, mine, part_loss = local_call(
        functools.partial(own_kernel, batch_images),
        (
            scalars,
            late_a,
            late_other,
            left_outputs,
            other_a0,
            row_own,
            row_other,
            own_all,
            late_low_b,
            late_low_other,
            right_outputs,
            other_b0,
            dcorr_left,
            dcorr_right,
            mine_left,
            mine_right,
            vec_own,
            vec_other,
        ),
        (
            quarter_f32,
            quarter_f32,
            quarter_bf16,
            jax.ShapeDtypeStruct((width, half), jnp.float32),
            jax.ShapeDtypeStruct((1, 1), jnp.float32),
        ),
        [
            low(rows, half),
            low(rows + 16, half),
            low(rows + 16, half),
            low(quart, half),
            pltpu.VMEM((quart, width), jnp.float32),
        ],
        8 * gemm,
        fetched=(3, 4, 8, 10, 11, 7),
        sent=(0, 1),
    )
    from_core = core_swap(partial_left)
    loss = part_loss[0, 0]
    loss = loss + core_swap(loss)
    (left_gradient,) = local_call(
        final_kernel, (left_own, from_core, vec_own), (quarter_bf16,), [], gemm // 16, fetched=(0,)
    )
    loss, from_x = after(loss, from_x)
    loss = loss + x_swap(loss)
    (right_gradient,) = local_call(
        final_kernel, (right_own, from_x, stats_b), (quarter_bf16,), [], gemm // 16, fetched=(0,)
    )
    return (left_gradient, right_gradient, mine[None, :, :], jnp.reshape(loss / feats, (1,)))


def solution(mesh):
    per_device = gathered_device if mesh.shape["dp"] == 4 else reduced_device
    return jax.shard_map(
        per_device,
        mesh=mesh,
        in_specs=(P(("groups", "dp"), "tile"), P(("groups", "dp"), "tile")),
        out_specs=(
            P(("groups", "dp"), "tile"),
            P(("groups", "dp"), "tile"),
            P(("groups", "tile"), "dp", None),
            P("groups"),
        ),
        check_vma=False,
    )
```

```python
import functools
import jax
import jax.numpy as jnp
from jax import lax
from jax.experimental import pallas as pl
from jax.experimental.pallas import tpu as pltpu
from jax.sharding import PartitionSpec as P

off_weight = 0.0051


def swapped(block, axis, bit):
    count = lax.axis_size(axis)
    route = []
    for low in range(count):
        high = low | 1 << bit
        if high != low and high < count:
            route += [(low, high), (high, low)]
    return lax.ppermute(block, axis, route)


def pair_views(first_moment, second_moment, row_halves, column_halves):
    other_a = swapped(first_moment, "tile", 0)
    other_b = swapped(second_moment, "tile", 1)
    joined_a = jnp.where(
        column_halves == 0,
        jnp.concatenate([first_moment, other_a], axis=1),
        jnp.concatenate([other_a, first_moment], axis=1),
    )
    joined_b = jnp.where(
        row_halves == 0,
        jnp.concatenate([second_moment, other_b], axis=1),
        jnp.concatenate([other_b, second_moment], axis=1),
    )
    return (joined_a, joined_b)


def moment_pair(total, squares, batch_images):
    column_mean = total / batch_images
    var = squares / batch_images - column_mean * column_mean
    return (column_mean, lax.rsqrt(var + 1e-05))


def col_sums(values):
    as_float = values.astype(jnp.float32)
    return (jnp.sum(as_float, axis=0), jnp.sum(as_float * as_float, axis=0))


def reduced_device(left_outputs, right_outputs):
    rows, quart = left_outputs.shape
    half = 2 * quart
    feats = 4 * quart
    dp_count = lax.axis_size("dp")
    batch_images = rows * dp_count
    tpos = lax.axis_index("tile")
    row_halves = tpos // 2
    column_halves = tpos % 2
    sum_a, sq_a = col_sums(left_outputs)
    sum_b, sq_b = col_sums(right_outputs)
    sum_a, sq_a, sum_b, sq_b = lax.psum((sum_a, sq_a, sum_b, sq_b), "dp")
    left_mean, left_inverse_deviation = moment_pair(sum_a, sq_a, batch_images)
    right_mean, right_inverse_deviation = moment_pair(sum_b, sq_b, batch_images)
    standardized_left = (left_outputs.astype(jnp.float32) - left_mean) * left_inverse_deviation
    standardized_right = (right_outputs.astype(jnp.float32) - right_mean) * right_inverse_deviation
    half_a, cols_b = pair_views(
        standardized_left.astype(jnp.bfloat16),
        standardized_right.astype(jnp.bfloat16),
        row_halves,
        column_halves,
    )
    col_local = jnp.arange(half, dtype=jnp.int32)
    col_ids = quart * column_halves + col_local + jnp.where(col_local >= quart, quart, 0)
    owned = half // dp_count
    picked = half_a
    corr_rows = (
        lax.psum_scatter(
            lax.dot_general(
                picked, cols_b, (((0,), (0,)), ((), ())), preferred_element_type=jnp.float32
            ),
            "dp",
            scatter_dimension=0,
            tiled=True,
        )
        / batch_images
    )
    row_ids = half * row_halves + lax.axis_index("dp") * owned + jnp.arange(owned, dtype=jnp.int32)
    diagonal = row_ids[:, None] == col_ids[None, :]
    part_loss = jnp.sum(
        jnp.where(diagonal, (1.0 - corr_rows) ** 2, off_weight * corr_rows * corr_rows)
    )
    loss = lax.psum(part_loss, ("dp", "tile")) / feats
    dcorr_part = jnp.where(diagonal, corr_rows - 1.0, off_weight * corr_rows).astype(jnp.bfloat16)
    piece = lax.all_gather(dcorr_part, "dp", axis=0, tiled=True)
    block_a = lax.dot_general(
        cols_b, piece, (((1,), (1,)), ((), ())), preferred_element_type=jnp.float32
    )
    picked = half_a
    into_b = jnp.dot(picked, piece, preferred_element_type=jnp.float32)
    other_a = swapped(block_a.astype(jnp.bfloat16), "tile", 0).astype(block_a.dtype)
    other_b = swapped(into_b.astype(jnp.bfloat16), "tile", 1).astype(into_b.dtype)
    normed_grad_left = lax.dynamic_slice_in_dim(block_a + other_a, column_halves * quart, quart, 1)
    normed_grad_right = lax.dynamic_slice_in_dim(into_b + other_b, row_halves * quart, quart, 1)
    first_moment_left, second_moment_left, first_moment_right, second_moment_right = lax.psum(
        (
            jnp.sum(normed_grad_left, axis=0),
            jnp.sum(normed_grad_left * standardized_left, axis=0),
            jnp.sum(normed_grad_right, axis=0),
            jnp.sum(normed_grad_right * standardized_right, axis=0),
        ),
        "dp",
    )
    left_gradient = (
        left_inverse_deviation
        * (
            normed_grad_left
            - first_moment_left / batch_images
            - standardized_left * (second_moment_left / batch_images)
        )
    ).astype(jnp.bfloat16)
    right_gradient = (
        right_inverse_deviation
        * (
            normed_grad_right
            - first_moment_right / batch_images
            - standardized_right * (second_moment_right / batch_images)
        )
    ).astype(jnp.bfloat16)
    return (left_gradient, right_gradient, corr_rows[None, :, :], jnp.reshape(loss, (1,)))


def fold_rows(values):
    rows, width = values.shape
    return jnp.sum(values.reshape(rows // 8, 8, width), axis=0)


def fold_lanes(values):
    return sum(values[:, at : at + 128] for at in range(0, values.shape[1], 128))


def column_mean(block):
    rows, width = block.shape
    folded = jnp.zeros((8, width), jnp.float32)
    for at in range(0, rows, 64):
        folded = folded + fold_rows(block[at : at + 64, :].astype(jnp.float32))
    return jnp.sum(folded, axis=0, keepdims=True) / rows


def add_sums(sums, centred, low):
    return [
        sums[0] + fold_rows(centred),
        sums[1] + fold_rows(centred * centred),
        sums[2] + fold_rows(low.astype(jnp.float32)),
    ]


def rows_of(values):
    pad = jnp.zeros((8 - len(values), values[0].shape[1]), jnp.float32)
    return jnp.concatenate([*values, pad], axis=0)


def joined_sums(row, sums):
    return [row[i + 1 : i + 2, :] + jnp.sum(s, axis=0, keepdims=True) for i, s in enumerate(sums)]


def moments(sums, images):
    total, squares, rounded = sums
    delta = total / images
    return delta, lax.rsqrt(squares / images - delta * delta + 1e-05), rounded / images - delta


def three_parts(row):
    high = row.astype(jnp.bfloat16)
    rest = row - high.astype(jnp.float32)
    middle = rest.astype(jnp.bfloat16)
    low = (rest - middle.astype(jnp.float32)).astype(jnp.bfloat16)
    return [high, middle, low]


def split_rows(values):
    parts = sum([three_parts(v) for v in values], [])
    pad = jnp.zeros((4, values[0].shape[1]), jnp.float32)
    return jnp.concatenate([*(p.astype(jnp.float32) for p in parts), pad], axis=0).astype(
        jnp.bfloat16
    )


def joined_rows(ref, at):
    parts = ref[at : at + 16, :].astype(jnp.float32)
    part = lambda i: parts[i : i + 1]
    return [part(3 * i) + part(3 * i + 1) + part(3 * i + 2) for i in range(4)]


def lanes_to_row(partial):
    ones = jnp.ones((16, partial.shape[1]), jnp.bfloat16)
    high = partial.astype(jnp.bfloat16)
    low = (partial - high.astype(jnp.float32)).astype(jnp.bfloat16)
    row = dot_rows(ones, high) + dot_rows(ones, low)
    return row[:1, :]


def dot_rows(left, right):
    return lax.dot_general(
        left, right, (((1,), (1,)), ((), ())), preferred_element_type=jnp.float32
    )


def dot(left, right):
    return jnp.dot(left, right, preferred_element_type=jnp.float32)


def pick_kernel(flags, outer, inner, out):
    @pl.when(flags[2] != 0)
    def _():
        out[...] = outer[...]

    @pl.when(flags[2] == 0)
    def _():
        out[...] = inner[...]


def right_sums_kernel(first, second, third, row):
    rows, quart = first.shape
    shift = column_mean(first)
    sums = [jnp.zeros((8, quart), jnp.float32)] * 3
    for block in (first, second, third):
        for at in range(0, rows, 64):
            centred = block[at : at + 64, :].astype(jnp.float32) - shift
            sums = add_sums(sums, centred, centred.astype(jnp.bfloat16))
    row[...] = rows_of([shift] + [jnp.sum(s, axis=0, keepdims=True) for s in sums])


def late_kernel(images, turned, flags, outer, inner, row, out, stats):
    rows, quart = outer.shape
    shift = row[0:1, :]
    sums = [jnp.zeros((8, quart), jnp.float32)] * 3
    from_outer = flags[2] != 0
    for at in range(0, rows, 128):
        piece = slice(at, at + 128)
        value = jnp.where(
            from_outer, outer[piece, :].astype(jnp.float32), inner[piece, :].astype(jnp.float32)
        )
        centred = value - shift
        low = centred.astype(jnp.bfloat16)
        if turned:
            out[:quart, piece] = jnp.transpose(low)
        else:
            out[piece, :] = low
        sums = add_sums(sums, centred, low)
    delta, rstd, gap = moments(joined_sums(row, sums), images)
    values = [shift + delta, rstd, gap, delta]
    stats[...] = rows_of(values)
    out[rows:, :] = split_rows(values)


def products_kernel(*refs):
    lefts, rights = refs[0:6], refs[6:12]
    partner_own, partner_other, own_all, row_other, zero_own, zero_other = refs[12:18]
    low_left, low_right = refs[18:]
    rows, quart = lefts[0].shape
    width = quart // 2
    for half in range(2):
        lanes = slice(half * quart, (half + 1) * quart)
        shift = column_mean(lefts[half])
        sums = [jnp.zeros((8, quart), jnp.float32)] * 3
        for block in range(3):
            source = lefts[2 * block + half]
            for at in range(0, rows, 64):
                centred = source[at : at + 64, :].astype(jnp.float32) - shift
                low = centred.astype(jnp.bfloat16)
                low_left[block * rows + at : block * rows + at + 64, lanes] = low
                if block == 0:
                    (zero_own, zero_other)[half][at : at + 64, :] = low
                if half:
                    sums = add_sums(sums, centred, low)
        if half:
            row_other[...] = rows_of([shift] + [jnp.sum(s, axis=0, keepdims=True) for s in sums])
    for half in range(2):
        lanes = slice(half * quart, (half + 1) * quart)
        shift = column_mean(rights[half])
        for block in range(3):
            source = rights[2 * block + half]
            for at in range(0, rows, 128):
                low = (source[at : at + 128, :].astype(jnp.float32) - shift).astype(jnp.bfloat16)
                low_right[lanes, block * rows + at : block * rows + at + 128] = jnp.transpose(low)
    for tile in range(4):
        wide = slice(tile * width, (tile + 1) * width)
        inner = slice((tile % 2) * width, (tile % 2 + 1) * width)
        target = partner_own if tile < 2 else partner_other
        target[:, inner] = dot(low_right[quart:, :], low_left[:, wide])
        own_all[:, wide] = dot(low_right[:quart, :], low_left[:, wide])


def left_operand(zero, late, target, lanes):
    rows, quart = zero.shape
    _, _, gap, delta = joined_rows(late, rows)
    high, middle, _ = three_parts(delta)
    target[:rows, lanes] = zero[...]
    extra = [high.astype(jnp.float32), middle.astype(jnp.float32), gap]
    pad = jnp.zeros((13, quart), jnp.float32)
    target[rows:, lanes] = jnp.concatenate([*extra, pad], axis=0).astype(jnp.bfloat16)


def without_extra(terms, rows):
    return terms[:rows] - (terms[rows : rows + 1] + terms[rows + 1 : rows + 2] + terms[rows + 2 : rows + 3])


def scale_columns(late_b, images):
    quart = late_b.shape[1]
    _, rstd, _, delta = joined_rows(late_b, quart)
    columns = jnp.transpose(rows_of([rstd / images, delta * rstd]))
    return columns[:, 0:1], columns[:, 1:2]


def partner_kernel(images, part, flags, late, zero, sums, late_b, *refs):
    if part:
        (first_b, terms_in, across_in, vec_in, partial_out, e_out, mine_out, vec_out, left) = refs
    else:
        (terms_out, across_out, e_out, mine_out, vec_out, left) = refs
    rows, quart = zero.shape
    width = quart // 2
    _, rstd, _, delta = joined_rows(late, rows)
    left_operand(zero, late, left, slice(0, quart))
    scale_col, delta_col = scale_columns(late_b, images)
    across = across_in[...] if part else jnp.zeros((quart, 128), jnp.float32)
    down = []
    for tile in range(2):
        at = slice(tile * width, (tile + 1) * width)
        total = sums[:, at] + dot(late_b[:quart, :], late[:rows, at])
        corr = (total * scale_col - delta_col * delta[:, at]) * rstd[:, at]
        e_out[:, at] = (corr * (off_weight * rstd[:, at])).astype(jnp.bfloat16)
        square = corr * corr
        across = across + fold_lanes(square)
        down.append(jnp.sum(square, axis=0, keepdims=True))

        @pl.when(flags[0] == 2 * part + tile)
        def _():
            mine_out[...] = corr

    second_a = off_weight * jnp.concatenate(down, axis=1)
    if part:
        vec_out[...] = rows_of([second_a, second_a + vec_in[0:1, :]])
        second = off_weight * lanes_to_row(across)
        offset_b, rstd_b, _, _ = joined_rows(late_b, quart)
    else:
        vec_out[...] = rows_of([second_a])
        across_out[...] = across
    for tile in range(2):
        at = slice(tile * width, (tile + 1) * width)
        terms = dot_rows(left[...], e_out[at, :])
        if part:
            xhat = (first_b[:, at].astype(jnp.float32) - offset_b[:, at]) * rstd_b[:, at]
            partial_out[:, at] = (
                without_extra(terms + terms_in[:, at], rows) - xhat * second[:, at]
            ).astype(jnp.bfloat16)
        else:
            terms_out[:, at] = terms


def own_kernel(images, flags, *refs):
    (late_own, late_other, first_own, first_other, zero_own, zero_other, sums, late_b) = refs[:8]
    (late_b_other, first_b, first_b_other, e_left, e_right, mine_left, mine_right) = refs[8:15]
    (vec_own, vec_other, vec_core, right_out, left_out, left_partial_out, mine_out) = refs[15:22]
    (own_loss_out, loss_out, left, norm_b, e_own, mine_own) = refs[22:]
    rows, quart = zero_own.shape
    width = quart // 2
    lower, upper = slice(0, quart), slice(quart, 2 * quart)
    stats_own, stats_other = joined_rows(late_own, rows), joined_rows(late_other, rows)
    both = lambda i: jnp.concatenate([stats_own[i], stats_other[i]], axis=1)
    offset, rstd, _, delta = [both(i) for i in range(4)]
    left_operand(zero_own, late_own, left, lower)
    left_operand(zero_other, late_other, left, upper)
    own_b = joined_rows(late_b, quart)
    other_b = joined_rows(late_b_other, quart)
    for source, stats, lanes in ((first_b, own_b, lower), (first_b_other, other_b, upper)):
        for at in range(0, rows, 64):
            piece = slice(at, at + 64)
            norm_b[piece, lanes] = (
                (source[piece, :].astype(jnp.float32) - stats[0]) * stats[1]
            ).astype(jnp.bfloat16)
        rest = jnp.broadcast_to(stats[2] * stats[1], (16, quart))
        norm_b[rows:, lanes] = rest.astype(jnp.bfloat16)

    scale_col, delta_col = scale_columns(late_b, images)
    across = jnp.zeros((quart, 128), jnp.float32)
    losses = jnp.zeros((8, 128), jnp.float32)
    down = []
    for tile in range(4):
        at = slice(tile * width, (tile + 1) * width)
        inner = slice((tile % 2) * width, (tile % 2 + 1) * width)
        late = late_own if tile < 2 else late_other
        total = sums[:, at] + dot(late_b[:quart, :], late[:rows, inner])
        corr = (total * scale_col - delta_col * delta[:, at]) * rstd[:, at]
        dcorr = off_weight * corr
        product = dcorr * corr
        loss = product
        if tile < 2:
            feature = lax.broadcasted_iota(jnp.int32, (quart, width), 0)
            lane = lax.broadcasted_iota(jnp.int32, (quart, width), 1) + tile * width
            diagonal = feature == lane
            dcorr = jnp.where(diagonal, corr - 1.0, dcorr)
            product = dcorr * corr
            loss = jnp.where(diagonal, dcorr * dcorr, product)
        e_own[:, at] = (dcorr * rstd[:, at]).astype(jnp.bfloat16)
        across = across + fold_lanes(product)
        losses = losses + fold_rows(fold_lanes(loss))
        down.append(jnp.sum(product, axis=0, keepdims=True))

        @pl.when(flags[0] == tile)
        def _():
            mine_own[...] = corr

    partner_second = jnp.concatenate([vec_own[0:1, :], vec_other[0:1, :]], axis=1)
    second_a = rstd * (partner_second + jnp.concatenate(down, axis=1))
    second_b = lanes_to_row(across)
    own_loss = jnp.sum(losses)
    own_loss_out[0, 0] = own_loss
    loss_out[0, 0] = own_loss + jnp.sum(vec_other[1:2, :] + vec_core[1:2, :])

    for tile in (2, 3, 0, 1):
        at = slice(tile * width, (tile + 1) * width)
        inner = slice((tile % 2) * width, (tile % 2 + 1) * width)
        source, e_partner = (first_own, e_left) if tile < 2 else (first_other, e_right)
        terms = dot(norm_b[:, lower], e_own[:, at]) + dot(norm_b[:, upper], e_partner[:, inner])
        xhat = (source[:, inner].astype(jnp.float32) - offset[:, at]) * rstd[:, at]
        value = terms[:rows] - terms[rows : rows + 1] - xhat * second_a[:, at]
        if tile < 2:
            left_out[:, inner] = value
        else:
            left_partial_out[:, inner] = value.astype(jnp.bfloat16)

    for tile in range(2):
        at = slice(tile * width, (tile + 1) * width)
        terms = dot_rows(left[...], e_own[at, :])
        xhat = (first_b[:, at].astype(jnp.float32) - own_b[0][:, at]) * own_b[1][:, at]
        right_out[:, at] = without_extra(terms, rows) - xhat * second_b[:, at]

    own_columns = jnp.transpose(mine_own[...])
    partner_columns = jnp.transpose(jnp.where(flags[0] < 2, mine_left[...], mine_right[...]))

    @pl.when(flags[1] == 0)
    def _():
        mine_out[:, lower] = own_columns
        mine_out[:, upper] = partner_columns

    @pl.when(flags[1] != 0)
    def _():
        mine_out[:, lower] = partner_columns
        mine_out[:, upper] = own_columns


def left_final_kernel(own, other, loss, core_loss, out, loss_out):
    for at in range(0, own.shape[0], 64):
        piece = slice(at, at + 64)
        out[piece, :] = (own[piece, :] + other[piece, :].astype(jnp.float32)).astype(jnp.bfloat16)
    loss_out[0, 0] = loss[0, 0] + core_loss[0, 0]


def right_final_kernel(own, other, stats, out):
    for at in range(0, own.shape[0], 64):
        piece = slice(at, at + 64)
        value = stats[1:2, :] * (own[piece, :] + other[piece, :].astype(jnp.float32))
        out[piece, :] = value.astype(jnp.bfloat16)


vmem = pl.BlockSpec(memory_space=pltpu.VMEM)
smem = pl.BlockSpec(memory_space=pltpu.SMEM)


def local_call(kernel, operands, outs, scratch=(), flops=2**20, room=8):
    moved = sum(x.size * x.dtype.itemsize for x in (*operands, *outs))

    def space(x):
        return smem if x.dtype == jnp.int32 or x.shape == (1, 1) else vmem

    return pl.pallas_call(
        kernel,
        out_shape=list(outs),
        in_specs=[space(x) for x in operands],
        out_specs=[space(x) for x in outs],
        scratch_shapes=list(scratch),
        compiler_params=pltpu.CompilerParams(vmem_limit_bytes=room * 2**20),
        cost_estimate=pl.CostEstimate(flops=flops, bytes_accessed=moved, transcendentals=0),
    )(*operands)


def gathered_device(left_outputs, right_outputs):
    rows, quart = left_outputs.shape
    half = 2 * quart
    feats = 4 * quart
    batch_images = rows * 4
    tpos = lax.axis_index("tile")
    dpos = lax.axis_index("dp")
    row_halves = tpos // 2
    column_halves = tpos % 2
    at_end = (dpos == 0) | (dpos == 3)
    owned_tile = jnp.where(dpos // 2 == column_halves, 0, 2) + dpos % 2
    flags = jnp.stack([owned_tile, row_halves, at_end, dpos]).astype(jnp.int32)

    pairs = [(0, 1), (1, 0), (2, 3), (3, 2)]
    middle = [(1, 2), (2, 1)]
    outward = [(1, 0), (2, 3)]

    def along(block, route):
        return lax.ppermute(block, "dp", route)

    def core_swap(block):
        return swapped(block, "tile", 0)

    def x_swap(block):
        return swapped(block, "tile", 1)

    def after(value, *others):
        return lax.optimization_barrier((value, *others))

    gemm = 2 * rows * quart * quart
    width = quart // 2
    quarter_f32 = jax.ShapeDtypeStruct((rows, quart), jnp.float32)
    quarter_bf16 = jax.ShapeDtypeStruct((rows, quart), jnp.bfloat16)
    extended = jax.ShapeDtypeStruct((rows + 16, quart), jnp.bfloat16)
    row_out = jax.ShapeDtypeStruct((8, quart), jnp.float32)
    one_out = jax.ShapeDtypeStruct((1, 1), jnp.float32)
    mine_shape = jax.ShapeDtypeStruct((quart, width), jnp.float32)
    across_shape = jax.ShapeDtypeStruct((quart, 128), jnp.float32)
    low = lambda n, m: pltpu.VMEM((n, m), jnp.bfloat16)

    def picked(outer, inner):
        return local_call(pick_kernel, (flags, outer, inner), (quarter_bf16,))[0]

    first_b = along(right_outputs, pairs)
    inner_b = along(right_outputs, middle)
    first_a = along(left_outputs, pairs)
    other_b0 = x_swap(right_outputs)
    other_a0 = core_swap(left_outputs)
    left_behind, first_a = after(left_outputs, first_a)
    inner_a = along(left_behind, middle)

    outer_b = along(inner_b, outward)
    third_b = along(first_b, middle)
    ready_b, other_b0 = after(first_b, other_b0)
    other_b1 = x_swap(ready_b)
    outer_a = along(inner_a, outward)
    third_a = along(first_a, middle)
    other_a1 = core_swap(first_a)

    last_b = along(third_b, outward)
    second_b = picked(outer_b, inner_b)
    row_b = local_call(right_sums_kernel, (right_outputs, first_b, second_b), (row_out,))[0]
    second_b, other_b1 = after(second_b, other_b1)
    other_b2 = x_swap(second_b)
    last_a = along(third_a, outward)
    second_a = picked(outer_a, inner_a)
    second_a, other_a1, row_b = after(second_a, other_a1, row_b)
    other_a2 = core_swap(second_a)

    late_b, stats_b = local_call(
        functools.partial(late_kernel, batch_images, True),
        (flags, last_b, third_b, row_b),
        (extended, row_out),
    )
    late_b_other = x_swap(late_b)
    partner_own, partner_other, own_all, row_other, zero_own, zero_other = local_call(
        products_kernel,
        (left_outputs, other_a0, first_a, other_a1, second_a, other_a2)
        + (right_outputs, other_b0, first_b, other_b1, second_b, other_b2),
        (
            quarter_f32,
            quarter_f32,
            jax.ShapeDtypeStruct((quart, half), jnp.float32),
            row_out,
            quarter_bf16,
            quarter_bf16,
        ),
        [low(3 * rows, half), low(half, 3 * rows)],
        12 * gemm,
        room=20,
    )
    row_a = core_swap(row_other)
    late_a, stats_a = local_call(
        functools.partial(late_kernel, batch_images, False),
        (flags, last_a, third_a, row_a),
        (extended, row_out),
    )
    late_a_other = core_swap(late_a)

    terms, across, e_left, mine_left, vec_own = local_call(
        functools.partial(partner_kernel, batch_images, 0),
        (flags, late_a, zero_own, partner_own, late_b_other),
        (
            jax.ShapeDtypeStruct((rows + 16, quart), jnp.float32),
            across_shape,
            quarter_bf16,
            mine_shape,
            row_out,
        ),
        [low(rows + 16, quart)],
        2 * gemm,
        room=12,
    )
    partial_right, e_right, mine_right, vec_other = local_call(
        functools.partial(partner_kernel, batch_images, 1),
        (flags, late_a_other, zero_other, partner_other, late_b_other, other_b0)
        + (terms, across, vec_own),
        (quarter_bf16, quarter_bf16, mine_shape, row_out),
        [low(rows + 16, quart)],
        2 * gemm,
        room=12,
    )
    from_x = x_swap(partial_right)
    vec_core = core_swap(vec_other)
    right_own, left_own, partial_left, mine, own_loss, loss = local_call(
        functools.partial(own_kernel, batch_images),
        (flags, late_a, late_a_other, left_outputs, other_a0, zero_own, zero_other, own_all)
        + (late_b, late_b_other, right_outputs, other_b0, e_left, e_right, mine_left, mine_right)
        + (vec_own, vec_other, vec_core),
        (
            quarter_f32,
            quarter_f32,
            quarter_bf16,
            jax.ShapeDtypeStruct((width, half), jnp.float32),
            one_out,
            one_out,
        ),
        [
            low(rows + 16, half),
            low(rows + 16, half),
            low(quart, half),
            pltpu.VMEM((quart, width), jnp.float32),
        ],
        8 * gemm,
        room=20,
    )
    from_core = core_swap(partial_left)
    core_loss = jnp.reshape(core_swap(jnp.reshape(own_loss, ())), (1, 1))
    left_gradient, loss = local_call(
        left_final_kernel, (left_own, from_core, loss, core_loss), (quarter_bf16, one_out)
    )
    loss = jnp.reshape(loss, ())
    right_own, loss = after(right_own, loss)
    loss = loss + x_swap(loss)
    (right_gradient,) = local_call(
        right_final_kernel, (right_own, from_x, stats_b), (quarter_bf16,)
    )
    return (left_gradient, right_gradient, mine[None, :, :], jnp.reshape(loss / feats, (1,)))


def solution(mesh):
    per_device = gathered_device if mesh.shape["dp"] == 4 else reduced_device
    return jax.shard_map(
        per_device,
        mesh=mesh,
        in_specs=(P(("groups", "dp"), "tile"), P(("groups", "dp"), "tile")),
        out_specs=(
            P(("groups", "dp"), "tile"),
            P(("groups", "dp"), "tile"),
            P(("groups", "tile"), "dp", None),
            P("groups"),
        ),
        check_vma=False,
    )
```

```python
import functools
import jax
import jax.numpy as jnp
from jax import lax
from jax.experimental import pallas as pl
from jax.experimental.pallas import tpu as pltpu
from jax.sharding import PartitionSpec as P

off_weight = 0.0051


def swapped(block, axis, bit):
    count = lax.axis_size(axis)
    route = []
    for low in range(count):
        high = low | 1 << bit
        if high != low and high < count:
            route += [(low, high), (high, low)]
    return lax.ppermute(block, axis, route)


def pair_views(first_moment, second_moment, row_halves, column_halves):
    other_a = swapped(first_moment, "tile", 0)
    other_b = swapped(second_moment, "tile", 1)
    joined_a = jnp.where(
        column_halves == 0,
        jnp.concatenate([first_moment, other_a], axis=1),
        jnp.concatenate([other_a, first_moment], axis=1),
    )
    joined_b = jnp.where(
        row_halves == 0,
        jnp.concatenate([second_moment, other_b], axis=1),
        jnp.concatenate([other_b, second_moment], axis=1),
    )
    return (joined_a, joined_b)


def moment_pair(total, squares, batch_images):
    column_mean = total / batch_images
    var = squares / batch_images - column_mean * column_mean
    return (column_mean, lax.rsqrt(var + 1e-05))


def col_sums(values):
    as_float = values.astype(jnp.float32)
    return (jnp.sum(as_float, axis=0), jnp.sum(as_float * as_float, axis=0))


def reduced_device(left_outputs, right_outputs):
    rows, quart = left_outputs.shape
    half = 2 * quart
    feats = 4 * quart
    dp_count = lax.axis_size("dp")
    batch_images = rows * dp_count
    tpos = lax.axis_index("tile")
    row_halves = tpos // 2
    column_halves = tpos % 2
    sum_a, sq_a = col_sums(left_outputs)
    sum_b, sq_b = col_sums(right_outputs)
    sum_a, sq_a, sum_b, sq_b = lax.psum((sum_a, sq_a, sum_b, sq_b), "dp")
    left_mean, left_inverse_deviation = moment_pair(sum_a, sq_a, batch_images)
    right_mean, right_inverse_deviation = moment_pair(sum_b, sq_b, batch_images)
    standardized_left = (left_outputs.astype(jnp.float32) - left_mean) * left_inverse_deviation
    standardized_right = (right_outputs.astype(jnp.float32) - right_mean) * right_inverse_deviation
    half_a, cols_b = pair_views(
        standardized_left.astype(jnp.bfloat16),
        standardized_right.astype(jnp.bfloat16),
        row_halves,
        column_halves,
    )
    col_local = jnp.arange(half, dtype=jnp.int32)
    col_ids = quart * column_halves + col_local + jnp.where(col_local >= quart, quart, 0)
    owned = half // dp_count
    picked = half_a
    corr_rows = (
        lax.psum_scatter(
            lax.dot_general(
                picked, cols_b, (((0,), (0,)), ((), ())), preferred_element_type=jnp.float32
            ),
            "dp",
            scatter_dimension=0,
            tiled=True,
        )
        / batch_images
    )
    row_ids = half * row_halves + lax.axis_index("dp") * owned + jnp.arange(owned, dtype=jnp.int32)
    diagonal = row_ids[:, None] == col_ids[None, :]
    part_loss = jnp.sum(
        jnp.where(diagonal, (1.0 - corr_rows) ** 2, off_weight * corr_rows * corr_rows)
    )
    loss = lax.psum(part_loss, ("dp", "tile")) / feats
    dcorr_part = jnp.where(diagonal, corr_rows - 1.0, off_weight * corr_rows).astype(jnp.bfloat16)
    piece = lax.all_gather(dcorr_part, "dp", axis=0, tiled=True)
    block_a = lax.dot_general(
        cols_b, piece, (((1,), (1,)), ((), ())), preferred_element_type=jnp.float32
    )
    picked = half_a
    into_b = jnp.dot(picked, piece, preferred_element_type=jnp.float32)
    other_a = swapped(block_a.astype(jnp.bfloat16), "tile", 0).astype(block_a.dtype)
    other_b = swapped(into_b.astype(jnp.bfloat16), "tile", 1).astype(into_b.dtype)
    normed_grad_left = lax.dynamic_slice_in_dim(block_a + other_a, column_halves * quart, quart, 1)
    normed_grad_right = lax.dynamic_slice_in_dim(into_b + other_b, row_halves * quart, quart, 1)
    first_moment_left, second_moment_left, first_moment_right, second_moment_right = lax.psum(
        (
            jnp.sum(normed_grad_left, axis=0),
            jnp.sum(normed_grad_left * standardized_left, axis=0),
            jnp.sum(normed_grad_right, axis=0),
            jnp.sum(normed_grad_right * standardized_right, axis=0),
        ),
        "dp",
    )
    left_gradient = (
        left_inverse_deviation
        * (
            normed_grad_left
            - first_moment_left / batch_images
            - standardized_left * (second_moment_left / batch_images)
        )
    ).astype(jnp.bfloat16)
    right_gradient = (
        right_inverse_deviation
        * (
            normed_grad_right
            - first_moment_right / batch_images
            - standardized_right * (second_moment_right / batch_images)
        )
    ).astype(jnp.bfloat16)
    return (left_gradient, right_gradient, corr_rows[None, :, :], jnp.reshape(loss, (1,)))


def fold_rows(values):
    rows, width = values.shape
    return jnp.sum(values.reshape(rows // 8, 8, width), axis=0)


def fold_lanes(values):
    return sum(values[:, at : at + 128] for at in range(0, values.shape[1], 128))


def column_mean(block):
    rows, width = block.shape
    folded = jnp.zeros((8, width), jnp.float32)
    for at in range(0, rows, 64):
        folded = folded + fold_rows(block[at : at + 64, :].astype(jnp.float32))
    return jnp.sum(folded, axis=0, keepdims=True) / rows


def add_sums(sums, centred, low):
    return [
        sums[0] + fold_rows(centred),
        sums[1] + fold_rows(centred * centred),
        sums[2] + fold_rows(low.astype(jnp.float32)),
    ]


def rows_of(values):
    pad = jnp.zeros((8 - len(values), values[0].shape[1]), jnp.float32)
    return jnp.concatenate([*values, pad], axis=0)


def joined_sums(row, sums):
    return [row[i + 1 : i + 2, :] + jnp.sum(s, axis=0, keepdims=True) for i, s in enumerate(sums)]


def moments(sums, images):
    total, squares, rounded = sums
    delta = total / images
    return delta, lax.rsqrt(squares / images - delta * delta + 1e-05), rounded / images - delta


def three_parts(row):
    high = row.astype(jnp.bfloat16)
    rest = row - high.astype(jnp.float32)
    middle = rest.astype(jnp.bfloat16)
    low = (rest - middle.astype(jnp.float32)).astype(jnp.bfloat16)
    return [high, middle, low]


def split_rows(values):
    parts = sum([three_parts(v) for v in values], [])
    pad = jnp.zeros((4, values[0].shape[1]), jnp.float32)
    return jnp.concatenate([*(p.astype(jnp.float32) for p in parts), pad], axis=0).astype(
        jnp.bfloat16
    )


def joined_rows(ref, at):
    parts = ref[at : at + 16, :].astype(jnp.float32)
    part = lambda i: parts[i : i + 1]
    return [part(3 * i) + part(3 * i + 1) + part(3 * i + 2) for i in range(4)]


def lanes_to_row(partial):
    ones = jnp.ones((16, partial.shape[1]), jnp.bfloat16)
    high = partial.astype(jnp.bfloat16)
    low = (partial - high.astype(jnp.float32)).astype(jnp.bfloat16)
    row = dot_rows(ones, high) + dot_rows(ones, low)
    return row[:1, :]


def dot_rows(left, right):
    return lax.dot_general(
        left, right, (((1,), (1,)), ((), ())), preferred_element_type=jnp.float32
    )


def dot(left, right):
    return jnp.dot(left, right, preferred_element_type=jnp.float32)


def pick(mask, outer, inner, piece):
    return jnp.where(
        mask[0:1, :] != 0.0, outer[piece, :].astype(jnp.float32), inner[piece, :].astype(jnp.float32)
    )


def pick_kernel(mask, outer, inner, out):
    for at in range(0, outer.shape[0], 64):
        piece = slice(at, at + 64)
        out[piece, :] = pick(mask, outer, inner, piece).astype(out.dtype)


def right_sums_kernel(first, second, third, row):
    rows, quart = first.shape
    shift = column_mean(first)
    sums = [jnp.zeros((8, quart), jnp.float32)] * 3
    for block in (first, second, third):
        for at in range(0, rows, 64):
            centred = block[at : at + 64, :].astype(jnp.float32) - shift
            sums = add_sums(sums, centred, centred.astype(jnp.bfloat16))
    row[...] = rows_of([shift] + [jnp.sum(s, axis=0, keepdims=True) for s in sums])


def late_kernel(images, turned, mask, outer, inner, row, out):
    rows, quart = outer.shape
    shift = row[0:1, :]
    sums = [jnp.zeros((8, quart), jnp.float32)] * 3
    for at in range(0, rows, 128):
        piece = slice(at, at + 128)
        centred = pick(mask, outer, inner, piece) - shift
        low = centred.astype(jnp.bfloat16)
        if turned:
            out[:quart, piece] = jnp.transpose(low)
        else:
            out[piece, :] = low
        sums = add_sums(sums, centred, low)
    delta, rstd, gap = moments(joined_sums(row, sums), images)
    out[rows:, :] = split_rows([shift + delta, rstd, gap, delta])


def products_kernel(*refs):
    lefts, rights = refs[0:6], refs[6:12]
    partner_own, partner_other, own_all, row_other, zero_own, zero_other = refs[12:18]
    low_left, low_right = refs[18:]
    rows, quart = lefts[0].shape
    width = quart // 2
    for half in range(2):
        lanes = slice(half * quart, (half + 1) * quart)
        shift = column_mean(lefts[half])
        sums = [jnp.zeros((8, quart), jnp.float32)] * 3
        for block in range(3):
            source = lefts[2 * block + half]
            for at in range(0, rows, 64):
                centred = source[at : at + 64, :].astype(jnp.float32) - shift
                low = centred.astype(jnp.bfloat16)
                low_left[block * rows + at : block * rows + at + 64, lanes] = low
                if block == 0:
                    (zero_own, zero_other)[half][at : at + 64, :] = low
                if half:
                    sums = add_sums(sums, centred, low)
        if half:
            row_other[...] = rows_of([shift] + [jnp.sum(s, axis=0, keepdims=True) for s in sums])
    for half in range(2):
        lanes = slice(half * quart, (half + 1) * quart)
        shift = column_mean(rights[half])
        for block in range(3):
            source = rights[2 * block + half]
            for at in range(0, rows, 128):
                low = (source[at : at + 128, :].astype(jnp.float32) - shift).astype(jnp.bfloat16)
                low_right[lanes, block * rows + at : block * rows + at + 128] = jnp.transpose(low)
    for tile in range(4):
        wide = slice(tile * width, (tile + 1) * width)
        inner = slice((tile % 2) * width, (tile % 2 + 1) * width)
        target = partner_own if tile < 2 else partner_other
        target[:, inner] = dot(low_right[quart:, :], low_left[:, wide])
        own_all[:, wide] = dot(low_right[:quart, :], low_left[:, wide])


def left_operand(zero, late, target, lanes):
    rows, quart = zero.shape
    _, _, gap, delta = joined_rows(late, rows)
    high, middle, _ = three_parts(delta)
    target[:rows, lanes] = zero[...]
    extra = [high.astype(jnp.float32), middle.astype(jnp.float32), gap]
    pad = jnp.zeros((13, quart), jnp.float32)
    target[rows:, lanes] = jnp.concatenate([*extra, pad], axis=0).astype(jnp.bfloat16)


def without_extra(terms, rows):
    return terms[:rows] - (terms[rows : rows + 1] + terms[rows + 1 : rows + 2] + terms[rows + 2 : rows + 3])


def scale_columns(late_b, images):
    quart = late_b.shape[1]
    _, rstd, _, delta = joined_rows(late_b, quart)
    columns = jnp.transpose(rows_of([rstd / images, delta * rstd]))
    return columns[:, 0:1], columns[:, 1:2]


def partner_kernel(images, part, late, zero, sums, late_b, *refs):
    if part:
        (terms_in, across_in, vec_in, partial_out, e_out, vec_out, left) = refs
    else:
        (terms_out, across_out, e_out, vec_out, left) = refs
    rows, quart = zero.shape
    width = quart // 2
    _, rstd, _, delta = joined_rows(late, rows)
    left_operand(zero, late, left, slice(0, quart))
    scale_col, delta_col = scale_columns(late_b, images)
    across = across_in[...] if part else jnp.zeros((quart, 128), jnp.float32)
    down = []
    for tile in range(2):
        at = slice(tile * width, (tile + 1) * width)
        total = sums[:, at] + dot(late_b[:quart, :], late[:rows, at])
        corr = (total * scale_col - delta_col * delta[:, at]) * rstd[:, at]
        e_out[:, at] = (corr * (off_weight * rstd[:, at])).astype(jnp.bfloat16)
        square = corr * corr
        across = across + fold_lanes(square)
        down.append(jnp.sum(square, axis=0, keepdims=True))
    second_a = off_weight * jnp.concatenate(down, axis=1)
    if part:
        vec_out[...] = rows_of([second_a, second_a + vec_in[0:1, :]])
        nothing = jnp.zeros((1, quart), jnp.float32)
        second = off_weight * lanes_to_row(across)
        partial_out[rows:, :] = split_rows([second, nothing, nothing, nothing])
    else:
        vec_out[...] = rows_of([second_a])
        across_out[...] = across
    for tile in range(2):
        at = slice(tile * width, (tile + 1) * width)
        terms = dot_rows(left[...], e_out[at, :])
        if part:
            partial_out[:rows, at] = without_extra(terms + terms_in[:, at], rows).astype(
                jnp.bfloat16
            )
        else:
            terms_out[:, at] = terms


def own_kernel(images, flags, *refs):
    (late_own, late_other, first_own, first_other, zero_own, zero_other, sums, late_b) = refs[:8]
    (late_b_other, first_b, first_b_other, e_left, e_right, partner_own, partner_other) = refs[8:15]
    (vec_own, vec_other, vec_core, right_out, left_out, left_partial_out, mine_out) = refs[15:22]
    (own_loss_out, loss_out, left, norm_b, e_own, mine_own, mine_partner) = refs[22:]
    rows, quart = zero_own.shape
    width = quart // 2
    lower, upper = slice(0, quart), slice(quart, 2 * quart)
    stats_own, stats_other = joined_rows(late_own, rows), joined_rows(late_other, rows)
    both = lambda i: jnp.concatenate([stats_own[i], stats_other[i]], axis=1)
    offset, rstd, _, delta = [both(i) for i in range(4)]
    left_operand(zero_own, late_own, left, lower)
    left_operand(zero_other, late_other, left, upper)
    own_b = joined_rows(late_b, quart)
    other_b = joined_rows(late_b_other, quart)
    for source, stats, lanes in ((first_b, own_b, lower), (first_b_other, other_b, upper)):
        for at in range(0, rows, 64):
            piece = slice(at, at + 64)
            norm_b[piece, lanes] = (
                (source[piece, :].astype(jnp.float32) - stats[0]) * stats[1]
            ).astype(jnp.bfloat16)
        rest = jnp.broadcast_to(stats[2] * stats[1], (16, quart))
        norm_b[rows:, lanes] = rest.astype(jnp.bfloat16)

    def tile_corr(late, inner, total, columns, block):
        scale_col, delta_col = columns
        total = total + dot(block[:quart, :], late[:rows, inner])
        row = joined_rows(late, rows)
        return (total * scale_col - delta_col * row[3][:, inner]) * row[1][:, inner]

    columns = scale_columns(late_b, images)
    columns_partner = scale_columns(late_b_other, images)
    across = jnp.zeros((quart, 128), jnp.float32)
    losses = jnp.zeros((8, 128), jnp.float32)
    down, diagonals = [], []
    for tile in range(4):
        at = slice(tile * width, (tile + 1) * width)
        inner = slice((tile % 2) * width, (tile % 2 + 1) * width)
        late = late_own if tile < 2 else late_other
        corr = tile_corr(late, inner, sums[:, at], columns, late_b)
        dcorr = off_weight * corr
        product = dcorr * corr
        loss = product
        if tile < 2:
            feature = lax.broadcasted_iota(jnp.int32, (quart, width), 0)
            lane = lax.broadcasted_iota(jnp.int32, (quart, width), 1) + tile * width
            diagonal = feature == lane
            slope = jnp.where(diagonal, (corr - 1.0).astype(jnp.bfloat16).astype(jnp.float32), 0.0)
            diagonals.append(jnp.sum(slope, axis=0, keepdims=True))
            dcorr = jnp.where(diagonal, 0.0, dcorr)
            product = jnp.where(diagonal, slope * corr, product)
            loss = jnp.where(diagonal, (1.0 - corr) * (1.0 - corr), loss)
        e_own[:, at] = (dcorr * rstd[:, at]).astype(jnp.bfloat16)
        across = across + fold_lanes(product)
        losses = losses + fold_rows(fold_lanes(loss))
        down.append(jnp.sum(product, axis=0, keepdims=True))

        @pl.when(flags[0] == tile)
        def _():
            mine_own[...] = corr
            partner = partner_own if tile < 2 else partner_other
            mine_partner[...] = tile_corr(
                late, inner, partner[:, inner], columns_partner, late_b_other
            )

    diagonal_row = jnp.concatenate(diagonals, axis=1)
    partner_second = jnp.concatenate([vec_own[0:1, :], vec_other[0:1, :]], axis=1)
    second_a = rstd * (partner_second + jnp.concatenate(down, axis=1))
    second_b = lanes_to_row(across)
    own_loss = jnp.sum(losses)
    own_loss_out[0, 0] = own_loss
    loss_out[0, 0] = own_loss + jnp.sum(vec_other[1:2, :] + vec_core[1:2, :])

    for tile in (2, 3, 0, 1):
        at = slice(tile * width, (tile + 1) * width)
        inner = slice((tile % 2) * width, (tile % 2 + 1) * width)
        source, e_partner = (first_own, e_left) if tile < 2 else (first_other, e_right)
        terms = dot(norm_b[:, lower], e_own[:, at]) + dot(norm_b[:, upper], e_partner[:, inner])
        xhat = (source[:, inner].astype(jnp.float32) - offset[:, at]) * rstd[:, at]
        value = terms[:rows] - terms[rows : rows + 1] - xhat * second_a[:, at]
        if tile < 2:
            slope = rstd[:, at] * diagonal_row[:, inner]
            left_out[:, inner] = value + norm_b[:rows, inner].astype(jnp.float32) * slope
        else:
            left_partial_out[:, inner] = value.astype(jnp.bfloat16)

    for tile in range(2):
        at = slice(tile * width, (tile + 1) * width)
        terms = dot_rows(left[...], e_own[at, :])
        xhat = (first_b[:, at].astype(jnp.float32) - own_b[0][:, at]) * own_b[1][:, at]
        norm_a = (first_own[:, at].astype(jnp.float32) - offset[:, at]) * rstd[:, at]
        norm_a = norm_a.astype(jnp.bfloat16).astype(jnp.float32)
        right_out[:, at] = (
            without_extra(terms, rows) - xhat * second_b[:, at] + norm_a * diagonal_row[:, at]
        )

    own_columns = jnp.transpose(mine_own[...])
    partner_columns = jnp.transpose(mine_partner[...])

    @pl.when(flags[1] == 0)
    def _():
        mine_out[:, lower] = own_columns
        mine_out[:, upper] = partner_columns

    @pl.when(flags[1] != 0)
    def _():
        mine_out[:, lower] = partner_columns
        mine_out[:, upper] = own_columns


def add_kernel(one, other, out):
    out[0, 0] = one[0, 0] + other[0, 0]


def final_kernel(right, from_x, late_b, first_b, left, from_core, right_out, left_out):
    rows, quart = left.shape
    offset, rstd, _, _ = joined_rows(late_b, quart)
    second = joined_rows(from_x, rows)[0]
    for at in range(0, rows, 64):
        piece = slice(at, at + 64)
        xhat = (first_b[piece, :].astype(jnp.float32) - offset) * rstd
        value = right[piece, :] + from_x[piece, :].astype(jnp.float32) - xhat * second
        right_out[piece, :] = (rstd * value).astype(jnp.bfloat16)
        value = left[piece, :] + from_core[piece, :].astype(jnp.float32)
        left_out[piece, :] = value.astype(jnp.bfloat16)


vmem = pl.BlockSpec(memory_space=pltpu.VMEM)
smem = pl.BlockSpec(memory_space=pltpu.SMEM)


def local_call(kernel, operands, outs, scratch=(), flops=2**20, room=8, held=()):
    moved = sum(x.size * x.dtype.itemsize for x in (*operands, *outs))

    def space(x):
        return smem if x.dtype == jnp.int32 or x.shape == (1, 1) else vmem

    return pl.pallas_call(
        kernel,
        out_shape=list(outs),
        in_specs=[space(x) for x in operands],
        out_specs=[space(x) for x in outs],
        scratch_shapes=list(scratch),
        compiler_params=pltpu.CompilerParams(vmem_limit_bytes=room * 2**20),
        cost_estimate=pl.CostEstimate(flops=flops, bytes_accessed=moved, transcendentals=0),
    )(*(pltpu.with_memory_space_constraint(x, pltpu.VMEM) if i in held else x for i, x in enumerate(operands)))


def gathered_device(left_outputs, right_outputs):
    rows, quart = left_outputs.shape
    half = 2 * quart
    feats = 4 * quart
    batch_images = rows * 4
    tpos = lax.axis_index("tile")
    dpos = lax.axis_index("dp")
    row_halves = tpos // 2
    column_halves = tpos % 2
    at_end = (dpos == 0) | (dpos == 3)
    owned_tile = jnp.where(dpos // 2 == column_halves, 0, 2) + dpos % 2
    flags = jnp.stack([owned_tile, row_halves]).astype(jnp.int32)
    mask = jnp.broadcast_to(at_end.astype(jnp.float32), (8, quart))
    mask, flags = lax.optimization_barrier((mask, flags))

    pairs = [(0, 1), (1, 0), (2, 3), (3, 2)]
    middle = [(1, 2), (2, 1)]
    outward = [(1, 0), (2, 3)]

    def along(block, route):
        return lax.ppermute(block, "dp", route)

    def core_swap(block):
        return swapped(block, "tile", 0)

    def x_swap(block):
        return swapped(block, "tile", 1)

    def after(value, *others):
        return lax.optimization_barrier((value, *others))

    gemm = 2 * rows * quart * quart
    width = quart // 2
    quarter_f32 = jax.ShapeDtypeStruct((rows, quart), jnp.float32)
    quarter_bf16 = jax.ShapeDtypeStruct((rows, quart), jnp.bfloat16)
    extended = jax.ShapeDtypeStruct((rows + 16, quart), jnp.bfloat16)
    row_out = jax.ShapeDtypeStruct((8, quart), jnp.float32)
    one_out = jax.ShapeDtypeStruct((1, 1), jnp.float32)
    across_shape = jax.ShapeDtypeStruct((quart, 128), jnp.float32)
    low = lambda n, m: pltpu.VMEM((n, m), jnp.bfloat16)

    def picked(outer, inner):
        return local_call(pick_kernel, (mask, outer, inner), (quarter_bf16,))[0]

    first_b = along(right_outputs, pairs)
    inner_b = along(right_outputs, middle)
    first_a = along(left_outputs, pairs)
    other_b0 = x_swap(right_outputs)
    other_a0 = core_swap(left_outputs)
    left_behind, first_a = after(left_outputs, first_a)
    inner_a = along(left_behind, middle)

    outer_b = along(inner_b, outward)
    third_b = along(first_b, middle)
    ready_b, other_b0 = after(first_b, other_b0)
    other_b1 = x_swap(ready_b)
    outer_a = along(inner_a, outward)
    third_a = along(first_a, middle)
    other_a1 = core_swap(first_a)

    last_b = along(third_b, outward)
    second_b = picked(outer_b, inner_b)
    row_b = local_call(right_sums_kernel, (right_outputs, first_b, second_b), (row_out,))[0]
    second_b, other_b1 = after(second_b, other_b1)
    other_b2 = x_swap(second_b)
    last_a = along(third_a, outward)
    second_a = picked(outer_a, inner_a)
    second_a, other_a1, row_b = after(second_a, other_a1, row_b)
    other_a2 = core_swap(second_a)

    (late_b,) = local_call(
        functools.partial(late_kernel, batch_images, True),
        (mask, last_b, third_b, row_b),
        (extended,),
        held=(0, 1, 2, 3),
    )
    late_b_other = x_swap(late_b)
    partner_own, partner_other, own_all, row_other, zero_own, zero_other = local_call(
        products_kernel,
        (left_outputs, other_a0, first_a, other_a1, second_a, other_a2)
        + (right_outputs, other_b0, first_b, other_b1, second_b, other_b2),
        (
            quarter_f32,
            quarter_f32,
            jax.ShapeDtypeStruct((quart, half), jnp.float32),
            row_out,
            quarter_bf16,
            quarter_bf16,
        ),
        [low(3 * rows, half), low(half, 3 * rows)],
        12 * gemm,
        room=20,
    )
    row_a = core_swap(row_other)
    (late_a,) = local_call(
        functools.partial(late_kernel, batch_images, False),
        (mask, last_a, third_a, row_a),
        (extended,),
        held=(0, 1, 2, 3),
    )
    late_a_other = core_swap(late_a)

    terms, across, e_left, vec_own = local_call(
        functools.partial(partner_kernel, batch_images, 0),
        (late_a, zero_own, partner_own, late_b_other),
        (
            jax.ShapeDtypeStruct((rows + 16, quart), jnp.float32),
            across_shape,
            quarter_bf16,
            row_out,
        ),
        [low(rows + 16, quart)],
        2 * gemm,
        room=12,
    )
    partial_right, e_right, vec_other = local_call(
        functools.partial(partner_kernel, batch_images, 1),
        (late_a_other, zero_other, partner_other, late_b_other, terms, across, vec_own),
        (extended, quarter_bf16, row_out),
        [low(rows + 16, quart)],
        2 * gemm,
        room=12,
    )
    from_x = x_swap(partial_right)
    vec_core = core_swap(vec_other)
    right_own, left_own, partial_left, mine, own_loss, loss = local_call(
        functools.partial(own_kernel, batch_images),
        (flags, late_a, late_a_other, left_outputs, other_a0, zero_own, zero_other, own_all)
        + (late_b, late_b_other, right_outputs, other_b0, e_left, e_right)
        + (partner_own, partner_other)
        + (vec_own, vec_other, vec_core),
        (
            quarter_f32,
            quarter_f32,
            quarter_bf16,
            jax.ShapeDtypeStruct((width, half), jnp.float32),
            one_out,
            one_out,
        ),
        [
            low(rows + 16, half),
            low(rows + 16, half),
            low(quart, half),
            pltpu.VMEM((quart, width), jnp.float32),
            pltpu.VMEM((quart, width), jnp.float32),
        ],
        8 * gemm,
        room=20,
    )
    from_core = core_swap(partial_left)
    core_loss = jnp.reshape(core_swap(jnp.reshape(own_loss, ())), (1, 1))
    (loss,) = local_call(add_kernel, (loss, core_loss), (one_out,))
    loss = jnp.reshape(loss, ())
    x_loss = x_swap(loss)
    right_gradient, left_gradient = local_call(
        final_kernel,
        (right_own, from_x, late_b, right_outputs, left_own, from_core),
        (quarter_bf16, quarter_bf16),
    )
    right_gradient, x_loss = after(right_gradient, x_loss)
    loss = jnp.reshape((loss + x_loss) / feats, (1,))
    return (left_gradient, right_gradient, mine[None, :, :], loss)


def solution(mesh):
    per_device = gathered_device if mesh.shape["dp"] == 4 else reduced_device
    return jax.shard_map(
        per_device,
        mesh=mesh,
        in_specs=(P(("groups", "dp"), "tile"), P(("groups", "dp"), "tile")),
        out_specs=(
            P(("groups", "dp"), "tile"),
            P(("groups", "dp"), "tile"),
            P(("groups", "tile"), "dp", None),
            P("groups"),
        ),
        check_vma=False,
    )
```

```python
import functools
import jax
import jax.numpy as jnp
from jax import lax
from jax.experimental import pallas as pl
from jax.experimental.pallas import tpu as pltpu
from jax.sharding import PartitionSpec as P

off_weight = 0.0051


def swapped(block, axis, bit):
    count = lax.axis_size(axis)
    route = []
    for low in range(count):
        high = low | 1 << bit
        if high != low and high < count:
            route += [(low, high), (high, low)]
    return lax.ppermute(block, axis, route)


def pair_views(first_moment, second_moment, row_halves, column_halves):
    other_a = swapped(first_moment, "tile", 0)
    other_b = swapped(second_moment, "tile", 1)
    joined_a = jnp.where(
        column_halves == 0,
        jnp.concatenate([first_moment, other_a], axis=1),
        jnp.concatenate([other_a, first_moment], axis=1),
    )
    joined_b = jnp.where(
        row_halves == 0,
        jnp.concatenate([second_moment, other_b], axis=1),
        jnp.concatenate([other_b, second_moment], axis=1),
    )
    return (joined_a, joined_b)


def moment_pair(total, squares, batch_images):
    column_mean = total / batch_images
    var = squares / batch_images - column_mean * column_mean
    return (column_mean, lax.rsqrt(var + 1e-05))


def col_sums(values):
    as_float = values.astype(jnp.float32)
    return (jnp.sum(as_float, axis=0), jnp.sum(as_float * as_float, axis=0))


def reduced_device(left_outputs, right_outputs):
    rows, quart = left_outputs.shape
    half = 2 * quart
    feats = 4 * quart
    dp_count = lax.axis_size("dp")
    batch_images = rows * dp_count
    tpos = lax.axis_index("tile")
    row_halves = tpos // 2
    column_halves = tpos % 2
    sum_a, sq_a = col_sums(left_outputs)
    sum_b, sq_b = col_sums(right_outputs)
    sum_a, sq_a, sum_b, sq_b = lax.psum((sum_a, sq_a, sum_b, sq_b), "dp")
    left_mean, left_inverse_deviation = moment_pair(sum_a, sq_a, batch_images)
    right_mean, right_inverse_deviation = moment_pair(sum_b, sq_b, batch_images)
    standardized_left = (left_outputs.astype(jnp.float32) - left_mean) * left_inverse_deviation
    standardized_right = (right_outputs.astype(jnp.float32) - right_mean) * right_inverse_deviation
    half_a, cols_b = pair_views(
        standardized_left.astype(jnp.bfloat16),
        standardized_right.astype(jnp.bfloat16),
        row_halves,
        column_halves,
    )
    col_local = jnp.arange(half, dtype=jnp.int32)
    col_ids = quart * column_halves + col_local + jnp.where(col_local >= quart, quart, 0)
    owned = half // dp_count
    picked = half_a
    corr_rows = (
        lax.psum_scatter(
            lax.dot_general(
                picked, cols_b, (((0,), (0,)), ((), ())), preferred_element_type=jnp.float32
            ),
            "dp",
            scatter_dimension=0,
            tiled=True,
        )
        / batch_images
    )
    row_ids = half * row_halves + lax.axis_index("dp") * owned + jnp.arange(owned, dtype=jnp.int32)
    diagonal = row_ids[:, None] == col_ids[None, :]
    part_loss = jnp.sum(
        jnp.where(diagonal, (1.0 - corr_rows) ** 2, off_weight * corr_rows * corr_rows)
    )
    loss = lax.psum(part_loss, ("dp", "tile")) / feats
    dcorr_part = jnp.where(diagonal, corr_rows - 1.0, off_weight * corr_rows).astype(jnp.bfloat16)
    piece = lax.all_gather(dcorr_part, "dp", axis=0, tiled=True)
    block_a = lax.dot_general(
        cols_b, piece, (((1,), (1,)), ((), ())), preferred_element_type=jnp.float32
    )
    picked = half_a
    into_b = jnp.dot(picked, piece, preferred_element_type=jnp.float32)
    other_a = swapped(block_a.astype(jnp.bfloat16), "tile", 0).astype(block_a.dtype)
    other_b = swapped(into_b.astype(jnp.bfloat16), "tile", 1).astype(into_b.dtype)
    normed_grad_left = lax.dynamic_slice_in_dim(block_a + other_a, column_halves * quart, quart, 1)
    normed_grad_right = lax.dynamic_slice_in_dim(into_b + other_b, row_halves * quart, quart, 1)
    first_moment_left, second_moment_left, first_moment_right, second_moment_right = lax.psum(
        (
            jnp.sum(normed_grad_left, axis=0),
            jnp.sum(normed_grad_left * standardized_left, axis=0),
            jnp.sum(normed_grad_right, axis=0),
            jnp.sum(normed_grad_right * standardized_right, axis=0),
        ),
        "dp",
    )
    left_gradient = (
        left_inverse_deviation
        * (
            normed_grad_left
            - first_moment_left / batch_images
            - standardized_left * (second_moment_left / batch_images)
        )
    ).astype(jnp.bfloat16)
    right_gradient = (
        right_inverse_deviation
        * (
            normed_grad_right
            - first_moment_right / batch_images
            - standardized_right * (second_moment_right / batch_images)
        )
    ).astype(jnp.bfloat16)
    return (left_gradient, right_gradient, corr_rows[None, :, :], jnp.reshape(loss, (1,)))


def fold_rows(values):
    rows, width = values.shape
    return jnp.sum(values.reshape(rows // 8, 8, width), axis=0)


def fold_lanes(values):
    return sum(values[:, at : at + 128] for at in range(0, values.shape[1], 128))


def column_mean(block):
    rows, width = block.shape
    folded = jnp.zeros((8, width), jnp.float32)
    for at in range(0, rows, 64):
        folded = folded + fold_rows(block[at : at + 64, :].astype(jnp.float32))
    return jnp.sum(folded, axis=0, keepdims=True) / rows


def add_sums(sums, centred, low):
    return [
        sums[0] + fold_rows(centred),
        sums[1] + fold_rows(centred * centred),
        sums[2] + fold_rows(low.astype(jnp.float32)),
    ]


def rows_of(values):
    pad = jnp.zeros((8 - len(values), values[0].shape[1]), jnp.float32)
    return jnp.concatenate([*values, pad], axis=0)


def joined_sums(row, sums):
    return [row[i + 1 : i + 2, :] + jnp.sum(s, axis=0, keepdims=True) for i, s in enumerate(sums)]


def moments(sums, images):
    total, squares, rounded = sums
    delta = total / images
    return delta, lax.rsqrt(squares / images - delta * delta + 1e-05), rounded / images - delta


def three_parts(row):
    high = row.astype(jnp.bfloat16)
    rest = row - high.astype(jnp.float32)
    middle = rest.astype(jnp.bfloat16)
    low = (rest - middle.astype(jnp.float32)).astype(jnp.bfloat16)
    return [high, middle, low]


def split_rows(values):
    parts = sum([three_parts(v) for v in values], [])
    pad = jnp.zeros((4, values[0].shape[1]), jnp.float32)
    return jnp.concatenate([*(p.astype(jnp.float32) for p in parts), pad], axis=0).astype(
        jnp.bfloat16
    )


def joined_rows(ref, at):
    parts = ref[at : at + 16, :].astype(jnp.float32)
    part = lambda i: parts[i : i + 1]
    return [part(3 * i) + part(3 * i + 1) + part(3 * i + 2) for i in range(4)]


def lanes_to_row(partial):
    ones = jnp.ones((16, partial.shape[1]), jnp.bfloat16)
    high = partial.astype(jnp.bfloat16)
    low = (partial - high.astype(jnp.float32)).astype(jnp.bfloat16)
    row = dot_rows(ones, high) + dot_rows(ones, low)
    return row[:1, :]


def dot_rows(left, right):
    return lax.dot_general(
        left, right, (((1,), (1,)), ((), ())), preferred_element_type=jnp.float32
    )


def dot(left, right):
    return jnp.dot(left, right, preferred_element_type=jnp.float32)


def pick(mask, outer, inner, piece):
    return jnp.where(
        mask[0:1, :] != 0.0, outer[piece, :].astype(jnp.float32), inner[piece, :].astype(jnp.float32)
    )


def pick_kernel(mask, outer, inner, out):
    for at in range(0, outer.shape[0], 64):
        piece = slice(at, at + 64)
        out[piece, :] = pick(mask, outer, inner, piece).astype(out.dtype)


def right_sums_kernel(first, second, third, row):
    rows, quart = first.shape
    shift = column_mean(first)
    sums = [jnp.zeros((8, quart), jnp.float32)] * 3
    for block in (first, second, third):
        for at in range(0, rows, 64):
            centred = block[at : at + 64, :].astype(jnp.float32) - shift
            sums = add_sums(sums, centred, centred.astype(jnp.bfloat16))
    row[...] = rows_of([shift] + [jnp.sum(s, axis=0, keepdims=True) for s in sums])


def late_kernel(images, turned, mask, outer, inner, row, out):
    rows, quart = outer.shape
    shift = row[0:1, :]
    sums = [jnp.zeros((8, quart), jnp.float32)] * 3
    for at in range(0, rows, 128):
        piece = slice(at, at + 128)
        centred = pick(mask, outer, inner, piece) - shift
        low = centred.astype(jnp.bfloat16)
        if turned:
            out[:quart, piece] = jnp.transpose(low)
        else:
            out[piece, :] = low
        sums = add_sums(sums, centred, low)
    delta, rstd, gap = moments(joined_sums(row, sums), images)
    out[rows:, :] = split_rows([shift + delta, rstd, gap, delta])


def products_kernel(*refs):
    lefts, rights = refs[0:6], refs[6:12]
    partner_own, partner_other, own_all, row_other, zero_own, zero_other = refs[12:18]
    low_left, low_right = refs[18:]
    rows, quart = lefts[0].shape
    width = quart // 2
    for half in range(2):
        lanes = slice(half * quart, (half + 1) * quart)
        shift = column_mean(lefts[half])
        sums = [jnp.zeros((8, quart), jnp.float32)] * 3
        for block in range(3):
            source = lefts[2 * block + half]
            for at in range(0, rows, 64):
                centred = source[at : at + 64, :].astype(jnp.float32) - shift
                low = centred.astype(jnp.bfloat16)
                low_left[block * rows + at : block * rows + at + 64, lanes] = low
                if block == 0:
                    (zero_own, zero_other)[half][at : at + 64, :] = low
                if half:
                    sums = add_sums(sums, centred, low)
        if half:
            row_other[...] = rows_of([shift] + [jnp.sum(s, axis=0, keepdims=True) for s in sums])
    for half in range(2):
        lanes = slice(half * quart, (half + 1) * quart)
        shift = column_mean(rights[half])
        for block in range(3):
            source = rights[2 * block + half]
            for at in range(0, rows, 128):
                low = (source[at : at + 128, :].astype(jnp.float32) - shift).astype(jnp.bfloat16)
                low_right[lanes, block * rows + at : block * rows + at + 128] = jnp.transpose(low)
    for tile in range(4):
        wide = slice(tile * width, (tile + 1) * width)
        inner = slice((tile % 2) * width, (tile % 2 + 1) * width)
        target = partner_own if tile < 2 else partner_other
        target[:, inner] = dot(low_right[quart:, :], low_left[:, wide])
        own_all[:, wide] = dot(low_right[:quart, :], low_left[:, wide])


def left_operand(zero, late, target, lanes):
    rows, quart = zero.shape
    _, _, gap, delta = joined_rows(late, rows)
    high, middle, _ = three_parts(delta)
    target[:rows, lanes] = zero[...]
    extra = [high.astype(jnp.float32), middle.astype(jnp.float32), gap]
    pad = jnp.zeros((13, quart), jnp.float32)
    target[rows:, lanes] = jnp.concatenate([*extra, pad], axis=0).astype(jnp.bfloat16)


def without_extra(terms, rows):
    return terms[:rows] - (terms[rows : rows + 1] + terms[rows + 1 : rows + 2] + terms[rows + 2 : rows + 3])


def scale_columns(late_b, images):
    quart = late_b.shape[1]
    _, rstd, _, delta = joined_rows(late_b, quart)
    columns = jnp.transpose(rows_of([rstd / images, delta * rstd]))
    return columns[:, 0:1], columns[:, 1:2]


def partner_kernel(images, part, late, zero, sums, late_b, *refs):
    if part:
        (terms_in, across_in, vec_in, partial_out, e_out, vec_out, left) = refs
    else:
        (terms_out, across_out, e_out, vec_out, left) = refs
    rows, quart = zero.shape
    width = quart // 2
    _, rstd, _, delta = joined_rows(late, rows)
    left_operand(zero, late, left, slice(0, quart))
    scale_col, delta_col = scale_columns(late_b, images)
    across = across_in[...] if part else jnp.zeros((quart, 128), jnp.float32)
    down = []
    for tile in range(2):
        at = slice(tile * width, (tile + 1) * width)
        total = sums[:, at] + dot(late_b[:quart, :], late[:rows, at])
        corr = (total * scale_col - delta_col * delta[:, at]) * rstd[:, at]
        e_out[:, at] = (corr * (off_weight * rstd[:, at])).astype(jnp.bfloat16)
        square = corr * corr
        across = across + fold_lanes(square)
        down.append(jnp.sum(square, axis=0, keepdims=True))
    second_a = off_weight * jnp.concatenate(down, axis=1)
    if part:
        vec_out[...] = rows_of([second_a, second_a + vec_in[0:1, :]])
        nothing = jnp.zeros((1, quart), jnp.float32)
        second = off_weight * lanes_to_row(across)
        partial_out[rows:, :] = split_rows([second, nothing, nothing, nothing])
    else:
        vec_out[...] = rows_of([second_a])
        across_out[...] = across
    for tile in range(2):
        at = slice(tile * width, (tile + 1) * width)
        terms = dot_rows(left[...], e_out[at, :])
        if part:
            partial_out[:rows, at] = without_extra(terms + terms_in[:, at], rows).astype(
                jnp.bfloat16
            )
        else:
            terms_out[:, at] = terms


def own_kernel(images, flags, *refs):
    (late_own, late_other, first_own, first_other, zero_own, zero_other, sums, late_b) = refs[:8]
    (late_b_other, first_b, first_b_other, e_left, e_right, partner_own, partner_other) = refs[8:15]
    (vec_own, vec_other, vec_core, right_out, left_out, left_partial_out, mine_out) = refs[15:22]
    (own_loss_out, loss_out, left, norm_b, e_own, mine_own, mine_partner) = refs[22:]
    rows, quart = zero_own.shape
    width = quart // 2
    lower, upper = slice(0, quart), slice(quart, 2 * quart)
    stats_own, stats_other = joined_rows(late_own, rows), joined_rows(late_other, rows)
    both = lambda i: jnp.concatenate([stats_own[i], stats_other[i]], axis=1)
    offset, rstd, _, delta = [both(i) for i in range(4)]
    left_operand(zero_own, late_own, left, lower)
    left_operand(zero_other, late_other, left, upper)
    own_b = joined_rows(late_b, quart)
    other_b = joined_rows(late_b_other, quart)
    for source, stats, lanes in ((first_b, own_b, lower), (first_b_other, other_b, upper)):
        for at in range(0, rows, 64):
            piece = slice(at, at + 64)
            norm_b[piece, lanes] = (
                (source[piece, :].astype(jnp.float32) - stats[0]) * stats[1]
            ).astype(jnp.bfloat16)
        rest = jnp.broadcast_to(stats[2] * stats[1], (16, quart))
        norm_b[rows:, lanes] = rest.astype(jnp.bfloat16)

    def tile_corr(late, inner, total, columns, block):
        scale_col, delta_col = columns
        total = total + dot(block[:quart, :], late[:rows, inner])
        row = joined_rows(late, rows)
        return (total * scale_col - delta_col * row[3][:, inner]) * row[1][:, inner]

    columns = scale_columns(late_b, images)
    columns_partner = scale_columns(late_b_other, images)
    across = jnp.zeros((quart, 128), jnp.float32)
    losses = jnp.zeros((8, 128), jnp.float32)
    down, diagonals = [], []
    for tile in range(4):
        at = slice(tile * width, (tile + 1) * width)
        inner = slice((tile % 2) * width, (tile % 2 + 1) * width)
        late = late_own if tile < 2 else late_other
        corr = tile_corr(late, inner, sums[:, at], columns, late_b)
        dcorr = off_weight * corr
        product = dcorr * corr
        loss = product
        if tile < 2:
            feature = lax.broadcasted_iota(jnp.int32, (quart, width), 0)
            lane = lax.broadcasted_iota(jnp.int32, (quart, width), 1) + tile * width
            diagonal = feature == lane
            slope = jnp.where(diagonal, (corr - 1.0).astype(jnp.bfloat16).astype(jnp.float32), 0.0)
            diagonals.append(jnp.sum(slope, axis=0, keepdims=True))
            dcorr = jnp.where(diagonal, 0.0, dcorr)
            product = jnp.where(diagonal, slope * corr, product)
            loss = jnp.where(diagonal, (1.0 - corr) * (1.0 - corr), loss)
        e_own[:, at] = (dcorr * rstd[:, at]).astype(jnp.bfloat16)
        across = across + fold_lanes(product)
        losses = losses + fold_rows(fold_lanes(loss))
        down.append(jnp.sum(product, axis=0, keepdims=True))

        @pl.when(flags[0] == tile)
        def _():
            mine_own[...] = corr
            partner = partner_own if tile < 2 else partner_other
            mine_partner[...] = tile_corr(
                late, inner, partner[:, inner], columns_partner, late_b_other
            )

    diagonal_row = jnp.concatenate(diagonals, axis=1)
    partner_second = jnp.concatenate([vec_own[0:1, :], vec_other[0:1, :]], axis=1)
    second_a = rstd * (partner_second + jnp.concatenate(down, axis=1))
    second_b = lanes_to_row(across)
    own_loss = jnp.sum(losses)
    own_loss_out[...] = jnp.broadcast_to(own_loss, (8, 128))
    loss = own_loss + jnp.sum(vec_other[1:2, :] + vec_core[1:2, :])
    loss_out[...] = jnp.broadcast_to(loss, (8, 128))

    for tile in (2, 3, 0, 1):
        at = slice(tile * width, (tile + 1) * width)
        inner = slice((tile % 2) * width, (tile % 2 + 1) * width)
        source, e_partner = (first_own, e_left) if tile < 2 else (first_other, e_right)
        terms = dot(norm_b[:, lower], e_own[:, at]) + dot(norm_b[:, upper], e_partner[:, inner])
        xhat = (source[:, inner].astype(jnp.float32) - offset[:, at]) * rstd[:, at]
        value = terms[:rows] - terms[rows : rows + 1] - xhat * second_a[:, at]
        if tile < 2:
            slope = rstd[:, at] * diagonal_row[:, inner]
            left_out[:, inner] = value + norm_b[:rows, inner].astype(jnp.float32) * slope
        else:
            left_partial_out[:, inner] = value.astype(jnp.bfloat16)

    for tile in range(2):
        at = slice(tile * width, (tile + 1) * width)
        terms = dot_rows(left[...], e_own[at, :])
        xhat = (first_b[:, at].astype(jnp.float32) - own_b[0][:, at]) * own_b[1][:, at]
        norm_a = (first_own[:, at].astype(jnp.float32) - offset[:, at]) * rstd[:, at]
        norm_a = norm_a.astype(jnp.bfloat16).astype(jnp.float32)
        right_out[:, at] = (
            without_extra(terms, rows) - xhat * second_b[:, at] + norm_a * diagonal_row[:, at]
        )

    own_columns = jnp.transpose(mine_own[...])
    partner_columns = jnp.transpose(mine_partner[...])

    @pl.when(flags[1] == 0)
    def _():
        mine_out[:, lower] = own_columns
        mine_out[:, upper] = partner_columns

    @pl.when(flags[1] != 0)
    def _():
        mine_out[:, lower] = partner_columns
        mine_out[:, upper] = own_columns


def add_kernel(one, other, out):
    out[...] = one[...] + other[...]


def loss_kernel(feats, one, other, out):
    out[0] = (one[0, 0] + other[0, 0]) / feats


def final_kernel(right, from_x, late_b, first_b, left, from_core, right_out, left_out):
    rows, quart = left.shape
    offset, rstd, _, _ = joined_rows(late_b, quart)
    second = joined_rows(from_x, rows)[0]
    for at in range(0, rows, 64):
        piece = slice(at, at + 64)
        xhat = (first_b[piece, :].astype(jnp.float32) - offset) * rstd
        value = right[piece, :] + from_x[piece, :].astype(jnp.float32) - xhat * second
        right_out[piece, :] = (rstd * value).astype(jnp.bfloat16)
        value = left[piece, :] + from_core[piece, :].astype(jnp.float32)
        left_out[piece, :] = value.astype(jnp.bfloat16)


vmem = pl.BlockSpec(memory_space=pltpu.VMEM)
smem = pl.BlockSpec(memory_space=pltpu.SMEM)


def local_call(kernel, operands, outs, scratch=(), flops=2**20, room=8, held=()):
    moved = sum(x.size * x.dtype.itemsize for x in (*operands, *outs))

    def space(x):
        return smem if x.ndim == 1 else vmem

    return pl.pallas_call(
        kernel,
        out_shape=list(outs),
        in_specs=[space(x) for x in operands],
        out_specs=[space(x) for x in outs],
        scratch_shapes=list(scratch),
        compiler_params=pltpu.CompilerParams(vmem_limit_bytes=room * 2**20),
        cost_estimate=pl.CostEstimate(flops=flops, bytes_accessed=moved, transcendentals=0),
    )(*(pltpu.with_memory_space_constraint(x, pltpu.VMEM) if i in held else x for i, x in enumerate(operands)))


def gathered_device(left_outputs, right_outputs):
    rows, quart = left_outputs.shape
    half = 2 * quart
    feats = 4 * quart
    batch_images = rows * 4
    tpos = lax.axis_index("tile")
    dpos = lax.axis_index("dp")
    row_halves = tpos // 2
    column_halves = tpos % 2
    at_end = (dpos == 0) | (dpos == 3)
    owned_tile = jnp.where(dpos // 2 == column_halves, 0, 2) + dpos % 2
    flags = jnp.stack([owned_tile, row_halves]).astype(jnp.int32)
    mask = jnp.broadcast_to(at_end.astype(jnp.float32), (8, quart))

    pairs = [(0, 1), (1, 0), (2, 3), (3, 2)]
    middle = [(1, 2), (2, 1)]
    outward = [(1, 0), (2, 3)]

    def along(block, route):
        return lax.ppermute(block, "dp", route)

    def core_swap(block):
        return swapped(block, "tile", 0)

    def x_swap(block):
        return swapped(block, "tile", 1)

    def after(value, *others):
        return lax.optimization_barrier((value, *others))

    gemm = 2 * rows * quart * quart
    width = quart // 2
    quarter_f32 = jax.ShapeDtypeStruct((rows, quart), jnp.float32)
    quarter_bf16 = jax.ShapeDtypeStruct((rows, quart), jnp.bfloat16)
    extended = jax.ShapeDtypeStruct((rows + 16, quart), jnp.bfloat16)
    row_out = jax.ShapeDtypeStruct((8, quart), jnp.float32)
    one_out = jax.ShapeDtypeStruct((8, 128), jnp.float32)
    across_shape = jax.ShapeDtypeStruct((quart, 128), jnp.float32)
    low = lambda n, m: pltpu.VMEM((n, m), jnp.bfloat16)

    def picked(outer, inner):
        return local_call(pick_kernel, (mask, outer, inner), (quarter_bf16,))[0]

    first_b = along(right_outputs, pairs)
    inner_b = along(right_outputs, middle)
    first_a = along(left_outputs, pairs)
    other_b0 = x_swap(right_outputs)
    other_a0, mask, flags = after(core_swap(left_outputs), mask, flags)
    left_behind, first_a, other_a0 = after(left_outputs, first_a, other_a0)
    inner_a = along(left_behind, middle)

    outer_b = along(inner_b, outward)
    third_b = along(first_b, middle)
    ready_b, other_b0 = after(first_b, other_b0)
    other_b1 = x_swap(ready_b)
    outer_a = along(inner_a, outward)
    third_a = along(first_a, middle)
    other_a1 = core_swap(first_a)

    last_b = along(third_b, outward)
    second_b = picked(outer_b, inner_b)
    row_b = local_call(right_sums_kernel, (right_outputs, first_b, second_b), (row_out,))[0]
    second_b, other_b1, other_a1 = after(second_b, other_b1, other_a1)
    other_b2 = x_swap(second_b)
    last_a = along(third_a, outward)
    second_a = picked(outer_a, inner_a)
    second_a, row_b = after(second_a, row_b)
    other_a2 = core_swap(second_a)

    (late_b,) = local_call(
        functools.partial(late_kernel, batch_images, True),
        (mask, last_b, third_b, row_b),
        (extended,),
        held=(0, 1, 2, 3),
    )
    late_b_other = x_swap(late_b)
    partner_own, partner_other, own_all, row_other, zero_own, zero_other = local_call(
        products_kernel,
        (left_outputs, other_a0, first_a, other_a1, second_a, other_a2)
        + (right_outputs, other_b0, first_b, other_b1, second_b, other_b2),
        (
            quarter_f32,
            quarter_f32,
            jax.ShapeDtypeStruct((quart, half), jnp.float32),
            row_out,
            quarter_bf16,
            quarter_bf16,
        ),
        [low(3 * rows, half), low(half, 3 * rows)],
        12 * gemm,
        room=20,
    )
    row_a = core_swap(row_other)
    (late_a,) = local_call(
        functools.partial(late_kernel, batch_images, False),
        (mask, last_a, third_a, row_a),
        (extended,),
        held=(0, 1, 2, 3),
    )
    late_a_other = core_swap(late_a)

    terms, across, e_left, vec_own = local_call(
        functools.partial(partner_kernel, batch_images, 0),
        (late_a, zero_own, partner_own, late_b_other),
        (
            jax.ShapeDtypeStruct((rows + 16, quart), jnp.float32),
            across_shape,
            quarter_bf16,
            row_out,
        ),
        [low(rows + 16, quart)],
        2 * gemm,
        room=12,
    )
    partial_right, e_right, vec_other = local_call(
        functools.partial(partner_kernel, batch_images, 1),
        (late_a_other, zero_other, partner_other, late_b_other, terms, across, vec_own),
        (extended, quarter_bf16, row_out),
        [low(rows + 16, quart)],
        2 * gemm,
        room=12,
    )
    from_x = x_swap(partial_right)
    vec_core = core_swap(vec_other)
    right_own, left_own, partial_left, mine, own_loss, loss = local_call(
        functools.partial(own_kernel, batch_images),
        (flags, late_a, late_a_other, left_outputs, other_a0, zero_own, zero_other, own_all)
        + (late_b, late_b_other, right_outputs, other_b0, e_left, e_right)
        + (partner_own, partner_other)
        + (vec_own, vec_other, vec_core),
        (
            quarter_f32,
            quarter_f32,
            quarter_bf16,
            jax.ShapeDtypeStruct((width, half), jnp.float32),
            one_out,
            one_out,
        ),
        [
            low(rows + 16, half),
            low(rows + 16, half),
            low(quart, half),
            pltpu.VMEM((quart, width), jnp.float32),
            pltpu.VMEM((quart, width), jnp.float32),
        ],
        8 * gemm,
        room=20,
    )
    from_core = core_swap(partial_left)
    core_loss = core_swap(own_loss)
    (loss,) = local_call(add_kernel, (loss, core_loss), (one_out,))
    x_loss = x_swap(loss)
    right_gradient, left_gradient = local_call(
        final_kernel,
        (right_own, from_x, late_b, right_outputs, left_own, from_core),
        (quarter_bf16, quarter_bf16),
    )
    right_gradient, x_loss = after(right_gradient, x_loss)
    (loss,) = local_call(
        functools.partial(loss_kernel, feats),
        (loss, x_loss),
        (jax.ShapeDtypeStruct((1,), jnp.float32),),
    )
    return (left_gradient, right_gradient, mine[None, :, :], loss)


def solution(mesh):
    per_device = gathered_device if mesh.shape["dp"] == 4 else reduced_device
    return jax.shard_map(
        per_device,
        mesh=mesh,
        in_specs=(P(("groups", "dp"), "tile"), P(("groups", "dp"), "tile")),
        out_specs=(
            P(("groups", "dp"), "tile"),
            P(("groups", "dp"), "tile"),
            P(("groups", "tile"), "dp", None),
            P("groups"),
        ),
        check_vma=False,
    )
```

```python
import functools
import jax
import jax.numpy as jnp
from jax import lax
from jax.experimental import pallas as pl
from jax.experimental.pallas import tpu as pltpu
from jax.sharding import PartitionSpec as P

off_weight = 0.0051


def swapped(block, axis, bit):
    count = lax.axis_size(axis)
    route = []
    for low in range(count):
        high = low | 1 << bit
        if high != low and high < count:
            route += [(low, high), (high, low)]
    return lax.ppermute(block, axis, route)


def pair_views(first_moment, second_moment, row_halves, column_halves):
    other_a = swapped(first_moment, "tile", 0)
    other_b = swapped(second_moment, "tile", 1)
    joined_a = jnp.where(
        column_halves == 0,
        jnp.concatenate([first_moment, other_a], axis=1),
        jnp.concatenate([other_a, first_moment], axis=1),
    )
    joined_b = jnp.where(
        row_halves == 0,
        jnp.concatenate([second_moment, other_b], axis=1),
        jnp.concatenate([other_b, second_moment], axis=1),
    )
    return (joined_a, joined_b)


def moment_pair(total, squares, batch_images):
    column_mean = total / batch_images
    var = squares / batch_images - column_mean * column_mean
    return (column_mean, lax.rsqrt(var + 1e-05))


def col_sums(values):
    as_float = values.astype(jnp.float32)
    return (jnp.sum(as_float, axis=0), jnp.sum(as_float * as_float, axis=0))


def reduced_device(left_outputs, right_outputs):
    rows, quart = left_outputs.shape
    half = 2 * quart
    feats = 4 * quart
    dp_count = lax.axis_size("dp")
    batch_images = rows * dp_count
    tpos = lax.axis_index("tile")
    row_halves = tpos // 2
    column_halves = tpos % 2
    sum_a, sq_a = col_sums(left_outputs)
    sum_b, sq_b = col_sums(right_outputs)
    sum_a, sq_a, sum_b, sq_b = lax.psum((sum_a, sq_a, sum_b, sq_b), "dp")
    left_mean, left_inverse_deviation = moment_pair(sum_a, sq_a, batch_images)
    right_mean, right_inverse_deviation = moment_pair(sum_b, sq_b, batch_images)
    standardized_left = (left_outputs.astype(jnp.float32) - left_mean) * left_inverse_deviation
    standardized_right = (right_outputs.astype(jnp.float32) - right_mean) * right_inverse_deviation
    half_a, cols_b = pair_views(
        standardized_left.astype(jnp.bfloat16),
        standardized_right.astype(jnp.bfloat16),
        row_halves,
        column_halves,
    )
    col_local = jnp.arange(half, dtype=jnp.int32)
    col_ids = quart * column_halves + col_local + jnp.where(col_local >= quart, quart, 0)
    owned = half // dp_count
    picked = half_a
    corr_rows = (
        lax.psum_scatter(
            lax.dot_general(
                picked, cols_b, (((0,), (0,)), ((), ())), preferred_element_type=jnp.float32
            ),
            "dp",
            scatter_dimension=0,
            tiled=True,
        )
        / batch_images
    )
    row_ids = half * row_halves + lax.axis_index("dp") * owned + jnp.arange(owned, dtype=jnp.int32)
    diagonal = row_ids[:, None] == col_ids[None, :]
    part_loss = jnp.sum(
        jnp.where(diagonal, (1.0 - corr_rows) ** 2, off_weight * corr_rows * corr_rows)
    )
    loss = lax.psum(part_loss, ("dp", "tile")) / feats
    dcorr_part = jnp.where(diagonal, corr_rows - 1.0, off_weight * corr_rows).astype(jnp.bfloat16)
    piece = lax.all_gather(dcorr_part, "dp", axis=0, tiled=True)
    block_a = lax.dot_general(
        cols_b, piece, (((1,), (1,)), ((), ())), preferred_element_type=jnp.float32
    )
    picked = half_a
    into_b = jnp.dot(picked, piece, preferred_element_type=jnp.float32)
    other_a = swapped(block_a.astype(jnp.bfloat16), "tile", 0).astype(block_a.dtype)
    other_b = swapped(into_b.astype(jnp.bfloat16), "tile", 1).astype(into_b.dtype)
    normed_grad_left = lax.dynamic_slice_in_dim(block_a + other_a, column_halves * quart, quart, 1)
    normed_grad_right = lax.dynamic_slice_in_dim(into_b + other_b, row_halves * quart, quart, 1)
    first_moment_left, second_moment_left, first_moment_right, second_moment_right = lax.psum(
        (
            jnp.sum(normed_grad_left, axis=0),
            jnp.sum(normed_grad_left * standardized_left, axis=0),
            jnp.sum(normed_grad_right, axis=0),
            jnp.sum(normed_grad_right * standardized_right, axis=0),
        ),
        "dp",
    )
    left_gradient = (
        left_inverse_deviation
        * (
            normed_grad_left
            - first_moment_left / batch_images
            - standardized_left * (second_moment_left / batch_images)
        )
    ).astype(jnp.bfloat16)
    right_gradient = (
        right_inverse_deviation
        * (
            normed_grad_right
            - first_moment_right / batch_images
            - standardized_right * (second_moment_right / batch_images)
        )
    ).astype(jnp.bfloat16)
    return (left_gradient, right_gradient, corr_rows[None, :, :], jnp.reshape(loss, (1,)))


def fold_rows(values):
    rows, width = values.shape
    return jnp.sum(values.reshape(rows // 8, 8, width), axis=0)


def fold_lanes(values):
    return sum(values[:, at : at + 128] for at in range(0, values.shape[1], 128))


def column_mean(block):
    rows, width = block.shape
    folded = jnp.zeros((8, width), jnp.float32)
    for at in range(0, rows, 64):
        folded = folded + fold_rows(block[at : at + 64, :].astype(jnp.float32))
    return jnp.sum(folded, axis=0, keepdims=True) / rows


def add_sums(sums, centred, low):
    return [
        sums[0] + fold_rows(centred),
        sums[1] + fold_rows(centred * centred),
        sums[2] + fold_rows(low.astype(jnp.float32)),
    ]


def rows_of(values):
    pad = jnp.zeros((8 - len(values), values[0].shape[1]), jnp.float32)
    return jnp.concatenate([*values, pad], axis=0)


def joined_sums(row, sums):
    return [row[i + 1 : i + 2, :] + jnp.sum(s, axis=0, keepdims=True) for i, s in enumerate(sums)]


def moments(sums, images):
    total, squares, rounded = sums
    delta = total / images
    return delta, lax.rsqrt(squares / images - delta * delta + 1e-05), rounded / images - delta


def three_parts(row):
    high = row.astype(jnp.bfloat16)
    rest = row - high.astype(jnp.float32)
    middle = rest.astype(jnp.bfloat16)
    low = (rest - middle.astype(jnp.float32)).astype(jnp.bfloat16)
    return [high, middle, low]


def split_rows(values):
    parts = sum([three_parts(v) for v in values], [])
    pad = jnp.zeros((4, values[0].shape[1]), jnp.float32)
    return jnp.concatenate([*(p.astype(jnp.float32) for p in parts), pad], axis=0).astype(
        jnp.bfloat16
    )


def joined_rows(ref, at):
    parts = ref[at : at + 16, :].astype(jnp.float32)
    part = lambda i: parts[i : i + 1]
    return [part(3 * i) + part(3 * i + 1) + part(3 * i + 2) for i in range(4)]


def lanes_to_row(partial):
    ones = jnp.ones((16, partial.shape[1]), jnp.bfloat16)
    high = partial.astype(jnp.bfloat16)
    low = (partial - high.astype(jnp.float32)).astype(jnp.bfloat16)
    row = dot_rows(ones, high) + dot_rows(ones, low)
    return row[:1, :]


def dot_rows(left, right):
    return lax.dot_general(
        left, right, (((1,), (1,)), ((), ())), preferred_element_type=jnp.float32
    )


def dot(left, right):
    return jnp.dot(left, right, preferred_element_type=jnp.float32)


def pick(mask, outer, inner, piece):
    return jnp.where(
        mask[0:1, :] != 0.0, outer[piece, :].astype(jnp.float32), inner[piece, :].astype(jnp.float32)
    )


def pick_kernel(mask, outer, inner, out):
    for at in range(0, outer.shape[0], 64):
        piece = slice(at, at + 64)
        out[piece, :] = pick(mask, outer, inner, piece).astype(out.dtype)


def right_sums_kernel(first, second, third, row):
    rows, quart = first.shape
    shift = column_mean(first)
    sums = [jnp.zeros((8, quart), jnp.float32)] * 3
    for block in (first, second, third):
        for at in range(0, rows, 64):
            centred = block[at : at + 64, :].astype(jnp.float32) - shift
            sums = add_sums(sums, centred, centred.astype(jnp.bfloat16))
    row[...] = rows_of([shift] + [jnp.sum(s, axis=0, keepdims=True) for s in sums])


def late_kernel(images, turned, mask, outer, inner, row, out):
    rows, quart = outer.shape
    shift = row[0:1, :]
    sums = [jnp.zeros((8, quart), jnp.float32)] * 3
    for at in range(0, rows, 128):
        piece = slice(at, at + 128)
        centred = pick(mask, outer, inner, piece) - shift
        low = centred.astype(jnp.bfloat16)
        if turned:
            out[:quart, piece] = jnp.transpose(low)
        else:
            out[piece, :] = low
        sums = add_sums(sums, centred, low)
    delta, rstd, gap = moments(joined_sums(row, sums), images)
    out[rows:, :] = split_rows([shift + delta, rstd, gap, delta])


def products_kernel(*refs):
    lefts, rights = refs[0:6], refs[6:12]
    partner_all, own_all, row_other, zero_own, zero_other, low_left, low_right = refs[12:]
    rows, quart = lefts[0].shape
    width = quart // 2
    for half in range(2):
        lanes = slice(half * quart, (half + 1) * quart)
        shift = column_mean(lefts[half])
        sums = [jnp.zeros((8, quart), jnp.float32)] * 3
        for block in range(3):
            source = lefts[2 * block + half]
            for at in range(0, rows, 64):
                centred = source[at : at + 64, :].astype(jnp.float32) - shift
                low = centred.astype(jnp.bfloat16)
                low_left[block * rows + at : block * rows + at + 64, lanes] = low
                if block == 0:
                    (zero_own, zero_other)[half][at : at + 64, :] = low
                if half:
                    sums = add_sums(sums, centred, low)
        if half:
            row_other[...] = rows_of([shift] + [jnp.sum(s, axis=0, keepdims=True) for s in sums])
    for half in range(2):
        lanes = slice(half * quart, (half + 1) * quart)
        shift = column_mean(rights[half])
        for block in range(3):
            source = rights[2 * block + half]
            for at in range(0, rows, 128):
                low = (source[at : at + 128, :].astype(jnp.float32) - shift).astype(jnp.bfloat16)
                low_right[lanes, block * rows + at : block * rows + at + 128] = jnp.transpose(low)
    for tile in range(4):
        wide = slice(tile * width, (tile + 1) * width)
        partner_all[:, wide] = dot(low_right[quart:, :], low_left[:, wide])
        own_all[:, wide] = dot(low_right[:quart, :], low_left[:, wide])


def left_operand(zero, late, target, lanes):
    rows, quart = zero.shape
    _, _, gap, delta = joined_rows(late, rows)
    high, middle, _ = three_parts(delta)
    target[:rows, lanes] = zero[...]
    extra = [high.astype(jnp.float32), middle.astype(jnp.float32), gap]
    pad = jnp.zeros((13, quart), jnp.float32)
    target[rows:, lanes] = jnp.concatenate([*extra, pad], axis=0).astype(jnp.bfloat16)


def without_extra(terms, rows):
    return terms[:rows] - (terms[rows : rows + 1] + terms[rows + 1 : rows + 2] + terms[rows + 2 : rows + 3])


def scale_columns(late_b, images):
    quart = late_b.shape[1]
    _, rstd, _, delta = joined_rows(late_b, quart)
    columns = jnp.transpose(rows_of([rstd / images, delta * rstd]))
    return columns[:, 0:1], columns[:, 1:2]


def partner_kernel(images, late_own, late_other, zero_own, zero_other, sums, late_b, *refs):
    partial_out, e_out, vec_out, left = refs
    rows, quart = zero_own.shape
    width = quart // 2
    scale_col, delta_col = scale_columns(late_b, images)
    across = jnp.zeros((quart, 128), jnp.float32)
    for part, late in enumerate((late_own, late_other)):
        zero = (zero_own, zero_other)[part]
        left_operand(zero, late, left, slice(part * quart, (part + 1) * quart))
        _, rstd, _, delta = joined_rows(late, rows)
        for tile in range(2):
            at = slice(tile * width, (tile + 1) * width)
            wide = slice(part * quart + tile * width, part * quart + (tile + 1) * width)
            total = sums[:, wide] + dot(late_b[:quart, :], late[:rows, at])
            corr = (total * scale_col - delta_col * delta[:, at]) * rstd[:, at]
            e_out[:, wide] = (corr * (off_weight * rstd[:, at])).astype(jnp.bfloat16)
            square = corr * corr
            across = across + fold_lanes(square)
            vec_out[:, wide] = rows_of([off_weight * jnp.sum(square, axis=0, keepdims=True)])
    nothing = jnp.zeros((1, quart), jnp.float32)
    second = off_weight * lanes_to_row(across)
    partial_out[rows:, :] = split_rows([second, nothing, nothing, nothing])
    for tile in range(2):
        at = slice(tile * width, (tile + 1) * width)
        terms = dot_rows(left[...], e_out[at, :])
        partial_out[:rows, at] = without_extra(terms, rows).astype(jnp.bfloat16)


def own_kernel(images, flags, *refs):
    (late_own, late_other, first_own, first_other, zero_own, zero_other, sums, late_b) = refs[:8]
    (late_b_other, first_b, first_b_other, e_partner, partner_sums) = refs[8:13]
    (vec_partner, vec_core, right_out, left_out, left_partial_out, mine_out) = refs[13:19]
    (own_loss_out, loss_out, left, norm_b, e_own, mine_own, mine_partner) = refs[19:]
    rows, quart = zero_own.shape
    width = quart // 2
    lower, upper = slice(0, quart), slice(quart, 2 * quart)
    stats_own, stats_other = joined_rows(late_own, rows), joined_rows(late_other, rows)
    both = lambda i: jnp.concatenate([stats_own[i], stats_other[i]], axis=1)
    offset, rstd, _, delta = [both(i) for i in range(4)]
    left_operand(zero_own, late_own, left, lower)
    left_operand(zero_other, late_other, left, upper)
    own_b = joined_rows(late_b, quart)
    other_b = joined_rows(late_b_other, quart)
    for source, stats, lanes in ((first_b, own_b, lower), (first_b_other, other_b, upper)):
        for at in range(0, rows, 64):
            piece = slice(at, at + 64)
            norm_b[piece, lanes] = (
                (source[piece, :].astype(jnp.float32) - stats[0]) * stats[1]
            ).astype(jnp.bfloat16)
        rest = jnp.broadcast_to(stats[2] * stats[1], (16, quart))
        norm_b[rows:, lanes] = rest.astype(jnp.bfloat16)

    def tile_corr(late, inner, total, columns, block):
        scale_col, delta_col = columns
        total = total + dot(block[:quart, :], late[:rows, inner])
        row = joined_rows(late, rows)
        return (total * scale_col - delta_col * row[3][:, inner]) * row[1][:, inner]

    columns = scale_columns(late_b, images)
    columns_partner = scale_columns(late_b_other, images)
    across = jnp.zeros((quart, 128), jnp.float32)
    losses = jnp.zeros((8, 128), jnp.float32)
    down, diagonals = [], []
    for tile in range(4):
        at = slice(tile * width, (tile + 1) * width)
        inner = slice((tile % 2) * width, (tile % 2 + 1) * width)
        late = late_own if tile < 2 else late_other
        corr = tile_corr(late, inner, sums[:, at], columns, late_b)
        dcorr = off_weight * corr
        product = dcorr * corr
        loss = product
        if tile < 2:
            feature = lax.broadcasted_iota(jnp.int32, (quart, width), 0)
            lane = lax.broadcasted_iota(jnp.int32, (quart, width), 1) + tile * width
            diagonal = feature == lane
            slope = jnp.where(diagonal, (corr - 1.0).astype(jnp.bfloat16).astype(jnp.float32), 0.0)
            diagonals.append(jnp.sum(slope, axis=0, keepdims=True))
            dcorr = jnp.where(diagonal, 0.0, dcorr)
            product = jnp.where(diagonal, slope * corr, product)
            loss = jnp.where(diagonal, (1.0 - corr) * (1.0 - corr), loss)
        e_own[:, at] = (dcorr * rstd[:, at]).astype(jnp.bfloat16)
        across = across + fold_lanes(product)
        losses = losses + fold_rows(fold_lanes(loss))
        down.append(jnp.sum(product, axis=0, keepdims=True))

        @pl.when(flags[0] == tile)
        def _():
            mine_own[...] = corr
            mine_partner[...] = tile_corr(
                late, inner, partner_sums[:, at], columns_partner, late_b_other
            )

    diagonal_row = jnp.concatenate(diagonals, axis=1)
    second_a = rstd * (vec_partner[0:1, :] + jnp.concatenate(down, axis=1))
    second_b = lanes_to_row(across)
    own_loss = jnp.sum(losses)
    own_loss_out[...] = jnp.broadcast_to(own_loss, (8, 128))
    loss = own_loss + jnp.sum(vec_partner[0:1, :] + vec_core[0:1, :])
    loss_out[...] = jnp.broadcast_to(loss, (8, 128))

    for tile in (2, 3, 0, 1):
        at = slice(tile * width, (tile + 1) * width)
        inner = slice((tile % 2) * width, (tile % 2 + 1) * width)
        source = first_own if tile < 2 else first_other
        terms = dot(norm_b[:, lower], e_own[:, at]) + dot(norm_b[:, upper], e_partner[:, at])
        xhat = (source[:, inner].astype(jnp.float32) - offset[:, at]) * rstd[:, at]
        value = terms[:rows] - terms[rows : rows + 1] - xhat * second_a[:, at]
        if tile < 2:
            slope = rstd[:, at] * diagonal_row[:, inner]
            left_out[:, inner] = value + norm_b[:rows, inner].astype(jnp.float32) * slope
        else:
            left_partial_out[:, inner] = value.astype(jnp.bfloat16)

    for tile in range(2):
        at = slice(tile * width, (tile + 1) * width)
        terms = dot_rows(left[...], e_own[at, :])
        xhat = (first_b[:, at].astype(jnp.float32) - own_b[0][:, at]) * own_b[1][:, at]
        norm_a = (first_own[:, at].astype(jnp.float32) - offset[:, at]) * rstd[:, at]
        norm_a = norm_a.astype(jnp.bfloat16).astype(jnp.float32)
        right_out[:, at] = (
            without_extra(terms, rows) - xhat * second_b[:, at] + norm_a * diagonal_row[:, at]
        )

    own_columns = jnp.transpose(mine_own[...])
    partner_columns = jnp.transpose(mine_partner[...])

    @pl.when(flags[1] == 0)
    def _():
        mine_out[:, lower] = own_columns
        mine_out[:, upper] = partner_columns

    @pl.when(flags[1] != 0)
    def _():
        mine_out[:, lower] = partner_columns
        mine_out[:, upper] = own_columns


def add_kernel(one, other, out):
    out[...] = one[...] + other[...]


def loss_kernel(feats, one, other, out):
    out[0] = (one[0, 0] + other[0, 0]) / feats


def left_final_kernel(left, from_core, left_out):
    for at in range(0, left.shape[0], 64):
        piece = slice(at, at + 64)
        value = left[piece, :] + from_core[piece, :].astype(jnp.float32)
        left_out[piece, :] = value.astype(jnp.bfloat16)


def right_final_kernel(right, from_x, late_b, first_b, right_out):
    rows, quart = right.shape
    offset, rstd, _, _ = joined_rows(late_b, quart)
    second = joined_rows(from_x, rows)[0]
    for at in range(0, rows, 64):
        piece = slice(at, at + 64)
        xhat = (first_b[piece, :].astype(jnp.float32) - offset) * rstd
        value = right[piece, :] + from_x[piece, :].astype(jnp.float32) - xhat * second
        right_out[piece, :] = (rstd * value).astype(jnp.bfloat16)


vmem = pl.BlockSpec(memory_space=pltpu.VMEM)
smem = pl.BlockSpec(memory_space=pltpu.SMEM)


def local_call(kernel, operands, outs, scratch=(), flops=2**20, room=8, held=()):
    moved = sum(x.size * x.dtype.itemsize for x in (*operands, *outs))

    def space(x):
        return smem if x.ndim == 1 else vmem

    return pl.pallas_call(
        kernel,
        out_shape=list(outs),
        in_specs=[space(x) for x in operands],
        out_specs=[space(x) for x in outs],
        scratch_shapes=list(scratch),
        compiler_params=pltpu.CompilerParams(vmem_limit_bytes=room * 2**20),
        cost_estimate=pl.CostEstimate(flops=flops, bytes_accessed=moved, transcendentals=0),
    )(*(pltpu.with_memory_space_constraint(x, pltpu.VMEM) if i in held else x for i, x in enumerate(operands)))


def gathered_device(left_outputs, right_outputs):
    rows, quart = left_outputs.shape
    half = 2 * quart
    feats = 4 * quart
    batch_images = rows * 4
    tpos = lax.axis_index("tile")
    dpos = lax.axis_index("dp")
    row_halves = tpos // 2
    column_halves = tpos % 2
    at_end = (dpos == 0) | (dpos == 3)
    owned_tile = jnp.where(dpos // 2 == column_halves, 0, 2) + dpos % 2
    flags = jnp.stack([owned_tile, row_halves]).astype(jnp.int32)
    mask = jnp.broadcast_to(at_end.astype(jnp.float32), (8, quart))

    pairs = [(0, 1), (1, 0), (2, 3), (3, 2)]
    middle = [(1, 2), (2, 1)]
    outward = [(1, 0), (2, 3)]

    def along(block, route):
        return lax.ppermute(block, "dp", route)

    def core_swap(block):
        return swapped(block, "tile", 0)

    def x_swap(block):
        return swapped(block, "tile", 1)

    def after(value, *others):
        return lax.optimization_barrier((value, *others))

    gemm = 2 * rows * quart * quart
    width = quart // 2
    quarter_f32 = jax.ShapeDtypeStruct((rows, quart), jnp.float32)
    quarter_bf16 = jax.ShapeDtypeStruct((rows, quart), jnp.bfloat16)
    extended = jax.ShapeDtypeStruct((rows + 16, quart), jnp.bfloat16)
    row_out = jax.ShapeDtypeStruct((8, quart), jnp.float32)
    one_out = jax.ShapeDtypeStruct((8, 128), jnp.float32)
    low = lambda n, m: pltpu.VMEM((n, m), jnp.bfloat16)

    def picked(outer, inner):
        return local_call(pick_kernel, (mask, outer, inner), (quarter_bf16,))[0]

    first_b = along(right_outputs, pairs)
    inner_b = along(right_outputs, middle)
    first_a = along(left_outputs, pairs)
    other_b0 = x_swap(right_outputs)
    other_a0, mask, flags = after(core_swap(left_outputs), mask, flags)
    left_behind, first_a, other_a0 = after(left_outputs, first_a, other_a0)
    inner_a = along(left_behind, middle)

    outer_b = along(inner_b, outward)
    third_b = along(first_b, middle)
    ready_b, other_b0 = after(first_b, other_b0)
    other_b1 = x_swap(ready_b)
    outer_a = along(inner_a, outward)
    third_a = along(first_a, middle)
    other_a1 = core_swap(first_a)

    last_b = along(third_b, outward)
    second_b = picked(outer_b, inner_b)
    row_b = local_call(right_sums_kernel, (right_outputs, first_b, second_b), (row_out,))[0]
    second_b, other_b1, other_a1 = after(second_b, other_b1, other_a1)
    other_b2 = x_swap(second_b)
    last_a = along(third_a, outward)
    second_a = picked(outer_a, inner_a)
    second_a, row_b = after(second_a, row_b)
    other_a2 = core_swap(second_a)

    (late_b,) = local_call(
        functools.partial(late_kernel, batch_images, True),
        (mask, last_b, third_b, row_b),
        (extended,),
        held=(0, 1, 2, 3),
    )
    late_b_other = x_swap(late_b)
    partner_all, own_all, row_other, zero_own, zero_other = local_call(
        products_kernel,
        (left_outputs, other_a0, first_a, other_a1, second_a, other_a2)
        + (right_outputs, other_b0, first_b, other_b1, second_b, other_b2),
        (
            jax.ShapeDtypeStruct((quart, half), jnp.float32),
            jax.ShapeDtypeStruct((quart, half), jnp.float32),
            row_out,
            quarter_bf16,
            quarter_bf16,
        ),
        [low(3 * rows, half), low(half, 3 * rows)],
        12 * gemm,
        room=20,
    )
    row_a = core_swap(row_other)
    (late_a,) = local_call(
        functools.partial(late_kernel, batch_images, False),
        (mask, last_a, third_a, row_a),
        (extended,),
        held=(0, 1, 2, 3),
    )
    late_a_other = core_swap(late_a)

    partial_right, e_partner, vec_partner = local_call(
        functools.partial(partner_kernel, batch_images),
        (late_a, late_a_other, zero_own, zero_other, partner_all, late_b_other),
        (
            extended,
            jax.ShapeDtypeStruct((quart, half), jnp.bfloat16),
            jax.ShapeDtypeStruct((8, half), jnp.float32),
        ),
        [low(rows + 16, half)],
        4 * gemm,
        room=16,
    )
    from_x = x_swap(partial_right)
    vec_core = core_swap(vec_partner)
    right_own, left_own, partial_left, mine, own_loss, loss = local_call(
        functools.partial(own_kernel, batch_images),
        (flags, late_a, late_a_other, left_outputs, other_a0, zero_own, zero_other, own_all)
        + (late_b, late_b_other, right_outputs, other_b0, e_partner)
        + (partner_all, vec_partner, vec_core),
        (
            quarter_f32,
            quarter_f32,
            quarter_bf16,
            jax.ShapeDtypeStruct((width, half), jnp.float32),
            one_out,
            one_out,
        ),
        [
            low(rows + 16, half),
            low(rows + 16, half),
            low(quart, half),
            pltpu.VMEM((quart, width), jnp.float32),
            pltpu.VMEM((quart, width), jnp.float32),
        ],
        8 * gemm,
        room=20,
    )
    from_core = core_swap(partial_left)
    core_loss = core_swap(own_loss)
    (loss,) = local_call(add_kernel, (loss, core_loss), (one_out,))
    x_loss = x_swap(loss)
    (left_gradient,) = local_call(left_final_kernel, (left_own, from_core), (quarter_bf16,))
    right_own, left_gradient = after(right_own, left_gradient)
    (right_gradient,) = local_call(
        right_final_kernel, (right_own, from_x, late_b, right_outputs), (quarter_bf16,)
    )
    right_gradient, x_loss = after(right_gradient, x_loss)
    (loss,) = local_call(
        functools.partial(loss_kernel, feats),
        (loss, x_loss),
        (jax.ShapeDtypeStruct((1,), jnp.float32),),
    )
    return (left_gradient, right_gradient, mine[None, :, :], loss)


def solution(mesh):
    per_device = gathered_device if mesh.shape["dp"] == 4 else reduced_device
    return jax.shard_map(
        per_device,
        mesh=mesh,
        in_specs=(P(("groups", "dp"), "tile"), P(("groups", "dp"), "tile")),
        out_specs=(
            P(("groups", "dp"), "tile"),
            P(("groups", "dp"), "tile"),
            P(("groups", "tile"), "dp", None),
            P("groups"),
        ),
        check_vma=False,
    )
```

```python
import functools
import jax
import jax.numpy as jnp
from jax import lax
from jax.experimental import pallas as pl
from jax.experimental.pallas import tpu as pltpu
from jax.sharding import PartitionSpec as P

off_weight = 0.0051


def swapped(block, axis, bit):
    count = lax.axis_size(axis)
    route = []
    for low in range(count):
        high = low | 1 << bit
        if high != low and high < count:
            route += [(low, high), (high, low)]
    return lax.ppermute(block, axis, route)


def pair_views(first_moment, second_moment, row_halves, column_halves):
    other_a = swapped(first_moment, "tile", 0)
    other_b = swapped(second_moment, "tile", 1)
    joined_a = jnp.where(
        column_halves == 0,
        jnp.concatenate([first_moment, other_a], axis=1),
        jnp.concatenate([other_a, first_moment], axis=1),
    )
    joined_b = jnp.where(
        row_halves == 0,
        jnp.concatenate([second_moment, other_b], axis=1),
        jnp.concatenate([other_b, second_moment], axis=1),
    )
    return (joined_a, joined_b)


def moment_pair(total, squares, batch_images):
    column_mean = total / batch_images
    var = squares / batch_images - column_mean * column_mean
    return (column_mean, lax.rsqrt(var + 1e-05))


def col_sums(values):
    as_float = values.astype(jnp.float32)
    return (jnp.sum(as_float, axis=0), jnp.sum(as_float * as_float, axis=0))


def reduced_device(left_outputs, right_outputs):
    rows, quart = left_outputs.shape
    half = 2 * quart
    feats = 4 * quart
    dp_count = lax.axis_size("dp")
    batch_images = rows * dp_count
    tpos = lax.axis_index("tile")
    row_halves = tpos // 2
    column_halves = tpos % 2
    sum_a, sq_a = col_sums(left_outputs)
    sum_b, sq_b = col_sums(right_outputs)
    sum_a, sq_a, sum_b, sq_b = lax.psum((sum_a, sq_a, sum_b, sq_b), "dp")
    left_mean, left_inverse_deviation = moment_pair(sum_a, sq_a, batch_images)
    right_mean, right_inverse_deviation = moment_pair(sum_b, sq_b, batch_images)
    standardized_left = (left_outputs.astype(jnp.float32) - left_mean) * left_inverse_deviation
    standardized_right = (right_outputs.astype(jnp.float32) - right_mean) * right_inverse_deviation
    half_a, cols_b = pair_views(
        standardized_left.astype(jnp.bfloat16),
        standardized_right.astype(jnp.bfloat16),
        row_halves,
        column_halves,
    )
    col_local = jnp.arange(half, dtype=jnp.int32)
    col_ids = quart * column_halves + col_local + jnp.where(col_local >= quart, quart, 0)
    owned = half // dp_count
    picked = half_a
    corr_rows = (
        lax.psum_scatter(
            lax.dot_general(
                picked, cols_b, (((0,), (0,)), ((), ())), preferred_element_type=jnp.float32
            ),
            "dp",
            scatter_dimension=0,
            tiled=True,
        )
        / batch_images
    )
    row_ids = half * row_halves + lax.axis_index("dp") * owned + jnp.arange(owned, dtype=jnp.int32)
    diagonal = row_ids[:, None] == col_ids[None, :]
    part_loss = jnp.sum(
        jnp.where(diagonal, (1.0 - corr_rows) ** 2, off_weight * corr_rows * corr_rows)
    )
    loss = lax.psum(part_loss, ("dp", "tile")) / feats
    dcorr_part = jnp.where(diagonal, corr_rows - 1.0, off_weight * corr_rows).astype(jnp.bfloat16)
    piece = lax.all_gather(dcorr_part, "dp", axis=0, tiled=True)
    block_a = lax.dot_general(
        cols_b, piece, (((1,), (1,)), ((), ())), preferred_element_type=jnp.float32
    )
    picked = half_a
    into_b = jnp.dot(picked, piece, preferred_element_type=jnp.float32)
    other_a = swapped(block_a.astype(jnp.bfloat16), "tile", 0).astype(block_a.dtype)
    other_b = swapped(into_b.astype(jnp.bfloat16), "tile", 1).astype(into_b.dtype)
    normed_grad_left = lax.dynamic_slice_in_dim(block_a + other_a, column_halves * quart, quart, 1)
    normed_grad_right = lax.dynamic_slice_in_dim(into_b + other_b, row_halves * quart, quart, 1)
    first_moment_left, second_moment_left, first_moment_right, second_moment_right = lax.psum(
        (
            jnp.sum(normed_grad_left, axis=0),
            jnp.sum(normed_grad_left * standardized_left, axis=0),
            jnp.sum(normed_grad_right, axis=0),
            jnp.sum(normed_grad_right * standardized_right, axis=0),
        ),
        "dp",
    )
    left_gradient = (
        left_inverse_deviation
        * (
            normed_grad_left
            - first_moment_left / batch_images
            - standardized_left * (second_moment_left / batch_images)
        )
    ).astype(jnp.bfloat16)
    right_gradient = (
        right_inverse_deviation
        * (
            normed_grad_right
            - first_moment_right / batch_images
            - standardized_right * (second_moment_right / batch_images)
        )
    ).astype(jnp.bfloat16)
    return (left_gradient, right_gradient, corr_rows[None, :, :], jnp.reshape(loss, (1,)))


def fold_rows(values):
    rows, width = values.shape
    return jnp.sum(values.reshape(rows // 8, 8, width), axis=0)


def fold_lanes(values):
    return sum(values[:, at : at + 128] for at in range(0, values.shape[1], 128))


def column_mean(block):
    rows, width = block.shape
    folded = jnp.zeros((8, width), jnp.float32)
    for at in range(0, rows, 64):
        folded = folded + fold_rows(block[at : at + 64, :].astype(jnp.float32))
    return jnp.sum(folded, axis=0, keepdims=True) / rows


def add_sums(sums, centred, low):
    return [
        sums[0] + fold_rows(centred),
        sums[1] + fold_rows(centred * centred),
        sums[2] + fold_rows(low.astype(jnp.float32)),
    ]


def rows_of(values):
    pad = jnp.zeros((8 - len(values), values[0].shape[1]), jnp.float32)
    return jnp.concatenate([*values, pad], axis=0)


def joined_sums(row, sums):
    return [row[i + 1 : i + 2, :] + jnp.sum(s, axis=0, keepdims=True) for i, s in enumerate(sums)]


def moments(sums, images):
    total, squares, rounded = sums
    delta = total / images
    return delta, lax.rsqrt(squares / images - delta * delta + 1e-05), rounded / images - delta


def three_parts(row):
    high = row.astype(jnp.bfloat16)
    rest = row - high.astype(jnp.float32)
    middle = rest.astype(jnp.bfloat16)
    low = (rest - middle.astype(jnp.float32)).astype(jnp.bfloat16)
    return [high, middle, low]


def split_rows(values):
    parts = sum([three_parts(v) for v in values], [])
    pad = jnp.zeros((4, values[0].shape[1]), jnp.float32)
    return jnp.concatenate([*(p.astype(jnp.float32) for p in parts), pad], axis=0).astype(
        jnp.bfloat16
    )


def joined_rows(ref, at):
    parts = ref[at : at + 16, :].astype(jnp.float32)
    part = lambda i: parts[i : i + 1]
    return [part(3 * i) + part(3 * i + 1) + part(3 * i + 2) for i in range(4)]


def lanes_to_row(partial):
    ones = jnp.ones((16, partial.shape[1]), jnp.bfloat16)
    high = partial.astype(jnp.bfloat16)
    low = (partial - high.astype(jnp.float32)).astype(jnp.bfloat16)
    row = dot_rows(ones, high) + dot_rows(ones, low)
    return row[:1, :]


def dot_rows(left, right):
    return lax.dot_general(
        left, right, (((1,), (1,)), ((), ())), preferred_element_type=jnp.float32
    )


def dot(left, right):
    return jnp.dot(left, right, preferred_element_type=jnp.float32)


def pick(mask, outer, inner, piece):
    return jnp.where(
        mask[0:1, :] != 0.0, outer[piece, :].astype(jnp.float32), inner[piece, :].astype(jnp.float32)
    )


def pick_kernel(mask, outer, inner, out):
    for at in range(0, outer.shape[0], 64):
        piece = slice(at, at + 64)
        out[piece, :] = pick(mask, outer, inner, piece).astype(out.dtype)


def right_sums_kernel(first, second, third, row):
    rows, quart = first.shape
    shift = column_mean(first)
    sums = [jnp.zeros((8, quart), jnp.float32)] * 3
    for block in (first, second, third):
        for at in range(0, rows, 64):
            centred = block[at : at + 64, :].astype(jnp.float32) - shift
            sums = add_sums(sums, centred, centred.astype(jnp.bfloat16))
    row[...] = rows_of([shift] + [jnp.sum(s, axis=0, keepdims=True) for s in sums])


def late_kernel(images, turned, mask, outer, inner, row, out):
    rows, quart = outer.shape
    shift = row[0:1, :]
    sums = [jnp.zeros((8, quart), jnp.float32)] * 3
    for at in range(0, rows, 128):
        piece = slice(at, at + 128)
        centred = pick(mask, outer, inner, piece) - shift
        low = centred.astype(jnp.bfloat16)
        if turned:
            out[:quart, piece] = jnp.transpose(low)
        else:
            out[piece, :] = low
        sums = add_sums(sums, centred, low)
    delta, rstd, gap = moments(joined_sums(row, sums), images)
    out[rows:, :] = split_rows([shift + delta, rstd, gap, delta])


def products_kernel(*refs):
    lefts, rights = refs[0:6], refs[6:12]
    partner_all, own_all, row_other, zero_own, zero_other, low_left, low_right = refs[12:]
    rows, quart = lefts[0].shape
    width = quart // 2
    for half in range(2):
        lanes = slice(half * quart, (half + 1) * quart)
        shift = column_mean(lefts[half])
        sums = [jnp.zeros((8, quart), jnp.float32)] * 3
        for block in range(3):
            source = lefts[2 * block + half]
            for at in range(0, rows, 64):
                centred = source[at : at + 64, :].astype(jnp.float32) - shift
                low = centred.astype(jnp.bfloat16)
                low_left[block * rows + at : block * rows + at + 64, lanes] = low
                if block == 0:
                    (zero_own, zero_other)[half][at : at + 64, :] = low
                if half:
                    sums = add_sums(sums, centred, low)
        if half:
            row_other[...] = rows_of([shift] + [jnp.sum(s, axis=0, keepdims=True) for s in sums])
    for half in range(2):
        lanes = slice(half * quart, (half + 1) * quart)
        shift = column_mean(rights[half])
        for block in range(3):
            source = rights[2 * block + half]
            for at in range(0, rows, 128):
                low = (source[at : at + 128, :].astype(jnp.float32) - shift).astype(jnp.bfloat16)
                low_right[lanes, block * rows + at : block * rows + at + 128] = jnp.transpose(low)
    for tile in range(4):
        wide = slice(tile * width, (tile + 1) * width)
        partner_all[:, wide] = dot(low_right[quart:, :], low_left[:, wide])
        own_all[:, wide] = dot(low_right[:quart, :], low_left[:, wide])


def left_operand(zero, late, target, lanes):
    rows, quart = zero.shape
    _, _, gap, delta = joined_rows(late, rows)
    high, middle, _ = three_parts(delta)
    target[:rows, lanes] = zero[...]
    extra = [high.astype(jnp.float32), middle.astype(jnp.float32), gap]
    pad = jnp.zeros((13, quart), jnp.float32)
    target[rows:, lanes] = jnp.concatenate([*extra, pad], axis=0).astype(jnp.bfloat16)


def without_extra(terms, rows):
    return terms[:rows] - (terms[rows : rows + 1] + terms[rows + 1 : rows + 2] + terms[rows + 2 : rows + 3])


def scale_columns(late_b, images):
    quart = late_b.shape[1]
    _, rstd, _, delta = joined_rows(late_b, quart)
    columns = jnp.transpose(rows_of([rstd / images, delta * rstd]))
    return columns[:, 0:1], columns[:, 1:2]


def columns_kernel(images, late_b, late, zero, columns_out, left_out):
    rows, quart = zero.shape
    _, rstd, _, delta = joined_rows(late_b, quart)
    columns_out[...] = jnp.transpose(rows_of([rstd / images, delta * rstd]))
    left_operand(zero, late, left_out, slice(0, quart))


def partner_kernel(columns, left_own, late_own, late_other, zero_other, sums, late_b, *refs):
    partial_out, e_out, vec_out, left_other = refs
    rows, quart = zero_other.shape
    width = quart // 2
    scale_col, delta_col = columns[:, 0:1], columns[:, 1:2]
    left_operand(zero_other, late_other, left_other, slice(0, quart))
    across = jnp.zeros((quart, 128), jnp.float32)
    for part, late in enumerate((late_own, late_other)):
        _, rstd, _, delta = joined_rows(late, rows)
        for tile in range(2):
            at = slice(tile * width, (tile + 1) * width)
            wide = slice(part * quart + tile * width, part * quart + (tile + 1) * width)
            total = sums[:, wide] + dot(late_b[:quart, :], late[:rows, at])
            corr = (total * scale_col - delta_col * delta[:, at]) * rstd[:, at]
            e_out[:, wide] = (corr * (off_weight * rstd[:, at])).astype(jnp.bfloat16)
            square = corr * corr
            across = across + fold_lanes(square)
            vec_out[:, wide] = rows_of([off_weight * jnp.sum(square, axis=0, keepdims=True)])
    nothing = jnp.zeros((1, quart), jnp.float32)
    second = off_weight * lanes_to_row(across)
    partial_out[rows:, :] = split_rows([second, nothing, nothing, nothing])
    for tile in range(2):
        at = slice(tile * width, (tile + 1) * width)
        terms = dot_rows(left_own[...], e_out[at, :quart])
        terms = terms + dot_rows(left_other[...], e_out[at, quart:])
        partial_out[:rows, at] = without_extra(terms, rows).astype(jnp.bfloat16)


def own_kernel(images, flags, *refs):
    (late_own, late_other, first_own, first_other, zero_own, zero_other, sums, late_b) = refs[:8]
    (late_b_other, first_b, first_b_other, e_partner, partner_sums) = refs[8:13]
    (vec_partner, vec_core, right_out, left_out, left_partial_out, mine_out) = refs[13:19]
    (own_loss_out, loss_out, left, norm_b, e_own, mine_own, mine_partner) = refs[19:]
    rows, quart = zero_own.shape
    width = quart // 2
    lower, upper = slice(0, quart), slice(quart, 2 * quart)
    stats_own, stats_other = joined_rows(late_own, rows), joined_rows(late_other, rows)
    both = lambda i: jnp.concatenate([stats_own[i], stats_other[i]], axis=1)
    offset, rstd, _, delta = [both(i) for i in range(4)]
    left_operand(zero_own, late_own, left, lower)
    left_operand(zero_other, late_other, left, upper)
    own_b = joined_rows(late_b, quart)
    other_b = joined_rows(late_b_other, quart)
    for source, stats, lanes in ((first_b, own_b, lower), (first_b_other, other_b, upper)):
        for at in range(0, rows, 64):
            piece = slice(at, at + 64)
            norm_b[piece, lanes] = (
                (source[piece, :].astype(jnp.float32) - stats[0]) * stats[1]
            ).astype(jnp.bfloat16)
        rest = jnp.broadcast_to(stats[2] * stats[1], (16, quart))
        norm_b[rows:, lanes] = rest.astype(jnp.bfloat16)

    def tile_corr(late, inner, total, columns, block):
        scale_col, delta_col = columns
        total = total + dot(block[:quart, :], late[:rows, inner])
        row = joined_rows(late, rows)
        return (total * scale_col - delta_col * row[3][:, inner]) * row[1][:, inner]

    columns = scale_columns(late_b, images)
    columns_partner = scale_columns(late_b_other, images)
    across = jnp.zeros((quart, 128), jnp.float32)
    losses = jnp.zeros((8, 128), jnp.float32)
    down, diagonals = [], []
    for tile in range(4):
        at = slice(tile * width, (tile + 1) * width)
        inner = slice((tile % 2) * width, (tile % 2 + 1) * width)
        late = late_own if tile < 2 else late_other
        corr = tile_corr(late, inner, sums[:, at], columns, late_b)
        dcorr = off_weight * corr
        product = dcorr * corr
        loss = product
        if tile < 2:
            feature = lax.broadcasted_iota(jnp.int32, (quart, width), 0)
            lane = lax.broadcasted_iota(jnp.int32, (quart, width), 1) + tile * width
            diagonal = feature == lane
            slope = jnp.where(diagonal, (corr - 1.0).astype(jnp.bfloat16).astype(jnp.float32), 0.0)
            diagonals.append(jnp.sum(slope, axis=0, keepdims=True))
            dcorr = jnp.where(diagonal, 0.0, dcorr)
            product = jnp.where(diagonal, slope * corr, product)
            loss = jnp.where(diagonal, (1.0 - corr) * (1.0 - corr), loss)
        e_own[:, at] = (dcorr * rstd[:, at]).astype(jnp.bfloat16)
        across = across + fold_lanes(product)
        losses = losses + fold_rows(fold_lanes(loss))
        down.append(jnp.sum(product, axis=0, keepdims=True))

        @pl.when(flags[0] == tile)
        def _():
            mine_own[...] = corr
            mine_partner[...] = tile_corr(
                late, inner, partner_sums[:, at], columns_partner, late_b_other
            )

    diagonal_row = jnp.concatenate(diagonals, axis=1)
    second_a = rstd * (vec_partner[0:1, :] + jnp.concatenate(down, axis=1))
    second_b = lanes_to_row(across)
    own_loss = jnp.sum(losses)
    own_loss_out[...] = jnp.broadcast_to(own_loss, (8, 128))
    loss = own_loss + jnp.sum(vec_partner[0:1, :] + vec_core[0:1, :])
    loss_out[...] = jnp.broadcast_to(loss, (8, 128))

    for tile in (2, 3, 0, 1):
        at = slice(tile * width, (tile + 1) * width)
        inner = slice((tile % 2) * width, (tile % 2 + 1) * width)
        source = first_own if tile < 2 else first_other
        terms = dot(norm_b[:, lower], e_own[:, at]) + dot(norm_b[:, upper], e_partner[:, at])
        xhat = (source[:, inner].astype(jnp.float32) - offset[:, at]) * rstd[:, at]
        value = terms[:rows] - terms[rows : rows + 1] - xhat * second_a[:, at]
        if tile < 2:
            slope = rstd[:, at] * diagonal_row[:, inner]
            left_out[:, inner] = value + norm_b[:rows, inner].astype(jnp.float32) * slope
        else:
            left_partial_out[:, inner] = value.astype(jnp.bfloat16)

    for tile in range(2):
        at = slice(tile * width, (tile + 1) * width)
        terms = dot_rows(left[...], e_own[at, :])
        xhat = (first_b[:, at].astype(jnp.float32) - own_b[0][:, at]) * own_b[1][:, at]
        norm_a = (first_own[:, at].astype(jnp.float32) - offset[:, at]) * rstd[:, at]
        norm_a = norm_a.astype(jnp.bfloat16).astype(jnp.float32)
        right_out[:, at] = (
            without_extra(terms, rows) - xhat * second_b[:, at] + norm_a * diagonal_row[:, at]
        )

    own_columns = jnp.transpose(mine_own[...])
    partner_columns = jnp.transpose(mine_partner[...])

    @pl.when(flags[1] == 0)
    def _():
        mine_out[:, lower] = own_columns
        mine_out[:, upper] = partner_columns

    @pl.when(flags[1] != 0)
    def _():
        mine_out[:, lower] = partner_columns
        mine_out[:, upper] = own_columns


def add_kernel(one, other, out):
    out[...] = one[...] + other[...]


def loss_kernel(feats, one, other, out):
    out[0] = (one[0, 0] + other[0, 0]) / feats


def left_final_kernel(left, from_core, left_out):
    for at in range(0, left.shape[0], 64):
        piece = slice(at, at + 64)
        value = left[piece, :] + from_core[piece, :].astype(jnp.float32)
        left_out[piece, :] = value.astype(jnp.bfloat16)


def right_final_kernel(right, from_x, late_b, first_b, right_out):
    rows, quart = right.shape
    offset, rstd, _, _ = joined_rows(late_b, quart)
    second = joined_rows(from_x, rows)[0]
    for at in range(0, rows, 64):
        piece = slice(at, at + 64)
        xhat = (first_b[piece, :].astype(jnp.float32) - offset) * rstd
        value = right[piece, :] + from_x[piece, :].astype(jnp.float32) - xhat * second
        right_out[piece, :] = (rstd * value).astype(jnp.bfloat16)


vmem = pl.BlockSpec(memory_space=pltpu.VMEM)
smem = pl.BlockSpec(memory_space=pltpu.SMEM)


def local_call(kernel, operands, outs, scratch=(), flops=2**20, room=8, held=()):
    moved = sum(x.size * x.dtype.itemsize for x in (*operands, *outs))

    def space(x):
        return smem if x.ndim == 1 else vmem

    return pl.pallas_call(
        kernel,
        out_shape=list(outs),
        in_specs=[space(x) for x in operands],
        out_specs=[space(x) for x in outs],
        scratch_shapes=list(scratch),
        compiler_params=pltpu.CompilerParams(vmem_limit_bytes=room * 2**20),
        cost_estimate=pl.CostEstimate(flops=flops, bytes_accessed=moved, transcendentals=0),
    )(*(pltpu.with_memory_space_constraint(x, pltpu.VMEM) if i in held else x for i, x in enumerate(operands)))


def gathered_device(left_outputs, right_outputs):
    rows, quart = left_outputs.shape
    half = 2 * quart
    feats = 4 * quart
    batch_images = rows * 4
    tpos = lax.axis_index("tile")
    dpos = lax.axis_index("dp")
    row_halves = tpos // 2
    column_halves = tpos % 2
    at_end = (dpos == 0) | (dpos == 3)
    owned_tile = jnp.where(dpos // 2 == column_halves, 0, 2) + dpos % 2
    flags = jnp.stack([owned_tile, row_halves]).astype(jnp.int32)
    mask = jnp.broadcast_to(at_end.astype(jnp.float32), (8, quart))

    pairs = [(0, 1), (1, 0), (2, 3), (3, 2)]
    middle = [(1, 2), (2, 1)]
    outward = [(1, 0), (2, 3)]

    def along(block, route):
        return lax.ppermute(block, "dp", route)

    def core_swap(block):
        return swapped(block, "tile", 0)

    def x_swap(block):
        return swapped(block, "tile", 1)

    def after(value, *others):
        return lax.optimization_barrier((value, *others))

    gemm = 2 * rows * quart * quart
    width = quart // 2
    quarter_f32 = jax.ShapeDtypeStruct((rows, quart), jnp.float32)
    quarter_bf16 = jax.ShapeDtypeStruct((rows, quart), jnp.bfloat16)
    extended = jax.ShapeDtypeStruct((rows + 16, quart), jnp.bfloat16)
    row_out = jax.ShapeDtypeStruct((8, quart), jnp.float32)
    one_out = jax.ShapeDtypeStruct((8, 128), jnp.float32)
    low = lambda n, m: pltpu.VMEM((n, m), jnp.bfloat16)

    def picked(outer, inner):
        return local_call(pick_kernel, (mask, outer, inner), (quarter_bf16,))[0]

    first_b = along(right_outputs, pairs)
    inner_b = along(right_outputs, middle)
    first_a = along(left_outputs, pairs)
    other_b0 = x_swap(right_outputs)
    other_a0, mask, flags = after(core_swap(left_outputs), mask, flags)
    left_behind, first_a, other_a0 = after(left_outputs, first_a, other_a0)
    inner_a = along(left_behind, middle)

    outer_b = along(inner_b, outward)
    third_b = along(first_b, middle)
    ready_b, other_b0 = after(first_b, other_b0)
    other_b1 = x_swap(ready_b)
    outer_a = along(inner_a, outward)
    third_a = along(first_a, middle)
    other_a1 = core_swap(first_a)

    last_b = along(third_b, outward)
    second_b = picked(outer_b, inner_b)
    row_b = local_call(right_sums_kernel, (right_outputs, first_b, second_b), (row_out,))[0]
    second_b, other_b1, other_a1 = after(second_b, other_b1, other_a1)
    other_b2 = x_swap(second_b)
    last_a = along(third_a, outward)
    second_a = picked(outer_a, inner_a)
    second_a, row_b = after(second_a, row_b)
    other_a2 = core_swap(second_a)

    (late_b,) = local_call(
        functools.partial(late_kernel, batch_images, True),
        (mask, last_b, third_b, row_b),
        (extended,),
        held=(0, 1, 2, 3),
    )
    late_b_other = x_swap(late_b)
    other_b2, late_b = after(other_b2, late_b)
    partner_all, own_all, row_other, zero_own, zero_other = local_call(
        products_kernel,
        (left_outputs, other_a0, first_a, other_a1, second_a, other_a2)
        + (right_outputs, other_b0, first_b, other_b1, second_b, other_b2),
        (
            jax.ShapeDtypeStruct((quart, half), jnp.float32),
            jax.ShapeDtypeStruct((quart, half), jnp.float32),
            row_out,
            quarter_bf16,
            quarter_bf16,
        ),
        [low(3 * rows, half), low(half, 3 * rows)],
        12 * gemm,
        room=20,
    )
    row_a = core_swap(row_other)
    (late_a,) = local_call(
        functools.partial(late_kernel, batch_images, False),
        (mask, last_a, third_a, row_a),
        (extended,),
        held=(0, 1, 2, 3),
    )
    late_a_other = core_swap(late_a)

    columns, left_own_operand = local_call(
        functools.partial(columns_kernel, batch_images),
        (late_b_other, late_a, zero_own),
        (jax.ShapeDtypeStruct((quart, 8), jnp.float32), extended),
        flops=4 * gemm,
    )
    partial_right, e_partner, vec_partner = local_call(
        partner_kernel,
        (columns, left_own_operand, late_a, late_a_other, zero_other, partner_all, late_b_other),
        (
            extended,
            jax.ShapeDtypeStruct((quart, half), jnp.bfloat16),
            jax.ShapeDtypeStruct((8, half), jnp.float32),
        ),
        [low(rows + 16, quart)],
        4 * gemm,
        room=16,
    )
    from_x = x_swap(partial_right)
    vec_core = core_swap(vec_partner)
    right_own, left_own, partial_left, mine, own_loss, loss = local_call(
        functools.partial(own_kernel, batch_images),
        (flags, late_a, late_a_other, left_outputs, other_a0, zero_own, zero_other, own_all)
        + (late_b, late_b_other, right_outputs, other_b0, e_partner)
        + (partner_all, vec_partner, vec_core),
        (
            quarter_f32,
            quarter_f32,
            quarter_bf16,
            jax.ShapeDtypeStruct((width, half), jnp.float32),
            one_out,
            one_out,
        ),
        [
            low(rows + 16, half),
            low(rows + 16, half),
            low(quart, half),
            pltpu.VMEM((quart, width), jnp.float32),
            pltpu.VMEM((quart, width), jnp.float32),
        ],
        8 * gemm,
        room=20,
    )
    from_core = core_swap(partial_left)
    core_loss = core_swap(own_loss)
    (loss,) = local_call(add_kernel, (loss, core_loss), (one_out,))
    x_loss = x_swap(loss)
    (left_gradient,) = local_call(left_final_kernel, (left_own, from_core), (quarter_bf16,))
    right_own, left_gradient = after(right_own, left_gradient)
    (right_gradient,) = local_call(
        right_final_kernel, (right_own, from_x, late_b, right_outputs), (quarter_bf16,)
    )
    right_gradient, x_loss = after(right_gradient, x_loss)
    (loss,) = local_call(
        functools.partial(loss_kernel, feats),
        (loss, x_loss),
        (jax.ShapeDtypeStruct((1,), jnp.float32),),
    )
    return (left_gradient, right_gradient, mine[None, :, :], loss)


def solution(mesh):
    per_device = gathered_device if mesh.shape["dp"] == 4 else reduced_device
    return jax.shard_map(
        per_device,
        mesh=mesh,
        in_specs=(P(("groups", "dp"), "tile"), P(("groups", "dp"), "tile")),
        out_specs=(
            P(("groups", "dp"), "tile"),
            P(("groups", "dp"), "tile"),
            P(("groups", "tile"), "dp", None),
            P("groups"),
        ),
        check_vma=False,
    )
```

```python
import functools
import jax
import jax.numpy as jnp
from jax import lax
from jax.experimental import pallas as pl
from jax.experimental.pallas import tpu as pltpu
from jax.sharding import PartitionSpec as P

off_weight = 0.0051


def swapped(block, axis, bit):
    count = lax.axis_size(axis)
    route = []
    for low in range(count):
        high = low | 1 << bit
        if high != low and high < count:
            route += [(low, high), (high, low)]
    return lax.ppermute(block, axis, route)


def pair_views(first_moment, second_moment, row_halves, column_halves):
    other_a = swapped(first_moment, "tile", 0)
    other_b = swapped(second_moment, "tile", 1)
    joined_a = jnp.where(
        column_halves == 0,
        jnp.concatenate([first_moment, other_a], axis=1),
        jnp.concatenate([other_a, first_moment], axis=1),
    )
    joined_b = jnp.where(
        row_halves == 0,
        jnp.concatenate([second_moment, other_b], axis=1),
        jnp.concatenate([other_b, second_moment], axis=1),
    )
    return (joined_a, joined_b)


def moment_pair(total, squares, batch_images):
    column_mean = total / batch_images
    var = squares / batch_images - column_mean * column_mean
    return (column_mean, lax.rsqrt(var + 1e-05))


def col_sums(values):
    as_float = values.astype(jnp.float32)
    return (jnp.sum(as_float, axis=0), jnp.sum(as_float * as_float, axis=0))


def reduced_device(left_outputs, right_outputs):
    rows, quart = left_outputs.shape
    half = 2 * quart
    feats = 4 * quart
    dp_count = lax.axis_size("dp")
    batch_images = rows * dp_count
    tpos = lax.axis_index("tile")
    row_halves = tpos // 2
    column_halves = tpos % 2
    sum_a, sq_a = col_sums(left_outputs)
    sum_b, sq_b = col_sums(right_outputs)
    sum_a, sq_a, sum_b, sq_b = lax.psum((sum_a, sq_a, sum_b, sq_b), "dp")
    left_mean, left_inverse_deviation = moment_pair(sum_a, sq_a, batch_images)
    right_mean, right_inverse_deviation = moment_pair(sum_b, sq_b, batch_images)
    standardized_left = (left_outputs.astype(jnp.float32) - left_mean) * left_inverse_deviation
    standardized_right = (right_outputs.astype(jnp.float32) - right_mean) * right_inverse_deviation
    half_a, cols_b = pair_views(
        standardized_left.astype(jnp.bfloat16),
        standardized_right.astype(jnp.bfloat16),
        row_halves,
        column_halves,
    )
    col_local = jnp.arange(half, dtype=jnp.int32)
    col_ids = quart * column_halves + col_local + jnp.where(col_local >= quart, quart, 0)
    owned = half // dp_count
    picked = half_a
    corr_rows = (
        lax.psum_scatter(
            lax.dot_general(
                picked, cols_b, (((0,), (0,)), ((), ())), preferred_element_type=jnp.float32
            ),
            "dp",
            scatter_dimension=0,
            tiled=True,
        )
        / batch_images
    )
    row_ids = half * row_halves + lax.axis_index("dp") * owned + jnp.arange(owned, dtype=jnp.int32)
    diagonal = row_ids[:, None] == col_ids[None, :]
    part_loss = jnp.sum(
        jnp.where(diagonal, (1.0 - corr_rows) ** 2, off_weight * corr_rows * corr_rows)
    )
    loss = lax.psum(part_loss, ("dp", "tile")) / feats
    dcorr_part = jnp.where(diagonal, corr_rows - 1.0, off_weight * corr_rows).astype(jnp.bfloat16)
    piece = lax.all_gather(dcorr_part, "dp", axis=0, tiled=True)
    block_a = lax.dot_general(
        cols_b, piece, (((1,), (1,)), ((), ())), preferred_element_type=jnp.float32
    )
    picked = half_a
    into_b = jnp.dot(picked, piece, preferred_element_type=jnp.float32)
    other_a = swapped(block_a.astype(jnp.bfloat16), "tile", 0).astype(block_a.dtype)
    other_b = swapped(into_b.astype(jnp.bfloat16), "tile", 1).astype(into_b.dtype)
    normed_grad_left = lax.dynamic_slice_in_dim(block_a + other_a, column_halves * quart, quart, 1)
    normed_grad_right = lax.dynamic_slice_in_dim(into_b + other_b, row_halves * quart, quart, 1)
    first_moment_left, second_moment_left, first_moment_right, second_moment_right = lax.psum(
        (
            jnp.sum(normed_grad_left, axis=0),
            jnp.sum(normed_grad_left * standardized_left, axis=0),
            jnp.sum(normed_grad_right, axis=0),
            jnp.sum(normed_grad_right * standardized_right, axis=0),
        ),
        "dp",
    )
    left_gradient = (
        left_inverse_deviation
        * (
            normed_grad_left
            - first_moment_left / batch_images
            - standardized_left * (second_moment_left / batch_images)
        )
    ).astype(jnp.bfloat16)
    right_gradient = (
        right_inverse_deviation
        * (
            normed_grad_right
            - first_moment_right / batch_images
            - standardized_right * (second_moment_right / batch_images)
        )
    ).astype(jnp.bfloat16)
    return (left_gradient, right_gradient, corr_rows[None, :, :], jnp.reshape(loss, (1,)))


def fold_rows(values):
    rows, width = values.shape
    return jnp.sum(values.reshape(rows // 8, 8, width), axis=0)


def fold_lanes(values):
    return sum(values[:, at : at + 128] for at in range(0, values.shape[1], 128))


def column_mean(block):
    rows, width = block.shape
    folded = jnp.zeros((8, width), jnp.float32)
    for at in range(0, rows, 64):
        folded = folded + fold_rows(block[at : at + 64, :].astype(jnp.float32))
    return jnp.sum(folded, axis=0, keepdims=True) / rows


def add_sums(sums, centred, low):
    return [
        sums[0] + fold_rows(centred),
        sums[1] + fold_rows(centred * centred),
        sums[2] + fold_rows(low.astype(jnp.float32)),
    ]


def rows_of(values):
    pad = jnp.zeros((8 - len(values), values[0].shape[1]), jnp.float32)
    return jnp.concatenate([*values, pad], axis=0)


def joined_sums(row, sums):
    return [row[i + 1 : i + 2, :] + jnp.sum(s, axis=0, keepdims=True) for i, s in enumerate(sums)]


def moments(sums, images):
    total, squares, rounded = sums
    delta = total / images
    return delta, lax.rsqrt(squares / images - delta * delta + 1e-05), rounded / images - delta


def three_parts(row):
    high = row.astype(jnp.bfloat16)
    rest = row - high.astype(jnp.float32)
    middle = rest.astype(jnp.bfloat16)
    low = (rest - middle.astype(jnp.float32)).astype(jnp.bfloat16)
    return [high, middle, low]


def split_rows(values):
    parts = sum([three_parts(v) for v in values], [])
    pad = jnp.zeros((4, values[0].shape[1]), jnp.float32)
    return jnp.concatenate([*(p.astype(jnp.float32) for p in parts), pad], axis=0).astype(
        jnp.bfloat16
    )


def joined_rows(ref, at):
    parts = ref[at : at + 16, :].astype(jnp.float32)
    part = lambda i: parts[i : i + 1]
    return [part(3 * i) + part(3 * i + 1) + part(3 * i + 2) for i in range(4)]


def lanes_to_row(partial):
    ones = jnp.ones((16, partial.shape[1]), jnp.bfloat16)
    high = partial.astype(jnp.bfloat16)
    low = (partial - high.astype(jnp.float32)).astype(jnp.bfloat16)
    row = dot_rows(ones, high) + dot_rows(ones, low)
    return row[:1, :]


def dot_rows(left, right):
    return lax.dot_general(
        left, right, (((1,), (1,)), ((), ())), preferred_element_type=jnp.float32
    )


def dot(left, right):
    return jnp.dot(left, right, preferred_element_type=jnp.float32)


def pick(mask, outer, inner, piece):
    return jnp.where(
        mask[0:1, :] != 0.0, outer[piece, :].astype(jnp.float32), inner[piece, :].astype(jnp.float32)
    )


def pick_kernel(mask, outer, inner, out):
    for at in range(0, outer.shape[0], 64):
        piece = slice(at, at + 64)
        out[piece, :] = pick(mask, outer, inner, piece).astype(out.dtype)


def right_sums_kernel(first, second, third, row):
    rows, quart = first.shape
    shift = column_mean(first)
    sums = [jnp.zeros((8, quart), jnp.float32)] * 3
    for block in (first, second, third):
        for at in range(0, rows, 64):
            centred = block[at : at + 64, :].astype(jnp.float32) - shift
            sums = add_sums(sums, centred, centred.astype(jnp.bfloat16))
    row[...] = rows_of([shift] + [jnp.sum(s, axis=0, keepdims=True) for s in sums])


def late_kernel(images, turned, mask, outer, inner, row, out):
    rows, quart = outer.shape
    shift = row[0:1, :]
    sums = [jnp.zeros((8, quart), jnp.float32)] * 3
    for at in range(0, rows, 128):
        piece = slice(at, at + 128)
        centred = pick(mask, outer, inner, piece) - shift
        low = centred.astype(jnp.bfloat16)
        if turned:
            out[:quart, piece] = jnp.transpose(low)
        else:
            out[piece, :] = low
        sums = add_sums(sums, centred, low)
    delta, rstd, gap = moments(joined_sums(row, sums), images)
    out[rows:, :] = split_rows([shift + delta, rstd, gap, delta])


def products_kernel(*refs):
    lefts, rights = refs[0:6], refs[6:12]
    partner_all, own_all, row_other, zero_own, zero_other, low_left, low_right = refs[12:]
    rows, quart = lefts[0].shape
    width = quart // 2
    for half in range(2):
        lanes = slice(half * quart, (half + 1) * quart)
        shift = column_mean(lefts[half])
        sums = [jnp.zeros((8, quart), jnp.float32)] * 3
        for block in range(3):
            source = lefts[2 * block + half]
            for at in range(0, rows, 64):
                centred = source[at : at + 64, :].astype(jnp.float32) - shift
                low = centred.astype(jnp.bfloat16)
                low_left[block * rows + at : block * rows + at + 64, lanes] = low
                if block == 0:
                    (zero_own, zero_other)[half][at : at + 64, :] = low
                if half:
                    sums = add_sums(sums, centred, low)
        if half:
            row_other[...] = rows_of([shift] + [jnp.sum(s, axis=0, keepdims=True) for s in sums])
    for half in range(2):
        lanes = slice(half * quart, (half + 1) * quart)
        shift = column_mean(rights[half])
        for block in range(3):
            source = rights[2 * block + half]
            for at in range(0, rows, 128):
                low = (source[at : at + 128, :].astype(jnp.float32) - shift).astype(jnp.bfloat16)
                low_right[lanes, block * rows + at : block * rows + at + 128] = jnp.transpose(low)
    for tile in range(4):
        wide = slice(tile * width, (tile + 1) * width)
        partner_all[:, wide] = dot(low_right[quart:, :], low_left[:, wide])
        own_all[:, wide] = dot(low_right[:quart, :], low_left[:, wide])


def left_operand(zero, late, target, lanes):
    rows, quart = zero.shape
    _, _, gap, delta = joined_rows(late, rows)
    high, middle, _ = three_parts(delta)
    target[:rows, lanes] = zero[...]
    extra = [high.astype(jnp.float32), middle.astype(jnp.float32), gap]
    pad = jnp.zeros((13, quart), jnp.float32)
    target[rows:, lanes] = jnp.concatenate([*extra, pad], axis=0).astype(jnp.bfloat16)


def without_extra(terms, rows):
    return terms[:rows] - (terms[rows : rows + 1] + terms[rows + 1 : rows + 2] + terms[rows + 2 : rows + 3])


def scale_columns(late_b, images):
    quart = late_b.shape[1]
    _, rstd, _, delta = joined_rows(late_b, quart)
    columns = jnp.transpose(rows_of([rstd / images, delta * rstd]))
    return columns[:, 0:1], columns[:, 1:2]


def columns_kernel(images, late_b, late, zero, columns_out, left_out):
    rows, quart = zero.shape
    _, rstd, _, delta = joined_rows(late_b, quart)
    columns_out[...] = jnp.transpose(rows_of([rstd / images, delta * rstd]))
    left_operand(zero, late, left_out, slice(0, quart))


def partner_kernel(columns, left_own, late_own, late_other, zero_other, sums, late_b, *refs):
    partial_out, e_out, vec_out, left_other, terms_own = refs
    rows, quart = zero_other.shape
    width = quart // 2
    scale_col, delta_col = columns[:, 0:1], columns[:, 1:2]
    left_operand(zero_other, late_other, left_other, slice(0, quart))
    across = jnp.zeros((quart, 128), jnp.float32)
    for part, late in enumerate((late_own, late_other)):
        _, rstd, _, delta = joined_rows(late, rows)
        for tile in range(2):
            at = slice(tile * width, (tile + 1) * width)
            wide = slice(part * quart + tile * width, part * quart + (tile + 1) * width)
            total = sums[:, wide] + dot(late_b[:quart, :], late[:rows, at])
            corr = (total * scale_col - delta_col * delta[:, at]) * rstd[:, at]
            e_out[:, wide] = (corr * (off_weight * rstd[:, at])).astype(jnp.bfloat16)
            square = corr * corr
            across = across + fold_lanes(square)
            vec_out[:, wide] = rows_of([off_weight * jnp.sum(square, axis=0, keepdims=True)])
        if part == 0:
            for tile in range(2):
                at = slice(tile * width, (tile + 1) * width)
                terms_own[:, at] = dot_rows(left_own[...], e_out[at, :quart])
    nothing = jnp.zeros((1, quart), jnp.float32)
    second = off_weight * lanes_to_row(across)
    partial_out[rows:, :] = split_rows([second, nothing, nothing, nothing])
    for tile in range(2):
        at = slice(tile * width, (tile + 1) * width)
        terms = terms_own[:, at] + dot_rows(left_other[...], e_out[at, quart:])
        partial_out[:rows, at] = without_extra(terms, rows).astype(jnp.bfloat16)


def own_kernel(images, flags, *refs):
    (late_own, late_other, first_own, first_other, zero_own, zero_other, sums, late_b) = refs[:8]
    (late_b_other, first_b, first_b_other, e_partner, partner_sums) = refs[8:13]
    (vec_partner, vec_core, right_out, left_out, left_partial_out, mine_out) = refs[13:19]
    (own_loss_out, loss_out, left, norm_b, e_own, mine_own, mine_partner) = refs[19:]
    rows, quart = zero_own.shape
    width = quart // 2
    lower, upper = slice(0, quart), slice(quart, 2 * quart)
    stats_own, stats_other = joined_rows(late_own, rows), joined_rows(late_other, rows)
    both = lambda i: jnp.concatenate([stats_own[i], stats_other[i]], axis=1)
    offset, rstd, _, delta = [both(i) for i in range(4)]
    left_operand(zero_own, late_own, left, lower)
    left_operand(zero_other, late_other, left, upper)
    own_b = joined_rows(late_b, quart)
    other_b = joined_rows(late_b_other, quart)
    for source, stats, lanes in ((first_b, own_b, lower), (first_b_other, other_b, upper)):
        for at in range(0, rows, 64):
            piece = slice(at, at + 64)
            norm_b[piece, lanes] = (
                (source[piece, :].astype(jnp.float32) - stats[0]) * stats[1]
            ).astype(jnp.bfloat16)
        rest = jnp.broadcast_to(stats[2] * stats[1], (16, quart))
        norm_b[rows:, lanes] = rest.astype(jnp.bfloat16)

    def tile_corr(late, inner, total, columns, block):
        scale_col, delta_col = columns
        total = total + dot(block[:quart, :], late[:rows, inner])
        row = joined_rows(late, rows)
        return (total * scale_col - delta_col * row[3][:, inner]) * row[1][:, inner]

    columns = scale_columns(late_b, images)
    columns_partner = scale_columns(late_b_other, images)
    across = jnp.zeros((quart, 128), jnp.float32)
    losses = jnp.zeros((8, 128), jnp.float32)
    down, diagonals = [], []
    for tile in range(4):
        at = slice(tile * width, (tile + 1) * width)
        inner = slice((tile % 2) * width, (tile % 2 + 1) * width)
        late = late_own if tile < 2 else late_other
        corr = tile_corr(late, inner, sums[:, at], columns, late_b)
        dcorr = off_weight * corr
        product = dcorr * corr
        loss = product
        if tile < 2:
            feature = lax.broadcasted_iota(jnp.int32, (quart, width), 0)
            lane = lax.broadcasted_iota(jnp.int32, (quart, width), 1) + tile * width
            diagonal = feature == lane
            slope = jnp.where(diagonal, (corr - 1.0).astype(jnp.bfloat16).astype(jnp.float32), 0.0)
            diagonals.append(jnp.sum(slope, axis=0, keepdims=True))
            dcorr = jnp.where(diagonal, 0.0, dcorr)
            product = jnp.where(diagonal, slope * corr, product)
            loss = jnp.where(diagonal, (1.0 - corr) * (1.0 - corr), loss)
        e_own[:, at] = (dcorr * rstd[:, at]).astype(jnp.bfloat16)
        across = across + fold_lanes(product)
        losses = losses + fold_rows(fold_lanes(loss))
        down.append(jnp.sum(product, axis=0, keepdims=True))

        @pl.when(flags[0] == tile)
        def _():
            mine_own[...] = corr
            mine_partner[...] = tile_corr(
                late, inner, partner_sums[:, at], columns_partner, late_b_other
            )

    diagonal_row = jnp.concatenate(diagonals, axis=1)
    second_a = rstd * (vec_partner[0:1, :] + jnp.concatenate(down, axis=1))
    second_b = lanes_to_row(across)
    own_loss = jnp.sum(losses)
    own_loss_out[...] = jnp.broadcast_to(own_loss, (8, 128))
    loss = own_loss + jnp.sum(vec_partner[0:1, :] + vec_core[0:1, :])
    loss_out[...] = jnp.broadcast_to(loss, (8, 128))

    for tile in (2, 3, 0, 1):
        at = slice(tile * width, (tile + 1) * width)
        inner = slice((tile % 2) * width, (tile % 2 + 1) * width)
        source = first_own if tile < 2 else first_other
        terms = dot(norm_b[:, lower], e_own[:, at]) + dot(norm_b[:, upper], e_partner[:, at])
        xhat = (source[:, inner].astype(jnp.float32) - offset[:, at]) * rstd[:, at]
        value = terms[:rows] - terms[rows : rows + 1] - xhat * second_a[:, at]
        if tile < 2:
            slope = rstd[:, at] * diagonal_row[:, inner]
            left_out[:, inner] = value + norm_b[:rows, inner].astype(jnp.float32) * slope
        else:
            left_partial_out[:, inner] = value.astype(jnp.bfloat16)

    for tile in range(2):
        at = slice(tile * width, (tile + 1) * width)
        terms = dot_rows(left[...], e_own[at, :])
        xhat = (first_b[:, at].astype(jnp.float32) - own_b[0][:, at]) * own_b[1][:, at]
        norm_a = (first_own[:, at].astype(jnp.float32) - offset[:, at]) * rstd[:, at]
        norm_a = norm_a.astype(jnp.bfloat16).astype(jnp.float32)
        right_out[:, at] = (
            without_extra(terms, rows) - xhat * second_b[:, at] + norm_a * diagonal_row[:, at]
        )

    own_columns = jnp.transpose(mine_own[...])
    partner_columns = jnp.transpose(mine_partner[...])

    @pl.when(flags[1] == 0)
    def _():
        mine_out[:, lower] = own_columns
        mine_out[:, upper] = partner_columns

    @pl.when(flags[1] != 0)
    def _():
        mine_out[:, lower] = partner_columns
        mine_out[:, upper] = own_columns


def add_kernel(one, other, out):
    out[...] = one[...] + other[...]


def left_final_kernel(left, from_core, left_out):
    for at in range(0, left.shape[0], 64):
        piece = slice(at, at + 64)
        value = left[piece, :] + from_core[piece, :].astype(jnp.float32)
        left_out[piece, :] = value.astype(jnp.bfloat16)


def right_final_kernel(feats, right, from_x, late_b, first_b, loss, x_loss, right_out, loss_out, made, sems):
    rows, quart = right.shape
    offset, rstd, _, _ = joined_rows(late_b, quart)
    second = joined_rows(from_x, rows)[0]
    step = rows // 4
    sent = []
    for part in range(4):
        for at in range(part * step, (part + 1) * step, 64):
            piece = slice(at, at + 64)
            xhat = (first_b[piece, :].astype(jnp.float32) - offset) * rstd
            value = right[piece, :] + from_x[piece, :].astype(jnp.float32) - xhat * second
            made[piece, :] = (rstd * value).astype(jnp.bfloat16)
        piece = pl.ds(part * step, step)
        sent.append(
            pltpu.make_async_copy(made.at[piece, :], right_out.at[piece, :], sems.at[part])
        )
        sent[-1].start()
    loss_out[0] = (loss[0, 0] + x_loss[0, 0]) / feats
    for copy in sent:
        copy.wait()


vmem = pl.BlockSpec(memory_space=pltpu.VMEM)
smem = pl.BlockSpec(memory_space=pltpu.SMEM)
hbm = pl.BlockSpec(memory_space=pltpu.HBM)


def local_call(kernel, operands, outs, scratch=(), flops=2**20, room=8, held=(), sent=()):
    moved = sum(x.size * x.dtype.itemsize for x in (*operands, *outs))

    def space(x):
        return smem if x.ndim == 1 else vmem

    return pl.pallas_call(
        kernel,
        out_shape=[pltpu.HBM(x.shape, x.dtype) if i in sent else x for i, x in enumerate(outs)],
        in_specs=[space(x) for x in operands],
        out_specs=[hbm if i in sent else space(x) for i, x in enumerate(outs)],
        scratch_shapes=list(scratch),
        compiler_params=pltpu.CompilerParams(vmem_limit_bytes=room * 2**20),
        cost_estimate=pl.CostEstimate(flops=flops, bytes_accessed=moved, transcendentals=0),
    )(*(pltpu.with_memory_space_constraint(x, pltpu.VMEM) if i in held else x for i, x in enumerate(operands)))


def gathered_device(left_outputs, right_outputs):
    rows, quart = left_outputs.shape
    half = 2 * quart
    feats = 4 * quart
    batch_images = rows * 4
    tpos = lax.axis_index("tile")
    dpos = lax.axis_index("dp")
    row_halves = tpos // 2
    column_halves = tpos % 2
    at_end = (dpos == 0) | (dpos == 3)
    owned_tile = jnp.where(dpos // 2 == column_halves, 0, 2) + dpos % 2
    flags = jnp.stack([owned_tile, row_halves]).astype(jnp.int32)
    mask = jnp.broadcast_to(at_end.astype(jnp.float32), (8, quart))

    pairs = [(0, 1), (1, 0), (2, 3), (3, 2)]
    middle = [(1, 2), (2, 1)]
    outward = [(1, 0), (2, 3)]

    def along(block, route):
        return lax.ppermute(block, "dp", route)

    def core_swap(block):
        return swapped(block, "tile", 0)

    def x_swap(block):
        return swapped(block, "tile", 1)

    def after(value, *others):
        return lax.optimization_barrier((value, *others))

    gemm = 2 * rows * quart * quart
    width = quart // 2
    quarter_f32 = jax.ShapeDtypeStruct((rows, quart), jnp.float32)
    quarter_bf16 = jax.ShapeDtypeStruct((rows, quart), jnp.bfloat16)
    extended = jax.ShapeDtypeStruct((rows + 16, quart), jnp.bfloat16)
    row_out = jax.ShapeDtypeStruct((8, quart), jnp.float32)
    one_out = jax.ShapeDtypeStruct((8, 128), jnp.float32)
    low = lambda n, m: pltpu.VMEM((n, m), jnp.bfloat16)

    def picked(outer, inner):
        return local_call(pick_kernel, (mask, outer, inner), (quarter_bf16,))[0]

    first_b = along(right_outputs, pairs)
    inner_b = along(right_outputs, middle)
    first_a = along(left_outputs, pairs)
    other_b0 = x_swap(right_outputs)
    other_a0, mask, flags = after(core_swap(left_outputs), mask, flags)
    left_behind, first_a, other_a0 = after(left_outputs, first_a, other_a0)
    inner_a = along(left_behind, middle)

    outer_b = along(inner_b, outward)
    third_b = along(first_b, middle)
    ready_b, other_b0 = after(first_b, other_b0)
    other_b1 = x_swap(ready_b)
    outer_a = along(inner_a, outward)
    third_a = along(first_a, middle)
    other_a1 = core_swap(first_a)

    last_b = along(third_b, outward)
    second_b = picked(outer_b, inner_b)
    row_b = local_call(right_sums_kernel, (right_outputs, first_b, second_b), (row_out,))[0]
    second_b, other_b1, other_a1 = after(second_b, other_b1, other_a1)
    other_b2 = x_swap(second_b)
    last_a = along(third_a, outward)
    second_a = picked(outer_a, inner_a)
    second_a, row_b = after(second_a, row_b)
    other_a2 = core_swap(second_a)

    (late_b,) = local_call(
        functools.partial(late_kernel, batch_images, True),
        (mask, last_b, third_b, row_b),
        (extended,),
        held=(0, 1, 2, 3),
    )
    late_b_other = x_swap(late_b)
    other_b2, late_b = after(other_b2, late_b)
    partner_all, own_all, row_other, zero_own, zero_other = local_call(
        products_kernel,
        (left_outputs, other_a0, first_a, other_a1, second_a, other_a2)
        + (right_outputs, other_b0, first_b, other_b1, second_b, other_b2),
        (
            jax.ShapeDtypeStruct((quart, half), jnp.float32),
            jax.ShapeDtypeStruct((quart, half), jnp.float32),
            row_out,
            quarter_bf16,
            quarter_bf16,
        ),
        [low(3 * rows, half), low(half, 3 * rows)],
        12 * gemm,
        room=20,
    )
    row_a = core_swap(row_other)
    (late_a,) = local_call(
        functools.partial(late_kernel, batch_images, False),
        (mask, last_a, third_a, row_a),
        (extended,),
        held=(0, 1, 2, 3),
    )
    late_a_other = core_swap(late_a)

    columns, left_own_operand = local_call(
        functools.partial(columns_kernel, batch_images),
        (late_b_other, late_a, zero_own),
        (jax.ShapeDtypeStruct((quart, 8), jnp.float32), extended),
        flops=4 * gemm,
    )
    partial_right, e_partner, vec_partner = local_call(
        partner_kernel,
        (columns, left_own_operand, late_a, late_a_other, zero_other, partner_all, late_b_other),
        (
            extended,
            jax.ShapeDtypeStruct((quart, half), jnp.bfloat16),
            jax.ShapeDtypeStruct((8, half), jnp.float32),
        ),
        [low(rows + 16, quart), pltpu.VMEM((rows + 16, quart), jnp.float32)],
        4 * gemm,
        room=16,
    )
    from_x = x_swap(partial_right)
    vec_core = core_swap(vec_partner)
    right_own, left_own, partial_left, mine, own_loss, loss = local_call(
        functools.partial(own_kernel, batch_images),
        (flags, late_a, late_a_other, left_outputs, other_a0, zero_own, zero_other, own_all)
        + (late_b, late_b_other, right_outputs, other_b0, e_partner)
        + (partner_all, vec_partner, vec_core),
        (
            quarter_f32,
            quarter_f32,
            quarter_bf16,
            jax.ShapeDtypeStruct((width, half), jnp.float32),
            one_out,
            one_out,
        ),
        [
            low(rows + 16, half),
            low(rows + 16, half),
            low(quart, half),
            pltpu.VMEM((quart, width), jnp.float32),
            pltpu.VMEM((quart, width), jnp.float32),
        ],
        8 * gemm,
        room=20,
    )
    from_core = core_swap(partial_left)
    core_loss = core_swap(own_loss)
    (loss,) = local_call(add_kernel, (loss, core_loss), (one_out,))
    x_loss = x_swap(loss)
    (left_gradient,) = local_call(left_final_kernel, (left_own, from_core), (quarter_bf16,))
    right_own, left_gradient = after(right_own, left_gradient)
    right_gradient, loss = local_call(
        functools.partial(right_final_kernel, feats),
        (right_own, from_x, late_b, right_outputs, loss, x_loss),
        (quarter_bf16, jax.ShapeDtypeStruct((1,), jnp.float32)),
        [low(rows, quart), pltpu.SemaphoreType.DMA((4,))],
        sent=(0,),
    )
    return (left_gradient, right_gradient, mine[None, :, :], loss)


def solution(mesh):
    per_device = gathered_device if mesh.shape["dp"] == 4 else reduced_device
    return jax.shard_map(
        per_device,
        mesh=mesh,
        in_specs=(P(("groups", "dp"), "tile"), P(("groups", "dp"), "tile")),
        out_specs=(
            P(("groups", "dp"), "tile"),
            P(("groups", "dp"), "tile"),
            P(("groups", "tile"), "dp", None),
            P("groups"),
        ),
        check_vma=False,
    )
```

```python
import functools
import jax
import jax.numpy as jnp
from jax import lax
from jax.experimental import pallas as pl
from jax.experimental.pallas import tpu as pltpu
from jax.sharding import PartitionSpec as P

off_weight = 0.0051


def swapped(block, axis, bit):
    count = lax.axis_size(axis)
    route = []
    for low in range(count):
        high = low | 1 << bit
        if high != low and high < count:
            route += [(low, high), (high, low)]
    return lax.ppermute(block, axis, route)


def pair_views(first_moment, second_moment, row_halves, column_halves):
    other_a = swapped(first_moment, "tile", 0)
    other_b = swapped(second_moment, "tile", 1)
    joined_a = jnp.where(
        column_halves == 0,
        jnp.concatenate([first_moment, other_a], axis=1),
        jnp.concatenate([other_a, first_moment], axis=1),
    )
    joined_b = jnp.where(
        row_halves == 0,
        jnp.concatenate([second_moment, other_b], axis=1),
        jnp.concatenate([other_b, second_moment], axis=1),
    )
    return (joined_a, joined_b)


def moment_pair(total, squares, batch_images):
    column_mean = total / batch_images
    var = squares / batch_images - column_mean * column_mean
    return (column_mean, lax.rsqrt(var + 1e-05))


def col_sums(values):
    as_float = values.astype(jnp.float32)
    return (jnp.sum(as_float, axis=0), jnp.sum(as_float * as_float, axis=0))


def reduced_device(left_outputs, right_outputs):
    rows, quart = left_outputs.shape
    half = 2 * quart
    feats = 4 * quart
    dp_count = lax.axis_size("dp")
    batch_images = rows * dp_count
    tpos = lax.axis_index("tile")
    row_halves = tpos // 2
    column_halves = tpos % 2
    sum_a, sq_a = col_sums(left_outputs)
    sum_b, sq_b = col_sums(right_outputs)
    sum_a, sq_a, sum_b, sq_b = lax.psum((sum_a, sq_a, sum_b, sq_b), "dp")
    left_mean, left_inverse_deviation = moment_pair(sum_a, sq_a, batch_images)
    right_mean, right_inverse_deviation = moment_pair(sum_b, sq_b, batch_images)
    standardized_left = (left_outputs.astype(jnp.float32) - left_mean) * left_inverse_deviation
    standardized_right = (right_outputs.astype(jnp.float32) - right_mean) * right_inverse_deviation
    half_a, cols_b = pair_views(
        standardized_left.astype(jnp.bfloat16),
        standardized_right.astype(jnp.bfloat16),
        row_halves,
        column_halves,
    )
    col_local = jnp.arange(half, dtype=jnp.int32)
    col_ids = quart * column_halves + col_local + jnp.where(col_local >= quart, quart, 0)
    owned = half // dp_count
    picked = half_a
    corr_rows = (
        lax.psum_scatter(
            lax.dot_general(
                picked, cols_b, (((0,), (0,)), ((), ())), preferred_element_type=jnp.float32
            ),
            "dp",
            scatter_dimension=0,
            tiled=True,
        )
        / batch_images
    )
    row_ids = half * row_halves + lax.axis_index("dp") * owned + jnp.arange(owned, dtype=jnp.int32)
    diagonal = row_ids[:, None] == col_ids[None, :]
    part_loss = jnp.sum(
        jnp.where(diagonal, (1.0 - corr_rows) ** 2, off_weight * corr_rows * corr_rows)
    )
    loss = lax.psum(part_loss, ("dp", "tile")) / feats
    dcorr_part = jnp.where(diagonal, corr_rows - 1.0, off_weight * corr_rows).astype(jnp.bfloat16)
    piece = lax.all_gather(dcorr_part, "dp", axis=0, tiled=True)
    block_a = lax.dot_general(
        cols_b, piece, (((1,), (1,)), ((), ())), preferred_element_type=jnp.float32
    )
    picked = half_a
    into_b = jnp.dot(picked, piece, preferred_element_type=jnp.float32)
    other_a = swapped(block_a.astype(jnp.bfloat16), "tile", 0).astype(block_a.dtype)
    other_b = swapped(into_b.astype(jnp.bfloat16), "tile", 1).astype(into_b.dtype)
    normed_grad_left = lax.dynamic_slice_in_dim(block_a + other_a, column_halves * quart, quart, 1)
    normed_grad_right = lax.dynamic_slice_in_dim(into_b + other_b, row_halves * quart, quart, 1)
    first_moment_left, second_moment_left, first_moment_right, second_moment_right = lax.psum(
        (
            jnp.sum(normed_grad_left, axis=0),
            jnp.sum(normed_grad_left * standardized_left, axis=0),
            jnp.sum(normed_grad_right, axis=0),
            jnp.sum(normed_grad_right * standardized_right, axis=0),
        ),
        "dp",
    )
    left_gradient = (
        left_inverse_deviation
        * (
            normed_grad_left
            - first_moment_left / batch_images
            - standardized_left * (second_moment_left / batch_images)
        )
    ).astype(jnp.bfloat16)
    right_gradient = (
        right_inverse_deviation
        * (
            normed_grad_right
            - first_moment_right / batch_images
            - standardized_right * (second_moment_right / batch_images)
        )
    ).astype(jnp.bfloat16)
    return (left_gradient, right_gradient, corr_rows[None, :, :], jnp.reshape(loss, (1,)))


def fold_rows(values):
    rows, width = values.shape
    return jnp.sum(values.reshape(rows // 8, 8, width), axis=0)


def fold_lanes(values):
    return sum(values[:, at : at + 128] for at in range(0, values.shape[1], 128))


def column_mean(block):
    rows, width = block.shape
    folded = jnp.zeros((8, width), jnp.float32)
    for at in range(0, rows, 64):
        folded = folded + fold_rows(block[at : at + 64, :].astype(jnp.float32))
    return jnp.sum(folded, axis=0, keepdims=True) / rows


def add_sums(sums, centred, low):
    return [
        sums[0] + fold_rows(centred),
        sums[1] + fold_rows(centred * centred),
        sums[2] + fold_rows(low.astype(jnp.float32)),
    ]


def rows_of(values):
    pad = jnp.zeros((8 - len(values), values[0].shape[1]), jnp.float32)
    return jnp.concatenate([*values, pad], axis=0)


def joined_sums(row, sums):
    return [row[i + 1 : i + 2, :] + jnp.sum(s, axis=0, keepdims=True) for i, s in enumerate(sums)]


def moments(sums, images):
    total, squares, rounded = sums
    delta = total / images
    return delta, lax.rsqrt(squares / images - delta * delta + 1e-05), rounded / images - delta


def three_parts(row):
    high = row.astype(jnp.bfloat16)
    rest = row - high.astype(jnp.float32)
    middle = rest.astype(jnp.bfloat16)
    low = (rest - middle.astype(jnp.float32)).astype(jnp.bfloat16)
    return [high, middle, low]


def split_rows(values):
    parts = sum([three_parts(v) for v in values], [])
    pad = jnp.zeros((4, values[0].shape[1]), jnp.float32)
    return jnp.concatenate([*(p.astype(jnp.float32) for p in parts), pad], axis=0).astype(
        jnp.bfloat16
    )


def joined_rows(ref, at):
    parts = ref[at : at + 16, :].astype(jnp.float32)
    part = lambda i: parts[i : i + 1]
    return [part(3 * i) + part(3 * i + 1) + part(3 * i + 2) for i in range(4)]


def lanes_to_row(partial):
    ones = jnp.ones((16, partial.shape[1]), jnp.bfloat16)
    high = partial.astype(jnp.bfloat16)
    low = (partial - high.astype(jnp.float32)).astype(jnp.bfloat16)
    row = dot_rows(ones, high) + dot_rows(ones, low)
    return row[:1, :]


def dot_rows(left, right):
    return lax.dot_general(
        left, right, (((1,), (1,)), ((), ())), preferred_element_type=jnp.float32
    )


def dot(left, right):
    return jnp.dot(left, right, preferred_element_type=jnp.float32)


def pick(mask, outer, inner, piece):
    return jnp.where(
        mask[0:1, :] != 0.0, outer[piece, :].astype(jnp.float32), inner[piece, :].astype(jnp.float32)
    )


def pick_kernel(mask, outer, inner, out):
    for at in range(0, outer.shape[0], 64):
        piece = slice(at, at + 64)
        out[piece, :] = pick(mask, outer, inner, piece).astype(out.dtype)


def right_sums_kernel(first, second, third, row):
    rows, quart = first.shape
    shift = column_mean(first)
    sums = [jnp.zeros((8, quart), jnp.float32)] * 3
    for block in (first, second, third):
        for at in range(0, rows, 64):
            centred = block[at : at + 64, :].astype(jnp.float32) - shift
            sums = add_sums(sums, centred, centred.astype(jnp.bfloat16))
    row[...] = rows_of([shift] + [jnp.sum(s, axis=0, keepdims=True) for s in sums])


def halves_kernel(block, first, second):
    half = first.shape[0]
    first[...] = block[:half, :]
    second[...] = block[half:, :]


def late_left_kernel(images, mask, outer, inner, row, out):
    rows, quart = outer.shape
    shift = row[0:1, :]
    sums = [jnp.zeros((8, quart), jnp.float32)] * 3
    for at in range(0, rows, 128):
        piece = slice(at, at + 128)
        centred = pick(mask, outer, inner, piece) - shift
        low = centred.astype(jnp.bfloat16)
        out[piece, :] = low
        sums = add_sums(sums, centred, low)
    delta, rstd, gap = moments(joined_sums(row, sums), images)
    out[rows:, :] = split_rows([shift + delta, rstd, gap, delta])


def late_right_kernel(images, last, mask, outer, inner, row, out, *rest):
    some, quart = outer.shape
    shift = row[0:1, :]
    sums = [jnp.zeros((8, quart), jnp.float32)] * 3
    for at in range(0, some, 128):
        piece = slice(at, at + 128)
        centred = pick(mask, outer, inner, piece) - shift
        low = centred.astype(jnp.bfloat16)
        out[:quart, piece] = jnp.transpose(low)
        sums = add_sums(sums, centred, low)
    sums = joined_sums(row, sums)
    if not last:
        (row_out,) = rest
        row_out[...] = rows_of([shift, *sums])
        return
    delta, rstd, gap = moments(sums, images)
    parts = split_rows([shift + delta, rstd, gap, delta])
    for i in range(quart // some):
        below = quart + 16 * i
        out[below : below + 16, :] = parts[:, i * some : (i + 1) * some]


def right_stats(late):
    quart, some = late[0].shape
    found = [joined_rows(late[1], quart + 16 * i) for i in range(quart // some)]
    return [jnp.concatenate(values, axis=1) for values in zip(*found)]


def late_products(right, left, lanes):
    quart, some = right[0].shape
    first = dot(right[0][...], left[:some, lanes])
    return first + dot(right[1][:quart, :], left[some : 2 * some, lanes])


def products_kernel(*refs):
    lefts, rights = refs[0:6], refs[6:12]
    partner_own, partner_other, own_all, row_other, zero_own, zero_other = refs[12:18]
    low_left, low_right = refs[18:]
    rows, quart = lefts[0].shape
    width = quart // 2
    for half in range(2):
        lanes = slice(half * quart, (half + 1) * quart)
        shift = column_mean(lefts[half])
        sums = [jnp.zeros((8, quart), jnp.float32)] * 3
        for block in range(3):
            source = lefts[2 * block + half]
            for at in range(0, rows, 64):
                centred = source[at : at + 64, :].astype(jnp.float32) - shift
                low = centred.astype(jnp.bfloat16)
                low_left[block * rows + at : block * rows + at + 64, lanes] = low
                if block == 0:
                    (zero_own, zero_other)[half][at : at + 64, :] = low
                if half:
                    sums = add_sums(sums, centred, low)
        if half:
            row_other[...] = rows_of([shift] + [jnp.sum(s, axis=0, keepdims=True) for s in sums])
    for half in range(2):
        lanes = slice(half * quart, (half + 1) * quart)
        shift = column_mean(rights[half])
        for block in range(3):
            source = rights[2 * block + half]
            for at in range(0, rows, 128):
                low = (source[at : at + 128, :].astype(jnp.float32) - shift).astype(jnp.bfloat16)
                low_right[lanes, block * rows + at : block * rows + at + 128] = jnp.transpose(low)
    for tile in range(4):
        wide = slice(tile * width, (tile + 1) * width)
        inner = slice((tile % 2) * width, (tile % 2 + 1) * width)
        target = partner_own if tile < 2 else partner_other
        target[:, inner] = dot(low_right[quart:, :], low_left[:, wide])
        own_all[:, wide] = dot(low_right[:quart, :], low_left[:, wide])


def left_operand(zero, late, target, lanes):
    rows, quart = zero.shape
    _, _, gap, delta = joined_rows(late, rows)
    high, middle, _ = three_parts(delta)
    target[:rows, lanes] = zero[...]
    extra = [high.astype(jnp.float32), middle.astype(jnp.float32), gap]
    pad = jnp.zeros((13, quart), jnp.float32)
    target[rows:, lanes] = jnp.concatenate([*extra, pad], axis=0).astype(jnp.bfloat16)


def without_extra(terms, rows):
    return terms[:rows] - (terms[rows : rows + 1] + terms[rows + 1 : rows + 2] + terms[rows + 2 : rows + 3])


def scale_columns(late_b, images):
    _, rstd, _, delta = right_stats(late_b)
    columns = jnp.transpose(rows_of([rstd / images, delta * rstd]))
    return columns[:, 0:1], columns[:, 1:2]


def partner_kernel(images, part, late, zero, sums, late_b_0, late_b_1, *refs):
    if part:
        (terms_in, across_in, vec_in, partial_out, e_out, vec_out, left) = refs
    else:
        (terms_out, across_out, e_out, vec_out, left) = refs
    late_b = (late_b_0, late_b_1)
    rows, quart = zero.shape
    width = quart // 2
    _, rstd, _, delta = joined_rows(late, rows)
    left_operand(zero, late, left, slice(0, quart))
    scale_col, delta_col = scale_columns(late_b, images)
    across = across_in[...] if part else jnp.zeros((quart, 128), jnp.float32)
    down = []
    for tile in range(2):
        at = slice(tile * width, (tile + 1) * width)
        total = sums[:, at] + late_products(late_b, late, at)
        corr = (total * scale_col - delta_col * delta[:, at]) * rstd[:, at]
        e_out[:, at] = (corr * (off_weight * rstd[:, at])).astype(jnp.bfloat16)
        square = corr * corr
        across = across + fold_lanes(square)
        down.append(jnp.sum(square, axis=0, keepdims=True))
    second_a = off_weight * jnp.concatenate(down, axis=1)
    if part:
        vec_out[...] = rows_of([second_a, second_a + vec_in[0:1, :]])
        nothing = jnp.zeros((1, quart), jnp.float32)
        second = off_weight * lanes_to_row(across)
        partial_out[rows:, :] = split_rows([second, nothing, nothing, nothing])
    else:
        vec_out[...] = rows_of([second_a])
        across_out[...] = across
    for tile in range(2):
        at = slice(tile * width, (tile + 1) * width)
        terms = dot_rows(left[...], e_out[at, :])
        if part:
            partial_out[:rows, at] = without_extra(terms + terms_in[:, at], rows).astype(
                jnp.bfloat16
            )
        else:
            terms_out[:, at] = terms


def own_kernel(images, flags, *refs):
    late_b, late_b_other, refs = refs[:2], refs[2:4], refs[4:]
    (late_own, late_other, first_own, first_other, zero_own, zero_other, sums) = refs[:7]
    (first_b, first_b_other, e_left, e_right, partner_own, partner_other) = refs[7:13]
    (vec_own, vec_other, vec_core, right_out, left_out, left_partial_out, mine_out) = refs[13:20]
    (own_loss_out, loss_out, left, norm_b, e_own, mine_own, mine_partner) = refs[20:]
    rows, quart = zero_own.shape
    width = quart // 2
    lower, upper = slice(0, quart), slice(quart, 2 * quart)
    stats_own, stats_other = joined_rows(late_own, rows), joined_rows(late_other, rows)
    both = lambda i: jnp.concatenate([stats_own[i], stats_other[i]], axis=1)
    offset, rstd, _, delta = [both(i) for i in range(4)]
    left_operand(zero_own, late_own, left, lower)
    left_operand(zero_other, late_other, left, upper)
    own_b = right_stats(late_b)
    other_b = right_stats(late_b_other)
    for source, stats, lanes in ((first_b, own_b, lower), (first_b_other, other_b, upper)):
        for at in range(0, rows, 64):
            piece = slice(at, at + 64)
            norm_b[piece, lanes] = (
                (source[piece, :].astype(jnp.float32) - stats[0]) * stats[1]
            ).astype(jnp.bfloat16)
        rest = jnp.broadcast_to(stats[2] * stats[1], (16, quart))
        norm_b[rows:, lanes] = rest.astype(jnp.bfloat16)

    def tile_corr(late, inner, total, columns, block):
        scale_col, delta_col = columns
        total = total + late_products(block, late, inner)
        row = joined_rows(late, rows)
        return (total * scale_col - delta_col * row[3][:, inner]) * row[1][:, inner]

    columns = scale_columns(late_b, images)
    columns_partner = scale_columns(late_b_other, images)
    across = jnp.zeros((quart, 128), jnp.float32)
    losses = jnp.zeros((8, 128), jnp.float32)
    down, diagonals = [], []
    for tile in range(4):
        at = slice(tile * width, (tile + 1) * width)
        inner = slice((tile % 2) * width, (tile % 2 + 1) * width)
        late = late_own if tile < 2 else late_other
        corr = tile_corr(late, inner, sums[:, at], columns, late_b)
        dcorr = off_weight * corr
        product = dcorr * corr
        loss = product
        if tile < 2:
            feature = lax.broadcasted_iota(jnp.int32, (quart, width), 0)
            lane = lax.broadcasted_iota(jnp.int32, (quart, width), 1) + tile * width
            diagonal = feature == lane
            slope = jnp.where(diagonal, (corr - 1.0).astype(jnp.bfloat16).astype(jnp.float32), 0.0)
            diagonals.append(jnp.sum(slope, axis=0, keepdims=True))
            dcorr = jnp.where(diagonal, 0.0, dcorr)
            product = jnp.where(diagonal, slope * corr, product)
            loss = jnp.where(diagonal, (1.0 - corr) * (1.0 - corr), loss)
        e_own[:, at] = (dcorr * rstd[:, at]).astype(jnp.bfloat16)
        across = across + fold_lanes(product)
        losses = losses + fold_rows(fold_lanes(loss))
        down.append(jnp.sum(product, axis=0, keepdims=True))

        @pl.when(flags[0] == tile)
        def _():
            mine_own[...] = corr
            partner = partner_own if tile < 2 else partner_other
            mine_partner[...] = tile_corr(
                late, inner, partner[:, inner], columns_partner, late_b_other
            )

    diagonal_row = jnp.concatenate(diagonals, axis=1)
    partner_second = jnp.concatenate([vec_own[0:1, :], vec_other[0:1, :]], axis=1)
    second_a = rstd * (partner_second + jnp.concatenate(down, axis=1))
    second_b = lanes_to_row(across)
    own_loss = jnp.sum(losses)
    own_loss_out[...] = jnp.broadcast_to(own_loss, (8, 128))
    loss = own_loss + jnp.sum(vec_other[1:2, :] + vec_core[1:2, :])
    loss_out[...] = jnp.broadcast_to(loss, (8, 128))

    for tile in (2, 3, 0, 1):
        at = slice(tile * width, (tile + 1) * width)
        inner = slice((tile % 2) * width, (tile % 2 + 1) * width)
        source, e_partner = (first_own, e_left) if tile < 2 else (first_other, e_right)
        terms = dot(norm_b[:, lower], e_own[:, at]) + dot(norm_b[:, upper], e_partner[:, inner])
        xhat = (source[:, inner].astype(jnp.float32) - offset[:, at]) * rstd[:, at]
        value = terms[:rows] - terms[rows : rows + 1] - xhat * second_a[:, at]
        if tile < 2:
            slope = rstd[:, at] * diagonal_row[:, inner]
            left_out[:, inner] = value + norm_b[:rows, inner].astype(jnp.float32) * slope
        else:
            left_partial_out[:, inner] = value.astype(jnp.bfloat16)

    for tile in range(2):
        at = slice(tile * width, (tile + 1) * width)
        terms = dot_rows(left[...], e_own[at, :])
        xhat = (first_b[:, at].astype(jnp.float32) - own_b[0][:, at]) * own_b[1][:, at]
        norm_a = (first_own[:, at].astype(jnp.float32) - offset[:, at]) * rstd[:, at]
        norm_a = norm_a.astype(jnp.bfloat16).astype(jnp.float32)
        right_out[:, at] = (
            without_extra(terms, rows) - xhat * second_b[:, at] + norm_a * diagonal_row[:, at]
        )

    own_columns = jnp.transpose(mine_own[...])
    partner_columns = jnp.transpose(mine_partner[...])

    @pl.when(flags[1] == 0)
    def _():
        mine_out[:, lower] = own_columns
        mine_out[:, upper] = partner_columns

    @pl.when(flags[1] != 0)
    def _():
        mine_out[:, lower] = partner_columns
        mine_out[:, upper] = own_columns


def add_kernel(one, other, out):
    out[...] = one[...] + other[...]


def loss_kernel(feats, one, other, out):
    out[0] = (one[0, 0] + other[0, 0]) / feats


def left_final_kernel(left, from_core, left_out):
    for at in range(0, left.shape[0], 64):
        piece = slice(at, at + 64)
        value = left[piece, :] + from_core[piece, :].astype(jnp.float32)
        left_out[piece, :] = value.astype(jnp.bfloat16)


def right_final_kernel(right, from_x, late_b_0, late_b_1, first_b, right_out):
    rows = right.shape[0]
    offset, rstd, _, _ = right_stats((late_b_0, late_b_1))
    second = joined_rows(from_x, rows)[0]
    for at in range(0, rows, 64):
        piece = slice(at, at + 64)
        xhat = (first_b[piece, :].astype(jnp.float32) - offset) * rstd
        value = right[piece, :] + from_x[piece, :].astype(jnp.float32) - xhat * second
        right_out[piece, :] = (rstd * value).astype(jnp.bfloat16)


vmem = pl.BlockSpec(memory_space=pltpu.VMEM)
smem = pl.BlockSpec(memory_space=pltpu.SMEM)


def local_call(kernel, operands, outs, scratch=(), flops=2**20, room=8, held=(), moved=None):
    if moved is None:
        moved = sum(x.size * x.dtype.itemsize for x in (*operands, *outs))

    def space(x):
        return smem if x.ndim == 1 else vmem

    return pl.pallas_call(
        kernel,
        out_shape=list(outs),
        in_specs=[space(x) for x in operands],
        out_specs=[space(x) for x in outs],
        scratch_shapes=list(scratch),
        compiler_params=pltpu.CompilerParams(vmem_limit_bytes=room * 2**20),
        cost_estimate=pl.CostEstimate(flops=flops, bytes_accessed=moved, transcendentals=0),
    )(*(pltpu.with_memory_space_constraint(x, pltpu.VMEM) if i in held else x for i, x in enumerate(operands)))


def gathered_device(left_outputs, right_outputs):
    rows, quart = left_outputs.shape
    half = 2 * quart
    feats = 4 * quart
    batch_images = rows * 4
    tpos = lax.axis_index("tile")
    dpos = lax.axis_index("dp")
    row_halves = tpos // 2
    column_halves = tpos % 2
    at_end = (dpos == 0) | (dpos == 3)
    owned_tile = jnp.where(dpos // 2 == column_halves, 0, 2) + dpos % 2
    flags = jnp.stack([owned_tile, row_halves]).astype(jnp.int32)
    mask = jnp.broadcast_to(at_end.astype(jnp.float32), (8, quart))

    pairs = [(0, 1), (1, 0), (2, 3), (3, 2)]
    middle = [(1, 2), (2, 1)]
    outward = [(1, 0), (2, 3)]

    def along(block, route):
        return lax.ppermute(block, "dp", route)

    def core_swap(block):
        return swapped(block, "tile", 0)

    def x_swap(block):
        return swapped(block, "tile", 1)

    def after(value, *others):
        return lax.optimization_barrier((value, *others))

    gemm = 2 * rows * quart * quart
    width = quart // 2
    quarter_f32 = jax.ShapeDtypeStruct((rows, quart), jnp.float32)
    quarter_bf16 = jax.ShapeDtypeStruct((rows, quart), jnp.bfloat16)
    extended = jax.ShapeDtypeStruct((rows + 16, quart), jnp.bfloat16)
    row_out = jax.ShapeDtypeStruct((8, quart), jnp.float32)
    one_out = jax.ShapeDtypeStruct((8, 128), jnp.float32)
    across_shape = jax.ShapeDtypeStruct((quart, 128), jnp.float32)
    low = lambda n, m: pltpu.VMEM((n, m), jnp.bfloat16)

    def picked(outer, inner):
        return local_call(pick_kernel, (mask, outer, inner), (quarter_bf16,))[0]

    some = rows // 2
    half_block = jax.ShapeDtypeStruct((some, quart), jnp.bfloat16)
    first_b = along(right_outputs, pairs)
    inner_b = along(right_outputs, middle)
    first_a = along(left_outputs, pairs)
    other_b0 = x_swap(right_outputs)
    other_a0, mask, flags = after(core_swap(left_outputs), mask, flags)
    left_behind, first_a, other_a0 = after(left_outputs, first_a, other_a0)
    inner_a = along(left_behind, middle)

    outer_b = along(inner_b, outward)
    third_b = along(first_b, middle)
    ready_b, other_b0 = after(first_b, other_b0)
    other_b1 = x_swap(ready_b)
    outer_a = along(inner_a, outward)
    third_a = along(first_a, middle)
    other_a1 = core_swap(first_a)

    third_b = local_call(halves_kernel, (third_b,), (half_block, half_block))
    last_b = [along(x, outward) for x in third_b]
    second_b = picked(outer_b, inner_b)
    row_b = local_call(right_sums_kernel, (right_outputs, first_b, second_b), (row_out,))[0]
    second_b, other_b1, other_a1 = after(second_b, other_b1, other_a1)
    other_b2 = x_swap(second_b)
    last_a = along(third_a, outward)
    second_a = picked(outer_a, inner_a)
    second_a, row_b = after(second_a, row_b)
    other_a2 = core_swap(second_a)

    late_b_0, row_b = local_call(
        functools.partial(late_right_kernel, batch_images, False),
        (mask, last_b[0], third_b[0], row_b),
        (jax.ShapeDtypeStruct((quart, some), jnp.bfloat16), row_out),
        held=(0, 1, 2, 3),
    )
    late_b_other_0 = x_swap(late_b_0)
    (late_b_1,) = local_call(
        functools.partial(late_right_kernel, batch_images, True),
        (mask, last_b[1], third_b[1], row_b),
        (jax.ShapeDtypeStruct((quart + 16 * (quart // some), some), jnp.bfloat16),),
        held=(0, 1, 2, 3),
    )
    late_b_other_1 = x_swap(late_b_1)
    late_b = (late_b_0, late_b_1)
    other_b2, late_b_1, late_b_other_0 = after(other_b2, late_b_1, late_b_other_0)
    partner_own, partner_other, own_all, row_other, zero_own, zero_other = local_call(
        products_kernel,
        (left_outputs, other_a0, first_a, other_a1, second_a, other_a2)
        + (right_outputs, other_b0, first_b, other_b1, second_b, other_b2),
        (
            quarter_f32,
            quarter_f32,
            jax.ShapeDtypeStruct((quart, half), jnp.float32),
            row_out,
            quarter_bf16,
            quarter_bf16,
        ),
        [low(3 * rows, half), low(half, 3 * rows)],
        room=20,
        moved=2**16,
    )
    row_a, late_b_other_1 = after(core_swap(row_other), late_b_other_1)
    late_b_other = (late_b_other_0, late_b_other_1)
    (late_a,) = local_call(
        functools.partial(late_left_kernel, batch_images),
        (mask, last_a, third_a, row_a),
        (extended,),
        held=(0, 1, 2, 3),
    )
    late_a_other = core_swap(late_a)

    terms, across, e_left, vec_own = local_call(
        functools.partial(partner_kernel, batch_images, 0),
        (late_a, zero_own, partner_own, *late_b_other),
        (
            jax.ShapeDtypeStruct((rows + 16, quart), jnp.float32),
            across_shape,
            quarter_bf16,
            row_out,
        ),
        [low(rows + 16, quart)],
        2 * gemm,
        room=12,
    )
    partial_right, e_right, vec_other = local_call(
        functools.partial(partner_kernel, batch_images, 1),
        (late_a_other, zero_other, partner_other, *late_b_other, terms, across, vec_own),
        (extended, quarter_bf16, row_out),
        [low(rows + 16, quart)],
        2 * gemm,
        room=12,
    )
    from_x = x_swap(partial_right)
    vec_core = core_swap(vec_other)
    right_own, left_own, partial_left, mine, own_loss, loss = local_call(
        functools.partial(own_kernel, batch_images),
        (flags, *late_b, *late_b_other)
        + (late_a, late_a_other, left_outputs, other_a0, zero_own, zero_other, own_all)
        + (right_outputs, other_b0, e_left, e_right)
        + (partner_own, partner_other)
        + (vec_own, vec_other, vec_core),
        (
            quarter_f32,
            quarter_f32,
            quarter_bf16,
            jax.ShapeDtypeStruct((width, half), jnp.float32),
            one_out,
            one_out,
        ),
        [
            low(rows + 16, half),
            low(rows + 16, half),
            low(quart, half),
            pltpu.VMEM((quart, width), jnp.float32),
            pltpu.VMEM((quart, width), jnp.float32),
        ],
        8 * gemm,
        room=20,
    )
    from_core = core_swap(partial_left)
    core_loss = core_swap(own_loss)
    (loss,) = local_call(add_kernel, (loss, core_loss), (one_out,))
    x_loss = x_swap(loss)
    (left_gradient,) = local_call(left_final_kernel, (left_own, from_core), (quarter_bf16,))
    right_own, left_gradient = after(right_own, left_gradient)
    (right_gradient,) = local_call(
        right_final_kernel, (right_own, from_x, *late_b, right_outputs), (quarter_bf16,)
    )
    right_gradient, x_loss = after(right_gradient, x_loss)
    (loss,) = local_call(
        functools.partial(loss_kernel, feats),
        (loss, x_loss),
        (jax.ShapeDtypeStruct((1,), jnp.float32),),
    )
    return (left_gradient, right_gradient, mine[None, :, :], loss)


def solution(mesh):
    per_device = gathered_device if mesh.shape["dp"] == 4 else reduced_device
    return jax.shard_map(
        per_device,
        mesh=mesh,
        in_specs=(P(("groups", "dp"), "tile"), P(("groups", "dp"), "tile")),
        out_specs=(
            P(("groups", "dp"), "tile"),
            P(("groups", "dp"), "tile"),
            P(("groups", "tile"), "dp", None),
            P("groups"),
        ),
        check_vma=False,
    )
```

```python
import functools
import jax
import jax.numpy as jnp
from jax import lax
from jax.experimental import pallas as pl
from jax.experimental.pallas import tpu as pltpu
from jax.sharding import PartitionSpec as P

off_weight = 0.0051


def swapped(block, axis, bit):
    count = lax.axis_size(axis)
    route = []
    for low in range(count):
        high = low | 1 << bit
        if high != low and high < count:
            route += [(low, high), (high, low)]
    return lax.ppermute(block, axis, route)


def pair_views(first_moment, second_moment, row_halves, column_halves):
    other_a = swapped(first_moment, "tile", 0)
    other_b = swapped(second_moment, "tile", 1)
    joined_a = jnp.where(
        column_halves == 0,
        jnp.concatenate([first_moment, other_a], axis=1),
        jnp.concatenate([other_a, first_moment], axis=1),
    )
    joined_b = jnp.where(
        row_halves == 0,
        jnp.concatenate([second_moment, other_b], axis=1),
        jnp.concatenate([other_b, second_moment], axis=1),
    )
    return (joined_a, joined_b)


def moment_pair(total, squares, batch_images):
    column_mean = total / batch_images
    var = squares / batch_images - column_mean * column_mean
    return (column_mean, lax.rsqrt(var + 1e-05))


def col_sums(values):
    as_float = values.astype(jnp.float32)
    return (jnp.sum(as_float, axis=0), jnp.sum(as_float * as_float, axis=0))


def reduced_device(left_outputs, right_outputs):
    rows, quart = left_outputs.shape
    half = 2 * quart
    feats = 4 * quart
    dp_count = lax.axis_size("dp")
    batch_images = rows * dp_count
    tpos = lax.axis_index("tile")
    row_halves = tpos // 2
    column_halves = tpos % 2
    sum_a, sq_a = col_sums(left_outputs)
    sum_b, sq_b = col_sums(right_outputs)
    sum_a, sq_a, sum_b, sq_b = lax.psum((sum_a, sq_a, sum_b, sq_b), "dp")
    left_mean, left_inverse_deviation = moment_pair(sum_a, sq_a, batch_images)
    right_mean, right_inverse_deviation = moment_pair(sum_b, sq_b, batch_images)
    standardized_left = (left_outputs.astype(jnp.float32) - left_mean) * left_inverse_deviation
    standardized_right = (right_outputs.astype(jnp.float32) - right_mean) * right_inverse_deviation
    half_a, cols_b = pair_views(
        standardized_left.astype(jnp.bfloat16),
        standardized_right.astype(jnp.bfloat16),
        row_halves,
        column_halves,
    )
    col_local = jnp.arange(half, dtype=jnp.int32)
    col_ids = quart * column_halves + col_local + jnp.where(col_local >= quart, quart, 0)
    owned = half // dp_count
    picked = half_a
    corr_rows = (
        lax.psum_scatter(
            lax.dot_general(
                picked, cols_b, (((0,), (0,)), ((), ())), preferred_element_type=jnp.float32
            ),
            "dp",
            scatter_dimension=0,
            tiled=True,
        )
        / batch_images
    )
    row_ids = half * row_halves + lax.axis_index("dp") * owned + jnp.arange(owned, dtype=jnp.int32)
    diagonal = row_ids[:, None] == col_ids[None, :]
    part_loss = jnp.sum(
        jnp.where(diagonal, (1.0 - corr_rows) ** 2, off_weight * corr_rows * corr_rows)
    )
    loss = lax.psum(part_loss, ("dp", "tile")) / feats
    dcorr_part = jnp.where(diagonal, corr_rows - 1.0, off_weight * corr_rows).astype(jnp.bfloat16)
    piece = lax.all_gather(dcorr_part, "dp", axis=0, tiled=True)
    block_a = lax.dot_general(
        cols_b, piece, (((1,), (1,)), ((), ())), preferred_element_type=jnp.float32
    )
    picked = half_a
    into_b = jnp.dot(picked, piece, preferred_element_type=jnp.float32)
    other_a = swapped(block_a.astype(jnp.bfloat16), "tile", 0).astype(block_a.dtype)
    other_b = swapped(into_b.astype(jnp.bfloat16), "tile", 1).astype(into_b.dtype)
    normed_grad_left = lax.dynamic_slice_in_dim(block_a + other_a, column_halves * quart, quart, 1)
    normed_grad_right = lax.dynamic_slice_in_dim(into_b + other_b, row_halves * quart, quart, 1)
    first_moment_left, second_moment_left, first_moment_right, second_moment_right = lax.psum(
        (
            jnp.sum(normed_grad_left, axis=0),
            jnp.sum(normed_grad_left * standardized_left, axis=0),
            jnp.sum(normed_grad_right, axis=0),
            jnp.sum(normed_grad_right * standardized_right, axis=0),
        ),
        "dp",
    )
    left_gradient = (
        left_inverse_deviation
        * (
            normed_grad_left
            - first_moment_left / batch_images
            - standardized_left * (second_moment_left / batch_images)
        )
    ).astype(jnp.bfloat16)
    right_gradient = (
        right_inverse_deviation
        * (
            normed_grad_right
            - first_moment_right / batch_images
            - standardized_right * (second_moment_right / batch_images)
        )
    ).astype(jnp.bfloat16)
    return (left_gradient, right_gradient, corr_rows[None, :, :], jnp.reshape(loss, (1,)))


def fold_rows(values):
    rows, width = values.shape
    return jnp.sum(values.reshape(rows // 8, 8, width), axis=0)


def fold_lanes(values):
    return sum(values[:, at : at + 128] for at in range(0, values.shape[1], 128))


def column_mean(block):
    rows, width = block.shape
    folded = jnp.zeros((8, width), jnp.float32)
    for at in range(0, rows, 64):
        folded = folded + fold_rows(block[at : at + 64, :].astype(jnp.float32))
    return jnp.sum(folded, axis=0, keepdims=True) / rows


def add_sums(sums, centred, low):
    return [
        sums[0] + fold_rows(centred),
        sums[1] + fold_rows(centred * centred),
        sums[2] + fold_rows(low.astype(jnp.float32)),
    ]


def rows_of(values):
    pad = jnp.zeros((8 - len(values), values[0].shape[1]), jnp.float32)
    return jnp.concatenate([*values, pad], axis=0)


def joined_sums(row, sums):
    return [row[i + 1 : i + 2, :] + jnp.sum(s, axis=0, keepdims=True) for i, s in enumerate(sums)]


def moments(sums, images):
    total, squares, rounded = sums
    delta = total / images
    return delta, lax.rsqrt(squares / images - delta * delta + 1e-05), rounded / images - delta


def three_parts(row):
    high = row.astype(jnp.bfloat16)
    rest = row - high.astype(jnp.float32)
    middle = rest.astype(jnp.bfloat16)
    low = (rest - middle.astype(jnp.float32)).astype(jnp.bfloat16)
    return [high, middle, low]


def split_rows(values):
    parts = sum([three_parts(v) for v in values], [])
    pad = jnp.zeros((4, values[0].shape[1]), jnp.float32)
    return jnp.concatenate([*(p.astype(jnp.float32) for p in parts), pad], axis=0).astype(
        jnp.bfloat16
    )


def joined_rows(ref, at):
    parts = ref[at : at + 16, :].astype(jnp.float32)
    part = lambda i: parts[i : i + 1]
    return [part(3 * i) + part(3 * i + 1) + part(3 * i + 2) for i in range(4)]


def lanes_to_row(partial):
    ones = jnp.ones((16, partial.shape[1]), jnp.bfloat16)
    high = partial.astype(jnp.bfloat16)
    low = (partial - high.astype(jnp.float32)).astype(jnp.bfloat16)
    row = dot_rows(ones, high) + dot_rows(ones, low)
    return row[:1, :]


def dot_rows(left, right):
    return lax.dot_general(
        left, right, (((1,), (1,)), ((), ())), preferred_element_type=jnp.float32
    )


def dot(left, right):
    return jnp.dot(left, right, preferred_element_type=jnp.float32)


def pick(mask, outer, inner, piece):
    return jnp.where(
        mask[0:1, :] != 0.0, outer[piece, :].astype(jnp.float32), inner[piece, :].astype(jnp.float32)
    )


def pick_kernel(mask, outer, inner, out):
    for at in range(0, outer.shape[0], 64):
        piece = slice(at, at + 64)
        out[piece, :] = pick(mask, outer, inner, piece).astype(out.dtype)


def right_sums_kernel(first, second, third, row):
    rows, quart = first.shape
    shift = column_mean(first)
    sums = [jnp.zeros((8, quart), jnp.float32)] * 3
    for block in (first, second, third):
        for at in range(0, rows, 64):
            centred = block[at : at + 64, :].astype(jnp.float32) - shift
            sums = add_sums(sums, centred, centred.astype(jnp.bfloat16))
    row[...] = rows_of([shift] + [jnp.sum(s, axis=0, keepdims=True) for s in sums])


def halves_kernel(block, first, second):
    half = first.shape[0]
    first[...] = block[:half, :]
    second[...] = block[half:, :]


def late_left_kernel(images, mask, outer, inner, row, out):
    rows, quart = outer.shape
    shift = row[0:1, :]
    sums = [jnp.zeros((8, quart), jnp.float32)] * 3
    for at in range(0, rows, 128):
        piece = slice(at, at + 128)
        centred = pick(mask, outer, inner, piece) - shift
        low = centred.astype(jnp.bfloat16)
        out[piece, :] = low
        sums = add_sums(sums, centred, low)
    delta, rstd, gap = moments(joined_sums(row, sums), images)
    out[rows:, :] = split_rows([shift + delta, rstd, gap, delta])


def late_right_kernel(images, last, mask, outer, inner, row, out, *rest):
    some, quart = outer.shape
    shift = row[0:1, :]
    sums = [jnp.zeros((8, quart), jnp.float32)] * 3
    for at in range(0, some, 128):
        piece = slice(at, at + 128)
        centred = pick(mask, outer, inner, piece) - shift
        low = centred.astype(jnp.bfloat16)
        out[:quart, piece] = jnp.transpose(low)
        sums = add_sums(sums, centred, low)
    sums = joined_sums(row, sums)
    if not last:
        (row_out,) = rest
        row_out[...] = rows_of([shift, *sums])
        return
    delta, rstd, gap = moments(sums, images)
    parts = split_rows([shift + delta, rstd, gap, delta])
    for i in range(quart // some):
        below = quart + 16 * i
        out[below : below + 16, :] = parts[:, i * some : (i + 1) * some]


def right_stats(late):
    quart, some = late[0].shape
    found = [joined_rows(late[1], quart + 16 * i) for i in range(quart // some)]
    return [jnp.concatenate(values, axis=1) for values in zip(*found)]


def late_products(right, left, lanes):
    quart, some = right[0].shape
    first = dot(right[0][...], left[:some, lanes])
    return first + dot(right[1][:quart, :], left[some : 2 * some, lanes])


def products_kernel(*refs):
    lefts, rights = refs[0:6], refs[6:12]
    partner_own, partner_other, own_all, row_other, zero_own, zero_other = refs[12:18]
    low_left, low_right = refs[18:]
    rows, quart = lefts[0].shape
    width = quart // 2
    for half in range(2):
        lanes = slice(half * quart, (half + 1) * quart)
        shift = column_mean(lefts[half])
        sums = [jnp.zeros((8, quart), jnp.float32)] * 3
        for block in range(3):
            source = lefts[2 * block + half]
            for at in range(0, rows, 64):
                centred = source[at : at + 64, :].astype(jnp.float32) - shift
                low = centred.astype(jnp.bfloat16)
                low_left[block * rows + at : block * rows + at + 64, lanes] = low
                if block == 0:
                    (zero_own, zero_other)[half][at : at + 64, :] = low
                if half:
                    sums = add_sums(sums, centred, low)
        if half:
            row_other[...] = rows_of([shift] + [jnp.sum(s, axis=0, keepdims=True) for s in sums])
    for half in range(2):
        lanes = slice(half * quart, (half + 1) * quart)
        shift = column_mean(rights[half])
        for block in range(3):
            source = rights[2 * block + half]
            for at in range(0, rows, 128):
                low = (source[at : at + 128, :].astype(jnp.float32) - shift).astype(jnp.bfloat16)
                low_right[lanes, block * rows + at : block * rows + at + 128] = jnp.transpose(low)
    for tile in range(4):
        wide = slice(tile * width, (tile + 1) * width)
        inner = slice((tile % 2) * width, (tile % 2 + 1) * width)
        target = partner_own if tile < 2 else partner_other
        target[:, inner] = dot(low_right[quart:, :], low_left[:, wide])
        own_all[:, wide] = dot(low_right[:quart, :], low_left[:, wide])


def left_operand(zero, late, target, lanes):
    rows, quart = zero.shape
    _, _, gap, delta = joined_rows(late, rows)
    high, middle, _ = three_parts(delta)
    target[:rows, lanes] = zero[...]
    extra = [high.astype(jnp.float32), middle.astype(jnp.float32), gap]
    pad = jnp.zeros((13, quart), jnp.float32)
    target[rows:, lanes] = jnp.concatenate([*extra, pad], axis=0).astype(jnp.bfloat16)


def without_extra(terms, rows):
    return terms[:rows] - (terms[rows : rows + 1] + terms[rows + 1 : rows + 2] + terms[rows + 2 : rows + 3])


def scale_columns(late_b, images):
    _, rstd, _, delta = right_stats(late_b)
    columns = jnp.transpose(rows_of([rstd / images, delta * rstd]))
    return columns[:, 0:1], columns[:, 1:2]


def partner_kernel(images, part, late, zero, sums, late_b_0, late_b_1, *refs):
    if part:
        (terms_in, across_in, vec_in, columns, partial_out, e_out, vec_out, left) = refs
    else:
        (terms_out, across_out, e_out, vec_out, columns, left) = refs
        _, rstd_b, _, delta_b = right_stats((late_b_0, late_b_1))
        columns[...] = jnp.transpose(rows_of([rstd_b / images, delta_b * rstd_b]))
    late_b = (late_b_0, late_b_1)
    rows, quart = zero.shape
    width = quart // 2
    _, rstd, _, delta = joined_rows(late, rows)
    left_operand(zero, late, left, slice(0, quart))
    scale_col, delta_col = columns[:, 0:1], columns[:, 1:2]
    across = across_in[...] if part else jnp.zeros((quart, 128), jnp.float32)
    down = []
    for tile in range(2):
        at = slice(tile * width, (tile + 1) * width)
        total = sums[:, at] + late_products(late_b, late, at)
        corr = (total * scale_col - delta_col * delta[:, at]) * rstd[:, at]
        e_out[:, at] = (corr * (off_weight * rstd[:, at])).astype(jnp.bfloat16)
        square = corr * corr
        across = across + fold_lanes(square)
        down.append(jnp.sum(square, axis=0, keepdims=True))
    second_a = off_weight * jnp.concatenate(down, axis=1)
    if part:
        vec_out[...] = rows_of([second_a, second_a + vec_in[0:1, :]])
        nothing = jnp.zeros((1, quart), jnp.float32)
        second = off_weight * lanes_to_row(across)
        partial_out[rows:, :] = split_rows([second, nothing, nothing, nothing])
    else:
        vec_out[...] = rows_of([second_a])
        across_out[...] = across
    for tile in range(2):
        at = slice(tile * width, (tile + 1) * width)
        terms = dot_rows(left[...], e_out[at, :])
        if part:
            partial_out[:rows, at] = without_extra(terms + terms_in[:, at], rows).astype(
                jnp.bfloat16
            )
        else:
            terms_out[:, at] = terms


def own_kernel(images, flags, *refs):
    late_b, late_b_other, refs = refs[:2], refs[2:4], refs[4:]
    (late_own, late_other, first_own, first_other, zero_own, zero_other, sums) = refs[:7]
    (first_b, first_b_other, e_left, e_right, partner_own, partner_other) = refs[7:13]
    (vec_own, vec_other, vec_core, right_out, left_out, left_partial_out, mine_out) = refs[13:20]
    (own_loss_out, loss_out, left, norm_b, e_own, mine_own, mine_partner) = refs[20:]
    rows, quart = zero_own.shape
    width = quart // 2
    lower, upper = slice(0, quart), slice(quart, 2 * quart)
    stats_own, stats_other = joined_rows(late_own, rows), joined_rows(late_other, rows)
    both = lambda i: jnp.concatenate([stats_own[i], stats_other[i]], axis=1)
    offset, rstd, _, delta = [both(i) for i in range(4)]
    left_operand(zero_own, late_own, left, lower)
    left_operand(zero_other, late_other, left, upper)
    own_b = right_stats(late_b)
    other_b = right_stats(late_b_other)
    for source, stats, lanes in ((first_b, own_b, lower), (first_b_other, other_b, upper)):
        for at in range(0, rows, 64):
            piece = slice(at, at + 64)
            norm_b[piece, lanes] = (
                (source[piece, :].astype(jnp.float32) - stats[0]) * stats[1]
            ).astype(jnp.bfloat16)
        rest = jnp.broadcast_to(stats[2] * stats[1], (16, quart))
        norm_b[rows:, lanes] = rest.astype(jnp.bfloat16)

    def tile_corr(late, inner, total, columns, block):
        scale_col, delta_col = columns
        total = total + late_products(block, late, inner)
        row = joined_rows(late, rows)
        return (total * scale_col - delta_col * row[3][:, inner]) * row[1][:, inner]

    columns = scale_columns(late_b, images)
    columns_partner = scale_columns(late_b_other, images)
    across = jnp.zeros((quart, 128), jnp.float32)
    losses = jnp.zeros((8, 128), jnp.float32)
    down, diagonals = [], []
    for tile in range(4):
        at = slice(tile * width, (tile + 1) * width)
        inner = slice((tile % 2) * width, (tile % 2 + 1) * width)
        late = late_own if tile < 2 else late_other
        corr = tile_corr(late, inner, sums[:, at], columns, late_b)
        dcorr = off_weight * corr
        product = dcorr * corr
        loss = product
        if tile < 2:
            feature = lax.broadcasted_iota(jnp.int32, (quart, width), 0)
            lane = lax.broadcasted_iota(jnp.int32, (quart, width), 1) + tile * width
            diagonal = feature == lane
            slope = jnp.where(diagonal, (corr - 1.0).astype(jnp.bfloat16).astype(jnp.float32), 0.0)
            diagonals.append(jnp.sum(slope, axis=0, keepdims=True))
            dcorr = jnp.where(diagonal, 0.0, dcorr)
            product = jnp.where(diagonal, slope * corr, product)
            loss = jnp.where(diagonal, (1.0 - corr) * (1.0 - corr), loss)
        e_own[:, at] = (dcorr * rstd[:, at]).astype(jnp.bfloat16)
        across = across + fold_lanes(product)
        losses = losses + fold_rows(fold_lanes(loss))
        down.append(jnp.sum(product, axis=0, keepdims=True))

        @pl.when(flags[0] == tile)
        def _():
            mine_own[...] = corr
            partner = partner_own if tile < 2 else partner_other
            mine_partner[...] = tile_corr(
                late, inner, partner[:, inner], columns_partner, late_b_other
            )

    diagonal_row = jnp.concatenate(diagonals, axis=1)
    partner_second = jnp.concatenate([vec_own[0:1, :], vec_other[0:1, :]], axis=1)
    second_a = rstd * (partner_second + jnp.concatenate(down, axis=1))
    second_b = lanes_to_row(across)
    own_loss = jnp.sum(losses)
    own_loss_out[...] = jnp.broadcast_to(own_loss, (8, 128))
    loss = own_loss + jnp.sum(vec_other[1:2, :] + vec_core[1:2, :])
    loss_out[...] = jnp.broadcast_to(loss, (8, 128))

    for tile in (2, 3, 0, 1):
        at = slice(tile * width, (tile + 1) * width)
        inner = slice((tile % 2) * width, (tile % 2 + 1) * width)
        source, e_partner = (first_own, e_left) if tile < 2 else (first_other, e_right)
        terms = dot(norm_b[:, lower], e_own[:, at]) + dot(norm_b[:, upper], e_partner[:, inner])
        xhat = (source[:, inner].astype(jnp.float32) - offset[:, at]) * rstd[:, at]
        value = terms[:rows] - terms[rows : rows + 1] - xhat * second_a[:, at]
        if tile < 2:
            slope = rstd[:, at] * diagonal_row[:, inner]
            left_out[:, inner] = value + norm_b[:rows, inner].astype(jnp.float32) * slope
        else:
            left_partial_out[:, inner] = value.astype(jnp.bfloat16)

    for tile in range(2):
        at = slice(tile * width, (tile + 1) * width)
        terms = dot_rows(left[...], e_own[at, :])
        xhat = (first_b[:, at].astype(jnp.float32) - own_b[0][:, at]) * own_b[1][:, at]
        norm_a = (first_own[:, at].astype(jnp.float32) - offset[:, at]) * rstd[:, at]
        norm_a = norm_a.astype(jnp.bfloat16).astype(jnp.float32)
        right_out[:, at] = (
            without_extra(terms, rows) - xhat * second_b[:, at] + norm_a * diagonal_row[:, at]
        )

    own_columns = jnp.transpose(mine_own[...])
    partner_columns = jnp.transpose(mine_partner[...])

    @pl.when(flags[1] == 0)
    def _():
        mine_out[:, lower] = own_columns
        mine_out[:, upper] = partner_columns

    @pl.when(flags[1] != 0)
    def _():
        mine_out[:, lower] = partner_columns
        mine_out[:, upper] = own_columns


def add_kernel(one, other, out):
    out[...] = one[...] + other[...]


def left_final_kernel(left, from_core, left_out):
    for at in range(0, left.shape[0], 64):
        piece = slice(at, at + 64)
        value = left[piece, :] + from_core[piece, :].astype(jnp.float32)
        left_out[piece, :] = value.astype(jnp.bfloat16)


def right_final_kernel(feats, right, from_x, late_b_0, late_b_1, first_b, loss, x_loss, right_out, loss_out):
    rows = right.shape[0]
    offset, rstd, _, _ = right_stats((late_b_0, late_b_1))
    second = joined_rows(from_x, rows)[0]
    loss_out[0] = (loss[0, 0] + x_loss[0, 0]) / feats
    for at in range(0, rows, 64):
        piece = slice(at, at + 64)
        xhat = (first_b[piece, :].astype(jnp.float32) - offset) * rstd
        value = right[piece, :] + from_x[piece, :].astype(jnp.float32) - xhat * second
        right_out[piece, :] = (rstd * value).astype(jnp.bfloat16)


vmem = pl.BlockSpec(memory_space=pltpu.VMEM)
smem = pl.BlockSpec(memory_space=pltpu.SMEM)


def local_call(kernel, operands, outs, scratch=(), flops=2**20, room=8, held=(), moved=None):
    if moved is None:
        moved = sum(x.size * x.dtype.itemsize for x in (*operands, *outs))

    def space(x):
        return smem if x.ndim == 1 else vmem

    return pl.pallas_call(
        kernel,
        out_shape=list(outs),
        in_specs=[space(x) for x in operands],
        out_specs=[space(x) for x in outs],
        scratch_shapes=list(scratch),
        compiler_params=pltpu.CompilerParams(vmem_limit_bytes=room * 2**20),
        cost_estimate=pl.CostEstimate(flops=flops, bytes_accessed=moved, transcendentals=0),
    )(*(pltpu.with_memory_space_constraint(x, pltpu.VMEM) if i in held else x for i, x in enumerate(operands)))


def gathered_device(left_outputs, right_outputs):
    rows, quart = left_outputs.shape
    half = 2 * quart
    feats = 4 * quart
    batch_images = rows * 4
    tpos = lax.axis_index("tile")
    dpos = lax.axis_index("dp")
    row_halves = tpos // 2
    column_halves = tpos % 2
    at_end = (dpos == 0) | (dpos == 3)
    owned_tile = jnp.where(dpos // 2 == column_halves, 0, 2) + dpos % 2
    flags = jnp.stack([owned_tile, row_halves]).astype(jnp.int32)
    mask = jnp.broadcast_to(at_end.astype(jnp.float32), (8, quart))

    pairs = [(0, 1), (1, 0), (2, 3), (3, 2)]
    middle = [(1, 2), (2, 1)]
    outward = [(1, 0), (2, 3)]

    def along(block, route):
        return lax.ppermute(block, "dp", route)

    def core_swap(block):
        return swapped(block, "tile", 0)

    def x_swap(block):
        return swapped(block, "tile", 1)

    def after(value, *others):
        return lax.optimization_barrier((value, *others))

    gemm = 2 * rows * quart * quart
    width = quart // 2
    quarter_f32 = jax.ShapeDtypeStruct((rows, quart), jnp.float32)
    quarter_bf16 = jax.ShapeDtypeStruct((rows, quart), jnp.bfloat16)
    extended = jax.ShapeDtypeStruct((rows + 16, quart), jnp.bfloat16)
    row_out = jax.ShapeDtypeStruct((8, quart), jnp.float32)
    one_out = jax.ShapeDtypeStruct((8, 128), jnp.float32)
    across_shape = jax.ShapeDtypeStruct((quart, 128), jnp.float32)
    low = lambda n, m: pltpu.VMEM((n, m), jnp.bfloat16)

    def picked(outer, inner):
        return local_call(pick_kernel, (mask, outer, inner), (quarter_bf16,))[0]

    some = rows // 2
    half_block = jax.ShapeDtypeStruct((some, quart), jnp.bfloat16)
    first_b = along(right_outputs, pairs)
    inner_b = along(right_outputs, middle)
    first_a = along(left_outputs, pairs)
    other_b0 = x_swap(right_outputs)
    other_a0, mask, flags = after(core_swap(left_outputs), mask, flags)
    left_behind, first_a, other_a0 = after(left_outputs, first_a, other_a0)
    inner_a = along(left_behind, middle)

    outer_b = along(inner_b, outward)
    third_b = along(first_b, middle)
    ready_b, other_b0 = after(first_b, other_b0)
    other_b1 = x_swap(ready_b)
    outer_a = along(inner_a, outward)
    third_a = along(first_a, middle)
    other_a1 = core_swap(first_a)

    third_b = local_call(halves_kernel, (third_b,), (half_block, half_block))
    last_b = [along(x, outward) for x in third_b]
    second_b = picked(outer_b, inner_b)
    row_b = local_call(right_sums_kernel, (right_outputs, first_b, second_b), (row_out,))[0]
    second_b, other_b1, other_a1 = after(second_b, other_b1, other_a1)
    other_b2 = x_swap(second_b)
    last_a = along(third_a, outward)
    second_a = picked(outer_a, inner_a)
    second_a, row_b = after(second_a, row_b)
    other_a2 = core_swap(second_a)

    late_b_0, row_b = local_call(
        functools.partial(late_right_kernel, batch_images, False),
        (mask, last_b[0], third_b[0], row_b),
        (jax.ShapeDtypeStruct((quart, some), jnp.bfloat16), row_out),
        held=(0, 1, 2, 3),
    )
    late_b_other_0 = x_swap(late_b_0)
    (late_b_1,) = local_call(
        functools.partial(late_right_kernel, batch_images, True),
        (mask, last_b[1], third_b[1], row_b),
        (jax.ShapeDtypeStruct((quart + 16 * (quart // some), some), jnp.bfloat16),),
        held=(0, 1, 2, 3),
    )
    late_b_other_1 = x_swap(late_b_1)
    late_b = (late_b_0, late_b_1)
    other_b2, late_b_1, late_b_other_0 = after(other_b2, late_b_1, late_b_other_0)
    partner_own, partner_other, own_all, row_other, zero_own, zero_other = local_call(
        products_kernel,
        (left_outputs, other_a0, first_a, other_a1, second_a, other_a2)
        + (right_outputs, other_b0, first_b, other_b1, second_b, other_b2),
        (
            quarter_f32,
            quarter_f32,
            jax.ShapeDtypeStruct((quart, half), jnp.float32),
            row_out,
            quarter_bf16,
            quarter_bf16,
        ),
        [low(3 * rows, half), low(half, 3 * rows)],
        room=20,
        moved=2**16,
    )
    row_a, late_b_other_1 = after(core_swap(row_other), late_b_other_1)
    late_b_other = (late_b_other_0, late_b_other_1)
    (late_a,) = local_call(
        functools.partial(late_left_kernel, batch_images),
        (mask, last_a, third_a, row_a),
        (extended,),
        held=(0, 1, 2, 3),
    )
    late_a_other = core_swap(late_a)

    terms, across, e_left, vec_own, columns = local_call(
        functools.partial(partner_kernel, batch_images, 0),
        (late_a, zero_own, partner_own, *late_b_other),
        (
            jax.ShapeDtypeStruct((rows + 16, quart), jnp.float32),
            across_shape,
            quarter_bf16,
            row_out,
            jax.ShapeDtypeStruct((quart, 8), jnp.float32),
        ),
        [low(rows + 16, quart)],
        2 * gemm,
        room=12,
    )
    partial_right, e_right, vec_other = local_call(
        functools.partial(partner_kernel, batch_images, 1),
        (late_a_other, zero_other, partner_other, *late_b_other, terms, across, vec_own, columns),
        (extended, quarter_bf16, row_out),
        [low(rows + 16, quart)],
        2 * gemm,
        room=12,
    )
    from_x = x_swap(partial_right)
    vec_core = core_swap(vec_other)
    right_own, left_own, partial_left, mine, own_loss, loss = local_call(
        functools.partial(own_kernel, batch_images),
        (flags, *late_b, *late_b_other)
        + (late_a, late_a_other, left_outputs, other_a0, zero_own, zero_other, own_all)
        + (right_outputs, other_b0, e_left, e_right)
        + (partner_own, partner_other)
        + (vec_own, vec_other, vec_core),
        (
            quarter_f32,
            quarter_f32,
            quarter_bf16,
            jax.ShapeDtypeStruct((width, half), jnp.float32),
            one_out,
            one_out,
        ),
        [
            low(rows + 16, half),
            low(rows + 16, half),
            low(quart, half),
            pltpu.VMEM((quart, width), jnp.float32),
            pltpu.VMEM((quart, width), jnp.float32),
        ],
        8 * gemm,
        room=20,
    )
    from_core = core_swap(partial_left)
    core_loss = core_swap(own_loss)
    (loss,) = local_call(add_kernel, (loss, core_loss), (one_out,))
    x_loss = x_swap(loss)
    (left_gradient,) = local_call(left_final_kernel, (left_own, from_core), (quarter_bf16,))
    right_own, left_gradient = after(right_own, left_gradient)
    right_gradient, loss = local_call(
        functools.partial(right_final_kernel, feats),
        (right_own, from_x, *late_b, right_outputs, loss, x_loss),
        (quarter_bf16, jax.ShapeDtypeStruct((1,), jnp.float32)),
    )
    return (left_gradient, right_gradient, mine[None, :, :], loss)


def solution(mesh):
    per_device = gathered_device if mesh.shape["dp"] == 4 else reduced_device
    return jax.shard_map(
        per_device,
        mesh=mesh,
        in_specs=(P(("groups", "dp"), "tile"), P(("groups", "dp"), "tile")),
        out_specs=(
            P(("groups", "dp"), "tile"),
            P(("groups", "dp"), "tile"),
            P(("groups", "tile"), "dp", None),
            P("groups"),
        ),
        check_vma=False,
    )
```

```python
import functools
import jax
import jax.numpy as jnp
from jax import lax
from jax.experimental import pallas as pl
from jax.experimental.pallas import tpu as pltpu
from jax.sharding import PartitionSpec as P

off_weight = 0.0051


def swapped(block, axis, bit):
    count = lax.axis_size(axis)
    route = []
    for low in range(count):
        high = low | 1 << bit
        if high != low and high < count:
            route += [(low, high), (high, low)]
    return lax.ppermute(block, axis, route)


def pair_views(first_moment, second_moment, row_halves, column_halves):
    other_a = swapped(first_moment, "tile", 0)
    other_b = swapped(second_moment, "tile", 1)
    joined_a = jnp.where(
        column_halves == 0,
        jnp.concatenate([first_moment, other_a], axis=1),
        jnp.concatenate([other_a, first_moment], axis=1),
    )
    joined_b = jnp.where(
        row_halves == 0,
        jnp.concatenate([second_moment, other_b], axis=1),
        jnp.concatenate([other_b, second_moment], axis=1),
    )
    return (joined_a, joined_b)


def moment_pair(total, squares, batch_images):
    column_mean = total / batch_images
    var = squares / batch_images - column_mean * column_mean
    return (column_mean, lax.rsqrt(var + 1e-05))


def col_sums(values):
    as_float = values.astype(jnp.float32)
    return (jnp.sum(as_float, axis=0), jnp.sum(as_float * as_float, axis=0))


def reduced_device(left_outputs, right_outputs):
    rows, quart = left_outputs.shape
    half = 2 * quart
    feats = 4 * quart
    dp_count = lax.axis_size("dp")
    batch_images = rows * dp_count
    tpos = lax.axis_index("tile")
    row_halves = tpos // 2
    column_halves = tpos % 2
    sum_a, sq_a = col_sums(left_outputs)
    sum_b, sq_b = col_sums(right_outputs)
    sum_a, sq_a, sum_b, sq_b = lax.psum((sum_a, sq_a, sum_b, sq_b), "dp")
    left_mean, left_inverse_deviation = moment_pair(sum_a, sq_a, batch_images)
    right_mean, right_inverse_deviation = moment_pair(sum_b, sq_b, batch_images)
    standardized_left = (left_outputs.astype(jnp.float32) - left_mean) * left_inverse_deviation
    standardized_right = (right_outputs.astype(jnp.float32) - right_mean) * right_inverse_deviation
    half_a, cols_b = pair_views(
        standardized_left.astype(jnp.bfloat16),
        standardized_right.astype(jnp.bfloat16),
        row_halves,
        column_halves,
    )
    col_local = jnp.arange(half, dtype=jnp.int32)
    col_ids = quart * column_halves + col_local + jnp.where(col_local >= quart, quart, 0)
    owned = half // dp_count
    picked = half_a
    corr_rows = (
        lax.psum_scatter(
            lax.dot_general(
                picked, cols_b, (((0,), (0,)), ((), ())), preferred_element_type=jnp.float32
            ),
            "dp",
            scatter_dimension=0,
            tiled=True,
        )
        / batch_images
    )
    row_ids = half * row_halves + lax.axis_index("dp") * owned + jnp.arange(owned, dtype=jnp.int32)
    diagonal = row_ids[:, None] == col_ids[None, :]
    part_loss = jnp.sum(
        jnp.where(diagonal, (1.0 - corr_rows) ** 2, off_weight * corr_rows * corr_rows)
    )
    loss = lax.psum(part_loss, ("dp", "tile")) / feats
    dcorr_part = jnp.where(diagonal, corr_rows - 1.0, off_weight * corr_rows).astype(jnp.bfloat16)
    piece = lax.all_gather(dcorr_part, "dp", axis=0, tiled=True)
    block_a = lax.dot_general(
        cols_b, piece, (((1,), (1,)), ((), ())), preferred_element_type=jnp.float32
    )
    picked = half_a
    into_b = jnp.dot(picked, piece, preferred_element_type=jnp.float32)
    other_a = swapped(block_a.astype(jnp.bfloat16), "tile", 0).astype(block_a.dtype)
    other_b = swapped(into_b.astype(jnp.bfloat16), "tile", 1).astype(into_b.dtype)
    normed_grad_left = lax.dynamic_slice_in_dim(block_a + other_a, column_halves * quart, quart, 1)
    normed_grad_right = lax.dynamic_slice_in_dim(into_b + other_b, row_halves * quart, quart, 1)
    first_moment_left, second_moment_left, first_moment_right, second_moment_right = lax.psum(
        (
            jnp.sum(normed_grad_left, axis=0),
            jnp.sum(normed_grad_left * standardized_left, axis=0),
            jnp.sum(normed_grad_right, axis=0),
            jnp.sum(normed_grad_right * standardized_right, axis=0),
        ),
        "dp",
    )
    left_gradient = (
        left_inverse_deviation
        * (
            normed_grad_left
            - first_moment_left / batch_images
            - standardized_left * (second_moment_left / batch_images)
        )
    ).astype(jnp.bfloat16)
    right_gradient = (
        right_inverse_deviation
        * (
            normed_grad_right
            - first_moment_right / batch_images
            - standardized_right * (second_moment_right / batch_images)
        )
    ).astype(jnp.bfloat16)
    return (left_gradient, right_gradient, corr_rows[None, :, :], jnp.reshape(loss, (1,)))


def fold_rows(values):
    rows, width = values.shape
    return jnp.sum(values.reshape(rows // 8, 8, width), axis=0)


def fold_lanes(values):
    return sum(values[:, at : at + 128] for at in range(0, values.shape[1], 128))


def column_mean(block):
    rows, width = block.shape
    folded = jnp.zeros((8, width), jnp.float32)
    for at in range(0, rows, 64):
        folded = folded + fold_rows(block[at : at + 64, :].astype(jnp.float32))
    return jnp.sum(folded, axis=0, keepdims=True) / rows


def add_sums(sums, centred, low):
    return [
        sums[0] + fold_rows(centred),
        sums[1] + fold_rows(centred * centred),
        sums[2] + fold_rows(low.astype(jnp.float32)),
    ]


def rows_of(values):
    pad = jnp.zeros((8 - len(values), values[0].shape[1]), jnp.float32)
    return jnp.concatenate([*values, pad], axis=0)


def joined_sums(row, sums):
    return [row[i + 1 : i + 2, :] + jnp.sum(s, axis=0, keepdims=True) for i, s in enumerate(sums)]


def moments(sums, images):
    total, squares, rounded = sums
    delta = total / images
    return delta, lax.rsqrt(squares / images - delta * delta + 1e-05), rounded / images - delta


def three_parts(row):
    high = row.astype(jnp.bfloat16)
    rest = row - high.astype(jnp.float32)
    middle = rest.astype(jnp.bfloat16)
    low = (rest - middle.astype(jnp.float32)).astype(jnp.bfloat16)
    return [high, middle, low]


def split_rows(values):
    parts = sum([three_parts(v) for v in values], [])
    pad = jnp.zeros((4, values[0].shape[1]), jnp.float32)
    return jnp.concatenate([*(p.astype(jnp.float32) for p in parts), pad], axis=0).astype(
        jnp.bfloat16
    )


def joined_rows(ref, at):
    parts = ref[at : at + 16, :].astype(jnp.float32)
    part = lambda i: parts[i : i + 1]
    return [part(3 * i) + part(3 * i + 1) + part(3 * i + 2) for i in range(4)]


def lanes_to_row(partial):
    ones = jnp.ones((16, partial.shape[1]), jnp.bfloat16)
    high = partial.astype(jnp.bfloat16)
    low = (partial - high.astype(jnp.float32)).astype(jnp.bfloat16)
    row = dot_rows(ones, high) + dot_rows(ones, low)
    return row[:1, :]


def dot_rows(left, right):
    return lax.dot_general(
        left, right, (((1,), (1,)), ((), ())), preferred_element_type=jnp.float32
    )


def dot(left, right):
    return jnp.dot(left, right, preferred_element_type=jnp.float32)


def pick(mask, outer, inner, piece):
    return jnp.where(
        mask[0:1, :] != 0.0, outer[piece, :].astype(jnp.float32), inner[piece, :].astype(jnp.float32)
    )


def pick_kernel(mask, outer, inner, out):
    for at in range(0, outer.shape[0], 64):
        piece = slice(at, at + 64)
        out[piece, :] = pick(mask, outer, inner, piece).astype(out.dtype)


def right_sums_kernel(first, second, third, row):
    rows, quart = first.shape
    shift = column_mean(first)
    sums = [jnp.zeros((8, quart), jnp.float32)] * 3
    for block in (first, second, third):
        for at in range(0, rows, 64):
            centred = block[at : at + 64, :].astype(jnp.float32) - shift
            sums = add_sums(sums, centred, centred.astype(jnp.bfloat16))
    row[...] = rows_of([shift] + [jnp.sum(s, axis=0, keepdims=True) for s in sums])


def halves_kernel(block, first, second):
    half = first.shape[0]
    first[...] = block[:half, :]
    second[...] = block[half:, :]


def late_left_kernel(images, mask, outer, inner, row, out):
    rows, quart = outer.shape
    shift = row[0:1, :]
    sums = [jnp.zeros((8, quart), jnp.float32)] * 3
    for at in range(0, rows, 128):
        piece = slice(at, at + 128)
        centred = pick(mask, outer, inner, piece) - shift
        low = centred.astype(jnp.bfloat16)
        out[piece, :] = low
        sums = add_sums(sums, centred, low)
    delta, rstd, gap = moments(joined_sums(row, sums), images)
    out[rows:, :] = split_rows([shift + delta, rstd, gap, delta])


def late_right_kernel(images, last, mask, outer, inner, row, out, *rest):
    some, quart = outer.shape
    shift = row[0:1, :]
    sums = [jnp.zeros((8, quart), jnp.float32)] * 3
    for at in range(0, some, 128):
        piece = slice(at, at + 128)
        centred = pick(mask, outer, inner, piece) - shift
        low = centred.astype(jnp.bfloat16)
        out[:quart, piece] = jnp.transpose(low)
        sums = add_sums(sums, centred, low)
    sums = joined_sums(row, sums)
    if not last:
        (row_out,) = rest
        row_out[...] = rows_of([shift, *sums])
        return
    delta, rstd, gap = moments(sums, images)
    parts = split_rows([shift + delta, rstd, gap, delta])
    for i in range(quart // some):
        below = quart + 16 * i
        out[below : below + 16, :] = parts[:, i * some : (i + 1) * some]


def right_stats(late):
    quart, some = late[0].shape
    found = [joined_rows(late[1], quart + 16 * i) for i in range(quart // some)]
    return [jnp.concatenate(values, axis=1) for values in zip(*found)]


def late_products(right, left, lanes):
    quart, some = right[0].shape
    first = dot(right[0][...], left[:some, lanes])
    return first + dot(right[1][:quart, :], left[some : 2 * some, lanes])


def products_kernel(*refs):
    lefts, rights = refs[0:6], refs[6:12]
    partner_own, partner_other, own_all, row_other, zero_own, zero_other = refs[12:18]
    low_left, low_right = refs[18:]
    rows, quart = lefts[0].shape
    width = quart // 2
    for half in range(2):
        lanes = slice(half * quart, (half + 1) * quart)
        shift = column_mean(lefts[half])
        sums = [jnp.zeros((8, quart), jnp.float32)] * 3
        for block in range(3):
            source = lefts[2 * block + half]
            for at in range(0, rows, 64):
                centred = source[at : at + 64, :].astype(jnp.float32) - shift
                low = centred.astype(jnp.bfloat16)
                low_left[block * rows + at : block * rows + at + 64, lanes] = low
                if block == 0:
                    (zero_own, zero_other)[half][at : at + 64, :] = low
                if half:
                    sums = add_sums(sums, centred, low)
        if half:
            row_other[...] = rows_of([shift] + [jnp.sum(s, axis=0, keepdims=True) for s in sums])
    for half in range(2):
        lanes = slice(half * quart, (half + 1) * quart)
        shift = column_mean(rights[half])
        for block in range(3):
            source = rights[2 * block + half]
            for at in range(0, rows, 128):
                low = (source[at : at + 128, :].astype(jnp.float32) - shift).astype(jnp.bfloat16)
                low_right[lanes, block * rows + at : block * rows + at + 128] = jnp.transpose(low)
    for tile in range(4):
        wide = slice(tile * width, (tile + 1) * width)
        inner = slice((tile % 2) * width, (tile % 2 + 1) * width)
        target = partner_own if tile < 2 else partner_other
        target[:, inner] = dot(low_right[quart:, :], low_left[:, wide])
        own_all[:, wide] = dot(low_right[:quart, :], low_left[:, wide])


def left_operand(zero, late, target, lanes):
    rows, quart = zero.shape
    _, _, gap, delta = joined_rows(late, rows)
    high, middle, _ = three_parts(delta)
    target[:rows, lanes] = zero[...]
    extra = [high.astype(jnp.float32), middle.astype(jnp.float32), gap]
    pad = jnp.zeros((13, quart), jnp.float32)
    target[rows:, lanes] = jnp.concatenate([*extra, pad], axis=0).astype(jnp.bfloat16)


def without_extra(terms, rows):
    return terms[:rows] - (terms[rows : rows + 1] + terms[rows + 1 : rows + 2] + terms[rows + 2 : rows + 3])


def scale_columns(late_b, images):
    _, rstd, _, delta = right_stats(late_b)
    columns = jnp.transpose(rows_of([rstd / images, delta * rstd]))
    return columns[:, 0:1], columns[:, 1:2]


def partner_kernel(images, part, late, zero, sums, late_b_0, late_b_1, *refs):
    if part:
        (terms_in, across_in, vec_in, columns) = refs[:4]
        (partial_out, second_out, e_out, vec_out, left) = refs[4:]
    else:
        (terms_out, across_out, e_out, vec_out, columns, left) = refs
        _, rstd_b, _, delta_b = right_stats((late_b_0, late_b_1))
        columns[...] = jnp.transpose(rows_of([rstd_b / images, delta_b * rstd_b]))
    late_b = (late_b_0, late_b_1)
    rows, quart = zero.shape
    width = quart // 2
    _, rstd, _, delta = joined_rows(late, rows)
    left_operand(zero, late, left, slice(0, quart))
    scale_col, delta_col = columns[:, 0:1], columns[:, 1:2]
    across = across_in[...] if part else jnp.zeros((quart, 128), jnp.float32)
    down = []
    for tile in range(2):
        at = slice(tile * width, (tile + 1) * width)
        total = sums[:, at] + late_products(late_b, late, at)
        corr = (total * scale_col - delta_col * delta[:, at]) * rstd[:, at]
        e_out[:, at] = (corr * (off_weight * rstd[:, at])).astype(jnp.bfloat16)
        square = corr * corr
        across = across + fold_lanes(square)
        down.append(jnp.sum(square, axis=0, keepdims=True))
    second_a = off_weight * jnp.concatenate(down, axis=1)
    if part:
        vec_out[...] = rows_of([second_a, second_a + vec_in[0:1, :]])
        second_out[...] = rows_of([off_weight * lanes_to_row(across)])
    else:
        vec_out[...] = rows_of([second_a])
        across_out[...] = across
    for tile in range(2):
        at = slice(tile * width, (tile + 1) * width)
        terms = dot_rows(left[...], e_out[at, :])
        if part:
            partial_out[:, at] = without_extra(terms + terms_in[:, at], rows).astype(
                jnp.bfloat16
            )
        else:
            terms_out[:, at] = terms


def own_kernel(images, flags, *refs):
    late_b, late_b_other, refs = refs[:2], refs[2:4], refs[4:]
    (late_own, late_other, first_own, first_other, zero_own, zero_other, sums) = refs[:7]
    (first_b, first_b_other, e_left, e_right, partner_own, partner_other) = refs[7:13]
    (vec_own, vec_other, vec_core, right_out, left_out, *left_partials_out, mine_out) = refs[13:21]
    (own_loss_out, loss_out, left, norm_b, e_own, mine_own, mine_partner) = refs[21:]
    rows, quart = zero_own.shape
    width = quart // 2
    lower, upper = slice(0, quart), slice(quart, 2 * quart)
    stats_own, stats_other = joined_rows(late_own, rows), joined_rows(late_other, rows)
    both = lambda i: jnp.concatenate([stats_own[i], stats_other[i]], axis=1)
    offset, rstd, _, delta = [both(i) for i in range(4)]
    left_operand(zero_own, late_own, left, lower)
    left_operand(zero_other, late_other, left, upper)
    own_b = right_stats(late_b)
    other_b = right_stats(late_b_other)
    for source, stats, lanes in ((first_b, own_b, lower), (first_b_other, other_b, upper)):
        for at in range(0, rows, 64):
            piece = slice(at, at + 64)
            norm_b[piece, lanes] = (
                (source[piece, :].astype(jnp.float32) - stats[0]) * stats[1]
            ).astype(jnp.bfloat16)
        rest = jnp.broadcast_to(stats[2] * stats[1], (16, quart))
        norm_b[rows:, lanes] = rest.astype(jnp.bfloat16)

    def tile_corr(late, inner, total, columns, block):
        scale_col, delta_col = columns
        total = total + late_products(block, late, inner)
        row = joined_rows(late, rows)
        return (total * scale_col - delta_col * row[3][:, inner]) * row[1][:, inner]

    columns = scale_columns(late_b, images)
    columns_partner = scale_columns(late_b_other, images)
    across = jnp.zeros((quart, 128), jnp.float32)
    losses = jnp.zeros((8, 128), jnp.float32)
    down, diagonals = [], []
    for tile in range(4):
        at = slice(tile * width, (tile + 1) * width)
        inner = slice((tile % 2) * width, (tile % 2 + 1) * width)
        late = late_own if tile < 2 else late_other
        corr = tile_corr(late, inner, sums[:, at], columns, late_b)
        dcorr = off_weight * corr
        product = dcorr * corr
        loss = product
        if tile < 2:
            feature = lax.broadcasted_iota(jnp.int32, (quart, width), 0)
            lane = lax.broadcasted_iota(jnp.int32, (quart, width), 1) + tile * width
            diagonal = feature == lane
            slope = jnp.where(diagonal, (corr - 1.0).astype(jnp.bfloat16).astype(jnp.float32), 0.0)
            diagonals.append(jnp.sum(slope, axis=0, keepdims=True))
            dcorr = jnp.where(diagonal, 0.0, dcorr)
            product = jnp.where(diagonal, slope * corr, product)
            loss = jnp.where(diagonal, (1.0 - corr) * (1.0 - corr), loss)
        e_own[:, at] = (dcorr * rstd[:, at]).astype(jnp.bfloat16)
        across = across + fold_lanes(product)
        losses = losses + fold_rows(fold_lanes(loss))
        down.append(jnp.sum(product, axis=0, keepdims=True))

        @pl.when(flags[0] == tile)
        def _():
            mine_own[...] = corr
            partner = partner_own if tile < 2 else partner_other
            mine_partner[...] = tile_corr(
                late, inner, partner[:, inner], columns_partner, late_b_other
            )

    diagonal_row = jnp.concatenate(diagonals, axis=1)
    partner_second = jnp.concatenate([vec_own[0:1, :], vec_other[0:1, :]], axis=1)
    second_a = rstd * (partner_second + jnp.concatenate(down, axis=1))
    second_b = lanes_to_row(across)
    own_loss = jnp.sum(losses)
    own_loss_out[...] = jnp.broadcast_to(own_loss, (8, 128))
    loss = own_loss + jnp.sum(vec_other[1:2, :] + vec_core[1:2, :])
    loss_out[...] = jnp.broadcast_to(loss, (8, 128))

    for tile in (2, 3, 0, 1):
        at = slice(tile * width, (tile + 1) * width)
        inner = slice((tile % 2) * width, (tile % 2 + 1) * width)
        source, e_partner = (first_own, e_left) if tile < 2 else (first_other, e_right)
        terms = dot(norm_b[:, lower], e_own[:, at]) + dot(norm_b[:, upper], e_partner[:, inner])
        xhat = (source[:, inner].astype(jnp.float32) - offset[:, at]) * rstd[:, at]
        value = terms[:rows] - terms[rows : rows + 1] - xhat * second_a[:, at]
        if tile < 2:
            slope = rstd[:, at] * diagonal_row[:, inner]
            left_out[:, inner] = value + norm_b[:rows, inner].astype(jnp.float32) * slope
        else:
            for half, out in enumerate(left_partials_out):
                some = out.shape[0]
                out[:, inner] = value[half * some : (half + 1) * some].astype(jnp.bfloat16)

    for tile in range(2):
        at = slice(tile * width, (tile + 1) * width)
        terms = dot_rows(left[...], e_own[at, :])
        xhat = (first_b[:, at].astype(jnp.float32) - own_b[0][:, at]) * own_b[1][:, at]
        norm_a = (first_own[:, at].astype(jnp.float32) - offset[:, at]) * rstd[:, at]
        norm_a = norm_a.astype(jnp.bfloat16).astype(jnp.float32)
        right_out[:, at] = (
            without_extra(terms, rows) - xhat * second_b[:, at] + norm_a * diagonal_row[:, at]
        )

    own_columns = jnp.transpose(mine_own[...])
    partner_columns = jnp.transpose(mine_partner[...])

    @pl.when(flags[1] == 0)
    def _():
        mine_out[:, lower] = own_columns
        mine_out[:, upper] = partner_columns

    @pl.when(flags[1] != 0)
    def _():
        mine_out[:, lower] = partner_columns
        mine_out[:, upper] = own_columns


def for_partner_kernel(loss, core_loss, second, out):
    total = loss[0:1, 0:1] + core_loss[0:1, 0:1]
    out[...] = rows_of([jnp.broadcast_to(total, (1, out.shape[1])), second[0:1, :]])


def left_final_kernel(left, from_core_0, from_core_1, left_out):
    some = from_core_0.shape[0]
    for half, from_core in enumerate((from_core_0, from_core_1)):
        for at in range(0, some, 64):
            piece = slice(half * some + at, half * some + at + 64)
            value = left[piece, :] + from_core[at : at + 64, :].astype(jnp.float32)
            left_out[piece, :] = value.astype(jnp.bfloat16)


def right_final_kernel(feats, right, from_x, late_b_0, late_b_1, first_b, sent, got, right_out, loss_out):
    rows = right.shape[0]
    offset, rstd, _, _ = right_stats((late_b_0, late_b_1))
    second = got[1:2, :]
    loss_out[0] = (sent[0, 0] + got[0, 0]) / feats
    for at in range(0, rows, 64):
        piece = slice(at, at + 64)
        xhat = (first_b[piece, :].astype(jnp.float32) - offset) * rstd
        value = right[piece, :] + from_x[piece, :].astype(jnp.float32) - xhat * second
        right_out[piece, :] = (rstd * value).astype(jnp.bfloat16)


vmem = pl.BlockSpec(memory_space=pltpu.VMEM)
smem = pl.BlockSpec(memory_space=pltpu.SMEM)


def local_call(kernel, operands, outs, scratch=(), flops=2**20, room=8, held=(), moved=None):
    if moved is None:
        moved = sum(x.size * x.dtype.itemsize for x in (*operands, *outs))

    def space(x):
        return smem if x.ndim == 1 else vmem

    return pl.pallas_call(
        kernel,
        out_shape=list(outs),
        in_specs=[space(x) for x in operands],
        out_specs=[space(x) for x in outs],
        scratch_shapes=list(scratch),
        compiler_params=pltpu.CompilerParams(vmem_limit_bytes=room * 2**20),
        cost_estimate=pl.CostEstimate(flops=flops, bytes_accessed=moved, transcendentals=0),
    )(*(pltpu.with_memory_space_constraint(x, pltpu.VMEM) if i in held else x for i, x in enumerate(operands)))


def gathered_device(left_outputs, right_outputs):
    rows, quart = left_outputs.shape
    half = 2 * quart
    feats = 4 * quart
    batch_images = rows * 4
    tpos = lax.axis_index("tile")
    dpos = lax.axis_index("dp")
    row_halves = tpos // 2
    column_halves = tpos % 2
    at_end = (dpos == 0) | (dpos == 3)
    owned_tile = jnp.where(dpos // 2 == column_halves, 0, 2) + dpos % 2
    flags = jnp.stack([owned_tile, row_halves]).astype(jnp.int32)
    mask = jnp.broadcast_to(at_end.astype(jnp.float32), (8, quart))

    pairs = [(0, 1), (1, 0), (2, 3), (3, 2)]
    middle = [(1, 2), (2, 1)]
    outward = [(1, 0), (2, 3)]

    def along(block, route):
        return lax.ppermute(block, "dp", route)

    def core_swap(block):
        return swapped(block, "tile", 0)

    def x_swap(block):
        return swapped(block, "tile", 1)

    def after(value, *others):
        return lax.optimization_barrier((value, *others))

    gemm = 2 * rows * quart * quart
    width = quart // 2
    quarter_f32 = jax.ShapeDtypeStruct((rows, quart), jnp.float32)
    quarter_bf16 = jax.ShapeDtypeStruct((rows, quart), jnp.bfloat16)
    extended = jax.ShapeDtypeStruct((rows + 16, quart), jnp.bfloat16)
    row_out = jax.ShapeDtypeStruct((8, quart), jnp.float32)
    one_out = jax.ShapeDtypeStruct((8, 128), jnp.float32)
    across_shape = jax.ShapeDtypeStruct((quart, 128), jnp.float32)
    low = lambda n, m: pltpu.VMEM((n, m), jnp.bfloat16)

    def picked(outer, inner):
        return local_call(pick_kernel, (mask, outer, inner), (quarter_bf16,))[0]

    some = rows // 2
    half_block = jax.ShapeDtypeStruct((some, quart), jnp.bfloat16)
    first_b = along(right_outputs, pairs)
    inner_b = along(right_outputs, middle)
    first_a = along(left_outputs, pairs)
    other_b0 = x_swap(right_outputs)
    other_a0, mask, flags = after(core_swap(left_outputs), mask, flags)
    left_behind, first_a, other_a0 = after(left_outputs, first_a, other_a0)
    inner_a = along(left_behind, middle)

    outer_b = along(inner_b, outward)
    third_b = along(first_b, middle)
    ready_b, other_b0 = after(first_b, other_b0)
    other_b1 = x_swap(ready_b)
    outer_a = along(inner_a, outward)
    third_a = along(first_a, middle)
    other_a1 = core_swap(first_a)

    third_b = local_call(halves_kernel, (third_b,), (half_block, half_block))
    last_b = [along(x, outward) for x in third_b]
    second_b = picked(outer_b, inner_b)
    row_b = local_call(right_sums_kernel, (right_outputs, first_b, second_b), (row_out,))[0]
    second_b, other_b1, other_a1 = after(second_b, other_b1, other_a1)
    other_b2 = x_swap(second_b)
    last_a = along(third_a, outward)
    second_a = picked(outer_a, inner_a)
    second_a, row_b = after(second_a, row_b)
    other_a2 = core_swap(second_a)

    late_b_0, row_b = local_call(
        functools.partial(late_right_kernel, batch_images, False),
        (mask, last_b[0], third_b[0], row_b),
        (jax.ShapeDtypeStruct((quart, some), jnp.bfloat16), row_out),
        held=(0, 1, 2, 3),
    )
    late_b_other_0 = x_swap(late_b_0)
    (late_b_1,) = local_call(
        functools.partial(late_right_kernel, batch_images, True),
        (mask, last_b[1], third_b[1], row_b),
        (jax.ShapeDtypeStruct((quart + 16 * (quart // some), some), jnp.bfloat16),),
        held=(0, 1, 2, 3),
    )
    late_b_other_1 = x_swap(late_b_1)
    late_b = (late_b_0, late_b_1)
    other_b2, late_b_1, late_b_other_0 = after(other_b2, late_b_1, late_b_other_0)
    partner_own, partner_other, own_all, row_other, zero_own, zero_other = local_call(
        products_kernel,
        (left_outputs, other_a0, first_a, other_a1, second_a, other_a2)
        + (right_outputs, other_b0, first_b, other_b1, second_b, other_b2),
        (
            quarter_f32,
            quarter_f32,
            jax.ShapeDtypeStruct((quart, half), jnp.float32),
            row_out,
            quarter_bf16,
            quarter_bf16,
        ),
        [low(3 * rows, half), low(half, 3 * rows)],
        room=20,
        moved=2**16,
    )
    row_a, late_b_other_1 = after(core_swap(row_other), late_b_other_1)
    late_b_other = (late_b_other_0, late_b_other_1)
    (late_a,) = local_call(
        functools.partial(late_left_kernel, batch_images),
        (mask, last_a, third_a, row_a),
        (extended,),
        held=(0, 1, 2, 3),
    )
    late_a_other = core_swap(late_a)

    terms, across, e_left, vec_own, columns = local_call(
        functools.partial(partner_kernel, batch_images, 0),
        (late_a, zero_own, partner_own, *late_b_other),
        (
            jax.ShapeDtypeStruct((rows + 16, quart), jnp.float32),
            across_shape,
            quarter_bf16,
            row_out,
            jax.ShapeDtypeStruct((quart, 8), jnp.float32),
        ),
        [low(rows + 16, quart)],
        2 * gemm,
        room=12,
    )
    partial_right, second, e_right, vec_other = local_call(
        functools.partial(partner_kernel, batch_images, 1),
        (late_a_other, zero_other, partner_other, *late_b_other, terms, across, vec_own, columns),
        (quarter_bf16, row_out, quarter_bf16, row_out),
        [low(rows + 16, quart)],
        2 * gemm,
        room=12,
    )
    from_x = x_swap(partial_right)
    vec_core = core_swap(vec_other)
    right_own, left_own, *partials_left, mine, own_loss, loss = local_call(
        functools.partial(own_kernel, batch_images),
        (flags, *late_b, *late_b_other)
        + (late_a, late_a_other, left_outputs, other_a0, zero_own, zero_other, own_all)
        + (right_outputs, other_b0, e_left, e_right)
        + (partner_own, partner_other)
        + (vec_own, vec_other, vec_core),
        (
            quarter_f32,
            quarter_f32,
            half_block,
            half_block,
            jax.ShapeDtypeStruct((width, half), jnp.float32),
            one_out,
            one_out,
        ),
        [
            low(rows + 16, half),
            low(rows + 16, half),
            low(quart, half),
            pltpu.VMEM((quart, width), jnp.float32),
            pltpu.VMEM((quart, width), jnp.float32),
        ],
        8 * gemm,
        room=20,
    )
    from_core = [core_swap(x) for x in partials_left]
    core_loss = core_swap(own_loss)
    (for_partner,) = local_call(for_partner_kernel, (loss, core_loss, second), (row_out,))
    from_partner = x_swap(for_partner)
    (left_gradient,) = local_call(left_final_kernel, (left_own, *from_core), (quarter_bf16,))
    right_own, left_gradient = after(right_own, left_gradient)
    right_gradient, loss = local_call(
        functools.partial(right_final_kernel, feats),
        (right_own, from_x, *late_b, right_outputs, for_partner, from_partner),
        (quarter_bf16, jax.ShapeDtypeStruct((1,), jnp.float32)),
    )
    return (left_gradient, right_gradient, mine[None, :, :], loss)


def solution(mesh):
    per_device = gathered_device if mesh.shape["dp"] == 4 else reduced_device
    return jax.shard_map(
        per_device,
        mesh=mesh,
        in_specs=(P(("groups", "dp"), "tile"), P(("groups", "dp"), "tile")),
        out_specs=(
            P(("groups", "dp"), "tile"),
            P(("groups", "dp"), "tile"),
            P(("groups", "tile"), "dp", None),
            P("groups"),
        ),
        check_vma=False,
    )
```

```python
import functools
import jax
import jax.numpy as jnp
from jax import lax
from jax.experimental import pallas as pl
from jax.experimental.pallas import tpu as pltpu
from jax.sharding import PartitionSpec as P

off_weight = 0.0051


def swapped(block, axis, bit):
    count = lax.axis_size(axis)
    route = []
    for low in range(count):
        high = low | 1 << bit
        if high != low and high < count:
            route += [(low, high), (high, low)]
    return lax.ppermute(block, axis, route)


def pair_views(first_moment, second_moment, row_halves, column_halves):
    other_a = swapped(first_moment, "tile", 0)
    other_b = swapped(second_moment, "tile", 1)
    joined_a = jnp.where(
        column_halves == 0,
        jnp.concatenate([first_moment, other_a], axis=1),
        jnp.concatenate([other_a, first_moment], axis=1),
    )
    joined_b = jnp.where(
        row_halves == 0,
        jnp.concatenate([second_moment, other_b], axis=1),
        jnp.concatenate([other_b, second_moment], axis=1),
    )
    return (joined_a, joined_b)


def moment_pair(total, squares, batch_images):
    column_mean = total / batch_images
    var = squares / batch_images - column_mean * column_mean
    return (column_mean, lax.rsqrt(var + 1e-05))


def col_sums(values):
    as_float = values.astype(jnp.float32)
    return (jnp.sum(as_float, axis=0), jnp.sum(as_float * as_float, axis=0))


def reduced_device(left_outputs, right_outputs):
    rows, quart = left_outputs.shape
    half = 2 * quart
    feats = 4 * quart
    dp_count = lax.axis_size("dp")
    batch_images = rows * dp_count
    tpos = lax.axis_index("tile")
    row_halves = tpos // 2
    column_halves = tpos % 2
    sum_a, sq_a = col_sums(left_outputs)
    sum_b, sq_b = col_sums(right_outputs)
    sum_a, sq_a, sum_b, sq_b = lax.psum((sum_a, sq_a, sum_b, sq_b), "dp")
    left_mean, left_inverse_deviation = moment_pair(sum_a, sq_a, batch_images)
    right_mean, right_inverse_deviation = moment_pair(sum_b, sq_b, batch_images)
    standardized_left = (left_outputs.astype(jnp.float32) - left_mean) * left_inverse_deviation
    standardized_right = (right_outputs.astype(jnp.float32) - right_mean) * right_inverse_deviation
    half_a, cols_b = pair_views(
        standardized_left.astype(jnp.bfloat16),
        standardized_right.astype(jnp.bfloat16),
        row_halves,
        column_halves,
    )
    col_local = jnp.arange(half, dtype=jnp.int32)
    col_ids = quart * column_halves + col_local + jnp.where(col_local >= quart, quart, 0)
    owned = half // dp_count
    picked = half_a
    corr_rows = (
        lax.psum_scatter(
            lax.dot_general(
                picked, cols_b, (((0,), (0,)), ((), ())), preferred_element_type=jnp.float32
            ),
            "dp",
            scatter_dimension=0,
            tiled=True,
        )
        / batch_images
    )
    row_ids = half * row_halves + lax.axis_index("dp") * owned + jnp.arange(owned, dtype=jnp.int32)
    diagonal = row_ids[:, None] == col_ids[None, :]
    part_loss = jnp.sum(
        jnp.where(diagonal, (1.0 - corr_rows) ** 2, off_weight * corr_rows * corr_rows)
    )
    loss = lax.psum(part_loss, ("dp", "tile")) / feats
    dcorr_part = jnp.where(diagonal, corr_rows - 1.0, off_weight * corr_rows).astype(jnp.bfloat16)
    piece = lax.all_gather(dcorr_part, "dp", axis=0, tiled=True)
    block_a = lax.dot_general(
        cols_b, piece, (((1,), (1,)), ((), ())), preferred_element_type=jnp.float32
    )
    picked = half_a
    into_b = jnp.dot(picked, piece, preferred_element_type=jnp.float32)
    other_a = swapped(block_a.astype(jnp.bfloat16), "tile", 0).astype(block_a.dtype)
    other_b = swapped(into_b.astype(jnp.bfloat16), "tile", 1).astype(into_b.dtype)
    normed_grad_left = lax.dynamic_slice_in_dim(block_a + other_a, column_halves * quart, quart, 1)
    normed_grad_right = lax.dynamic_slice_in_dim(into_b + other_b, row_halves * quart, quart, 1)
    first_moment_left, second_moment_left, first_moment_right, second_moment_right = lax.psum(
        (
            jnp.sum(normed_grad_left, axis=0),
            jnp.sum(normed_grad_left * standardized_left, axis=0),
            jnp.sum(normed_grad_right, axis=0),
            jnp.sum(normed_grad_right * standardized_right, axis=0),
        ),
        "dp",
    )
    left_gradient = (
        left_inverse_deviation
        * (
            normed_grad_left
            - first_moment_left / batch_images
            - standardized_left * (second_moment_left / batch_images)
        )
    ).astype(jnp.bfloat16)
    right_gradient = (
        right_inverse_deviation
        * (
            normed_grad_right
            - first_moment_right / batch_images
            - standardized_right * (second_moment_right / batch_images)
        )
    ).astype(jnp.bfloat16)
    return (left_gradient, right_gradient, corr_rows[None, :, :], jnp.reshape(loss, (1,)))


def fold_rows(values):
    rows, width = values.shape
    return jnp.sum(values.reshape(rows // 8, 8, width), axis=0)


def fold_lanes(values):
    return sum(values[:, at : at + 128] for at in range(0, values.shape[1], 128))


def column_mean(block):
    rows, width = block.shape
    folded = jnp.zeros((8, width), jnp.float32)
    for at in range(0, rows, 64):
        folded = folded + fold_rows(block[at : at + 64, :].astype(jnp.float32))
    return jnp.sum(folded, axis=0, keepdims=True) / rows


def add_sums(sums, centred, low):
    return [
        sums[0] + fold_rows(centred),
        sums[1] + fold_rows(centred * centred),
        sums[2] + fold_rows(low.astype(jnp.float32)),
    ]


def rows_of(values):
    pad = jnp.zeros((8 - len(values), values[0].shape[1]), jnp.float32)
    return jnp.concatenate([*values, pad], axis=0)


def joined_sums(row, sums):
    return [row[i + 1 : i + 2, :] + jnp.sum(s, axis=0, keepdims=True) for i, s in enumerate(sums)]


def moments(sums, images):
    total, squares, rounded = sums
    delta = total / images
    return delta, lax.rsqrt(squares / images - delta * delta + 1e-05), rounded / images - delta


def three_parts(row):
    high = row.astype(jnp.bfloat16)
    rest = row - high.astype(jnp.float32)
    middle = rest.astype(jnp.bfloat16)
    low = (rest - middle.astype(jnp.float32)).astype(jnp.bfloat16)
    return [high, middle, low]


def split_rows(values):
    parts = sum([three_parts(v) for v in values], [])
    pad = jnp.zeros((4, values[0].shape[1]), jnp.float32)
    return jnp.concatenate([*(p.astype(jnp.float32) for p in parts), pad], axis=0).astype(
        jnp.bfloat16
    )


def joined_rows(ref, at):
    parts = ref[at : at + 16, :].astype(jnp.float32)
    part = lambda i: parts[i : i + 1]
    return [part(3 * i) + part(3 * i + 1) + part(3 * i + 2) for i in range(4)]


def lanes_to_row(partial):
    ones = jnp.ones((16, partial.shape[1]), jnp.bfloat16)
    high = partial.astype(jnp.bfloat16)
    low = (partial - high.astype(jnp.float32)).astype(jnp.bfloat16)
    row = dot_rows(ones, high) + dot_rows(ones, low)
    return row[:1, :]


def dot_rows(left, right):
    return lax.dot_general(
        left, right, (((1,), (1,)), ((), ())), preferred_element_type=jnp.float32
    )


def dot(left, right):
    return jnp.dot(left, right, preferred_element_type=jnp.float32)


def pick(mask, outer, inner, piece):
    return jnp.where(
        mask[0:1, :] != 0.0, outer[piece, :].astype(jnp.float32), inner[piece, :].astype(jnp.float32)
    )


def pick_kernel(mask, outer, inner, out):
    for at in range(0, outer.shape[0], 64):
        piece = slice(at, at + 64)
        out[piece, :] = pick(mask, outer, inner, piece).astype(out.dtype)


def right_sums_kernel(first, second, third, row):
    rows, quart = first.shape
    shift = column_mean(first)
    sums = [jnp.zeros((8, quart), jnp.float32)] * 3
    for block in (first, second, third):
        for at in range(0, rows, 64):
            centred = block[at : at + 64, :].astype(jnp.float32) - shift
            sums = add_sums(sums, centred, centred.astype(jnp.bfloat16))
    row[...] = rows_of([shift] + [jnp.sum(s, axis=0, keepdims=True) for s in sums])


def halves_kernel(block, first, second):
    half = first.shape[0]
    first[...] = block[:half, :]
    second[...] = block[half:, :]


def late_left_kernel(images, mask, outer, inner, row, out):
    rows, quart = outer.shape
    shift = row[0:1, :]
    sums = [jnp.zeros((8, quart), jnp.float32)] * 3
    for at in range(0, rows, 128):
        piece = slice(at, at + 128)
        centred = pick(mask, outer, inner, piece) - shift
        low = centred.astype(jnp.bfloat16)
        out[piece, :] = low
        sums = add_sums(sums, centred, low)
    delta, rstd, gap = moments(joined_sums(row, sums), images)
    out[rows:, :] = split_rows([shift + delta, rstd, gap, delta])


def late_right_kernel(images, last, mask, outer, inner, row, out, *rest):
    some, quart = outer.shape
    shift = row[0:1, :]
    sums = [jnp.zeros((8, quart), jnp.float32)] * 3
    for at in range(0, some, 128):
        piece = slice(at, at + 128)
        centred = pick(mask, outer, inner, piece) - shift
        low = centred.astype(jnp.bfloat16)
        out[:quart, piece] = jnp.transpose(low)
        sums = add_sums(sums, centred, low)
    sums = joined_sums(row, sums)
    if not last:
        (row_out,) = rest
        row_out[...] = rows_of([shift, *sums])
        return
    delta, rstd, gap = moments(sums, images)
    parts = split_rows([shift + delta, rstd, gap, delta])
    for i in range(quart // some):
        below = quart + 16 * i
        out[below : below + 16, :] = parts[:, i * some : (i + 1) * some]


def right_stats(late):
    quart, some = late[0].shape
    found = [joined_rows(late[1], quart + 16 * i) for i in range(quart // some)]
    return [jnp.concatenate(values, axis=1) for values in zip(*found)]


def late_products(right, left, lanes):
    quart, some = right[0].shape
    first = dot(right[0][...], left[:some, lanes])
    return first + dot(right[1][:quart, :], left[some : 2 * some, lanes])


def products_kernel(*refs):
    lefts, rights = refs[0:6], refs[6:12]
    partner_own, partner_other, own_all, row_other, zero_own, zero_other = refs[12:18]
    low_left, low_right = refs[18:]
    rows, quart = lefts[0].shape
    width = quart // 2
    for half in range(2):
        lanes = slice(half * quart, (half + 1) * quart)
        shift = column_mean(lefts[half])
        sums = [jnp.zeros((8, quart), jnp.float32)] * 3
        for block in range(3):
            source = lefts[2 * block + half]
            for at in range(0, rows, 64):
                centred = source[at : at + 64, :].astype(jnp.float32) - shift
                low = centred.astype(jnp.bfloat16)
                low_left[block * rows + at : block * rows + at + 64, lanes] = low
                if block == 0:
                    (zero_own, zero_other)[half][at : at + 64, :] = low
                if half:
                    sums = add_sums(sums, centred, low)
        if half:
            row_other[...] = rows_of([shift] + [jnp.sum(s, axis=0, keepdims=True) for s in sums])
    for half in range(2):
        lanes = slice(half * quart, (half + 1) * quart)
        shift = column_mean(rights[half])
        for block in range(3):
            source = rights[2 * block + half]
            for at in range(0, rows, 128):
                low = (source[at : at + 128, :].astype(jnp.float32) - shift).astype(jnp.bfloat16)
                low_right[lanes, block * rows + at : block * rows + at + 128] = jnp.transpose(low)
    for tile in range(4):
        wide = slice(tile * width, (tile + 1) * width)
        inner = slice((tile % 2) * width, (tile % 2 + 1) * width)
        target = partner_own if tile < 2 else partner_other
        target[:, inner] = dot(low_right[quart:, :], low_left[:, wide])
        own_all[:, wide] = dot(low_right[:quart, :], low_left[:, wide])


def left_operand(zero, late, target, lanes):
    rows, quart = zero.shape
    _, _, gap, delta = joined_rows(late, rows)
    high, middle, _ = three_parts(delta)
    target[:rows, lanes] = zero[...]
    extra = [high.astype(jnp.float32), middle.astype(jnp.float32), gap]
    pad = jnp.zeros((13, quart), jnp.float32)
    target[rows:, lanes] = jnp.concatenate([*extra, pad], axis=0).astype(jnp.bfloat16)


def without_extra(terms, rows):
    return terms[:rows] - (terms[rows : rows + 1] + terms[rows + 1 : rows + 2] + terms[rows + 2 : rows + 3])


def scale_columns(late_b, images):
    _, rstd, _, delta = right_stats(late_b)
    columns = jnp.transpose(rows_of([rstd / images, delta * rstd]))
    return columns[:, 0:1], columns[:, 1:2]


def partner_kernel(images, part, late, zero, sums, late_b_0, late_b_1, *refs):
    if part:
        (terms_in, across_in, vec_in, columns) = refs[:4]
        (partial_out, second_out, e_out, vec_out, left) = refs[4:]
    else:
        (terms_out, across_out, e_out, vec_out, columns, left) = refs
        _, rstd_b, _, delta_b = right_stats((late_b_0, late_b_1))
        columns[...] = jnp.transpose(rows_of([rstd_b / images, delta_b * rstd_b]))
    late_b = (late_b_0, late_b_1)
    rows, quart = zero.shape
    width = quart // 2
    _, rstd, _, delta = joined_rows(late, rows)
    left_operand(zero, late, left, slice(0, quart))
    scale_col, delta_col = columns[:, 0:1], columns[:, 1:2]
    across = across_in[...] if part else jnp.zeros((quart, 128), jnp.float32)
    down = []
    for tile in range(2):
        at = slice(tile * width, (tile + 1) * width)
        total = sums[:, at] + late_products(late_b, late, at)
        corr = (total * scale_col - delta_col * delta[:, at]) * rstd[:, at]
        e_out[:, at] = (corr * (off_weight * rstd[:, at])).astype(jnp.bfloat16)
        square = corr * corr
        across = across + fold_lanes(square)
        down.append(jnp.sum(square, axis=0, keepdims=True))
    second_a = off_weight * jnp.concatenate(down, axis=1)
    if part:
        vec_out[...] = rows_of([second_a, second_a + vec_in[0:1, :]])
        second_out[...] = rows_of([off_weight * lanes_to_row(across)])
    else:
        vec_out[...] = rows_of([second_a])
        across_out[...] = across
    for tile in range(2):
        at = slice(tile * width, (tile + 1) * width)
        terms = dot_rows(left[...], e_out[at, :])
        if part:
            partial_out[:, at] = without_extra(terms + terms_in[:, at], rows).astype(
                jnp.bfloat16
            )
        else:
            terms_out[:, at] = terms


def own_kernel(images, flags, *refs):
    late_b, late_b_other, refs = refs[:2], refs[2:4], refs[4:]
    (late_own, late_other, first_own, first_other, zero_own, zero_other, sums) = refs[:7]
    (first_b, first_b_other, e_left, e_right, partner_own, partner_other) = refs[7:13]
    (vec_own, vec_other, right_out, left_out, *left_partials_out, mine_out) = refs[13:20]
    (loss_out, left, norm_b, e_own, mine_own, mine_partner) = refs[20:]
    rows, quart = zero_own.shape
    width = quart // 2
    lower, upper = slice(0, quart), slice(quart, 2 * quart)
    stats_own, stats_other = joined_rows(late_own, rows), joined_rows(late_other, rows)
    both = lambda i: jnp.concatenate([stats_own[i], stats_other[i]], axis=1)
    offset, rstd, _, delta = [both(i) for i in range(4)]
    left_operand(zero_own, late_own, left, lower)
    left_operand(zero_other, late_other, left, upper)
    own_b = right_stats(late_b)
    other_b = right_stats(late_b_other)
    for source, stats, lanes in ((first_b, own_b, lower), (first_b_other, other_b, upper)):
        for at in range(0, rows, 64):
            piece = slice(at, at + 64)
            norm_b[piece, lanes] = (
                (source[piece, :].astype(jnp.float32) - stats[0]) * stats[1]
            ).astype(jnp.bfloat16)
        rest = jnp.broadcast_to(stats[2] * stats[1], (16, quart))
        norm_b[rows:, lanes] = rest.astype(jnp.bfloat16)

    def tile_corr(late, inner, total, columns, block):
        scale_col, delta_col = columns
        total = total + late_products(block, late, inner)
        row = joined_rows(late, rows)
        return (total * scale_col - delta_col * row[3][:, inner]) * row[1][:, inner]

    columns = scale_columns(late_b, images)
    columns_partner = scale_columns(late_b_other, images)
    across = jnp.zeros((quart, 128), jnp.float32)
    losses = jnp.zeros((8, 128), jnp.float32)
    down, diagonals = [], []
    for tile in range(4):
        at = slice(tile * width, (tile + 1) * width)
        inner = slice((tile % 2) * width, (tile % 2 + 1) * width)
        late = late_own if tile < 2 else late_other
        corr = tile_corr(late, inner, sums[:, at], columns, late_b)
        dcorr = off_weight * corr
        product = dcorr * corr
        loss = product
        if tile < 2:
            feature = lax.broadcasted_iota(jnp.int32, (quart, width), 0)
            lane = lax.broadcasted_iota(jnp.int32, (quart, width), 1) + tile * width
            diagonal = feature == lane
            slope = jnp.where(diagonal, (corr - 1.0).astype(jnp.bfloat16).astype(jnp.float32), 0.0)
            diagonals.append(jnp.sum(slope, axis=0, keepdims=True))
            dcorr = jnp.where(diagonal, 0.0, dcorr)
            product = jnp.where(diagonal, slope * corr, product)
            loss = jnp.where(diagonal, (1.0 - corr) * (1.0 - corr), loss)
        e_own[:, at] = (dcorr * rstd[:, at]).astype(jnp.bfloat16)
        across = across + fold_lanes(product)
        losses = losses + fold_rows(fold_lanes(loss))
        down.append(jnp.sum(product, axis=0, keepdims=True))

        @pl.when(flags[0] == tile)
        def _():
            mine_own[...] = corr
            partner = partner_own if tile < 2 else partner_other
            mine_partner[...] = tile_corr(
                late, inner, partner[:, inner], columns_partner, late_b_other
            )

    diagonal_row = jnp.concatenate(diagonals, axis=1)
    partner_second = jnp.concatenate([vec_own[0:1, :], vec_other[0:1, :]], axis=1)
    second_a = rstd * (partner_second + jnp.concatenate(down, axis=1))
    second_b = lanes_to_row(across)
    loss = jnp.sum(losses) + jnp.sum(vec_other[1:2, :])
    loss_out[...] = jnp.broadcast_to(loss, (8, 128))

    for tile in (2, 3, 0, 1):
        at = slice(tile * width, (tile + 1) * width)
        inner = slice((tile % 2) * width, (tile % 2 + 1) * width)
        source, e_partner = (first_own, e_left) if tile < 2 else (first_other, e_right)
        terms = dot(norm_b[:, lower], e_own[:, at]) + dot(norm_b[:, upper], e_partner[:, inner])
        xhat = (source[:, inner].astype(jnp.float32) - offset[:, at]) * rstd[:, at]
        value = terms[:rows] - terms[rows : rows + 1] - xhat * second_a[:, at]
        if tile < 2:
            slope = rstd[:, at] * diagonal_row[:, inner]
            left_out[:, inner] = value + norm_b[:rows, inner].astype(jnp.float32) * slope
        else:
            for half, out in enumerate(left_partials_out):
                some = out.shape[0]
                out[:, inner] = value[half * some : (half + 1) * some].astype(jnp.bfloat16)

    for tile in range(2):
        at = slice(tile * width, (tile + 1) * width)
        terms = dot_rows(left[...], e_own[at, :])
        xhat = (first_b[:, at].astype(jnp.float32) - own_b[0][:, at]) * own_b[1][:, at]
        norm_a = (first_own[:, at].astype(jnp.float32) - offset[:, at]) * rstd[:, at]
        norm_a = norm_a.astype(jnp.bfloat16).astype(jnp.float32)
        right_out[:, at] = (
            without_extra(terms, rows) - xhat * second_b[:, at] + norm_a * diagonal_row[:, at]
        )

    own_columns = jnp.transpose(mine_own[...])
    partner_columns = jnp.transpose(mine_partner[...])

    @pl.when(flags[1] == 0)
    def _():
        mine_out[:, lower] = own_columns
        mine_out[:, upper] = partner_columns

    @pl.when(flags[1] != 0)
    def _():
        mine_out[:, lower] = partner_columns
        mine_out[:, upper] = own_columns


def for_partner_kernel(loss, core_loss, second, out):
    total = loss[0:1, 0:1] + core_loss[0:1, 0:1]
    out[...] = rows_of([jnp.broadcast_to(total, (1, out.shape[1])), second[0:1, :]])


def left_final_kernel(left, from_core_0, from_core_1, left_out):
    some = from_core_0.shape[0]
    for half, from_core in enumerate((from_core_0, from_core_1)):
        for at in range(0, some, 64):
            piece = slice(half * some + at, half * some + at + 64)
            value = left[piece, :] + from_core[at : at + 64, :].astype(jnp.float32)
            left_out[piece, :] = value.astype(jnp.bfloat16)


def right_final_kernel(feats, right, from_x, late_b_0, late_b_1, first_b, sent, got, right_out, loss_out):
    rows = right.shape[0]
    offset, rstd, _, _ = right_stats((late_b_0, late_b_1))
    second = got[1:2, :]
    loss_out[0] = (sent[0, 0] + got[0, 0]) / feats
    for at in range(0, rows, 64):
        piece = slice(at, at + 64)
        xhat = (first_b[piece, :].astype(jnp.float32) - offset) * rstd
        value = right[piece, :] + from_x[piece, :].astype(jnp.float32) - xhat * second
        right_out[piece, :] = (rstd * value).astype(jnp.bfloat16)


vmem = pl.BlockSpec(memory_space=pltpu.VMEM)
smem = pl.BlockSpec(memory_space=pltpu.SMEM)


def local_call(kernel, operands, outs, scratch=(), flops=2**20, room=8, held=(), moved=None):
    if moved is None:
        moved = sum(x.size * x.dtype.itemsize for x in (*operands, *outs))

    def space(x):
        return smem if x.ndim == 1 else vmem

    return pl.pallas_call(
        kernel,
        out_shape=list(outs),
        in_specs=[space(x) for x in operands],
        out_specs=[space(x) for x in outs],
        scratch_shapes=list(scratch),
        compiler_params=pltpu.CompilerParams(vmem_limit_bytes=room * 2**20),
        cost_estimate=pl.CostEstimate(flops=flops, bytes_accessed=moved, transcendentals=0),
    )(*(pltpu.with_memory_space_constraint(x, pltpu.VMEM) if i in held else x for i, x in enumerate(operands)))


def gathered_device(left_outputs, right_outputs):
    rows, quart = left_outputs.shape
    half = 2 * quart
    feats = 4 * quart
    batch_images = rows * 4
    tpos = lax.axis_index("tile")
    dpos = lax.axis_index("dp")
    row_halves = tpos // 2
    column_halves = tpos % 2
    at_end = (dpos == 0) | (dpos == 3)
    owned_tile = jnp.where(dpos // 2 == column_halves, 0, 2) + dpos % 2
    flags = jnp.stack([owned_tile, row_halves]).astype(jnp.int32)
    mask = jnp.broadcast_to(at_end.astype(jnp.float32), (8, quart))

    pairs = [(0, 1), (1, 0), (2, 3), (3, 2)]
    middle = [(1, 2), (2, 1)]
    outward = [(1, 0), (2, 3)]

    def along(block, route):
        return lax.ppermute(block, "dp", route)

    def core_swap(block):
        return swapped(block, "tile", 0)

    def x_swap(block):
        return swapped(block, "tile", 1)

    def after(value, *others):
        return lax.optimization_barrier((value, *others))

    gemm = 2 * rows * quart * quart
    width = quart // 2
    quarter_f32 = jax.ShapeDtypeStruct((rows, quart), jnp.float32)
    quarter_bf16 = jax.ShapeDtypeStruct((rows, quart), jnp.bfloat16)
    extended = jax.ShapeDtypeStruct((rows + 16, quart), jnp.bfloat16)
    row_out = jax.ShapeDtypeStruct((8, quart), jnp.float32)
    one_out = jax.ShapeDtypeStruct((8, 128), jnp.float32)
    across_shape = jax.ShapeDtypeStruct((quart, 128), jnp.float32)
    low = lambda n, m: pltpu.VMEM((n, m), jnp.bfloat16)

    def picked(outer, inner):
        return local_call(pick_kernel, (mask, outer, inner), (quarter_bf16,))[0]

    some = rows // 2
    half_block = jax.ShapeDtypeStruct((some, quart), jnp.bfloat16)
    first_b = along(right_outputs, pairs)
    inner_b = along(right_outputs, middle)
    first_a = along(left_outputs, pairs)
    other_b0 = x_swap(right_outputs)
    other_a0, mask, flags = after(core_swap(left_outputs), mask, flags)
    left_behind, first_a, other_a0 = after(left_outputs, first_a, other_a0)
    inner_a = along(left_behind, middle)

    outer_b = along(inner_b, outward)
    third_b = along(first_b, middle)
    ready_b, other_b0 = after(first_b, other_b0)
    other_b1 = x_swap(ready_b)
    outer_a = along(inner_a, outward)
    third_a = along(first_a, middle)
    other_a1 = core_swap(first_a)

    third_b = local_call(halves_kernel, (third_b,), (half_block, half_block))
    last_b = [along(x, outward) for x in third_b]
    second_b = picked(outer_b, inner_b)
    row_b = local_call(right_sums_kernel, (right_outputs, first_b, second_b), (row_out,))[0]
    second_b, other_b1, other_a1 = after(second_b, other_b1, other_a1)
    other_b2 = x_swap(second_b)
    last_a = along(third_a, outward)
    second_a = picked(outer_a, inner_a)
    second_a, row_b = after(second_a, row_b)
    other_a2 = core_swap(second_a)

    late_b_0, row_b = local_call(
        functools.partial(late_right_kernel, batch_images, False),
        (mask, last_b[0], third_b[0], row_b),
        (jax.ShapeDtypeStruct((quart, some), jnp.bfloat16), row_out),
        held=(0, 1, 2, 3),
    )
    late_b_other_0 = x_swap(late_b_0)
    (late_b_1,) = local_call(
        functools.partial(late_right_kernel, batch_images, True),
        (mask, last_b[1], third_b[1], row_b),
        (jax.ShapeDtypeStruct((quart + 16 * (quart // some), some), jnp.bfloat16),),
        held=(0, 1, 2, 3),
    )
    late_b_other_1 = x_swap(late_b_1)
    late_b = (late_b_0, late_b_1)
    other_b2, late_b_1, late_b_other_0 = after(other_b2, late_b_1, late_b_other_0)
    partner_own, partner_other, own_all, row_other, zero_own, zero_other = local_call(
        products_kernel,
        (left_outputs, other_a0, first_a, other_a1, second_a, other_a2)
        + (right_outputs, other_b0, first_b, other_b1, second_b, other_b2),
        (
            quarter_f32,
            quarter_f32,
            jax.ShapeDtypeStruct((quart, half), jnp.float32),
            row_out,
            quarter_bf16,
            quarter_bf16,
        ),
        [low(3 * rows, half), low(half, 3 * rows)],
        room=20,
        moved=2**16,
    )
    row_a, late_b_other_1 = after(core_swap(row_other), late_b_other_1)
    late_b_other = (late_b_other_0, late_b_other_1)
    (late_a,) = local_call(
        functools.partial(late_left_kernel, batch_images),
        (mask, last_a, third_a, row_a),
        (extended,),
        held=(0, 1, 2, 3),
    )
    late_a_other = core_swap(late_a)

    terms, across, e_left, vec_own, columns = local_call(
        functools.partial(partner_kernel, batch_images, 0),
        (late_a, zero_own, partner_own, *late_b_other),
        (
            jax.ShapeDtypeStruct((rows + 16, quart), jnp.float32),
            across_shape,
            quarter_bf16,
            row_out,
            jax.ShapeDtypeStruct((quart, 8), jnp.float32),
        ),
        [low(rows + 16, quart)],
        2 * gemm,
        room=12,
    )
    partial_right, second, e_right, vec_other = local_call(
        functools.partial(partner_kernel, batch_images, 1),
        (late_a_other, zero_other, partner_other, *late_b_other, terms, across, vec_own, columns),
        (quarter_bf16, row_out, quarter_bf16, row_out),
        [low(rows + 16, quart)],
        2 * gemm,
        room=12,
    )
    from_x = x_swap(partial_right)
    right_own, left_own, *partials_left, mine, loss = local_call(
        functools.partial(own_kernel, batch_images),
        (flags, *late_b, *late_b_other)
        + (late_a, late_a_other, left_outputs, other_a0, zero_own, zero_other, own_all)
        + (right_outputs, other_b0, e_left, e_right)
        + (partner_own, partner_other)
        + (vec_own, vec_other),
        (
            quarter_f32,
            quarter_f32,
            half_block,
            half_block,
            jax.ShapeDtypeStruct((width, half), jnp.float32),
            one_out,
        ),
        [
            low(rows + 16, half),
            low(rows + 16, half),
            low(quart, half),
            pltpu.VMEM((quart, width), jnp.float32),
            pltpu.VMEM((quart, width), jnp.float32),
        ],
        8 * gemm,
        room=20,
    )
    from_core = [core_swap(x) for x in partials_left]
    core_loss = core_swap(loss)
    (for_partner,) = local_call(for_partner_kernel, (loss, core_loss, second), (row_out,))
    from_partner = x_swap(for_partner)
    (left_gradient,) = local_call(left_final_kernel, (left_own, *from_core), (quarter_bf16,))
    right_own, left_gradient = after(right_own, left_gradient)
    right_gradient, loss = local_call(
        functools.partial(right_final_kernel, feats),
        (right_own, from_x, *late_b, right_outputs, for_partner, from_partner),
        (quarter_bf16, jax.ShapeDtypeStruct((1,), jnp.float32)),
    )
    return (left_gradient, right_gradient, mine[None, :, :], loss)


def solution(mesh):
    per_device = gathered_device if mesh.shape["dp"] == 4 else reduced_device
    return jax.shard_map(
        per_device,
        mesh=mesh,
        in_specs=(P(("groups", "dp"), "tile"), P(("groups", "dp"), "tile")),
        out_specs=(
            P(("groups", "dp"), "tile"),
            P(("groups", "dp"), "tile"),
            P(("groups", "tile"), "dp", None),
            P("groups"),
        ),
        check_vma=False,
    )
```

```python
import functools
import jax
import jax.numpy as jnp
from jax import lax
from jax.experimental import pallas as pl
from jax.experimental.pallas import tpu as pltpu
from jax.sharding import PartitionSpec as P

off_weight = 0.0051


def swapped(block, axis, bit):
    count = lax.axis_size(axis)
    route = []
    for low in range(count):
        high = low | 1 << bit
        if high != low and high < count:
            route += [(low, high), (high, low)]
    return lax.ppermute(block, axis, route)


def pair_views(first_moment, second_moment, row_halves, column_halves):
    other_a = swapped(first_moment, "tile", 0)
    other_b = swapped(second_moment, "tile", 1)
    joined_a = jnp.where(
        column_halves == 0,
        jnp.concatenate([first_moment, other_a], axis=1),
        jnp.concatenate([other_a, first_moment], axis=1),
    )
    joined_b = jnp.where(
        row_halves == 0,
        jnp.concatenate([second_moment, other_b], axis=1),
        jnp.concatenate([other_b, second_moment], axis=1),
    )
    return (joined_a, joined_b)


def moment_pair(total, squares, batch_images):
    column_mean = total / batch_images
    var = squares / batch_images - column_mean * column_mean
    return (column_mean, lax.rsqrt(var + 1e-05))


def col_sums(values):
    as_float = values.astype(jnp.float32)
    return (jnp.sum(as_float, axis=0), jnp.sum(as_float * as_float, axis=0))


def reduced_device(left_outputs, right_outputs):
    rows, quart = left_outputs.shape
    half = 2 * quart
    feats = 4 * quart
    dp_count = lax.axis_size("dp")
    batch_images = rows * dp_count
    tpos = lax.axis_index("tile")
    row_halves = tpos // 2
    column_halves = tpos % 2
    sum_a, sq_a = col_sums(left_outputs)
    sum_b, sq_b = col_sums(right_outputs)
    sum_a, sq_a, sum_b, sq_b = lax.psum((sum_a, sq_a, sum_b, sq_b), "dp")
    left_mean, left_inverse_deviation = moment_pair(sum_a, sq_a, batch_images)
    right_mean, right_inverse_deviation = moment_pair(sum_b, sq_b, batch_images)
    standardized_left = (left_outputs.astype(jnp.float32) - left_mean) * left_inverse_deviation
    standardized_right = (right_outputs.astype(jnp.float32) - right_mean) * right_inverse_deviation
    half_a, cols_b = pair_views(
        standardized_left.astype(jnp.bfloat16),
        standardized_right.astype(jnp.bfloat16),
        row_halves,
        column_halves,
    )
    col_local = jnp.arange(half, dtype=jnp.int32)
    col_ids = quart * column_halves + col_local + jnp.where(col_local >= quart, quart, 0)
    owned = half // dp_count
    picked = half_a
    corr_rows = (
        lax.psum_scatter(
            lax.dot_general(
                picked, cols_b, (((0,), (0,)), ((), ())), preferred_element_type=jnp.float32
            ),
            "dp",
            scatter_dimension=0,
            tiled=True,
        )
        / batch_images
    )
    row_ids = half * row_halves + lax.axis_index("dp") * owned + jnp.arange(owned, dtype=jnp.int32)
    diagonal = row_ids[:, None] == col_ids[None, :]
    part_loss = jnp.sum(
        jnp.where(diagonal, (1.0 - corr_rows) ** 2, off_weight * corr_rows * corr_rows)
    )
    loss = lax.psum(part_loss, ("dp", "tile")) / feats
    dcorr_part = jnp.where(diagonal, corr_rows - 1.0, off_weight * corr_rows).astype(jnp.bfloat16)
    piece = lax.all_gather(dcorr_part, "dp", axis=0, tiled=True)
    block_a = lax.dot_general(
        cols_b, piece, (((1,), (1,)), ((), ())), preferred_element_type=jnp.float32
    )
    picked = half_a
    into_b = jnp.dot(picked, piece, preferred_element_type=jnp.float32)
    other_a = swapped(block_a.astype(jnp.bfloat16), "tile", 0).astype(block_a.dtype)
    other_b = swapped(into_b.astype(jnp.bfloat16), "tile", 1).astype(into_b.dtype)
    normed_grad_left = lax.dynamic_slice_in_dim(block_a + other_a, column_halves * quart, quart, 1)
    normed_grad_right = lax.dynamic_slice_in_dim(into_b + other_b, row_halves * quart, quart, 1)
    first_moment_left, second_moment_left, first_moment_right, second_moment_right = lax.psum(
        (
            jnp.sum(normed_grad_left, axis=0),
            jnp.sum(normed_grad_left * standardized_left, axis=0),
            jnp.sum(normed_grad_right, axis=0),
            jnp.sum(normed_grad_right * standardized_right, axis=0),
        ),
        "dp",
    )
    left_gradient = (
        left_inverse_deviation
        * (
            normed_grad_left
            - first_moment_left / batch_images
            - standardized_left * (second_moment_left / batch_images)
        )
    ).astype(jnp.bfloat16)
    right_gradient = (
        right_inverse_deviation
        * (
            normed_grad_right
            - first_moment_right / batch_images
            - standardized_right * (second_moment_right / batch_images)
        )
    ).astype(jnp.bfloat16)
    return (left_gradient, right_gradient, corr_rows[None, :, :], jnp.reshape(loss, (1,)))


def fold_rows(values):
    rows, width = values.shape
    return jnp.sum(values.reshape(rows // 8, 8, width), axis=0)


def fold_lanes(values):
    return sum(values[:, at : at + 128] for at in range(0, values.shape[1], 128))


def column_mean(block):
    rows, width = block.shape
    folded = jnp.zeros((8, width), jnp.float32)
    for at in range(0, rows, 64):
        folded = folded + fold_rows(block[at : at + 64, :].astype(jnp.float32))
    return jnp.sum(folded, axis=0, keepdims=True) / rows


def add_sums(sums, centred, low):
    return [
        sums[0] + fold_rows(centred),
        sums[1] + fold_rows(centred * centred),
        sums[2] + fold_rows(low.astype(jnp.float32)),
    ]


def rows_of(values):
    pad = jnp.zeros((8 - len(values), values[0].shape[1]), jnp.float32)
    return jnp.concatenate([*values, pad], axis=0)


def joined_sums(row, sums):
    return [row[i + 1 : i + 2, :] + jnp.sum(s, axis=0, keepdims=True) for i, s in enumerate(sums)]


def moments(sums, images):
    total, squares, rounded = sums
    delta = total / images
    return delta, lax.rsqrt(squares / images - delta * delta + 1e-05), rounded / images - delta


def three_parts(row):
    high = row.astype(jnp.bfloat16)
    rest = row - high.astype(jnp.float32)
    middle = rest.astype(jnp.bfloat16)
    low = (rest - middle.astype(jnp.float32)).astype(jnp.bfloat16)
    return [high, middle, low]


def split_rows(values):
    parts = sum([three_parts(v) for v in values], [])
    pad = jnp.zeros((4, values[0].shape[1]), jnp.float32)
    return jnp.concatenate([*(p.astype(jnp.float32) for p in parts), pad], axis=0).astype(
        jnp.bfloat16
    )


def joined_rows(ref, at):
    parts = ref[at : at + 16, :].astype(jnp.float32)
    part = lambda i: parts[i : i + 1]
    return [part(3 * i) + part(3 * i + 1) + part(3 * i + 2) for i in range(4)]


def lanes_to_row(partial):
    ones = jnp.ones((16, partial.shape[1]), jnp.bfloat16)
    high = partial.astype(jnp.bfloat16)
    low = (partial - high.astype(jnp.float32)).astype(jnp.bfloat16)
    row = dot_rows(ones, high) + dot_rows(ones, low)
    return row[:1, :]


def dot_rows(left, right):
    return lax.dot_general(
        left, right, (((1,), (1,)), ((), ())), preferred_element_type=jnp.float32
    )


def dot(left, right):
    return jnp.dot(left, right, preferred_element_type=jnp.float32)


def pick(mask, outer, inner, piece):
    return jnp.where(
        mask[0:1, :] != 0.0, outer[piece, :].astype(jnp.float32), inner[piece, :].astype(jnp.float32)
    )


def pick_kernel(mask, outer, inner, out):
    for at in range(0, outer.shape[0], 64):
        piece = slice(at, at + 64)
        out[piece, :] = pick(mask, outer, inner, piece).astype(out.dtype)


def right_sums_kernel(first, second, third, row):
    rows, quart = first.shape
    shift = column_mean(first)
    sums = [jnp.zeros((8, quart), jnp.float32)] * 3
    for block in (first, second, third):
        for at in range(0, rows, 64):
            centred = block[at : at + 64, :].astype(jnp.float32) - shift
            sums = add_sums(sums, centred, centred.astype(jnp.bfloat16))
    row[...] = rows_of([shift] + [jnp.sum(s, axis=0, keepdims=True) for s in sums])


def halves_kernel(block, first, second):
    half = first.shape[0]
    first[...] = block[:half, :]
    second[...] = block[half:, :]


def late_left_kernel(images, mask, outer, inner, row, out):
    rows, quart = outer.shape
    shift = row[0:1, :]
    sums = [jnp.zeros((8, quart), jnp.float32)] * 3
    for at in range(0, rows, 128):
        piece = slice(at, at + 128)
        centred = pick(mask, outer, inner, piece) - shift
        low = centred.astype(jnp.bfloat16)
        out[piece, :] = low
        sums = add_sums(sums, centred, low)
    delta, rstd, gap = moments(joined_sums(row, sums), images)
    out[rows:, :] = split_rows([shift + delta, rstd, gap, delta])


def late_right_kernel(images, last, mask, outer, inner, row, out, *rest):
    some, quart = outer.shape
    shift = row[0:1, :]
    sums = [jnp.zeros((8, quart), jnp.float32)] * 3
    for at in range(0, some, 128):
        piece = slice(at, at + 128)
        centred = pick(mask, outer, inner, piece) - shift
        low = centred.astype(jnp.bfloat16)
        out[:quart, piece] = jnp.transpose(low)
        sums = add_sums(sums, centred, low)
    sums = joined_sums(row, sums)
    if not last:
        (row_out,) = rest
        row_out[...] = rows_of([shift, *sums])
        return
    delta, rstd, gap = moments(sums, images)
    parts = split_rows([shift + delta, rstd, gap, delta])
    for i in range(quart // some):
        below = quart + 16 * i
        out[below : below + 16, :] = parts[:, i * some : (i + 1) * some]


def right_stats(late):
    quart, some = late[0].shape
    found = [joined_rows(late[1], quart + 16 * i) for i in range(quart // some)]
    return [jnp.concatenate(values, axis=1) for values in zip(*found)]


def late_products(right, left, lanes):
    quart, some = right[0].shape
    first = dot(right[0][...], left[:some, lanes])
    return first + dot(right[1][:quart, :], left[some : 2 * some, lanes])


def products_kernel(*refs):
    lefts, rights = refs[0:6], refs[6:12]
    partner_own, partner_other, own_all, row_other, zero_own, zero_other = refs[12:18]
    low_left, low_right = refs[18:]
    rows, quart = lefts[0].shape
    width = quart // 2
    for half in range(2):
        lanes = slice(half * quart, (half + 1) * quart)
        shift = column_mean(lefts[half])
        sums = [jnp.zeros((8, quart), jnp.float32)] * 3
        for block in range(3):
            source = lefts[2 * block + half]
            for at in range(0, rows, 64):
                centred = source[at : at + 64, :].astype(jnp.float32) - shift
                low = centred.astype(jnp.bfloat16)
                low_left[block * rows + at : block * rows + at + 64, lanes] = low
                if block == 0:
                    (zero_own, zero_other)[half][at : at + 64, :] = low
                if half:
                    sums = add_sums(sums, centred, low)
        if half:
            row_other[...] = rows_of([shift] + [jnp.sum(s, axis=0, keepdims=True) for s in sums])
    for half in range(2):
        lanes = slice(half * quart, (half + 1) * quart)
        shift = column_mean(rights[half])
        for block in range(3):
            source = rights[2 * block + half]
            for at in range(0, rows, 128):
                low = (source[at : at + 128, :].astype(jnp.float32) - shift).astype(jnp.bfloat16)
                low_right[lanes, block * rows + at : block * rows + at + 128] = jnp.transpose(low)
    for tile in range(4):
        wide = slice(tile * width, (tile + 1) * width)
        inner = slice((tile % 2) * width, (tile % 2 + 1) * width)
        target = partner_own if tile < 2 else partner_other
        target[:, inner] = dot(low_right[quart:, :], low_left[:, wide])
        own_all[:, wide] = dot(low_right[:quart, :], low_left[:, wide])


def left_operand(zero, late, target, lanes):
    rows, quart = zero.shape
    _, _, gap, delta = joined_rows(late, rows)
    high, middle, _ = three_parts(delta)
    target[:rows, lanes] = zero[...]
    extra = [high.astype(jnp.float32), middle.astype(jnp.float32), gap]
    pad = jnp.zeros((13, quart), jnp.float32)
    target[rows:, lanes] = jnp.concatenate([*extra, pad], axis=0).astype(jnp.bfloat16)


def without_extra(terms, rows):
    return terms[:rows] - (terms[rows : rows + 1] + terms[rows + 1 : rows + 2] + terms[rows + 2 : rows + 3])


def scale_columns(late_b, images):
    _, rstd, _, delta = right_stats(late_b)
    columns = jnp.transpose(rows_of([rstd / images, delta * rstd]))
    return columns[:, 0:1], columns[:, 1:2]


def partner_kernel(images, part, late, zero, sums, late_b_0, late_b_1, *refs):
    if part:
        (terms_in, across_in, vec_in, columns, first_b) = refs[:5]
        (partial_out, e_out, vec_out, left) = refs[5:]
    else:
        (terms_out, across_out, e_out, vec_out, columns, left) = refs
        _, rstd_b, _, delta_b = right_stats((late_b_0, late_b_1))
        columns[...] = jnp.transpose(rows_of([rstd_b / images, delta_b * rstd_b]))
    late_b = (late_b_0, late_b_1)
    rows, quart = zero.shape
    width = quart // 2
    _, rstd, _, delta = joined_rows(late, rows)
    left_operand(zero, late, left, slice(0, quart))
    scale_col, delta_col = columns[:, 0:1], columns[:, 1:2]
    across = across_in[...] if part else jnp.zeros((quart, 128), jnp.float32)
    down = []
    for tile in range(2):
        at = slice(tile * width, (tile + 1) * width)
        total = sums[:, at] + late_products(late_b, late, at)
        corr = (total * scale_col - delta_col * delta[:, at]) * rstd[:, at]
        e_out[:, at] = (corr * (off_weight * rstd[:, at])).astype(jnp.bfloat16)
        square = corr * corr
        across = across + fold_lanes(square)
        down.append(jnp.sum(square, axis=0, keepdims=True))
    second_a = off_weight * jnp.concatenate(down, axis=1)
    if part:
        vec_out[...] = rows_of([second_a, second_a + vec_in[0:1, :]])
        second = off_weight * lanes_to_row(across)
        offset_b, rstd_b, _, _ = right_stats(late_b)
    else:
        vec_out[...] = rows_of([second_a])
        across_out[...] = across
    for tile in range(2):
        at = slice(tile * width, (tile + 1) * width)
        terms = dot_rows(left[...], e_out[at, :])
        if part:
            xhat = (first_b[:, at].astype(jnp.float32) - offset_b[:, at]) * rstd_b[:, at]
            partial_out[:, at] = (
                without_extra(terms + terms_in[:, at], rows) - xhat * second[:, at]
            ).astype(jnp.bfloat16)
        else:
            terms_out[:, at] = terms


def own_kernel(images, flags, *refs):
    late_b, late_b_other, refs = refs[:2], refs[2:4], refs[4:]
    (late_own, late_other, first_own, first_other, zero_own, zero_other, sums) = refs[:7]
    (first_b, first_b_other, e_left, e_right, partner_own, partner_other) = refs[7:13]
    (vec_own, vec_other, right_out, left_out, *left_partials_out, mine_out) = refs[13:20]
    (loss_out, left, norm_b, e_own, mine_own, mine_partner) = refs[20:]
    rows, quart = zero_own.shape
    width = quart // 2
    lower, upper = slice(0, quart), slice(quart, 2 * quart)
    stats_own, stats_other = joined_rows(late_own, rows), joined_rows(late_other, rows)
    both = lambda i: jnp.concatenate([stats_own[i], stats_other[i]], axis=1)
    offset, rstd, _, delta = [both(i) for i in range(4)]
    left_operand(zero_own, late_own, left, lower)
    left_operand(zero_other, late_other, left, upper)
    own_b = right_stats(late_b)
    other_b = right_stats(late_b_other)
    for source, stats, lanes in ((first_b, own_b, lower), (first_b_other, other_b, upper)):
        for at in range(0, rows, 64):
            piece = slice(at, at + 64)
            norm_b[piece, lanes] = (
                (source[piece, :].astype(jnp.float32) - stats[0]) * stats[1]
            ).astype(jnp.bfloat16)
        rest = jnp.broadcast_to(stats[2] * stats[1], (16, quart))
        norm_b[rows:, lanes] = rest.astype(jnp.bfloat16)

    def tile_corr(late, inner, total, columns, block):
        scale_col, delta_col = columns
        total = total + late_products(block, late, inner)
        row = joined_rows(late, rows)
        return (total * scale_col - delta_col * row[3][:, inner]) * row[1][:, inner]

    columns = scale_columns(late_b, images)
    columns_partner = scale_columns(late_b_other, images)
    across = jnp.zeros((quart, 128), jnp.float32)
    losses = jnp.zeros((8, 128), jnp.float32)
    down, diagonals = [], []
    for tile in range(4):
        at = slice(tile * width, (tile + 1) * width)
        inner = slice((tile % 2) * width, (tile % 2 + 1) * width)
        late = late_own if tile < 2 else late_other
        corr = tile_corr(late, inner, sums[:, at], columns, late_b)
        dcorr = off_weight * corr
        product = dcorr * corr
        loss = product
        if tile < 2:
            feature = lax.broadcasted_iota(jnp.int32, (quart, width), 0)
            lane = lax.broadcasted_iota(jnp.int32, (quart, width), 1) + tile * width
            diagonal = feature == lane
            slope = jnp.where(diagonal, (corr - 1.0).astype(jnp.bfloat16).astype(jnp.float32), 0.0)
            diagonals.append(jnp.sum(slope, axis=0, keepdims=True))
            dcorr = jnp.where(diagonal, 0.0, dcorr)
            product = jnp.where(diagonal, slope * corr, product)
            loss = jnp.where(diagonal, (1.0 - corr) * (1.0 - corr), loss)
        e_own[:, at] = (dcorr * rstd[:, at]).astype(jnp.bfloat16)
        across = across + fold_lanes(product)
        losses = losses + fold_rows(fold_lanes(loss))
        down.append(jnp.sum(product, axis=0, keepdims=True))

        @pl.when(flags[0] == tile)
        def _():
            mine_own[...] = corr
            partner = partner_own if tile < 2 else partner_other
            mine_partner[...] = tile_corr(
                late, inner, partner[:, inner], columns_partner, late_b_other
            )

    diagonal_row = jnp.concatenate(diagonals, axis=1)
    partner_second = jnp.concatenate([vec_own[0:1, :], vec_other[0:1, :]], axis=1)
    second_a = rstd * (partner_second + jnp.concatenate(down, axis=1))
    second_b = lanes_to_row(across)
    loss = jnp.sum(losses) + jnp.sum(vec_other[1:2, :])
    loss_out[...] = jnp.broadcast_to(loss, (8, 128))

    for tile in (2, 3, 0, 1):
        at = slice(tile * width, (tile + 1) * width)
        inner = slice((tile % 2) * width, (tile % 2 + 1) * width)
        source, e_partner = (first_own, e_left) if tile < 2 else (first_other, e_right)
        terms = dot(norm_b[:, lower], e_own[:, at]) + dot(norm_b[:, upper], e_partner[:, inner])
        xhat = (source[:, inner].astype(jnp.float32) - offset[:, at]) * rstd[:, at]
        value = terms[:rows] - terms[rows : rows + 1] - xhat * second_a[:, at]
        if tile < 2:
            slope = rstd[:, at] * diagonal_row[:, inner]
            left_out[:, inner] = value + norm_b[:rows, inner].astype(jnp.float32) * slope
        else:
            for half, out in enumerate(left_partials_out):
                some = out.shape[0]
                out[:, inner] = value[half * some : (half + 1) * some].astype(jnp.bfloat16)

    for tile in range(2):
        at = slice(tile * width, (tile + 1) * width)
        terms = dot_rows(left[...], e_own[at, :])
        xhat = (first_b[:, at].astype(jnp.float32) - own_b[0][:, at]) * own_b[1][:, at]
        norm_a = (first_own[:, at].astype(jnp.float32) - offset[:, at]) * rstd[:, at]
        norm_a = norm_a.astype(jnp.bfloat16).astype(jnp.float32)
        right_out[:, at] = (
            without_extra(terms, rows) - xhat * second_b[:, at] + norm_a * diagonal_row[:, at]
        )

    own_columns = jnp.transpose(mine_own[...])
    partner_columns = jnp.transpose(mine_partner[...])

    @pl.when(flags[1] == 0)
    def _():
        mine_out[:, lower] = own_columns
        mine_out[:, upper] = partner_columns

    @pl.when(flags[1] != 0)
    def _():
        mine_out[:, lower] = partner_columns
        mine_out[:, upper] = own_columns


def add_kernel(one, other, out):
    out[...] = one[...] + other[...]


def loss_kernel(feats, one, other, out):
    out[0] = (one[0, 0] + other[0, 0]) / feats


def left_final_kernel(left, from_core_0, from_core_1, left_out):
    some = from_core_0.shape[0]
    for half, from_core in enumerate((from_core_0, from_core_1)):
        for at in range(0, some, 64):
            piece = slice(half * some + at, half * some + at + 64)
            value = left[piece, :] + from_core[at : at + 64, :].astype(jnp.float32)
            left_out[piece, :] = value.astype(jnp.bfloat16)


def right_final_kernel(right, from_x, late_b_0, late_b_1, right_out):
    rstd = right_stats((late_b_0, late_b_1))[1]
    for at in range(0, right.shape[0], 64):
        piece = slice(at, at + 64)
        value = rstd * (right[piece, :] + from_x[piece, :].astype(jnp.float32))
        right_out[piece, :] = value.astype(jnp.bfloat16)


vmem = pl.BlockSpec(memory_space=pltpu.VMEM)
smem = pl.BlockSpec(memory_space=pltpu.SMEM)


def local_call(kernel, operands, outs, scratch=(), flops=2**20, room=8, held=(), moved=None):
    if moved is None:
        moved = sum(x.size * x.dtype.itemsize for x in (*operands, *outs))

    def space(x):
        return smem if x.ndim == 1 else vmem

    return pl.pallas_call(
        kernel,
        out_shape=list(outs),
        in_specs=[space(x) for x in operands],
        out_specs=[space(x) for x in outs],
        scratch_shapes=list(scratch),
        compiler_params=pltpu.CompilerParams(vmem_limit_bytes=room * 2**20),
        cost_estimate=pl.CostEstimate(flops=flops, bytes_accessed=moved, transcendentals=0),
    )(*(pltpu.with_memory_space_constraint(x, pltpu.VMEM) if i in held else x for i, x in enumerate(operands)))


def gathered_device(left_outputs, right_outputs):
    rows, quart = left_outputs.shape
    half = 2 * quart
    feats = 4 * quart
    batch_images = rows * 4
    tpos = lax.axis_index("tile")
    dpos = lax.axis_index("dp")
    row_halves = tpos // 2
    column_halves = tpos % 2
    at_end = (dpos == 0) | (dpos == 3)
    owned_tile = jnp.where(dpos // 2 == column_halves, 0, 2) + dpos % 2
    flags = jnp.stack([owned_tile, row_halves]).astype(jnp.int32)
    mask = jnp.broadcast_to(at_end.astype(jnp.float32), (8, quart))

    pairs = [(0, 1), (1, 0), (2, 3), (3, 2)]
    middle = [(1, 2), (2, 1)]
    outward = [(1, 0), (2, 3)]

    def along(block, route):
        return lax.ppermute(block, "dp", route)

    def core_swap(block):
        return swapped(block, "tile", 0)

    def x_swap(block):
        return swapped(block, "tile", 1)

    def after(value, *others):
        return lax.optimization_barrier((value, *others))

    gemm = 2 * rows * quart * quart
    width = quart // 2
    quarter_f32 = jax.ShapeDtypeStruct((rows, quart), jnp.float32)
    quarter_bf16 = jax.ShapeDtypeStruct((rows, quart), jnp.bfloat16)
    extended = jax.ShapeDtypeStruct((rows + 16, quart), jnp.bfloat16)
    row_out = jax.ShapeDtypeStruct((8, quart), jnp.float32)
    one_out = jax.ShapeDtypeStruct((8, 128), jnp.float32)
    across_shape = jax.ShapeDtypeStruct((quart, 128), jnp.float32)
    low = lambda n, m: pltpu.VMEM((n, m), jnp.bfloat16)

    def picked(outer, inner):
        return local_call(pick_kernel, (mask, outer, inner), (quarter_bf16,))[0]

    some = rows // 2
    half_block = jax.ShapeDtypeStruct((some, quart), jnp.bfloat16)
    first_b = along(right_outputs, pairs)
    inner_b = along(right_outputs, middle)
    first_a = along(left_outputs, pairs)
    other_b0 = x_swap(right_outputs)
    other_a0, mask, flags = after(core_swap(left_outputs), mask, flags)
    left_behind, first_a, other_a0 = after(left_outputs, first_a, other_a0)
    inner_a = along(left_behind, middle)

    outer_b = along(inner_b, outward)
    third_b = along(first_b, middle)
    ready_b, other_b0 = after(first_b, other_b0)
    other_b1 = x_swap(ready_b)
    outer_a = along(inner_a, outward)
    third_a = along(first_a, middle)
    other_a1 = core_swap(first_a)

    third_b = local_call(halves_kernel, (third_b,), (half_block, half_block))
    last_b = [along(x, outward) for x in third_b]
    second_b = picked(outer_b, inner_b)
    row_b = local_call(right_sums_kernel, (right_outputs, first_b, second_b), (row_out,))[0]
    second_b, other_b1, other_a1 = after(second_b, other_b1, other_a1)
    other_b2 = x_swap(second_b)
    last_a = along(third_a, outward)
    second_a = picked(outer_a, inner_a)
    second_a, row_b = after(second_a, row_b)
    other_a2 = core_swap(second_a)

    late_b_0, row_b = local_call(
        functools.partial(late_right_kernel, batch_images, False),
        (mask, last_b[0], third_b[0], row_b),
        (jax.ShapeDtypeStruct((quart, some), jnp.bfloat16), row_out),
        held=(0, 1, 2, 3),
    )
    late_b_other_0 = x_swap(late_b_0)
    (late_b_1,) = local_call(
        functools.partial(late_right_kernel, batch_images, True),
        (mask, last_b[1], third_b[1], row_b),
        (jax.ShapeDtypeStruct((quart + 16 * (quart // some), some), jnp.bfloat16),),
        held=(0, 1, 2, 3),
    )
    late_b_other_1 = x_swap(late_b_1)
    late_b = (late_b_0, late_b_1)
    other_b2, late_b_1, late_b_other_0 = after(other_b2, late_b_1, late_b_other_0)
    partner_own, partner_other, own_all, row_other, zero_own, zero_other = local_call(
        products_kernel,
        (left_outputs, other_a0, first_a, other_a1, second_a, other_a2)
        + (right_outputs, other_b0, first_b, other_b1, second_b, other_b2),
        (
            quarter_f32,
            quarter_f32,
            jax.ShapeDtypeStruct((quart, half), jnp.float32),
            row_out,
            quarter_bf16,
            quarter_bf16,
        ),
        [low(3 * rows, half), low(half, 3 * rows)],
        room=20,
        moved=2**16,
    )
    row_a, late_b_other_1 = after(core_swap(row_other), late_b_other_1)
    late_b_other = (late_b_other_0, late_b_other_1)
    (late_a,) = local_call(
        functools.partial(late_left_kernel, batch_images),
        (mask, last_a, third_a, row_a),
        (extended,),
        held=(0, 1, 2, 3),
    )
    late_a_other = core_swap(late_a)

    terms, across, e_left, vec_own, columns = local_call(
        functools.partial(partner_kernel, batch_images, 0),
        (late_a, zero_own, partner_own, *late_b_other),
        (
            jax.ShapeDtypeStruct((rows + 16, quart), jnp.float32),
            across_shape,
            quarter_bf16,
            row_out,
            jax.ShapeDtypeStruct((quart, 8), jnp.float32),
        ),
        [low(rows + 16, quart)],
        2 * gemm,
        room=12,
    )
    partial_right, e_right, vec_other = local_call(
        functools.partial(partner_kernel, batch_images, 1),
        (late_a_other, zero_other, partner_other, *late_b_other)
        + (terms, across, vec_own, columns, other_b0),
        (quarter_bf16, quarter_bf16, row_out),
        [low(rows + 16, quart)],
        2 * gemm,
        room=12,
    )
    from_x = x_swap(partial_right)
    right_own, left_own, *partials_left, mine, loss = local_call(
        functools.partial(own_kernel, batch_images),
        (flags, *late_b, *late_b_other)
        + (late_a, late_a_other, left_outputs, other_a0, zero_own, zero_other, own_all)
        + (right_outputs, other_b0, e_left, e_right)
        + (partner_own, partner_other)
        + (vec_own, vec_other),
        (
            quarter_f32,
            quarter_f32,
            half_block,
            half_block,
            jax.ShapeDtypeStruct((width, half), jnp.float32),
            one_out,
        ),
        [
            low(rows + 16, half),
            low(rows + 16, half),
            low(quart, half),
            pltpu.VMEM((quart, width), jnp.float32),
            pltpu.VMEM((quart, width), jnp.float32),
        ],
        8 * gemm,
        room=20,
    )
    from_core = [core_swap(x) for x in partials_left]
    core_loss = core_swap(loss)
    (loss,) = local_call(add_kernel, (loss, core_loss), (one_out,))
    x_loss = x_swap(loss)
    (left_gradient,) = local_call(left_final_kernel, (left_own, *from_core), (quarter_bf16,))
    right_own, left_gradient = after(right_own, left_gradient)
    (right_gradient,) = local_call(right_final_kernel, (right_own, from_x, *late_b), (quarter_bf16,))
    right_gradient, x_loss = after(right_gradient, x_loss)
    (loss,) = local_call(
        functools.partial(loss_kernel, feats),
        (loss, x_loss),
        (jax.ShapeDtypeStruct((1,), jnp.float32),),
    )
    return (left_gradient, right_gradient, mine[None, :, :], loss)


def solution(mesh):
    per_device = gathered_device if mesh.shape["dp"] == 4 else reduced_device
    return jax.shard_map(
        per_device,
        mesh=mesh,
        in_specs=(P(("groups", "dp"), "tile"), P(("groups", "dp"), "tile")),
        out_specs=(
            P(("groups", "dp"), "tile"),
            P(("groups", "dp"), "tile"),
            P(("groups", "tile"), "dp", None),
            P("groups"),
        ),
        check_vma=False,
    )
```

```python
import functools
import jax
import jax.numpy as jnp
from jax import lax
from jax.experimental import pallas as pl
from jax.experimental.pallas import tpu as pltpu
from jax.sharding import PartitionSpec as P

off_weight = 0.0051


def swapped(block, axis, bit):
    count = lax.axis_size(axis)
    route = []
    for low in range(count):
        high = low | 1 << bit
        if high != low and high < count:
            route += [(low, high), (high, low)]
    return lax.ppermute(block, axis, route)


def pair_views(first_moment, second_moment, row_halves, column_halves):
    other_a = swapped(first_moment, "tile", 0)
    other_b = swapped(second_moment, "tile", 1)
    joined_a = jnp.where(
        column_halves == 0,
        jnp.concatenate([first_moment, other_a], axis=1),
        jnp.concatenate([other_a, first_moment], axis=1),
    )
    joined_b = jnp.where(
        row_halves == 0,
        jnp.concatenate([second_moment, other_b], axis=1),
        jnp.concatenate([other_b, second_moment], axis=1),
    )
    return (joined_a, joined_b)


def moment_pair(total, squares, batch_images):
    column_mean = total / batch_images
    var = squares / batch_images - column_mean * column_mean
    return (column_mean, lax.rsqrt(var + 1e-05))


def col_sums(values):
    as_float = values.astype(jnp.float32)
    return (jnp.sum(as_float, axis=0), jnp.sum(as_float * as_float, axis=0))


def reduced_device(left_outputs, right_outputs):
    rows, quart = left_outputs.shape
    half = 2 * quart
    feats = 4 * quart
    dp_count = lax.axis_size("dp")
    batch_images = rows * dp_count
    tpos = lax.axis_index("tile")
    row_halves = tpos // 2
    column_halves = tpos % 2
    sum_a, sq_a = col_sums(left_outputs)
    sum_b, sq_b = col_sums(right_outputs)
    sum_a, sq_a, sum_b, sq_b = lax.psum((sum_a, sq_a, sum_b, sq_b), "dp")
    left_mean, left_inverse_deviation = moment_pair(sum_a, sq_a, batch_images)
    right_mean, right_inverse_deviation = moment_pair(sum_b, sq_b, batch_images)
    standardized_left = (left_outputs.astype(jnp.float32) - left_mean) * left_inverse_deviation
    standardized_right = (right_outputs.astype(jnp.float32) - right_mean) * right_inverse_deviation
    half_a, cols_b = pair_views(
        standardized_left.astype(jnp.bfloat16),
        standardized_right.astype(jnp.bfloat16),
        row_halves,
        column_halves,
    )
    col_local = jnp.arange(half, dtype=jnp.int32)
    col_ids = quart * column_halves + col_local + jnp.where(col_local >= quart, quart, 0)
    owned = half // dp_count
    picked = half_a
    corr_rows = (
        lax.psum_scatter(
            lax.dot_general(
                picked, cols_b, (((0,), (0,)), ((), ())), preferred_element_type=jnp.float32
            ),
            "dp",
            scatter_dimension=0,
            tiled=True,
        )
        / batch_images
    )
    row_ids = half * row_halves + lax.axis_index("dp") * owned + jnp.arange(owned, dtype=jnp.int32)
    diagonal = row_ids[:, None] == col_ids[None, :]
    part_loss = jnp.sum(
        jnp.where(diagonal, (1.0 - corr_rows) ** 2, off_weight * corr_rows * corr_rows)
    )
    loss = lax.psum(part_loss, ("dp", "tile")) / feats
    dcorr_part = jnp.where(diagonal, corr_rows - 1.0, off_weight * corr_rows).astype(jnp.bfloat16)
    piece = lax.all_gather(dcorr_part, "dp", axis=0, tiled=True)
    block_a = lax.dot_general(
        cols_b, piece, (((1,), (1,)), ((), ())), preferred_element_type=jnp.float32
    )
    picked = half_a
    into_b = jnp.dot(picked, piece, preferred_element_type=jnp.float32)
    other_a = swapped(block_a.astype(jnp.bfloat16), "tile", 0).astype(block_a.dtype)
    other_b = swapped(into_b.astype(jnp.bfloat16), "tile", 1).astype(into_b.dtype)
    normed_grad_left = lax.dynamic_slice_in_dim(block_a + other_a, column_halves * quart, quart, 1)
    normed_grad_right = lax.dynamic_slice_in_dim(into_b + other_b, row_halves * quart, quart, 1)
    first_moment_left, second_moment_left, first_moment_right, second_moment_right = lax.psum(
        (
            jnp.sum(normed_grad_left, axis=0),
            jnp.sum(normed_grad_left * standardized_left, axis=0),
            jnp.sum(normed_grad_right, axis=0),
            jnp.sum(normed_grad_right * standardized_right, axis=0),
        ),
        "dp",
    )
    left_gradient = (
        left_inverse_deviation
        * (
            normed_grad_left
            - first_moment_left / batch_images
            - standardized_left * (second_moment_left / batch_images)
        )
    ).astype(jnp.bfloat16)
    right_gradient = (
        right_inverse_deviation
        * (
            normed_grad_right
            - first_moment_right / batch_images
            - standardized_right * (second_moment_right / batch_images)
        )
    ).astype(jnp.bfloat16)
    return (left_gradient, right_gradient, corr_rows[None, :, :], jnp.reshape(loss, (1,)))


def fold_rows(values):
    rows, width = values.shape
    return jnp.sum(values.reshape(rows // 8, 8, width), axis=0)


def fold_lanes(values):
    return sum(values[:, at : at + 128] for at in range(0, values.shape[1], 128))


def column_mean(block):
    rows, width = block.shape
    folded = jnp.zeros((8, width), jnp.float32)
    for at in range(0, rows, 64):
        folded = folded + fold_rows(block[at : at + 64, :].astype(jnp.float32))
    return jnp.sum(folded, axis=0, keepdims=True) / rows


def add_sums(sums, centred, low):
    return [
        sums[0] + fold_rows(centred),
        sums[1] + fold_rows(centred * centred),
        sums[2] + fold_rows(low.astype(jnp.float32)),
    ]


def rows_of(values):
    pad = jnp.zeros((8 - len(values), values[0].shape[1]), jnp.float32)
    return jnp.concatenate([*values, pad], axis=0)


def joined_sums(row, sums):
    return [row[i + 1 : i + 2, :] + jnp.sum(s, axis=0, keepdims=True) for i, s in enumerate(sums)]


def moments(sums, images):
    total, squares, rounded = sums
    delta = total / images
    return delta, lax.rsqrt(squares / images - delta * delta + 1e-05), rounded / images - delta


def three_parts(row):
    high = row.astype(jnp.bfloat16)
    rest = row - high.astype(jnp.float32)
    middle = rest.astype(jnp.bfloat16)
    low = (rest - middle.astype(jnp.float32)).astype(jnp.bfloat16)
    return [high, middle, low]


def split_rows(values):
    parts = sum([three_parts(v) for v in values], [])
    pad = jnp.zeros((4, values[0].shape[1]), jnp.float32)
    return jnp.concatenate([*(p.astype(jnp.float32) for p in parts), pad], axis=0).astype(
        jnp.bfloat16
    )


def joined_rows(ref, at):
    parts = ref[at : at + 16, :].astype(jnp.float32)
    part = lambda i: parts[i : i + 1]
    return [part(3 * i) + part(3 * i + 1) + part(3 * i + 2) for i in range(4)]


def lanes_to_row(partial):
    ones = jnp.ones((16, partial.shape[1]), jnp.bfloat16)
    high = partial.astype(jnp.bfloat16)
    low = (partial - high.astype(jnp.float32)).astype(jnp.bfloat16)
    row = dot_rows(ones, high) + dot_rows(ones, low)
    return row[:1, :]


def dot_rows(left, right):
    return lax.dot_general(
        left, right, (((1,), (1,)), ((), ())), preferred_element_type=jnp.float32
    )


def dot(left, right):
    return jnp.dot(left, right, preferred_element_type=jnp.float32)


def pick(mask, outer, inner, piece):
    return jnp.where(
        mask[0:1, :] != 0.0, outer[piece, :].astype(jnp.float32), inner[piece, :].astype(jnp.float32)
    )


def pick_kernel(mask, outer, inner, out):
    for at in range(0, outer.shape[0], 64):
        piece = slice(at, at + 64)
        out[piece, :] = pick(mask, outer, inner, piece).astype(out.dtype)


def right_sums_kernel(first, second, third, row):
    rows, quart = first.shape
    shift = column_mean(first)
    sums = [jnp.zeros((8, quart), jnp.float32)] * 3
    for block in (first, second, third):
        for at in range(0, rows, 64):
            centred = block[at : at + 64, :].astype(jnp.float32) - shift
            sums = add_sums(sums, centred, centred.astype(jnp.bfloat16))
    row[...] = rows_of([shift] + [jnp.sum(s, axis=0, keepdims=True) for s in sums])


def halves_kernel(block, first, second):
    half = first.shape[0]
    first[...] = block[:half, :]
    second[...] = block[half:, :]


def late_left_kernel(mask, outer, inner, row, out):
    for at in range(0, out.shape[0], 64):
        piece = slice(at, at + 64)
        out[piece, :] = (pick(mask, outer, inner, piece) - row[0:1, :]).astype(out.dtype)


def left_stats_kernel(images, mask, outer, inner, row, stats):
    rows, quart = outer.shape
    shift = row[0:1, :]
    sums = [jnp.zeros((8, quart), jnp.float32)] * 3
    for at in range(0, rows, 64):
        centred = pick(mask, outer, inner, slice(at, at + 64)) - shift
        sums = add_sums(sums, centred, centred.astype(jnp.bfloat16))
    delta, rstd, gap = moments(joined_sums(row, sums), images)
    stats[...] = rows_of([shift + delta, rstd, gap, delta])


def stats_rows(stats):
    return [stats[i : i + 1, :] for i in range(4)]


def late_right_kernel(images, last, mask, outer, inner, row, out, *rest):
    some, quart = outer.shape
    shift = row[0:1, :]
    sums = [jnp.zeros((8, quart), jnp.float32)] * 3
    for at in range(0, some, 128):
        piece = slice(at, at + 128)
        centred = pick(mask, outer, inner, piece) - shift
        low = centred.astype(jnp.bfloat16)
        out[:quart, piece] = jnp.transpose(low)
        sums = add_sums(sums, centred, low)
    sums = joined_sums(row, sums)
    if not last:
        (row_out,) = rest
        row_out[...] = rows_of([shift, *sums])
        return
    delta, rstd, gap = moments(sums, images)
    parts = split_rows([shift + delta, rstd, gap, delta])
    for i in range(quart // some):
        below = quart + 16 * i
        out[below : below + 16, :] = parts[:, i * some : (i + 1) * some]


def right_stats(late):
    quart, some = late[0].shape
    found = [joined_rows(late[1], quart + 16 * i) for i in range(quart // some)]
    return [jnp.concatenate(values, axis=1) for values in zip(*found)]


def late_products(right, left, lanes):
    quart, some = right[0].shape
    first = dot(right[0][...], left[:some, lanes])
    return first + dot(right[1][:quart, :], left[some : 2 * some, lanes])


def products_kernel(*refs):
    lefts, rights = refs[0:6], refs[6:12]
    partner_own, partner_other, own_all, row_other, zero_own, zero_other = refs[12:18]
    low_left, low_right = refs[18:]
    rows, quart = lefts[0].shape
    width = quart // 2
    for half in range(2):
        lanes = slice(half * quart, (half + 1) * quart)
        shift = column_mean(lefts[half])
        sums = [jnp.zeros((8, quart), jnp.float32)] * 3
        for block in range(3):
            source = lefts[2 * block + half]
            for at in range(0, rows, 64):
                centred = source[at : at + 64, :].astype(jnp.float32) - shift
                low = centred.astype(jnp.bfloat16)
                low_left[block * rows + at : block * rows + at + 64, lanes] = low
                if block == 0:
                    (zero_own, zero_other)[half][at : at + 64, :] = low
                if half:
                    sums = add_sums(sums, centred, low)
        if half:
            row_other[...] = rows_of([shift] + [jnp.sum(s, axis=0, keepdims=True) for s in sums])
    for half in range(2):
        lanes = slice(half * quart, (half + 1) * quart)
        shift = column_mean(rights[half])
        for block in range(3):
            source = rights[2 * block + half]
            for at in range(0, rows, 128):
                low = (source[at : at + 128, :].astype(jnp.float32) - shift).astype(jnp.bfloat16)
                low_right[lanes, block * rows + at : block * rows + at + 128] = jnp.transpose(low)
    for tile in range(4):
        wide = slice(tile * width, (tile + 1) * width)
        inner = slice((tile % 2) * width, (tile % 2 + 1) * width)
        target = partner_own if tile < 2 else partner_other
        target[:, inner] = dot(low_right[quart:, :], low_left[:, wide])
        own_all[:, wide] = dot(low_right[:quart, :], low_left[:, wide])


def left_operand(zero, stats, target, lanes):
    rows, quart = zero.shape
    _, _, gap, delta = stats_rows(stats)
    high, middle, _ = three_parts(delta)
    target[:rows, lanes] = zero[...]
    extra = [high.astype(jnp.float32), middle.astype(jnp.float32), gap]
    pad = jnp.zeros((13, quart), jnp.float32)
    target[rows:, lanes] = jnp.concatenate([*extra, pad], axis=0).astype(jnp.bfloat16)


def without_extra(terms, rows):
    return terms[:rows] - (terms[rows : rows + 1] + terms[rows + 1 : rows + 2] + terms[rows + 2 : rows + 3])


def scale_columns(late_b, images):
    _, rstd, _, delta = right_stats(late_b)
    columns = jnp.transpose(rows_of([rstd / images, delta * rstd]))
    return columns[:, 0:1], columns[:, 1:2]


def partner_kernel(images, part, late, stats, zero, sums, late_b_0, late_b_1, *refs):
    if part:
        (terms_in, across_in, vec_in, columns, first_b) = refs[:5]
        (partial_out, e_out, vec_out, left) = refs[5:]
    else:
        (terms_out, across_out, e_out, vec_out, columns, left) = refs
        _, rstd_b, _, delta_b = right_stats((late_b_0, late_b_1))
        columns[...] = jnp.transpose(rows_of([rstd_b / images, delta_b * rstd_b]))
    late_b = (late_b_0, late_b_1)
    rows, quart = zero.shape
    width = quart // 2
    _, rstd, _, delta = stats_rows(stats)
    left_operand(zero, stats, left, slice(0, quart))
    scale_col, delta_col = columns[:, 0:1], columns[:, 1:2]
    across = across_in[...] if part else jnp.zeros((quart, 128), jnp.float32)
    down = []
    for tile in range(2):
        at = slice(tile * width, (tile + 1) * width)
        total = sums[:, at] + late_products(late_b, late, at)
        corr = (total * scale_col - delta_col * delta[:, at]) * rstd[:, at]
        e_out[:, at] = (corr * (off_weight * rstd[:, at])).astype(jnp.bfloat16)
        square = corr * corr
        across = across + fold_lanes(square)
        down.append(jnp.sum(square, axis=0, keepdims=True))
    second_a = off_weight * jnp.concatenate(down, axis=1)
    if part:
        vec_out[...] = rows_of([second_a, second_a + vec_in[0:1, :]])
        second = off_weight * lanes_to_row(across)
        offset_b, rstd_b, _, _ = right_stats(late_b)
    else:
        vec_out[...] = rows_of([second_a])
        across_out[...] = across
    for tile in range(2):
        at = slice(tile * width, (tile + 1) * width)
        terms = dot_rows(left[...], e_out[at, :])
        if part:
            xhat = (first_b[:, at].astype(jnp.float32) - offset_b[:, at]) * rstd_b[:, at]
            partial_out[:, at] = (
                without_extra(terms + terms_in[:, at], rows) - xhat * second[:, at]
            ).astype(jnp.bfloat16)
        else:
            terms_out[:, at] = terms


def own_kernel(images, flags, *refs):
    late_b, late_b_other = refs[:2], refs[2:4]
    (left_own, left_other), refs = refs[4:6], refs[6:]
    (late_own, late_other, first_own, first_other, zero_own, zero_other, sums) = refs[:7]
    (first_b, first_b_other, e_left, e_right, partner_own, partner_other) = refs[7:13]
    (vec_own, vec_other, right_out, left_out, *left_partials_out, mine_out) = refs[13:20]
    (loss_out, left, norm_b, e_own, mine_own, mine_partner) = refs[20:]
    rows, quart = zero_own.shape
    width = quart // 2
    lower, upper = slice(0, quart), slice(quart, 2 * quart)
    stats_own, stats_other = stats_rows(left_own), stats_rows(left_other)
    both = lambda i: jnp.concatenate([stats_own[i], stats_other[i]], axis=1)
    offset, rstd, _, delta = [both(i) for i in range(4)]
    left_operand(zero_own, left_own, left, lower)
    left_operand(zero_other, left_other, left, upper)
    own_b = right_stats(late_b)
    other_b = right_stats(late_b_other)
    for source, stats, lanes in ((first_b, own_b, lower), (first_b_other, other_b, upper)):
        for at in range(0, rows, 64):
            piece = slice(at, at + 64)
            norm_b[piece, lanes] = (
                (source[piece, :].astype(jnp.float32) - stats[0]) * stats[1]
            ).astype(jnp.bfloat16)
        rest = jnp.broadcast_to(stats[2] * stats[1], (16, quart))
        norm_b[rows:, lanes] = rest.astype(jnp.bfloat16)

    def tile_corr(late, inner, total, columns, block):
        scale_col, delta_col = columns
        total = total + late_products(block, late, inner)
        row = stats_own if late is late_own else stats_other
        return (total * scale_col - delta_col * row[3][:, inner]) * row[1][:, inner]

    columns = scale_columns(late_b, images)
    columns_partner = scale_columns(late_b_other, images)
    across = jnp.zeros((quart, 128), jnp.float32)
    losses = jnp.zeros((8, 128), jnp.float32)
    down, diagonals = [], []
    for tile in range(4):
        at = slice(tile * width, (tile + 1) * width)
        inner = slice((tile % 2) * width, (tile % 2 + 1) * width)
        late = late_own if tile < 2 else late_other
        corr = tile_corr(late, inner, sums[:, at], columns, late_b)
        dcorr = off_weight * corr
        product = dcorr * corr
        loss = product
        if tile < 2:
            feature = lax.broadcasted_iota(jnp.int32, (quart, width), 0)
            lane = lax.broadcasted_iota(jnp.int32, (quart, width), 1) + tile * width
            diagonal = feature == lane
            slope = jnp.where(diagonal, (corr - 1.0).astype(jnp.bfloat16).astype(jnp.float32), 0.0)
            diagonals.append(jnp.sum(slope, axis=0, keepdims=True))
            dcorr = jnp.where(diagonal, 0.0, dcorr)
            product = jnp.where(diagonal, slope * corr, product)
            loss = jnp.where(diagonal, (1.0 - corr) * (1.0 - corr), loss)
        e_own[:, at] = (dcorr * rstd[:, at]).astype(jnp.bfloat16)
        across = across + fold_lanes(product)
        losses = losses + fold_rows(fold_lanes(loss))
        down.append(jnp.sum(product, axis=0, keepdims=True))

        @pl.when(flags[0] == tile)
        def _():
            mine_own[...] = corr
            partner = partner_own if tile < 2 else partner_other
            mine_partner[...] = tile_corr(
                late, inner, partner[:, inner], columns_partner, late_b_other
            )

    diagonal_row = jnp.concatenate(diagonals, axis=1)
    partner_second = jnp.concatenate([vec_own[0:1, :], vec_other[0:1, :]], axis=1)
    second_a = rstd * (partner_second + jnp.concatenate(down, axis=1))
    second_b = lanes_to_row(across)
    loss = jnp.sum(losses) + jnp.sum(vec_other[1:2, :])
    loss_out[...] = jnp.broadcast_to(loss, (8, 128))

    for tile in (2, 3, 0, 1):
        at = slice(tile * width, (tile + 1) * width)
        inner = slice((tile % 2) * width, (tile % 2 + 1) * width)
        source, e_partner = (first_own, e_left) if tile < 2 else (first_other, e_right)
        terms = dot(norm_b[:, lower], e_own[:, at]) + dot(norm_b[:, upper], e_partner[:, inner])
        xhat = (source[:, inner].astype(jnp.float32) - offset[:, at]) * rstd[:, at]
        value = terms[:rows] - terms[rows : rows + 1] - xhat * second_a[:, at]
        if tile < 2:
            slope = rstd[:, at] * diagonal_row[:, inner]
            left_out[:, inner] = value + norm_b[:rows, inner].astype(jnp.float32) * slope
        else:
            for half, out in enumerate(left_partials_out):
                some = out.shape[0]
                out[:, inner] = value[half * some : (half + 1) * some].astype(jnp.bfloat16)

    for tile in range(2):
        at = slice(tile * width, (tile + 1) * width)
        terms = dot_rows(left[...], e_own[at, :])
        xhat = (first_b[:, at].astype(jnp.float32) - own_b[0][:, at]) * own_b[1][:, at]
        norm_a = (first_own[:, at].astype(jnp.float32) - offset[:, at]) * rstd[:, at]
        norm_a = norm_a.astype(jnp.bfloat16).astype(jnp.float32)
        right_out[:, at] = (
            without_extra(terms, rows) - xhat * second_b[:, at] + norm_a * diagonal_row[:, at]
        )

    own_columns = jnp.transpose(mine_own[...])
    partner_columns = jnp.transpose(mine_partner[...])

    @pl.when(flags[1] == 0)
    def _():
        mine_out[:, lower] = own_columns
        mine_out[:, upper] = partner_columns

    @pl.when(flags[1] != 0)
    def _():
        mine_out[:, lower] = partner_columns
        mine_out[:, upper] = own_columns


def add_kernel(one, other, out):
    out[...] = one[...] + other[...]


def loss_kernel(feats, one, other, out):
    out[0] = (one[0, 0] + other[0, 0]) / feats


def left_final_kernel(left, from_core_0, from_core_1, left_out):
    some = from_core_0.shape[0]
    for half, from_core in enumerate((from_core_0, from_core_1)):
        for at in range(0, some, 64):
            piece = slice(half * some + at, half * some + at + 64)
            value = left[piece, :] + from_core[at : at + 64, :].astype(jnp.float32)
            left_out[piece, :] = value.astype(jnp.bfloat16)


def right_final_kernel(right, from_x, late_b_0, late_b_1, right_out):
    rstd = right_stats((late_b_0, late_b_1))[1]
    for at in range(0, right.shape[0], 64):
        piece = slice(at, at + 64)
        value = rstd * (right[piece, :] + from_x[piece, :].astype(jnp.float32))
        right_out[piece, :] = value.astype(jnp.bfloat16)


vmem = pl.BlockSpec(memory_space=pltpu.VMEM)
smem = pl.BlockSpec(memory_space=pltpu.SMEM)


def local_call(kernel, operands, outs, scratch=(), flops=2**20, room=8, held=(), moved=None):
    if moved is None:
        moved = sum(x.size * x.dtype.itemsize for x in (*operands, *outs))

    def space(x):
        return smem if x.ndim == 1 else vmem

    return pl.pallas_call(
        kernel,
        out_shape=list(outs),
        in_specs=[space(x) for x in operands],
        out_specs=[space(x) for x in outs],
        scratch_shapes=list(scratch),
        compiler_params=pltpu.CompilerParams(vmem_limit_bytes=room * 2**20),
        cost_estimate=pl.CostEstimate(flops=flops, bytes_accessed=moved, transcendentals=0),
    )(*(pltpu.with_memory_space_constraint(x, pltpu.VMEM) if i in held else x for i, x in enumerate(operands)))


def gathered_device(left_outputs, right_outputs):
    rows, quart = left_outputs.shape
    half = 2 * quart
    feats = 4 * quart
    batch_images = rows * 4
    tpos = lax.axis_index("tile")
    dpos = lax.axis_index("dp")
    row_halves = tpos // 2
    column_halves = tpos % 2
    at_end = (dpos == 0) | (dpos == 3)
    owned_tile = jnp.where(dpos // 2 == column_halves, 0, 2) + dpos % 2
    flags = jnp.stack([owned_tile, row_halves]).astype(jnp.int32)
    mask = jnp.broadcast_to(at_end.astype(jnp.float32), (8, quart))

    pairs = [(0, 1), (1, 0), (2, 3), (3, 2)]
    middle = [(1, 2), (2, 1)]
    outward = [(1, 0), (2, 3)]

    def along(block, route):
        return lax.ppermute(block, "dp", route)

    def core_swap(block):
        return swapped(block, "tile", 0)

    def x_swap(block):
        return swapped(block, "tile", 1)

    def after(value, *others):
        return lax.optimization_barrier((value, *others))

    gemm = 2 * rows * quart * quart
    width = quart // 2
    quarter_f32 = jax.ShapeDtypeStruct((rows, quart), jnp.float32)
    quarter_bf16 = jax.ShapeDtypeStruct((rows, quart), jnp.bfloat16)
    extended = jax.ShapeDtypeStruct((rows + 16, quart), jnp.bfloat16)
    row_out = jax.ShapeDtypeStruct((8, quart), jnp.float32)
    one_out = jax.ShapeDtypeStruct((8, 128), jnp.float32)
    across_shape = jax.ShapeDtypeStruct((quart, 128), jnp.float32)
    low = lambda n, m: pltpu.VMEM((n, m), jnp.bfloat16)

    def picked(outer, inner):
        return local_call(pick_kernel, (mask, outer, inner), (quarter_bf16,))[0]

    some = rows // 2
    half_block = jax.ShapeDtypeStruct((some, quart), jnp.bfloat16)
    first_b = along(right_outputs, pairs)
    inner_b = along(right_outputs, middle)
    first_a = along(left_outputs, pairs)
    other_b0 = x_swap(right_outputs)
    other_a0, mask, flags = after(core_swap(left_outputs), mask, flags)
    left_behind, first_a, other_a0 = after(left_outputs, first_a, other_a0)
    inner_a = along(left_behind, middle)

    outer_b = along(inner_b, outward)
    third_b = along(first_b, middle)
    ready_b, other_b0 = after(first_b, other_b0)
    other_b1 = x_swap(ready_b)
    outer_a = along(inner_a, outward)
    third_a = along(first_a, middle)
    other_a1 = core_swap(first_a)

    third_b = local_call(halves_kernel, (third_b,), (half_block, half_block))
    last_b = [along(x, outward) for x in third_b]
    second_b = picked(outer_b, inner_b)
    row_b = local_call(right_sums_kernel, (right_outputs, first_b, second_b), (row_out,))[0]
    second_b, other_b1, other_a1 = after(second_b, other_b1, other_a1)
    other_b2 = x_swap(second_b)
    last_a = along(third_a, outward)
    second_a = picked(outer_a, inner_a)
    second_a, row_b = after(second_a, row_b)
    other_a2 = core_swap(second_a)

    late_b_0, row_b = local_call(
        functools.partial(late_right_kernel, batch_images, False),
        (mask, last_b[0], third_b[0], row_b),
        (jax.ShapeDtypeStruct((quart, some), jnp.bfloat16), row_out),
        held=(0, 1, 2, 3),
    )
    late_b_other_0 = x_swap(late_b_0)
    (late_b_1,) = local_call(
        functools.partial(late_right_kernel, batch_images, True),
        (mask, last_b[1], third_b[1], row_b),
        (jax.ShapeDtypeStruct((quart + 16 * (quart // some), some), jnp.bfloat16),),
        held=(0, 1, 2, 3),
    )
    late_b_other_1 = x_swap(late_b_1)
    late_b = (late_b_0, late_b_1)
    other_b2, late_b_1, late_b_other_0 = after(other_b2, late_b_1, late_b_other_0)
    partner_own, partner_other, own_all, row_other, zero_own, zero_other = local_call(
        products_kernel,
        (left_outputs, other_a0, first_a, other_a1, second_a, other_a2)
        + (right_outputs, other_b0, first_b, other_b1, second_b, other_b2),
        (
            quarter_f32,
            quarter_f32,
            jax.ShapeDtypeStruct((quart, half), jnp.float32),
            row_out,
            quarter_bf16,
            quarter_bf16,
        ),
        [low(3 * rows, half), low(half, 3 * rows)],
        room=20,
        moved=2**16,
    )
    row_a, late_b_other_1 = after(core_swap(row_other), late_b_other_1)
    late_b_other = (late_b_other_0, late_b_other_1)
    operands = (mask, last_a, third_a, row_a)
    (late_a,) = local_call(late_left_kernel, operands, (quarter_bf16,), held=(0, 1, 2, 3))
    late_a_other = core_swap(late_a)
    (stats_a,) = local_call(
        functools.partial(left_stats_kernel, batch_images), operands, (row_out,), held=(0, 1, 2, 3)
    )
    stats_a_other = core_swap(stats_a)

    terms, across, e_left, vec_own, columns = local_call(
        functools.partial(partner_kernel, batch_images, 0),
        (late_a, stats_a, zero_own, partner_own, *late_b_other),
        (
            jax.ShapeDtypeStruct((rows + 16, quart), jnp.float32),
            across_shape,
            quarter_bf16,
            row_out,
            jax.ShapeDtypeStruct((quart, 8), jnp.float32),
        ),
        [low(rows + 16, quart)],
        2 * gemm,
        room=12,
    )
    partial_right, e_right, vec_other = local_call(
        functools.partial(partner_kernel, batch_images, 1),
        (late_a_other, stats_a_other, zero_other, partner_other, *late_b_other)
        + (terms, across, vec_own, columns, other_b0),
        (quarter_bf16, quarter_bf16, row_out),
        [low(rows + 16, quart)],
        2 * gemm,
        room=12,
    )
    from_x = x_swap(partial_right)
    right_own, left_own, *partials_left, mine, loss = local_call(
        functools.partial(own_kernel, batch_images),
        (flags, *late_b, *late_b_other, stats_a, stats_a_other)
        + (late_a, late_a_other, left_outputs, other_a0, zero_own, zero_other, own_all)
        + (right_outputs, other_b0, e_left, e_right)
        + (partner_own, partner_other)
        + (vec_own, vec_other),
        (
            quarter_f32,
            quarter_f32,
            half_block,
            half_block,
            jax.ShapeDtypeStruct((width, half), jnp.float32),
            one_out,
        ),
        [
            low(rows + 16, half),
            low(rows + 16, half),
            low(quart, half),
            pltpu.VMEM((quart, width), jnp.float32),
            pltpu.VMEM((quart, width), jnp.float32),
        ],
        8 * gemm,
        room=20,
    )
    from_core = [core_swap(x) for x in partials_left]
    core_loss = core_swap(loss)
    (loss,) = local_call(add_kernel, (loss, core_loss), (one_out,))
    x_loss = x_swap(loss)
    (left_gradient,) = local_call(left_final_kernel, (left_own, *from_core), (quarter_bf16,))
    right_own, left_gradient = after(right_own, left_gradient)
    (right_gradient,) = local_call(right_final_kernel, (right_own, from_x, *late_b), (quarter_bf16,))
    right_gradient, x_loss = after(right_gradient, x_loss)
    (loss,) = local_call(
        functools.partial(loss_kernel, feats),
        (loss, x_loss),
        (jax.ShapeDtypeStruct((1,), jnp.float32),),
    )
    return (left_gradient, right_gradient, mine[None, :, :], loss)


def solution(mesh):
    per_device = gathered_device if mesh.shape["dp"] == 4 else reduced_device
    return jax.shard_map(
        per_device,
        mesh=mesh,
        in_specs=(P(("groups", "dp"), "tile"), P(("groups", "dp"), "tile")),
        out_specs=(
            P(("groups", "dp"), "tile"),
            P(("groups", "dp"), "tile"),
            P(("groups", "tile"), "dp", None),
            P("groups"),
        ),
        check_vma=False,
    )
```

```python
import functools
import jax
import jax.numpy as jnp
from jax import lax
from jax.experimental import pallas as pl
from jax.experimental.pallas import tpu as pltpu
from jax.sharding import PartitionSpec as P

off_weight = 0.0051


def swapped(block, axis, bit):
    count = lax.axis_size(axis)
    route = []
    for low in range(count):
        high = low | 1 << bit
        if high != low and high < count:
            route += [(low, high), (high, low)]
    return lax.ppermute(block, axis, route)


def pair_views(first_moment, second_moment, row_halves, column_halves):
    other_a = swapped(first_moment, "tile", 0)
    other_b = swapped(second_moment, "tile", 1)
    joined_a = jnp.where(
        column_halves == 0,
        jnp.concatenate([first_moment, other_a], axis=1),
        jnp.concatenate([other_a, first_moment], axis=1),
    )
    joined_b = jnp.where(
        row_halves == 0,
        jnp.concatenate([second_moment, other_b], axis=1),
        jnp.concatenate([other_b, second_moment], axis=1),
    )
    return (joined_a, joined_b)


def moment_pair(total, squares, batch_images):
    column_mean = total / batch_images
    var = squares / batch_images - column_mean * column_mean
    return (column_mean, lax.rsqrt(var + 1e-05))


def col_sums(values):
    as_float = values.astype(jnp.float32)
    return (jnp.sum(as_float, axis=0), jnp.sum(as_float * as_float, axis=0))


def reduced_device(left_outputs, right_outputs):
    rows, quart = left_outputs.shape
    half = 2 * quart
    feats = 4 * quart
    dp_count = lax.axis_size("dp")
    batch_images = rows * dp_count
    tpos = lax.axis_index("tile")
    row_halves = tpos // 2
    column_halves = tpos % 2
    sum_a, sq_a = col_sums(left_outputs)
    sum_b, sq_b = col_sums(right_outputs)
    sum_a, sq_a, sum_b, sq_b = lax.psum((sum_a, sq_a, sum_b, sq_b), "dp")
    left_mean, left_inverse_deviation = moment_pair(sum_a, sq_a, batch_images)
    right_mean, right_inverse_deviation = moment_pair(sum_b, sq_b, batch_images)
    standardized_left = (left_outputs.astype(jnp.float32) - left_mean) * left_inverse_deviation
    standardized_right = (right_outputs.astype(jnp.float32) - right_mean) * right_inverse_deviation
    half_a, cols_b = pair_views(
        standardized_left.astype(jnp.bfloat16),
        standardized_right.astype(jnp.bfloat16),
        row_halves,
        column_halves,
    )
    col_local = jnp.arange(half, dtype=jnp.int32)
    col_ids = quart * column_halves + col_local + jnp.where(col_local >= quart, quart, 0)
    owned = half // dp_count
    picked = half_a
    corr_rows = (
        lax.psum_scatter(
            lax.dot_general(
                picked, cols_b, (((0,), (0,)), ((), ())), preferred_element_type=jnp.float32
            ),
            "dp",
            scatter_dimension=0,
            tiled=True,
        )
        / batch_images
    )
    row_ids = half * row_halves + lax.axis_index("dp") * owned + jnp.arange(owned, dtype=jnp.int32)
    diagonal = row_ids[:, None] == col_ids[None, :]
    part_loss = jnp.sum(
        jnp.where(diagonal, (1.0 - corr_rows) ** 2, off_weight * corr_rows * corr_rows)
    )
    loss = lax.psum(part_loss, ("dp", "tile")) / feats
    dcorr_part = jnp.where(diagonal, corr_rows - 1.0, off_weight * corr_rows).astype(jnp.bfloat16)
    piece = lax.all_gather(dcorr_part, "dp", axis=0, tiled=True)
    block_a = lax.dot_general(
        cols_b, piece, (((1,), (1,)), ((), ())), preferred_element_type=jnp.float32
    )
    picked = half_a
    into_b = jnp.dot(picked, piece, preferred_element_type=jnp.float32)
    other_a = swapped(block_a.astype(jnp.bfloat16), "tile", 0).astype(block_a.dtype)
    other_b = swapped(into_b.astype(jnp.bfloat16), "tile", 1).astype(into_b.dtype)
    normed_grad_left = lax.dynamic_slice_in_dim(block_a + other_a, column_halves * quart, quart, 1)
    normed_grad_right = lax.dynamic_slice_in_dim(into_b + other_b, row_halves * quart, quart, 1)
    first_moment_left, second_moment_left, first_moment_right, second_moment_right = lax.psum(
        (
            jnp.sum(normed_grad_left, axis=0),
            jnp.sum(normed_grad_left * standardized_left, axis=0),
            jnp.sum(normed_grad_right, axis=0),
            jnp.sum(normed_grad_right * standardized_right, axis=0),
        ),
        "dp",
    )
    left_gradient = (
        left_inverse_deviation
        * (
            normed_grad_left
            - first_moment_left / batch_images
            - standardized_left * (second_moment_left / batch_images)
        )
    ).astype(jnp.bfloat16)
    right_gradient = (
        right_inverse_deviation
        * (
            normed_grad_right
            - first_moment_right / batch_images
            - standardized_right * (second_moment_right / batch_images)
        )
    ).astype(jnp.bfloat16)
    return (left_gradient, right_gradient, corr_rows[None, :, :], jnp.reshape(loss, (1,)))


def fold_rows(values):
    rows, width = values.shape
    return jnp.sum(values.reshape(rows // 8, 8, width), axis=0)


def fold_lanes(values):
    return sum(values[:, at : at + 128] for at in range(0, values.shape[1], 128))


def column_mean(block):
    rows, width = block.shape
    folded = jnp.zeros((8, width), jnp.float32)
    for at in range(0, rows, 64):
        folded = folded + fold_rows(block[at : at + 64, :].astype(jnp.float32))
    return jnp.sum(folded, axis=0, keepdims=True) / rows


def add_sums(sums, centred, low):
    return [
        sums[0] + fold_rows(centred),
        sums[1] + fold_rows(centred * centred),
        sums[2] + fold_rows(low.astype(jnp.float32)),
    ]


def rows_of(values):
    pad = jnp.zeros((8 - len(values), values[0].shape[1]), jnp.float32)
    return jnp.concatenate([*values, pad], axis=0)


def joined_sums(row, sums):
    return [row[i + 1 : i + 2, :] + jnp.sum(s, axis=0, keepdims=True) for i, s in enumerate(sums)]


def moments(sums, images):
    total, squares, rounded = sums
    delta = total / images
    return delta, lax.rsqrt(squares / images - delta * delta + 1e-05), rounded / images - delta


def three_parts(row):
    high = row.astype(jnp.bfloat16)
    rest = row - high.astype(jnp.float32)
    middle = rest.astype(jnp.bfloat16)
    low = (rest - middle.astype(jnp.float32)).astype(jnp.bfloat16)
    return [high, middle, low]


def split_rows(values):
    parts = sum([three_parts(v) for v in values], [])
    pad = jnp.zeros((4, values[0].shape[1]), jnp.float32)
    return jnp.concatenate([*(p.astype(jnp.float32) for p in parts), pad], axis=0).astype(
        jnp.bfloat16
    )


def joined_rows(ref, at):
    parts = ref[at : at + 16, :].astype(jnp.float32)
    part = lambda i: parts[i : i + 1]
    return [part(3 * i) + part(3 * i + 1) + part(3 * i + 2) for i in range(4)]


def lanes_to_row(partial):
    ones = jnp.ones((16, partial.shape[1]), jnp.bfloat16)
    high = partial.astype(jnp.bfloat16)
    low = (partial - high.astype(jnp.float32)).astype(jnp.bfloat16)
    row = dot_rows(ones, high) + dot_rows(ones, low)
    return row[:1, :]


def dot_rows(left, right):
    return lax.dot_general(
        left, right, (((1,), (1,)), ((), ())), preferred_element_type=jnp.float32
    )


def dot(left, right):
    return jnp.dot(left, right, preferred_element_type=jnp.float32)


def pick(mask, outer, inner, piece):
    return jnp.where(
        mask[0:1, :] != 0.0, outer[piece, :].astype(jnp.float32), inner[piece, :].astype(jnp.float32)
    )


def pick_kernel(mask, outer, inner, out):
    for at in range(0, outer.shape[0], 64):
        piece = slice(at, at + 64)
        out[piece, :] = pick(mask, outer, inner, piece).astype(out.dtype)


def right_sums_kernel(first, second, third, row):
    rows, quart = first.shape
    shift = column_mean(first)
    sums = [jnp.zeros((8, quart), jnp.float32)] * 3
    for block in (first, second, third):
        for at in range(0, rows, 64):
            centred = block[at : at + 64, :].astype(jnp.float32) - shift
            sums = add_sums(sums, centred, centred.astype(jnp.bfloat16))
    row[...] = rows_of([shift] + [jnp.sum(s, axis=0, keepdims=True) for s in sums])


def halves_kernel(block, first, second):
    half = first.shape[0]
    first[...] = block[:half, :]
    second[...] = block[half:, :]


def late_left_kernel(mask, outer, inner, row, out):
    for at in range(0, out.shape[0], 64):
        piece = slice(at, at + 64)
        out[piece, :] = (pick(mask, outer, inner, piece) - row[0:1, :]).astype(out.dtype)


def left_stats_kernel(images, mask, outer, inner, row, stats):
    rows, quart = outer.shape
    shift = row[0:1, :]
    sums = [jnp.zeros((8, quart), jnp.float32)] * 3
    for at in range(0, rows, 64):
        centred = pick(mask, outer, inner, slice(at, at + 64)) - shift
        sums = add_sums(sums, centred, centred.astype(jnp.bfloat16))
    delta, rstd, gap = moments(joined_sums(row, sums), images)
    stats[...] = rows_of([shift + delta, rstd, gap, delta])


def stats_rows(stats):
    return [stats[i : i + 1, :] for i in range(4)]


def late_right_kernel(images, last, mask, outer, inner, row, out, *rest):
    some, quart = outer.shape
    shift = row[0:1, :]
    sums = [jnp.zeros((8, quart), jnp.float32)] * 3
    for at in range(0, some, 128):
        piece = slice(at, at + 128)
        centred = pick(mask, outer, inner, piece) - shift
        low = centred.astype(jnp.bfloat16)
        out[:quart, piece] = jnp.transpose(low)
        sums = add_sums(sums, centred, low)
    sums = joined_sums(row, sums)
    if not last:
        (row_out,) = rest
        row_out[...] = rows_of([shift, *sums])
        return
    delta, rstd, gap = moments(sums, images)
    parts = split_rows([shift + delta, rstd, gap, delta])
    for i in range(quart // some):
        below = quart + 16 * i
        out[below : below + 16, :] = parts[:, i * some : (i + 1) * some]


def right_stats(late):
    quart, some = late[0].shape
    found = [joined_rows(late[1], quart + 16 * i) for i in range(quart // some)]
    return [jnp.concatenate(values, axis=1) for values in zip(*found)]


def late_products(right, left, lanes):
    quart, some = right[0].shape
    first = dot(right[0][...], left[:some, lanes])
    return first + dot(right[1][:quart, :], left[some : 2 * some, lanes])


def products_kernel(*refs):
    lefts, rights = refs[0:6], refs[6:12]
    partner_own, partner_other, own_all, row_other, zero_own, zero_other = refs[12:18]
    low_left, low_right = refs[18:]
    rows, quart = lefts[0].shape
    width = quart // 2
    for half in range(2):
        lanes = slice(half * quart, (half + 1) * quart)
        shift = column_mean(lefts[half])
        sums = [jnp.zeros((8, quart), jnp.float32)] * 3
        for block in range(3):
            source = lefts[2 * block + half]
            for at in range(0, rows, 64):
                centred = source[at : at + 64, :].astype(jnp.float32) - shift
                low = centred.astype(jnp.bfloat16)
                low_left[block * rows + at : block * rows + at + 64, lanes] = low
                if block == 0:
                    (zero_own, zero_other)[half][at : at + 64, :] = low
                if half:
                    sums = add_sums(sums, centred, low)
        if half:
            row_other[...] = rows_of([shift] + [jnp.sum(s, axis=0, keepdims=True) for s in sums])
    for half in range(2):
        lanes = slice(half * quart, (half + 1) * quart)
        shift = column_mean(rights[half])
        for block in range(3):
            source = rights[2 * block + half]
            for at in range(0, rows, 128):
                low = (source[at : at + 128, :].astype(jnp.float32) - shift).astype(jnp.bfloat16)
                low_right[lanes, block * rows + at : block * rows + at + 128] = jnp.transpose(low)
    for tile in range(4):
        wide = slice(tile * width, (tile + 1) * width)
        inner = slice((tile % 2) * width, (tile % 2 + 1) * width)
        target = partner_own if tile < 2 else partner_other
        target[:, inner] = dot(low_right[quart:, :], low_left[:, wide])
        own_all[:, wide] = dot(low_right[:quart, :], low_left[:, wide])


def left_operand(zero, stats, target, lanes):
    rows, quart = zero.shape
    _, _, gap, delta = stats_rows(stats)
    high, middle, _ = three_parts(delta)
    target[:rows, lanes] = zero[...]
    extra = [high.astype(jnp.float32), middle.astype(jnp.float32), gap]
    pad = jnp.zeros((13, quart), jnp.float32)
    target[rows:, lanes] = jnp.concatenate([*extra, pad], axis=0).astype(jnp.bfloat16)


def without_extra(terms, rows):
    return terms[:rows] - (terms[rows : rows + 1] + terms[rows + 1 : rows + 2] + terms[rows + 2 : rows + 3])


def scale_columns(late_b, images):
    _, rstd, _, delta = right_stats(late_b)
    columns = jnp.transpose(rows_of([rstd / images, delta * rstd]))
    return columns[:, 0:1], columns[:, 1:2]


def right_columns_kernel(images, late_b_0, late_b_1, columns, rows_b):
    offset, rstd, gap, delta = right_stats((late_b_0, late_b_1))
    columns[...] = jnp.transpose(rows_of([rstd / images, delta * rstd]))
    rows_b[...] = rows_of([offset, rstd, gap, delta])


def partner_kernel(images, part, late, stats, zero, sums, late_b_0, late_b_1, columns, rows_b, *refs):
    if part:
        (terms_in, across_in, vec_in, first_b) = refs[:4]
        (partial_out, e_out, vec_out, left) = refs[4:]
    else:
        (terms_out, across_out, e_out, vec_out, left) = refs
    late_b = (late_b_0, late_b_1)
    rows, quart = zero.shape
    width = quart // 2
    _, rstd, _, delta = stats_rows(stats)
    left_operand(zero, stats, left, slice(0, quart))
    scale_col, delta_col = columns[:, 0:1], columns[:, 1:2]
    across = across_in[...] if part else jnp.zeros((quart, 128), jnp.float32)
    down = []
    for tile in range(2):
        at = slice(tile * width, (tile + 1) * width)
        total = sums[:, at] + late_products(late_b, late, at)
        corr = (total * scale_col - delta_col * delta[:, at]) * rstd[:, at]
        e_out[:, at] = (corr * (off_weight * rstd[:, at])).astype(jnp.bfloat16)
        square = corr * corr
        across = across + fold_lanes(square)
        down.append(jnp.sum(square, axis=0, keepdims=True))
    second_a = off_weight * jnp.concatenate(down, axis=1)
    if part:
        vec_out[...] = rows_of([second_a, second_a + vec_in[0:1, :]])
        second = off_weight * lanes_to_row(across)
        offset_b, rstd_b, _, _ = stats_rows(rows_b)
    else:
        vec_out[...] = rows_of([second_a])
        across_out[...] = across
    for tile in range(2):
        at = slice(tile * width, (tile + 1) * width)
        terms = dot_rows(left[...], e_out[at, :])
        if part:
            xhat = (first_b[:, at].astype(jnp.float32) - offset_b[:, at]) * rstd_b[:, at]
            partial_out[:, at] = (
                without_extra(terms + terms_in[:, at], rows) - xhat * second[:, at]
            ).astype(jnp.bfloat16)
        else:
            terms_out[:, at] = terms


def own_kernel(images, flags, *refs):
    late_b, late_b_other = refs[:2], refs[2:4]
    (left_own, left_other), refs = refs[4:6], refs[6:]
    (late_own, late_other, first_own, first_other, zero_own, zero_other, sums) = refs[:7]
    (first_b, first_b_other, e_left, e_right, partner_own, partner_other) = refs[7:13]
    (vec_own, vec_other, right_out, left_out, *left_partials_out, mine_out) = refs[13:20]
    (loss_out, left, norm_b, e_own, mine_own, mine_partner) = refs[20:]
    rows, quart = zero_own.shape
    width = quart // 2
    lower, upper = slice(0, quart), slice(quart, 2 * quart)
    stats_own, stats_other = stats_rows(left_own), stats_rows(left_other)
    both = lambda i: jnp.concatenate([stats_own[i], stats_other[i]], axis=1)
    offset, rstd, _, delta = [both(i) for i in range(4)]
    left_operand(zero_own, left_own, left, lower)
    left_operand(zero_other, left_other, left, upper)
    own_b = right_stats(late_b)
    other_b = right_stats(late_b_other)
    for source, stats, lanes in ((first_b, own_b, lower), (first_b_other, other_b, upper)):
        for at in range(0, rows, 64):
            piece = slice(at, at + 64)
            norm_b[piece, lanes] = (
                (source[piece, :].astype(jnp.float32) - stats[0]) * stats[1]
            ).astype(jnp.bfloat16)
        rest = jnp.broadcast_to(stats[2] * stats[1], (16, quart))
        norm_b[rows:, lanes] = rest.astype(jnp.bfloat16)

    def tile_corr(late, inner, total, columns, block):
        scale_col, delta_col = columns
        total = total + late_products(block, late, inner)
        row = stats_own if late is late_own else stats_other
        return (total * scale_col - delta_col * row[3][:, inner]) * row[1][:, inner]

    columns = scale_columns(late_b, images)
    columns_partner = scale_columns(late_b_other, images)
    across = jnp.zeros((quart, 128), jnp.float32)
    losses = jnp.zeros((8, 128), jnp.float32)
    down, diagonals = [], []
    for tile in range(4):
        at = slice(tile * width, (tile + 1) * width)
        inner = slice((tile % 2) * width, (tile % 2 + 1) * width)
        late = late_own if tile < 2 else late_other
        corr = tile_corr(late, inner, sums[:, at], columns, late_b)
        dcorr = off_weight * corr
        product = dcorr * corr
        loss = product
        if tile < 2:
            feature = lax.broadcasted_iota(jnp.int32, (quart, width), 0)
            lane = lax.broadcasted_iota(jnp.int32, (quart, width), 1) + tile * width
            diagonal = feature == lane
            slope = jnp.where(diagonal, (corr - 1.0).astype(jnp.bfloat16).astype(jnp.float32), 0.0)
            diagonals.append(jnp.sum(slope, axis=0, keepdims=True))
            dcorr = jnp.where(diagonal, 0.0, dcorr)
            product = jnp.where(diagonal, slope * corr, product)
            loss = jnp.where(diagonal, (1.0 - corr) * (1.0 - corr), loss)
        e_own[:, at] = (dcorr * rstd[:, at]).astype(jnp.bfloat16)
        across = across + fold_lanes(product)
        losses = losses + fold_rows(fold_lanes(loss))
        down.append(jnp.sum(product, axis=0, keepdims=True))

        @pl.when(flags[0] == tile)
        def _():
            mine_own[...] = corr
            partner = partner_own if tile < 2 else partner_other
            mine_partner[...] = tile_corr(
                late, inner, partner[:, inner], columns_partner, late_b_other
            )

    diagonal_row = jnp.concatenate(diagonals, axis=1)
    partner_second = jnp.concatenate([vec_own[0:1, :], vec_other[0:1, :]], axis=1)
    second_a = rstd * (partner_second + jnp.concatenate(down, axis=1))
    second_b = lanes_to_row(across)
    loss = jnp.sum(losses) + jnp.sum(vec_other[1:2, :])
    loss_out[...] = jnp.broadcast_to(loss, (8, 128))

    for tile in (2, 3, 0, 1):
        at = slice(tile * width, (tile + 1) * width)
        inner = slice((tile % 2) * width, (tile % 2 + 1) * width)
        source, e_partner = (first_own, e_left) if tile < 2 else (first_other, e_right)
        terms = dot(norm_b[:, lower], e_own[:, at]) + dot(norm_b[:, upper], e_partner[:, inner])
        xhat = (source[:, inner].astype(jnp.float32) - offset[:, at]) * rstd[:, at]
        value = terms[:rows] - terms[rows : rows + 1] - xhat * second_a[:, at]
        if tile < 2:
            slope = rstd[:, at] * diagonal_row[:, inner]
            left_out[:, inner] = value + norm_b[:rows, inner].astype(jnp.float32) * slope
        else:
            for half, out in enumerate(left_partials_out):
                some = out.shape[0]
                out[:, inner] = value[half * some : (half + 1) * some].astype(jnp.bfloat16)

    for tile in range(2):
        at = slice(tile * width, (tile + 1) * width)
        terms = dot_rows(left[...], e_own[at, :])
        xhat = (first_b[:, at].astype(jnp.float32) - own_b[0][:, at]) * own_b[1][:, at]
        norm_a = (first_own[:, at].astype(jnp.float32) - offset[:, at]) * rstd[:, at]
        norm_a = norm_a.astype(jnp.bfloat16).astype(jnp.float32)
        right_out[:, at] = (
            without_extra(terms, rows) - xhat * second_b[:, at] + norm_a * diagonal_row[:, at]
        )

    own_columns = jnp.transpose(mine_own[...])
    partner_columns = jnp.transpose(mine_partner[...])

    @pl.when(flags[1] == 0)
    def _():
        mine_out[:, lower] = own_columns
        mine_out[:, upper] = partner_columns

    @pl.when(flags[1] != 0)
    def _():
        mine_out[:, lower] = partner_columns
        mine_out[:, upper] = own_columns


def add_kernel(one, other, out):
    out[...] = one[...] + other[...]


def loss_kernel(feats, one, other, out):
    out[0] = (one[0, 0] + other[0, 0]) / feats


def left_final_kernel(left, from_core_0, from_core_1, left_out):
    some = from_core_0.shape[0]
    for half, from_core in enumerate((from_core_0, from_core_1)):
        for at in range(0, some, 64):
            piece = slice(half * some + at, half * some + at + 64)
            value = left[piece, :] + from_core[at : at + 64, :].astype(jnp.float32)
            left_out[piece, :] = value.astype(jnp.bfloat16)


def right_final_kernel(right, from_x, late_b_0, late_b_1, right_out):
    rstd = right_stats((late_b_0, late_b_1))[1]
    for at in range(0, right.shape[0], 64):
        piece = slice(at, at + 64)
        value = rstd * (right[piece, :] + from_x[piece, :].astype(jnp.float32))
        right_out[piece, :] = value.astype(jnp.bfloat16)


vmem = pl.BlockSpec(memory_space=pltpu.VMEM)
smem = pl.BlockSpec(memory_space=pltpu.SMEM)


def local_call(kernel, operands, outs, scratch=(), flops=2**20, room=8, held=(), moved=None):
    if moved is None:
        moved = sum(x.size * x.dtype.itemsize for x in (*operands, *outs))

    def space(x):
        return smem if x.ndim == 1 else vmem

    return pl.pallas_call(
        kernel,
        out_shape=list(outs),
        in_specs=[space(x) for x in operands],
        out_specs=[space(x) for x in outs],
        scratch_shapes=list(scratch),
        compiler_params=pltpu.CompilerParams(vmem_limit_bytes=room * 2**20),
        cost_estimate=pl.CostEstimate(flops=flops, bytes_accessed=moved, transcendentals=0),
    )(*(pltpu.with_memory_space_constraint(x, pltpu.VMEM) if i in held else x for i, x in enumerate(operands)))


def gathered_device(left_outputs, right_outputs):
    rows, quart = left_outputs.shape
    half = 2 * quart
    feats = 4 * quart
    batch_images = rows * 4
    tpos = lax.axis_index("tile")
    dpos = lax.axis_index("dp")
    row_halves = tpos // 2
    column_halves = tpos % 2
    at_end = (dpos == 0) | (dpos == 3)
    owned_tile = jnp.where(dpos // 2 == column_halves, 0, 2) + dpos % 2
    flags = jnp.stack([owned_tile, row_halves]).astype(jnp.int32)
    mask = jnp.broadcast_to(at_end.astype(jnp.float32), (8, quart))

    pairs = [(0, 1), (1, 0), (2, 3), (3, 2)]
    middle = [(1, 2), (2, 1)]
    outward = [(1, 0), (2, 3)]

    def along(block, route):
        return lax.ppermute(block, "dp", route)

    def core_swap(block):
        return swapped(block, "tile", 0)

    def x_swap(block):
        return swapped(block, "tile", 1)

    def after(value, *others):
        return lax.optimization_barrier((value, *others))

    gemm = 2 * rows * quart * quart
    width = quart // 2
    quarter_f32 = jax.ShapeDtypeStruct((rows, quart), jnp.float32)
    quarter_bf16 = jax.ShapeDtypeStruct((rows, quart), jnp.bfloat16)
    extended = jax.ShapeDtypeStruct((rows + 16, quart), jnp.bfloat16)
    row_out = jax.ShapeDtypeStruct((8, quart), jnp.float32)
    one_out = jax.ShapeDtypeStruct((8, 128), jnp.float32)
    across_shape = jax.ShapeDtypeStruct((quart, 128), jnp.float32)
    low = lambda n, m: pltpu.VMEM((n, m), jnp.bfloat16)

    def picked(outer, inner):
        return local_call(pick_kernel, (mask, outer, inner), (quarter_bf16,))[0]

    some = rows // 2
    half_block = jax.ShapeDtypeStruct((some, quart), jnp.bfloat16)
    first_b = along(right_outputs, pairs)
    inner_b = along(right_outputs, middle)
    first_a = along(left_outputs, pairs)
    other_b0 = x_swap(right_outputs)
    other_a0, mask, flags = after(core_swap(left_outputs), mask, flags)
    left_behind, first_a, other_a0 = after(left_outputs, first_a, other_a0)
    inner_a = along(left_behind, middle)

    outer_b = along(inner_b, outward)
    third_b = along(first_b, middle)
    ready_b, other_b0 = after(first_b, other_b0)
    other_b1 = x_swap(ready_b)
    outer_a = along(inner_a, outward)
    third_a = along(first_a, middle)
    other_a1 = core_swap(first_a)

    third_b = local_call(halves_kernel, (third_b,), (half_block, half_block))
    last_b = [along(x, outward) for x in third_b]
    second_b = picked(outer_b, inner_b)
    row_b = local_call(right_sums_kernel, (right_outputs, first_b, second_b), (row_out,))[0]
    second_b, other_b1, other_a1 = after(second_b, other_b1, other_a1)
    other_b2 = x_swap(second_b)
    last_a = along(third_a, outward)
    second_a = picked(outer_a, inner_a)
    second_a, row_b = after(second_a, row_b)
    other_a2 = core_swap(second_a)

    late_b_0, row_b = local_call(
        functools.partial(late_right_kernel, batch_images, False),
        (mask, last_b[0], third_b[0], row_b),
        (jax.ShapeDtypeStruct((quart, some), jnp.bfloat16), row_out),
        held=(0, 1, 2, 3),
    )
    late_b_other_0 = x_swap(late_b_0)
    (late_b_1,) = local_call(
        functools.partial(late_right_kernel, batch_images, True),
        (mask, last_b[1], third_b[1], row_b),
        (jax.ShapeDtypeStruct((quart + 16 * (quart // some), some), jnp.bfloat16),),
        held=(0, 1, 2, 3),
    )
    late_b_other_1 = x_swap(late_b_1)
    late_b = (late_b_0, late_b_1)
    other_b2, late_b_1, late_b_other_0 = after(other_b2, late_b_1, late_b_other_0)
    partner_own, partner_other, own_all, row_other, zero_own, zero_other = local_call(
        products_kernel,
        (left_outputs, other_a0, first_a, other_a1, second_a, other_a2)
        + (right_outputs, other_b0, first_b, other_b1, second_b, other_b2),
        (
            quarter_f32,
            quarter_f32,
            jax.ShapeDtypeStruct((quart, half), jnp.float32),
            row_out,
            quarter_bf16,
            quarter_bf16,
        ),
        [low(3 * rows, half), low(half, 3 * rows)],
        room=20,
        moved=2**16,
    )
    row_a, late_b_other_1 = after(core_swap(row_other), late_b_other_1)
    late_b_other = (late_b_other_0, late_b_other_1)
    columns, rows_b = local_call(
        functools.partial(right_columns_kernel, batch_images),
        late_b_other,
        (jax.ShapeDtypeStruct((quart, 8), jnp.float32), row_out),
    )
    row_a, columns = after(row_a, columns)
    operands = (mask, last_a, third_a, row_a)
    (late_a,) = local_call(late_left_kernel, operands, (quarter_bf16,), held=(0, 1, 2, 3))
    late_a_other = core_swap(late_a)
    (stats_a,) = local_call(
        functools.partial(left_stats_kernel, batch_images), operands, (row_out,), held=(0, 1, 2, 3)
    )
    stats_a_other = core_swap(stats_a)

    terms, across, e_left, vec_own = local_call(
        functools.partial(partner_kernel, batch_images, 0),
        (late_a, stats_a, zero_own, partner_own, *late_b_other, columns, rows_b),
        (
            jax.ShapeDtypeStruct((rows + 16, quart), jnp.float32),
            across_shape,
            quarter_bf16,
            row_out,
        ),
        [low(rows + 16, quart)],
        2 * gemm,
        room=12,
    )
    partial_right, e_right, vec_other = local_call(
        functools.partial(partner_kernel, batch_images, 1),
        (late_a_other, stats_a_other, zero_other, partner_other, *late_b_other)
        + (columns, rows_b, terms, across, vec_own, other_b0),
        (quarter_bf16, quarter_bf16, row_out),
        [low(rows + 16, quart)],
        2 * gemm,
        room=12,
    )
    from_x = x_swap(partial_right)
    right_own, left_own, *partials_left, mine, loss = local_call(
        functools.partial(own_kernel, batch_images),
        (flags, *late_b, *late_b_other, stats_a, stats_a_other)
        + (late_a, late_a_other, left_outputs, other_a0, zero_own, zero_other, own_all)
        + (right_outputs, other_b0, e_left, e_right)
        + (partner_own, partner_other)
        + (vec_own, vec_other),
        (
            quarter_f32,
            quarter_f32,
            half_block,
            half_block,
            jax.ShapeDtypeStruct((width, half), jnp.float32),
            one_out,
        ),
        [
            low(rows + 16, half),
            low(rows + 16, half),
            low(quart, half),
            pltpu.VMEM((quart, width), jnp.float32),
            pltpu.VMEM((quart, width), jnp.float32),
        ],
        8 * gemm,
        room=20,
    )
    from_core = [core_swap(x) for x in partials_left]
    core_loss = core_swap(loss)
    (loss,) = local_call(add_kernel, (loss, core_loss), (one_out,))
    x_loss = x_swap(loss)
    (left_gradient,) = local_call(left_final_kernel, (left_own, *from_core), (quarter_bf16,))
    right_own, left_gradient = after(right_own, left_gradient)
    (right_gradient,) = local_call(right_final_kernel, (right_own, from_x, *late_b), (quarter_bf16,))
    right_gradient, x_loss = after(right_gradient, x_loss)
    (loss,) = local_call(
        functools.partial(loss_kernel, feats),
        (loss, x_loss),
        (jax.ShapeDtypeStruct((1,), jnp.float32),),
    )
    return (left_gradient, right_gradient, mine[None, :, :], loss)


def solution(mesh):
    per_device = gathered_device if mesh.shape["dp"] == 4 else reduced_device
    return jax.shard_map(
        per_device,
        mesh=mesh,
        in_specs=(P(("groups", "dp"), "tile"), P(("groups", "dp"), "tile")),
        out_specs=(
            P(("groups", "dp"), "tile"),
            P(("groups", "dp"), "tile"),
            P(("groups", "tile"), "dp", None),
            P("groups"),
        ),
        check_vma=False,
    )
```

```python
import functools
import jax
import jax.numpy as jnp
from jax import lax
from jax.experimental import pallas as pl
from jax.experimental.pallas import tpu as pltpu
from jax.sharding import PartitionSpec as P

off_weight = 0.0051


def swapped(block, axis, bit):
    count = lax.axis_size(axis)
    route = []
    for low in range(count):
        high = low | 1 << bit
        if high != low and high < count:
            route += [(low, high), (high, low)]
    return lax.ppermute(block, axis, route)


def pair_views(first_moment, second_moment, row_halves, column_halves):
    other_a = swapped(first_moment, "tile", 0)
    other_b = swapped(second_moment, "tile", 1)
    joined_a = jnp.where(
        column_halves == 0,
        jnp.concatenate([first_moment, other_a], axis=1),
        jnp.concatenate([other_a, first_moment], axis=1),
    )
    joined_b = jnp.where(
        row_halves == 0,
        jnp.concatenate([second_moment, other_b], axis=1),
        jnp.concatenate([other_b, second_moment], axis=1),
    )
    return (joined_a, joined_b)


def moment_pair(total, squares, batch_images):
    column_mean = total / batch_images
    var = squares / batch_images - column_mean * column_mean
    return (column_mean, lax.rsqrt(var + 1e-05))


def col_sums(values):
    as_float = values.astype(jnp.float32)
    return (jnp.sum(as_float, axis=0), jnp.sum(as_float * as_float, axis=0))


def reduced_device(left_outputs, right_outputs):
    rows, quart = left_outputs.shape
    half = 2 * quart
    feats = 4 * quart
    dp_count = lax.axis_size("dp")
    batch_images = rows * dp_count
    tpos = lax.axis_index("tile")
    row_halves = tpos // 2
    column_halves = tpos % 2
    sum_a, sq_a = col_sums(left_outputs)
    sum_b, sq_b = col_sums(right_outputs)
    sum_a, sq_a, sum_b, sq_b = lax.psum((sum_a, sq_a, sum_b, sq_b), "dp")
    left_mean, left_inverse_deviation = moment_pair(sum_a, sq_a, batch_images)
    right_mean, right_inverse_deviation = moment_pair(sum_b, sq_b, batch_images)
    standardized_left = (left_outputs.astype(jnp.float32) - left_mean) * left_inverse_deviation
    standardized_right = (right_outputs.astype(jnp.float32) - right_mean) * right_inverse_deviation
    half_a, cols_b = pair_views(
        standardized_left.astype(jnp.bfloat16),
        standardized_right.astype(jnp.bfloat16),
        row_halves,
        column_halves,
    )
    col_local = jnp.arange(half, dtype=jnp.int32)
    col_ids = quart * column_halves + col_local + jnp.where(col_local >= quart, quart, 0)
    owned = half // dp_count
    picked = half_a
    corr_rows = (
        lax.psum_scatter(
            lax.dot_general(
                picked, cols_b, (((0,), (0,)), ((), ())), preferred_element_type=jnp.float32
            ),
            "dp",
            scatter_dimension=0,
            tiled=True,
        )
        / batch_images
    )
    row_ids = half * row_halves + lax.axis_index("dp") * owned + jnp.arange(owned, dtype=jnp.int32)
    diagonal = row_ids[:, None] == col_ids[None, :]
    part_loss = jnp.sum(
        jnp.where(diagonal, (1.0 - corr_rows) ** 2, off_weight * corr_rows * corr_rows)
    )
    loss = lax.psum(part_loss, ("dp", "tile")) / feats
    dcorr_part = jnp.where(diagonal, corr_rows - 1.0, off_weight * corr_rows).astype(jnp.bfloat16)
    piece = lax.all_gather(dcorr_part, "dp", axis=0, tiled=True)
    block_a = lax.dot_general(
        cols_b, piece, (((1,), (1,)), ((), ())), preferred_element_type=jnp.float32
    )
    picked = half_a
    into_b = jnp.dot(picked, piece, preferred_element_type=jnp.float32)
    other_a = swapped(block_a.astype(jnp.bfloat16), "tile", 0).astype(block_a.dtype)
    other_b = swapped(into_b.astype(jnp.bfloat16), "tile", 1).astype(into_b.dtype)
    normed_grad_left = lax.dynamic_slice_in_dim(block_a + other_a, column_halves * quart, quart, 1)
    normed_grad_right = lax.dynamic_slice_in_dim(into_b + other_b, row_halves * quart, quart, 1)
    first_moment_left, second_moment_left, first_moment_right, second_moment_right = lax.psum(
        (
            jnp.sum(normed_grad_left, axis=0),
            jnp.sum(normed_grad_left * standardized_left, axis=0),
            jnp.sum(normed_grad_right, axis=0),
            jnp.sum(normed_grad_right * standardized_right, axis=0),
        ),
        "dp",
    )
    left_gradient = (
        left_inverse_deviation
        * (
            normed_grad_left
            - first_moment_left / batch_images
            - standardized_left * (second_moment_left / batch_images)
        )
    ).astype(jnp.bfloat16)
    right_gradient = (
        right_inverse_deviation
        * (
            normed_grad_right
            - first_moment_right / batch_images
            - standardized_right * (second_moment_right / batch_images)
        )
    ).astype(jnp.bfloat16)
    return (left_gradient, right_gradient, corr_rows[None, :, :], jnp.reshape(loss, (1,)))


def fold_rows(values):
    rows, width = values.shape
    return jnp.sum(values.reshape(rows // 8, 8, width), axis=0)


def fold_lanes(values):
    return sum(values[:, at : at + 128] for at in range(0, values.shape[1], 128))


def column_mean(block):
    rows, width = block.shape
    folded = jnp.zeros((8, width), jnp.float32)
    for at in range(0, rows, 64):
        folded = folded + fold_rows(block[at : at + 64, :].astype(jnp.float32))
    return jnp.sum(folded, axis=0, keepdims=True) / rows


def add_sums(sums, centred, low):
    return [
        sums[0] + fold_rows(centred),
        sums[1] + fold_rows(centred * centred),
        sums[2] + fold_rows(low.astype(jnp.float32)),
    ]


def rows_of(values):
    pad = jnp.zeros((8 - len(values), values[0].shape[1]), jnp.float32)
    return jnp.concatenate([*values, pad], axis=0)


def joined_sums(row, sums):
    return [row[i + 1 : i + 2, :] + jnp.sum(s, axis=0, keepdims=True) for i, s in enumerate(sums)]


def moments(sums, images):
    total, squares, rounded = sums
    delta = total / images
    return delta, lax.rsqrt(squares / images - delta * delta + 1e-05), rounded / images - delta


def three_parts(row):
    high = row.astype(jnp.bfloat16)
    rest = row - high.astype(jnp.float32)
    middle = rest.astype(jnp.bfloat16)
    low = (rest - middle.astype(jnp.float32)).astype(jnp.bfloat16)
    return [high, middle, low]


def split_rows(values):
    parts = sum([three_parts(v) for v in values], [])
    pad = jnp.zeros((4, values[0].shape[1]), jnp.float32)
    return jnp.concatenate([*(p.astype(jnp.float32) for p in parts), pad], axis=0).astype(
        jnp.bfloat16
    )


def joined_rows(ref, at):
    parts = ref[at : at + 16, :].astype(jnp.float32)
    part = lambda i: parts[i : i + 1]
    return [part(3 * i) + part(3 * i + 1) + part(3 * i + 2) for i in range(4)]


def lanes_to_row(partial):
    ones = jnp.ones((16, partial.shape[1]), jnp.bfloat16)
    high = partial.astype(jnp.bfloat16)
    low = (partial - high.astype(jnp.float32)).astype(jnp.bfloat16)
    row = dot_rows(ones, high) + dot_rows(ones, low)
    return row[:1, :]


def dot_rows(left, right):
    return lax.dot_general(
        left, right, (((1,), (1,)), ((), ())), preferred_element_type=jnp.float32
    )


def dot(left, right):
    return jnp.dot(left, right, preferred_element_type=jnp.float32)


def pick(mask, outer, inner, piece):
    return jnp.where(
        mask[0:1, :] != 0.0, outer[piece, :].astype(jnp.float32), inner[piece, :].astype(jnp.float32)
    )


def pick_kernel(mask, outer, inner, out):
    for at in range(0, outer.shape[0], 64):
        piece = slice(at, at + 64)
        out[piece, :] = pick(mask, outer, inner, piece).astype(out.dtype)


def right_sums_kernel(first, second, third, row):
    rows, quart = first.shape
    shift = column_mean(first)
    sums = [jnp.zeros((8, quart), jnp.float32)] * 3
    for block in (first, second, third):
        for at in range(0, rows, 64):
            centred = block[at : at + 64, :].astype(jnp.float32) - shift
            sums = add_sums(sums, centred, centred.astype(jnp.bfloat16))
    row[...] = rows_of([shift] + [jnp.sum(s, axis=0, keepdims=True) for s in sums])


def halves_kernel(block, first, second):
    half = first.shape[0]
    first[...] = block[:half, :]
    second[...] = block[half:, :]


def late_left_kernel(mask, outer, inner, row, out):
    for at in range(0, out.shape[0], 64):
        piece = slice(at, at + 64)
        out[piece, :] = (pick(mask, outer, inner, piece) - row[0:1, :]).astype(out.dtype)


def left_stats_kernel(images, mask, outer, inner, row, stats):
    rows, quart = outer.shape
    shift = row[0:1, :]
    sums = [jnp.zeros((8, quart), jnp.float32)] * 3
    for at in range(0, rows, 64):
        centred = pick(mask, outer, inner, slice(at, at + 64)) - shift
        sums = add_sums(sums, centred, centred.astype(jnp.bfloat16))
    delta, rstd, gap = moments(joined_sums(row, sums), images)
    stats[...] = rows_of([shift + delta, rstd, gap, delta])


def stats_rows(stats):
    return [stats[i : i + 1, :] for i in range(4)]


def late_right_kernel(images, last, mask, outer, inner, row, out, *rest):
    some, quart = outer.shape
    shift = row[0:1, :]
    sums = [jnp.zeros((8, quart), jnp.float32)] * 3
    for at in range(0, some, 128):
        piece = slice(at, at + 128)
        centred = pick(mask, outer, inner, piece) - shift
        low = centred.astype(jnp.bfloat16)
        out[:quart, piece] = jnp.transpose(low)
        sums = add_sums(sums, centred, low)
    sums = joined_sums(row, sums)
    if not last:
        (row_out,) = rest
        row_out[...] = rows_of([shift, *sums])
        return
    delta, rstd, gap = moments(sums, images)
    parts = split_rows([shift + delta, rstd, gap, delta])
    for i in range(quart // some):
        below = quart + 16 * i
        out[below : below + 16, :] = parts[:, i * some : (i + 1) * some]


def right_stats(late):
    quart, some = late[0].shape
    found = [joined_rows(late[1], quart + 16 * i) for i in range(quart // some)]
    return [jnp.concatenate(values, axis=1) for values in zip(*found)]


def late_products(right, left, lanes):
    quart, some = right[0].shape
    first = dot(right[0][...], left[:some, lanes])
    return first + dot(right[1][:quart, :], left[some : 2 * some, lanes])


def products_kernel(*refs):
    lefts, rights = refs[0:6], refs[6:12]
    partner_own, partner_other, own_all, row_other, zero_own, zero_other = refs[12:18]
    low_left, low_right = refs[18:]
    rows, quart = lefts[0].shape
    width = quart // 2
    for half in range(2):
        lanes = slice(half * quart, (half + 1) * quart)
        shift = column_mean(lefts[half])
        sums = [jnp.zeros((8, quart), jnp.float32)] * 3
        for block in range(3):
            source = lefts[2 * block + half]
            for at in range(0, rows, 64):
                centred = source[at : at + 64, :].astype(jnp.float32) - shift
                low = centred.astype(jnp.bfloat16)
                low_left[block * rows + at : block * rows + at + 64, lanes] = low
                if block == 0:
                    (zero_own, zero_other)[half][at : at + 64, :] = low
                if half:
                    sums = add_sums(sums, centred, low)
        if half:
            row_other[...] = rows_of([shift] + [jnp.sum(s, axis=0, keepdims=True) for s in sums])
    for half in range(2):
        lanes = slice(half * quart, (half + 1) * quart)
        shift = column_mean(rights[half])
        for block in range(3):
            source = rights[2 * block + half]
            for at in range(0, rows, 128):
                low = (source[at : at + 128, :].astype(jnp.float32) - shift).astype(jnp.bfloat16)
                low_right[lanes, block * rows + at : block * rows + at + 128] = jnp.transpose(low)
    for tile in range(4):
        wide = slice(tile * width, (tile + 1) * width)
        inner = slice((tile % 2) * width, (tile % 2 + 1) * width)
        target = partner_own if tile < 2 else partner_other
        target[:, inner] = dot(low_right[quart:, :], low_left[:, wide])
        own_all[:, wide] = dot(low_right[:quart, :], low_left[:, wide])


def left_operand(zero, stats, target, lanes):
    rows, quart = zero.shape
    _, _, gap, delta = stats_rows(stats)
    high, middle, _ = three_parts(delta)
    target[:rows, lanes] = zero[...]
    extra = [high.astype(jnp.float32), middle.astype(jnp.float32), gap]
    pad = jnp.zeros((13, quart), jnp.float32)
    target[rows:, lanes] = jnp.concatenate([*extra, pad], axis=0).astype(jnp.bfloat16)


def without_extra(terms, rows):
    return terms[:rows] - (terms[rows : rows + 1] + terms[rows + 1 : rows + 2] + terms[rows + 2 : rows + 3])


def scale_columns(late_b, images):
    _, rstd, _, delta = right_stats(late_b)
    columns = jnp.transpose(rows_of([rstd / images, delta * rstd]))
    return columns[:, 0:1], columns[:, 1:2]


def right_columns_kernel(images, late_b_0, late_b_1, first_b, columns, xhat):
    offset, rstd, _, delta = right_stats((late_b_0, late_b_1))
    columns[...] = jnp.transpose(rows_of([rstd / images, delta * rstd]))
    for at in range(0, first_b.shape[0], 64):
        piece = slice(at, at + 64)
        xhat[piece, :] = (first_b[piece, :].astype(jnp.float32) - offset) * rstd


def partner_kernel(images, part, late, stats, zero, sums, late_b_0, late_b_1, columns, *refs):
    if part:
        (terms_in, across_in, vec_in, xhat) = refs[:4]
        (partial_out, e_out, vec_out, left) = refs[4:]
    else:
        (terms_out, across_out, e_out, vec_out, left) = refs
    late_b = (late_b_0, late_b_1)
    rows, quart = zero.shape
    width = quart // 2
    _, rstd, _, delta = stats_rows(stats)
    left_operand(zero, stats, left, slice(0, quart))
    scale_col, delta_col = columns[:, 0:1], columns[:, 1:2]
    across = across_in[...] if part else jnp.zeros((quart, 128), jnp.float32)
    down = []
    for tile in range(2):
        at = slice(tile * width, (tile + 1) * width)
        total = sums[:, at] + late_products(late_b, late, at)
        corr = (total * scale_col - delta_col * delta[:, at]) * rstd[:, at]
        e_out[:, at] = (corr * (off_weight * rstd[:, at])).astype(jnp.bfloat16)
        square = corr * corr
        across = across + fold_lanes(square)
        down.append(jnp.sum(square, axis=0, keepdims=True))
    second_a = off_weight * jnp.concatenate(down, axis=1)
    if part:
        vec_out[...] = rows_of([second_a, second_a + vec_in[0:1, :]])
        second = off_weight * lanes_to_row(across)
    else:
        vec_out[...] = rows_of([second_a])
        across_out[...] = across
    for tile in range(2):
        at = slice(tile * width, (tile + 1) * width)
        terms = dot_rows(left[...], e_out[at, :])
        if part:
            partial_out[:, at] = (
                without_extra(terms + terms_in[:, at], rows) - xhat[:, at] * second[:, at]
            ).astype(jnp.bfloat16)
        else:
            terms_out[:, at] = terms


def own_kernel(images, flags, *refs):
    late_b, late_b_other = refs[:2], refs[2:4]
    (left_own, left_other), refs = refs[4:6], refs[6:]
    (late_own, late_other, first_own, first_other, zero_own, zero_other, sums) = refs[:7]
    (first_b, first_b_other, e_left, e_right, partner_own, partner_other) = refs[7:13]
    (vec_own, vec_other, right_out, left_out, *left_partials_out, mine_out) = refs[13:20]
    (loss_out, left, norm_b, e_own, mine_own, mine_partner) = refs[20:]
    rows, quart = zero_own.shape
    width = quart // 2
    lower, upper = slice(0, quart), slice(quart, 2 * quart)
    stats_own, stats_other = stats_rows(left_own), stats_rows(left_other)
    both = lambda i: jnp.concatenate([stats_own[i], stats_other[i]], axis=1)
    offset, rstd, _, delta = [both(i) for i in range(4)]
    left_operand(zero_own, left_own, left, lower)
    left_operand(zero_other, left_other, left, upper)
    own_b = right_stats(late_b)
    other_b = right_stats(late_b_other)
    for source, stats, lanes in ((first_b, own_b, lower), (first_b_other, other_b, upper)):
        for at in range(0, rows, 64):
            piece = slice(at, at + 64)
            norm_b[piece, lanes] = (
                (source[piece, :].astype(jnp.float32) - stats[0]) * stats[1]
            ).astype(jnp.bfloat16)
        rest = jnp.broadcast_to(stats[2] * stats[1], (16, quart))
        norm_b[rows:, lanes] = rest.astype(jnp.bfloat16)

    def tile_corr(late, inner, total, columns, block):
        scale_col, delta_col = columns
        total = total + late_products(block, late, inner)
        row = stats_own if late is late_own else stats_other
        return (total * scale_col - delta_col * row[3][:, inner]) * row[1][:, inner]

    columns = scale_columns(late_b, images)
    columns_partner = scale_columns(late_b_other, images)
    across = jnp.zeros((quart, 128), jnp.float32)
    losses = jnp.zeros((8, 128), jnp.float32)
    down, diagonals = [], []
    for tile in range(4):
        at = slice(tile * width, (tile + 1) * width)
        inner = slice((tile % 2) * width, (tile % 2 + 1) * width)
        late = late_own if tile < 2 else late_other
        corr = tile_corr(late, inner, sums[:, at], columns, late_b)
        dcorr = off_weight * corr
        product = dcorr * corr
        loss = product
        if tile < 2:
            feature = lax.broadcasted_iota(jnp.int32, (quart, width), 0)
            lane = lax.broadcasted_iota(jnp.int32, (quart, width), 1) + tile * width
            diagonal = feature == lane
            slope = jnp.where(diagonal, (corr - 1.0).astype(jnp.bfloat16).astype(jnp.float32), 0.0)
            diagonals.append(jnp.sum(slope, axis=0, keepdims=True))
            dcorr = jnp.where(diagonal, 0.0, dcorr)
            product = jnp.where(diagonal, slope * corr, product)
            loss = jnp.where(diagonal, (1.0 - corr) * (1.0 - corr), loss)
        e_own[:, at] = (dcorr * rstd[:, at]).astype(jnp.bfloat16)
        across = across + fold_lanes(product)
        losses = losses + fold_rows(fold_lanes(loss))
        down.append(jnp.sum(product, axis=0, keepdims=True))

        @pl.when(flags[0] == tile)
        def _():
            mine_own[...] = corr
            partner = partner_own if tile < 2 else partner_other
            mine_partner[...] = tile_corr(
                late, inner, partner[:, inner], columns_partner, late_b_other
            )

    diagonal_row = jnp.concatenate(diagonals, axis=1)
    partner_second = jnp.concatenate([vec_own[0:1, :], vec_other[0:1, :]], axis=1)
    second_a = rstd * (partner_second + jnp.concatenate(down, axis=1))
    second_b = lanes_to_row(across)
    loss = jnp.sum(losses) + jnp.sum(vec_other[1:2, :])
    loss_out[...] = jnp.broadcast_to(loss, (8, 128))

    for tile in (2, 3, 0, 1):
        at = slice(tile * width, (tile + 1) * width)
        inner = slice((tile % 2) * width, (tile % 2 + 1) * width)
        source, e_partner = (first_own, e_left) if tile < 2 else (first_other, e_right)
        terms = dot(norm_b[:, lower], e_own[:, at]) + dot(norm_b[:, upper], e_partner[:, inner])
        xhat = (source[:, inner].astype(jnp.float32) - offset[:, at]) * rstd[:, at]
        value = terms[:rows] - terms[rows : rows + 1] - xhat * second_a[:, at]
        if tile < 2:
            slope = rstd[:, at] * diagonal_row[:, inner]
            left_out[:, inner] = value + norm_b[:rows, inner].astype(jnp.float32) * slope
        else:
            for half, out in enumerate(left_partials_out):
                some = out.shape[0]
                out[:, inner] = value[half * some : (half + 1) * some].astype(jnp.bfloat16)

    for tile in range(2):
        at = slice(tile * width, (tile + 1) * width)
        terms = dot_rows(left[...], e_own[at, :])
        xhat = (first_b[:, at].astype(jnp.float32) - own_b[0][:, at]) * own_b[1][:, at]
        norm_a = (first_own[:, at].astype(jnp.float32) - offset[:, at]) * rstd[:, at]
        norm_a = norm_a.astype(jnp.bfloat16).astype(jnp.float32)
        right_out[:, at] = (
            without_extra(terms, rows) - xhat * second_b[:, at] + norm_a * diagonal_row[:, at]
        )

    own_columns = jnp.transpose(mine_own[...])
    partner_columns = jnp.transpose(mine_partner[...])

    @pl.when(flags[1] == 0)
    def _():
        mine_out[:, lower] = own_columns
        mine_out[:, upper] = partner_columns

    @pl.when(flags[1] != 0)
    def _():
        mine_out[:, lower] = partner_columns
        mine_out[:, upper] = own_columns


def add_kernel(one, other, out):
    out[...] = one[...] + other[...]


def loss_kernel(feats, one, other, out):
    out[0] = (one[0, 0] + other[0, 0]) / feats


def left_final_kernel(left, from_core_0, from_core_1, left_out):
    some = from_core_0.shape[0]
    for half, from_core in enumerate((from_core_0, from_core_1)):
        for at in range(0, some, 64):
            piece = slice(half * some + at, half * some + at + 64)
            value = left[piece, :] + from_core[at : at + 64, :].astype(jnp.float32)
            left_out[piece, :] = value.astype(jnp.bfloat16)


def right_final_kernel(right, from_x, late_b_0, late_b_1, right_out):
    rstd = right_stats((late_b_0, late_b_1))[1]
    for at in range(0, right.shape[0], 64):
        piece = slice(at, at + 64)
        value = rstd * (right[piece, :] + from_x[piece, :].astype(jnp.float32))
        right_out[piece, :] = value.astype(jnp.bfloat16)


vmem = pl.BlockSpec(memory_space=pltpu.VMEM)
smem = pl.BlockSpec(memory_space=pltpu.SMEM)


def local_call(kernel, operands, outs, scratch=(), flops=2**20, room=8, held=(), moved=None):
    if moved is None:
        moved = sum(x.size * x.dtype.itemsize for x in (*operands, *outs))

    def space(x):
        return smem if x.ndim == 1 else vmem

    return pl.pallas_call(
        kernel,
        out_shape=list(outs),
        in_specs=[space(x) for x in operands],
        out_specs=[space(x) for x in outs],
        scratch_shapes=list(scratch),
        compiler_params=pltpu.CompilerParams(vmem_limit_bytes=room * 2**20),
        cost_estimate=pl.CostEstimate(flops=flops, bytes_accessed=moved, transcendentals=0),
    )(*(pltpu.with_memory_space_constraint(x, pltpu.VMEM) if i in held else x for i, x in enumerate(operands)))


def gathered_device(left_outputs, right_outputs):
    rows, quart = left_outputs.shape
    half = 2 * quart
    feats = 4 * quart
    batch_images = rows * 4
    tpos = lax.axis_index("tile")
    dpos = lax.axis_index("dp")
    row_halves = tpos // 2
    column_halves = tpos % 2
    at_end = (dpos == 0) | (dpos == 3)
    owned_tile = jnp.where(dpos // 2 == column_halves, 0, 2) + dpos % 2
    flags = jnp.stack([owned_tile, row_halves]).astype(jnp.int32)
    mask = jnp.broadcast_to(at_end.astype(jnp.float32), (8, quart))

    pairs = [(0, 1), (1, 0), (2, 3), (3, 2)]
    middle = [(1, 2), (2, 1)]
    outward = [(1, 0), (2, 3)]

    def along(block, route):
        return lax.ppermute(block, "dp", route)

    def core_swap(block):
        return swapped(block, "tile", 0)

    def x_swap(block):
        return swapped(block, "tile", 1)

    def after(value, *others):
        return lax.optimization_barrier((value, *others))

    gemm = 2 * rows * quart * quart
    width = quart // 2
    quarter_f32 = jax.ShapeDtypeStruct((rows, quart), jnp.float32)
    quarter_bf16 = jax.ShapeDtypeStruct((rows, quart), jnp.bfloat16)
    extended = jax.ShapeDtypeStruct((rows + 16, quart), jnp.bfloat16)
    row_out = jax.ShapeDtypeStruct((8, quart), jnp.float32)
    one_out = jax.ShapeDtypeStruct((8, 128), jnp.float32)
    across_shape = jax.ShapeDtypeStruct((quart, 128), jnp.float32)
    low = lambda n, m: pltpu.VMEM((n, m), jnp.bfloat16)

    def picked(outer, inner):
        return local_call(pick_kernel, (mask, outer, inner), (quarter_bf16,))[0]

    some = rows // 2
    half_block = jax.ShapeDtypeStruct((some, quart), jnp.bfloat16)
    first_b = along(right_outputs, pairs)
    inner_b = along(right_outputs, middle)
    first_a = along(left_outputs, pairs)
    other_b0 = x_swap(right_outputs)
    other_a0, mask, flags = after(core_swap(left_outputs), mask, flags)
    left_behind, first_a, other_a0 = after(left_outputs, first_a, other_a0)
    inner_a = along(left_behind, middle)

    outer_b = along(inner_b, outward)
    third_b = along(first_b, middle)
    ready_b, other_b0 = after(first_b, other_b0)
    other_b1 = x_swap(ready_b)
    outer_a = along(inner_a, outward)
    third_a = along(first_a, middle)
    other_a1 = core_swap(first_a)

    third_b = local_call(halves_kernel, (third_b,), (half_block, half_block))
    last_b = [along(x, outward) for x in third_b]
    second_b = picked(outer_b, inner_b)
    row_b = local_call(right_sums_kernel, (right_outputs, first_b, second_b), (row_out,))[0]
    second_b, other_b1, other_a1 = after(second_b, other_b1, other_a1)
    other_b2 = x_swap(second_b)
    last_a = along(third_a, outward)
    second_a = picked(outer_a, inner_a)
    second_a, row_b = after(second_a, row_b)
    other_a2 = core_swap(second_a)

    late_b_0, row_b = local_call(
        functools.partial(late_right_kernel, batch_images, False),
        (mask, last_b[0], third_b[0], row_b),
        (jax.ShapeDtypeStruct((quart, some), jnp.bfloat16), row_out),
        held=(0, 1, 2, 3),
    )
    late_b_other_0 = x_swap(late_b_0)
    (late_b_1,) = local_call(
        functools.partial(late_right_kernel, batch_images, True),
        (mask, last_b[1], third_b[1], row_b),
        (jax.ShapeDtypeStruct((quart + 16 * (quart // some), some), jnp.bfloat16),),
        held=(0, 1, 2, 3),
    )
    late_b_other_1 = x_swap(late_b_1)
    late_b = (late_b_0, late_b_1)
    other_b2, late_b_1, late_b_other_0 = after(other_b2, late_b_1, late_b_other_0)
    partner_own, partner_other, own_all, row_other, zero_own, zero_other = local_call(
        products_kernel,
        (left_outputs, other_a0, first_a, other_a1, second_a, other_a2)
        + (right_outputs, other_b0, first_b, other_b1, second_b, other_b2),
        (
            quarter_f32,
            quarter_f32,
            jax.ShapeDtypeStruct((quart, half), jnp.float32),
            row_out,
            quarter_bf16,
            quarter_bf16,
        ),
        [low(3 * rows, half), low(half, 3 * rows)],
        room=20,
        moved=2**16,
    )
    row_a, late_b_other_1 = after(core_swap(row_other), late_b_other_1)
    late_b_other = (late_b_other_0, late_b_other_1)
    columns, xhat_other = local_call(
        functools.partial(right_columns_kernel, batch_images),
        (*late_b_other, other_b0),
        (jax.ShapeDtypeStruct((quart, 8), jnp.float32), quarter_f32),
    )
    row_a, columns = after(row_a, columns)
    operands = (mask, last_a, third_a, row_a)
    (late_a,) = local_call(late_left_kernel, operands, (quarter_bf16,), held=(0, 1, 2, 3))
    late_a_other = core_swap(late_a)
    (stats_a,) = local_call(
        functools.partial(left_stats_kernel, batch_images), operands, (row_out,), held=(0, 1, 2, 3)
    )
    stats_a_other = core_swap(stats_a)

    terms, across, e_left, vec_own = local_call(
        functools.partial(partner_kernel, batch_images, 0),
        (late_a, stats_a, zero_own, partner_own, *late_b_other, columns),
        (
            jax.ShapeDtypeStruct((rows + 16, quart), jnp.float32),
            across_shape,
            quarter_bf16,
            row_out,
        ),
        [low(rows + 16, quart)],
        2 * gemm,
        room=12,
    )
    partial_right, e_right, vec_other = local_call(
        functools.partial(partner_kernel, batch_images, 1),
        (late_a_other, stats_a_other, zero_other, partner_other, *late_b_other)
        + (columns, terms, across, vec_own, xhat_other),
        (quarter_bf16, quarter_bf16, row_out),
        [low(rows + 16, quart)],
        2 * gemm,
        room=12,
    )
    from_x = x_swap(partial_right)
    right_own, left_own, *partials_left, mine, loss = local_call(
        functools.partial(own_kernel, batch_images),
        (flags, *late_b, *late_b_other, stats_a, stats_a_other)
        + (late_a, late_a_other, left_outputs, other_a0, zero_own, zero_other, own_all)
        + (right_outputs, other_b0, e_left, e_right)
        + (partner_own, partner_other)
        + (vec_own, vec_other),
        (
            quarter_f32,
            quarter_f32,
            half_block,
            half_block,
            jax.ShapeDtypeStruct((width, half), jnp.float32),
            one_out,
        ),
        [
            low(rows + 16, half),
            low(rows + 16, half),
            low(quart, half),
            pltpu.VMEM((quart, width), jnp.float32),
            pltpu.VMEM((quart, width), jnp.float32),
        ],
        8 * gemm,
        room=20,
    )
    from_core = [core_swap(x) for x in partials_left]
    core_loss = core_swap(loss)
    (loss,) = local_call(add_kernel, (loss, core_loss), (one_out,))
    x_loss = x_swap(loss)
    (left_gradient,) = local_call(left_final_kernel, (left_own, *from_core), (quarter_bf16,))
    right_own, left_gradient = after(right_own, left_gradient)
    (right_gradient,) = local_call(right_final_kernel, (right_own, from_x, *late_b), (quarter_bf16,))
    right_gradient, x_loss = after(right_gradient, x_loss)
    (loss,) = local_call(
        functools.partial(loss_kernel, feats),
        (loss, x_loss),
        (jax.ShapeDtypeStruct((1,), jnp.float32),),
    )
    return (left_gradient, right_gradient, mine[None, :, :], loss)


def solution(mesh):
    per_device = gathered_device if mesh.shape["dp"] == 4 else reduced_device
    return jax.shard_map(
        per_device,
        mesh=mesh,
        in_specs=(P(("groups", "dp"), "tile"), P(("groups", "dp"), "tile")),
        out_specs=(
            P(("groups", "dp"), "tile"),
            P(("groups", "dp"), "tile"),
            P(("groups", "tile"), "dp", None),
            P("groups"),
        ),
        check_vma=False,
    )
```

```python
import functools
import jax
import jax.numpy as jnp
from jax import lax
from jax.experimental import pallas as pl
from jax.experimental.pallas import tpu as pltpu
from jax.sharding import PartitionSpec as P

off_weight = 0.0051


def swapped(block, axis, bit):
    count = lax.axis_size(axis)
    route = []
    for low in range(count):
        high = low | 1 << bit
        if high != low and high < count:
            route += [(low, high), (high, low)]
    return lax.ppermute(block, axis, route)


def pair_views(first_moment, second_moment, row_halves, column_halves):
    other_a = swapped(first_moment, "tile", 0)
    other_b = swapped(second_moment, "tile", 1)
    joined_a = jnp.where(
        column_halves == 0,
        jnp.concatenate([first_moment, other_a], axis=1),
        jnp.concatenate([other_a, first_moment], axis=1),
    )
    joined_b = jnp.where(
        row_halves == 0,
        jnp.concatenate([second_moment, other_b], axis=1),
        jnp.concatenate([other_b, second_moment], axis=1),
    )
    return (joined_a, joined_b)


def moment_pair(total, squares, batch_images):
    column_mean = total / batch_images
    var = squares / batch_images - column_mean * column_mean
    return (column_mean, lax.rsqrt(var + 1e-05))


def col_sums(values):
    as_float = values.astype(jnp.float32)
    return (jnp.sum(as_float, axis=0), jnp.sum(as_float * as_float, axis=0))


def reduced_device(left_outputs, right_outputs):
    rows, quart = left_outputs.shape
    half = 2 * quart
    feats = 4 * quart
    dp_count = lax.axis_size("dp")
    batch_images = rows * dp_count
    tpos = lax.axis_index("tile")
    row_halves = tpos // 2
    column_halves = tpos % 2
    sum_a, sq_a = col_sums(left_outputs)
    sum_b, sq_b = col_sums(right_outputs)
    sum_a, sq_a, sum_b, sq_b = lax.psum((sum_a, sq_a, sum_b, sq_b), "dp")
    left_mean, left_inverse_deviation = moment_pair(sum_a, sq_a, batch_images)
    right_mean, right_inverse_deviation = moment_pair(sum_b, sq_b, batch_images)
    standardized_left = (left_outputs.astype(jnp.float32) - left_mean) * left_inverse_deviation
    standardized_right = (right_outputs.astype(jnp.float32) - right_mean) * right_inverse_deviation
    half_a, cols_b = pair_views(
        standardized_left.astype(jnp.bfloat16),
        standardized_right.astype(jnp.bfloat16),
        row_halves,
        column_halves,
    )
    col_local = jnp.arange(half, dtype=jnp.int32)
    col_ids = quart * column_halves + col_local + jnp.where(col_local >= quart, quart, 0)
    owned = half // dp_count
    picked = half_a
    corr_rows = (
        lax.psum_scatter(
            lax.dot_general(
                picked, cols_b, (((0,), (0,)), ((), ())), preferred_element_type=jnp.float32
            ),
            "dp",
            scatter_dimension=0,
            tiled=True,
        )
        / batch_images
    )
    row_ids = half * row_halves + lax.axis_index("dp") * owned + jnp.arange(owned, dtype=jnp.int32)
    diagonal = row_ids[:, None] == col_ids[None, :]
    part_loss = jnp.sum(
        jnp.where(diagonal, (1.0 - corr_rows) ** 2, off_weight * corr_rows * corr_rows)
    )
    loss = lax.psum(part_loss, ("dp", "tile")) / feats
    dcorr_part = jnp.where(diagonal, corr_rows - 1.0, off_weight * corr_rows).astype(jnp.bfloat16)
    piece = lax.all_gather(dcorr_part, "dp", axis=0, tiled=True)
    block_a = lax.dot_general(
        cols_b, piece, (((1,), (1,)), ((), ())), preferred_element_type=jnp.float32
    )
    picked = half_a
    into_b = jnp.dot(picked, piece, preferred_element_type=jnp.float32)
    other_a = swapped(block_a.astype(jnp.bfloat16), "tile", 0).astype(block_a.dtype)
    other_b = swapped(into_b.astype(jnp.bfloat16), "tile", 1).astype(into_b.dtype)
    normed_grad_left = lax.dynamic_slice_in_dim(block_a + other_a, column_halves * quart, quart, 1)
    normed_grad_right = lax.dynamic_slice_in_dim(into_b + other_b, row_halves * quart, quart, 1)
    first_moment_left, second_moment_left, first_moment_right, second_moment_right = lax.psum(
        (
            jnp.sum(normed_grad_left, axis=0),
            jnp.sum(normed_grad_left * standardized_left, axis=0),
            jnp.sum(normed_grad_right, axis=0),
            jnp.sum(normed_grad_right * standardized_right, axis=0),
        ),
        "dp",
    )
    left_gradient = (
        left_inverse_deviation
        * (
            normed_grad_left
            - first_moment_left / batch_images
            - standardized_left * (second_moment_left / batch_images)
        )
    ).astype(jnp.bfloat16)
    right_gradient = (
        right_inverse_deviation
        * (
            normed_grad_right
            - first_moment_right / batch_images
            - standardized_right * (second_moment_right / batch_images)
        )
    ).astype(jnp.bfloat16)
    return (left_gradient, right_gradient, corr_rows[None, :, :], jnp.reshape(loss, (1,)))


def fold_rows(values):
    rows, width = values.shape
    return jnp.sum(values.reshape(rows // 8, 8, width), axis=0)


def fold_lanes(values):
    return sum(values[:, at : at + 128] for at in range(0, values.shape[1], 128))


def column_mean(block):
    rows, width = block.shape
    folded = jnp.zeros((8, width), jnp.float32)
    for at in range(0, rows, 64):
        folded = folded + fold_rows(block[at : at + 64, :].astype(jnp.float32))
    return jnp.sum(folded, axis=0, keepdims=True) / rows


def add_sums(sums, centred, low):
    return [
        sums[0] + fold_rows(centred),
        sums[1] + fold_rows(centred * centred),
        sums[2] + fold_rows(low.astype(jnp.float32)),
    ]


def rows_of(values):
    pad = jnp.zeros((8 - len(values), values[0].shape[1]), jnp.float32)
    return jnp.concatenate([*values, pad], axis=0)


def joined_sums(row, sums):
    return [row[i + 1 : i + 2, :] + jnp.sum(s, axis=0, keepdims=True) for i, s in enumerate(sums)]


def moments(sums, images):
    total, squares, rounded = sums
    delta = total / images
    return delta, lax.rsqrt(squares / images - delta * delta + 1e-05), rounded / images - delta


def three_parts(row):
    high = row.astype(jnp.bfloat16)
    rest = row - high.astype(jnp.float32)
    middle = rest.astype(jnp.bfloat16)
    low = (rest - middle.astype(jnp.float32)).astype(jnp.bfloat16)
    return [high, middle, low]


def split_rows(values):
    parts = sum([three_parts(v) for v in values], [])
    pad = jnp.zeros((4, values[0].shape[1]), jnp.float32)
    return jnp.concatenate([*(p.astype(jnp.float32) for p in parts), pad], axis=0).astype(
        jnp.bfloat16
    )


def joined_rows(ref, at):
    parts = ref[at : at + 16, :].astype(jnp.float32)
    part = lambda i: parts[i : i + 1]
    return [part(3 * i) + part(3 * i + 1) + part(3 * i + 2) for i in range(4)]


def lanes_to_row(partial):
    ones = jnp.ones((16, partial.shape[1]), jnp.bfloat16)
    high = partial.astype(jnp.bfloat16)
    low = (partial - high.astype(jnp.float32)).astype(jnp.bfloat16)
    row = dot_rows(ones, high) + dot_rows(ones, low)
    return row[:1, :]


def dot_rows(left, right):
    return lax.dot_general(
        left, right, (((1,), (1,)), ((), ())), preferred_element_type=jnp.float32
    )


def dot(left, right):
    return jnp.dot(left, right, preferred_element_type=jnp.float32)


def pick(mask, outer, inner, piece):
    return jnp.where(
        mask[0:1, :] != 0.0, outer[piece, :].astype(jnp.float32), inner[piece, :].astype(jnp.float32)
    )


def pick_kernel(mask, outer, inner, out):
    for at in range(0, outer.shape[0], 64):
        piece = slice(at, at + 64)
        out[piece, :] = pick(mask, outer, inner, piece).astype(out.dtype)


def right_sums_kernel(first, second, third, row):
    rows, quart = first.shape
    shift = column_mean(first)
    sums = [jnp.zeros((8, quart), jnp.float32)] * 3
    for block in (first, second, third):
        for at in range(0, rows, 64):
            centred = block[at : at + 64, :].astype(jnp.float32) - shift
            sums = add_sums(sums, centred, centred.astype(jnp.bfloat16))
    row[...] = rows_of([shift] + [jnp.sum(s, axis=0, keepdims=True) for s in sums])


def halves_kernel(block, first, second):
    half = first.shape[0]
    first[...] = block[:half, :]
    second[...] = block[half:, :]


def late_left_kernel(mask, outer, inner, row, out):
    for at in range(0, out.shape[0], 64):
        piece = slice(at, at + 64)
        out[piece, :] = (pick(mask, outer, inner, piece) - row[0:1, :]).astype(out.dtype)


def left_stats_kernel(images, mask, outer, inner, row, stats):
    rows, quart = outer.shape
    shift = row[0:1, :]
    sums = [jnp.zeros((8, quart), jnp.float32)] * 3
    for at in range(0, rows, 64):
        centred = pick(mask, outer, inner, slice(at, at + 64)) - shift
        sums = add_sums(sums, centred, centred.astype(jnp.bfloat16))
    delta, rstd, gap = moments(joined_sums(row, sums), images)
    stats[...] = rows_of([shift + delta, rstd, gap, delta])


def stats_rows(stats):
    return [stats[i : i + 1, :] for i in range(4)]


def late_right_kernel(images, last, mask, outer, inner, row, out, *rest):
    some, quart = outer.shape
    shift = row[0:1, :]
    sums = [jnp.zeros((8, quart), jnp.float32)] * 3
    for at in range(0, some, 128):
        piece = slice(at, at + 128)
        centred = pick(mask, outer, inner, piece) - shift
        low = centred.astype(jnp.bfloat16)
        out[:quart, piece] = jnp.transpose(low)
        sums = add_sums(sums, centred, low)
    sums = joined_sums(row, sums)
    if not last:
        (row_out,) = rest
        row_out[...] = rows_of([shift, *sums])
        return
    delta, rstd, gap = moments(sums, images)
    parts = split_rows([shift + delta, rstd, gap, delta])
    for i in range(quart // some):
        below = quart + 16 * i
        out[below : below + 16, :] = parts[:, i * some : (i + 1) * some]


def right_stats(late):
    quart, some = late[0].shape
    found = [joined_rows(late[1], quart + 16 * i) for i in range(quart // some)]
    return [jnp.concatenate(values, axis=1) for values in zip(*found)]


def late_products(right, left, lanes):
    quart, some = right[0].shape
    first = dot(right[0][...], left[:some, lanes])
    return first + dot(right[1][:quart, :], left[some : 2 * some, lanes])


def products_kernel(*refs):
    lefts, rights = refs[0:6], refs[6:12]
    partner_own, partner_other, own_all, row_other, zero_own, zero_other = refs[12:18]
    low_left, low_right = refs[18:]
    rows, quart = lefts[0].shape
    width = quart // 2
    for half in range(2):
        lanes = slice(half * quart, (half + 1) * quart)
        shift = column_mean(lefts[half])
        sums = [jnp.zeros((8, quart), jnp.float32)] * 3
        for block in range(3):
            source = lefts[2 * block + half]
            for at in range(0, rows, 64):
                centred = source[at : at + 64, :].astype(jnp.float32) - shift
                low = centred.astype(jnp.bfloat16)
                low_left[block * rows + at : block * rows + at + 64, lanes] = low
                if block == 0:
                    (zero_own, zero_other)[half][at : at + 64, :] = low
                if half:
                    sums = add_sums(sums, centred, low)
        if half:
            row_other[...] = rows_of([shift] + [jnp.sum(s, axis=0, keepdims=True) for s in sums])
    for half in range(2):
        lanes = slice(half * quart, (half + 1) * quart)
        shift = column_mean(rights[half])
        for block in range(3):
            source = rights[2 * block + half]
            for at in range(0, rows, 128):
                low = (source[at : at + 128, :].astype(jnp.float32) - shift).astype(jnp.bfloat16)
                low_right[lanes, block * rows + at : block * rows + at + 128] = jnp.transpose(low)
    for tile in range(4):
        wide = slice(tile * width, (tile + 1) * width)
        inner = slice((tile % 2) * width, (tile % 2 + 1) * width)
        target = partner_own if tile < 2 else partner_other
        target[:, inner] = dot(low_right[quart:, :], low_left[:, wide])
        own_all[:, wide] = dot(low_right[:quart, :], low_left[:, wide])


def left_operand(zero, stats, target, lanes):
    rows, quart = zero.shape
    _, _, gap, delta = stats_rows(stats)
    high, middle, _ = three_parts(delta)
    target[:rows, lanes] = zero[...]
    extra = [high.astype(jnp.float32), middle.astype(jnp.float32), gap]
    pad = jnp.zeros((13, quart), jnp.float32)
    target[rows:, lanes] = jnp.concatenate([*extra, pad], axis=0).astype(jnp.bfloat16)


def without_extra(terms, rows):
    return terms[:rows] - (terms[rows : rows + 1] + terms[rows + 1 : rows + 2] + terms[rows + 2 : rows + 3])


def scale_columns(late_b, images):
    _, rstd, _, delta = right_stats(late_b)
    columns = jnp.transpose(rows_of([rstd / images, delta * rstd]))
    return columns[:, 0:1], columns[:, 1:2]


def right_columns_kernel(images, late_b_0, late_b_1, first_b, columns, xhat):
    offset, rstd, _, delta = right_stats((late_b_0, late_b_1))
    columns[...] = jnp.transpose(rows_of([rstd / images, delta * rstd]))
    for at in range(0, first_b.shape[0], 64):
        piece = slice(at, at + 64)
        xhat[piece, :] = (first_b[piece, :].astype(jnp.float32) - offset) * rstd


def partner_kernel(images, part, late, stats, zero, sums, late_b_0, late_b_1, columns, *refs):
    if part:
        (terms_in, across_in, vec_in, xhat) = refs[:4]
        (partial_out, e_out, vec_out, left) = refs[4:]
    else:
        (terms_out, across_out, e_out, vec_out, left) = refs
    late_b = (late_b_0, late_b_1)
    rows, quart = zero.shape
    width = quart // 2
    _, rstd, _, delta = stats_rows(stats)
    left_operand(zero, stats, left, slice(0, quart))
    scale_col, delta_col = columns[:, 0:1], columns[:, 1:2]
    across = across_in[...] if part else jnp.zeros((quart, 128), jnp.float32)
    down = []
    for tile in range(2):
        at = slice(tile * width, (tile + 1) * width)
        total = sums[:, at] + late_products(late_b, late, at)
        corr = (total * scale_col - delta_col * delta[:, at]) * rstd[:, at]
        e_out[:, at] = (corr * (off_weight * rstd[:, at])).astype(jnp.bfloat16)
        square = corr * corr
        across = across + fold_lanes(square)
        down.append(jnp.sum(square, axis=0, keepdims=True))
    second_a = off_weight * jnp.concatenate(down, axis=1)
    if part:
        vec_out[...] = rows_of([second_a, second_a + vec_in[0:1, :]])
        second = off_weight * lanes_to_row(across)
    else:
        vec_out[...] = rows_of([second_a])
        across_out[...] = across
    for tile in range(2):
        at = slice(tile * width, (tile + 1) * width)
        terms = dot_rows(left[...], e_out[at, :])
        if part:
            partial_out[:, at] = (
                without_extra(terms + terms_in[:, at], rows) - xhat[:, at] * second[:, at]
            ).astype(jnp.bfloat16)
        else:
            terms_out[:, at] = terms


def own_kernel(images, flags, *refs):
    late_b, late_b_other = refs[:2], refs[2:4]
    (left_own, left_other), refs = refs[4:6], refs[6:]
    (late_own, late_other, first_own, first_other, zero_own, zero_other, sums) = refs[:7]
    (first_b, first_b_other, e_left, e_right, partner_own, partner_other) = refs[7:13]
    (vec_own, vec_other, right_out, left_out, *left_partials_out, mine_out) = refs[13:20]
    (loss_out, left, norm_b, e_own, mine_own, mine_partner) = refs[20:]
    rows, quart = zero_own.shape
    width = quart // 2
    lower, upper = slice(0, quart), slice(quart, 2 * quart)
    stats_own, stats_other = stats_rows(left_own), stats_rows(left_other)
    both = lambda i: jnp.concatenate([stats_own[i], stats_other[i]], axis=1)
    offset, rstd, _, delta = [both(i) for i in range(4)]
    left_operand(zero_own, left_own, left, lower)
    left_operand(zero_other, left_other, left, upper)
    own_b = right_stats(late_b)
    other_b = right_stats(late_b_other)
    for source, stats, lanes in ((first_b, own_b, lower), (first_b_other, other_b, upper)):
        for at in range(0, rows, 64):
            piece = slice(at, at + 64)
            norm_b[piece, lanes] = (
                (source[piece, :].astype(jnp.float32) - stats[0]) * stats[1]
            ).astype(jnp.bfloat16)
        rest = jnp.broadcast_to(stats[2] * stats[1], (16, quart))
        norm_b[rows:, lanes] = rest.astype(jnp.bfloat16)

    def tile_corr(late, inner, total, columns, block):
        scale_col, delta_col = columns
        total = total + late_products(block, late, inner)
        row = stats_own if late is late_own else stats_other
        return (total * scale_col - delta_col * row[3][:, inner]) * row[1][:, inner]

    columns = scale_columns(late_b, images)
    columns_partner = scale_columns(late_b_other, images)
    across = jnp.zeros((quart, 128), jnp.float32)
    losses = jnp.zeros((8, 128), jnp.float32)
    down, diagonals = [], []
    for tile in range(4):
        at = slice(tile * width, (tile + 1) * width)
        inner = slice((tile % 2) * width, (tile % 2 + 1) * width)
        late = late_own if tile < 2 else late_other
        corr = tile_corr(late, inner, sums[:, at], columns, late_b)
        dcorr = off_weight * corr
        product = dcorr * corr
        loss = product
        if tile < 2:
            feature = lax.broadcasted_iota(jnp.int32, (quart, width), 0)
            lane = lax.broadcasted_iota(jnp.int32, (quart, width), 1) + tile * width
            diagonal = feature == lane
            slope = jnp.where(diagonal, (corr - 1.0).astype(jnp.bfloat16).astype(jnp.float32), 0.0)
            diagonals.append(jnp.sum(slope, axis=0, keepdims=True))
            dcorr = jnp.where(diagonal, 0.0, dcorr)
            product = jnp.where(diagonal, slope * corr, product)
            loss = jnp.where(diagonal, (1.0 - corr) * (1.0 - corr), loss)
        e_own[:, at] = (dcorr * rstd[:, at]).astype(jnp.bfloat16)
        across = across + fold_lanes(product)
        losses = losses + fold_rows(fold_lanes(loss))
        down.append(jnp.sum(product, axis=0, keepdims=True))

        @pl.when(flags[0] == tile)
        def _():
            mine_own[...] = corr
            partner = partner_own if tile < 2 else partner_other
            mine_partner[...] = tile_corr(
                late, inner, partner[:, inner], columns_partner, late_b_other
            )

    diagonal_row = jnp.concatenate(diagonals, axis=1)
    partner_second = jnp.concatenate([vec_own[0:1, :], vec_other[0:1, :]], axis=1)
    second_a = rstd * (partner_second + jnp.concatenate(down, axis=1))
    second_b = lanes_to_row(across)
    loss = jnp.sum(losses) + jnp.sum(vec_other[1:2, :])
    loss_out[...] = jnp.broadcast_to(loss, (8, 128))

    for tile in (2, 3, 0, 1):
        at = slice(tile * width, (tile + 1) * width)
        inner = slice((tile % 2) * width, (tile % 2 + 1) * width)
        source, e_partner = (first_own, e_left) if tile < 2 else (first_other, e_right)
        terms = dot(norm_b[:, lower], e_own[:, at]) + dot(norm_b[:, upper], e_partner[:, inner])
        xhat = (source[:, inner].astype(jnp.float32) - offset[:, at]) * rstd[:, at]
        value = terms[:rows] - terms[rows : rows + 1] - xhat * second_a[:, at]
        if tile < 2:
            slope = rstd[:, at] * diagonal_row[:, inner]
            left_out[:, inner] = value + norm_b[:rows, inner].astype(jnp.float32) * slope
        else:
            for half, out in enumerate(left_partials_out):
                some = out.shape[0]
                out[:, inner] = value[half * some : (half + 1) * some].astype(jnp.bfloat16)

    for tile in range(2):
        at = slice(tile * width, (tile + 1) * width)
        terms = dot_rows(left[...], e_own[at, :])
        xhat = (first_b[:, at].astype(jnp.float32) - own_b[0][:, at]) * own_b[1][:, at]
        norm_a = (first_own[:, at].astype(jnp.float32) - offset[:, at]) * rstd[:, at]
        norm_a = norm_a.astype(jnp.bfloat16).astype(jnp.float32)
        value = without_extra(terms, rows) - xhat * second_b[:, at] + norm_a * diagonal_row[:, at]
        right_out[:, at] = own_b[1][:, at] * value

    own_columns = jnp.transpose(mine_own[...])
    partner_columns = jnp.transpose(mine_partner[...])

    @pl.when(flags[1] == 0)
    def _():
        mine_out[:, lower] = own_columns
        mine_out[:, upper] = partner_columns

    @pl.when(flags[1] != 0)
    def _():
        mine_out[:, lower] = partner_columns
        mine_out[:, upper] = own_columns


def add_kernel(one, other, out):
    out[...] = one[...] + other[...]


def loss_kernel(feats, one, other, out):
    out[0] = (one[0, 0] + other[0, 0]) / feats


def left_final_kernel(left, from_core_0, from_core_1, left_out):
    some = from_core_0.shape[0]
    for half, from_core in enumerate((from_core_0, from_core_1)):
        for at in range(0, some, 64):
            piece = slice(half * some + at, half * some + at + 64)
            value = left[piece, :] + from_core[at : at + 64, :].astype(jnp.float32)
            left_out[piece, :] = value.astype(jnp.bfloat16)


def right_final_kernel(right, from_x, late_b_0, late_b_1, right_out):
    rstd = right_stats((late_b_0, late_b_1))[1]
    for at in range(0, right.shape[0], 64):
        piece = slice(at, at + 64)
        value = right[piece, :] + rstd * from_x[piece, :].astype(jnp.float32)
        right_out[piece, :] = value.astype(jnp.bfloat16)


vmem = pl.BlockSpec(memory_space=pltpu.VMEM)
smem = pl.BlockSpec(memory_space=pltpu.SMEM)


def local_call(kernel, operands, outs, scratch=(), flops=2**20, room=8, held=(), moved=None):
    if moved is None:
        moved = sum(x.size * x.dtype.itemsize for x in (*operands, *outs))

    def space(x):
        return smem if x.ndim == 1 else vmem

    return pl.pallas_call(
        kernel,
        out_shape=list(outs),
        in_specs=[space(x) for x in operands],
        out_specs=[space(x) for x in outs],
        scratch_shapes=list(scratch),
        compiler_params=pltpu.CompilerParams(vmem_limit_bytes=room * 2**20),
        cost_estimate=pl.CostEstimate(flops=flops, bytes_accessed=moved, transcendentals=0),
    )(*(pltpu.with_memory_space_constraint(x, pltpu.VMEM) if i in held else x for i, x in enumerate(operands)))


def gathered_device(left_outputs, right_outputs):
    rows, quart = left_outputs.shape
    half = 2 * quart
    feats = 4 * quart
    batch_images = rows * 4
    tpos = lax.axis_index("tile")
    dpos = lax.axis_index("dp")
    row_halves = tpos // 2
    column_halves = tpos % 2
    at_end = (dpos == 0) | (dpos == 3)
    owned_tile = jnp.where(dpos // 2 == column_halves, 0, 2) + dpos % 2
    flags = jnp.stack([owned_tile, row_halves]).astype(jnp.int32)
    mask = jnp.broadcast_to(at_end.astype(jnp.float32), (8, quart))

    pairs = [(0, 1), (1, 0), (2, 3), (3, 2)]
    middle = [(1, 2), (2, 1)]
    outward = [(1, 0), (2, 3)]

    def along(block, route):
        return lax.ppermute(block, "dp", route)

    def core_swap(block):
        return swapped(block, "tile", 0)

    def x_swap(block):
        return swapped(block, "tile", 1)

    def after(value, *others):
        return lax.optimization_barrier((value, *others))

    gemm = 2 * rows * quart * quart
    width = quart // 2
    quarter_f32 = jax.ShapeDtypeStruct((rows, quart), jnp.float32)
    quarter_bf16 = jax.ShapeDtypeStruct((rows, quart), jnp.bfloat16)
    extended = jax.ShapeDtypeStruct((rows + 16, quart), jnp.bfloat16)
    row_out = jax.ShapeDtypeStruct((8, quart), jnp.float32)
    one_out = jax.ShapeDtypeStruct((8, 128), jnp.float32)
    across_shape = jax.ShapeDtypeStruct((quart, 128), jnp.float32)
    low = lambda n, m: pltpu.VMEM((n, m), jnp.bfloat16)

    def picked(outer, inner):
        return local_call(pick_kernel, (mask, outer, inner), (quarter_bf16,))[0]

    some = rows // 2
    half_block = jax.ShapeDtypeStruct((some, quart), jnp.bfloat16)
    first_b = along(right_outputs, pairs)
    inner_b = along(right_outputs, middle)
    first_a = along(left_outputs, pairs)
    other_b0 = x_swap(right_outputs)
    other_a0, mask, flags = after(core_swap(left_outputs), mask, flags)
    left_behind, first_a, other_a0 = after(left_outputs, first_a, other_a0)
    inner_a = along(left_behind, middle)

    outer_b = along(inner_b, outward)
    third_b = along(first_b, middle)
    ready_b, other_b0 = after(first_b, other_b0)
    other_b1 = x_swap(ready_b)
    outer_a = along(inner_a, outward)
    third_a = along(first_a, middle)
    other_a1 = core_swap(first_a)

    third_b = local_call(halves_kernel, (third_b,), (half_block, half_block))
    last_b = [along(x, outward) for x in third_b]
    second_b = picked(outer_b, inner_b)
    row_b = local_call(right_sums_kernel, (right_outputs, first_b, second_b), (row_out,))[0]
    second_b, other_b1, other_a1 = after(second_b, other_b1, other_a1)
    other_b2 = x_swap(second_b)
    last_a = along(third_a, outward)
    second_a = picked(outer_a, inner_a)
    second_a, row_b = after(second_a, row_b)
    other_a2 = core_swap(second_a)

    late_b_0, row_b = local_call(
        functools.partial(late_right_kernel, batch_images, False),
        (mask, last_b[0], third_b[0], row_b),
        (jax.ShapeDtypeStruct((quart, some), jnp.bfloat16), row_out),
        held=(0, 1, 2, 3),
    )
    late_b_other_0 = x_swap(late_b_0)
    (late_b_1,) = local_call(
        functools.partial(late_right_kernel, batch_images, True),
        (mask, last_b[1], third_b[1], row_b),
        (jax.ShapeDtypeStruct((quart + 16 * (quart // some), some), jnp.bfloat16),),
        held=(0, 1, 2, 3),
    )
    late_b_other_1 = x_swap(late_b_1)
    late_b = (late_b_0, late_b_1)
    other_b2, late_b_1, late_b_other_0 = after(other_b2, late_b_1, late_b_other_0)
    partner_own, partner_other, own_all, row_other, zero_own, zero_other = local_call(
        products_kernel,
        (left_outputs, other_a0, first_a, other_a1, second_a, other_a2)
        + (right_outputs, other_b0, first_b, other_b1, second_b, other_b2),
        (
            quarter_f32,
            quarter_f32,
            jax.ShapeDtypeStruct((quart, half), jnp.float32),
            row_out,
            quarter_bf16,
            quarter_bf16,
        ),
        [low(3 * rows, half), low(half, 3 * rows)],
        room=20,
        moved=2**16,
    )
    row_a, late_b_other_1 = after(core_swap(row_other), late_b_other_1)
    late_b_other = (late_b_other_0, late_b_other_1)
    columns, xhat_other = local_call(
        functools.partial(right_columns_kernel, batch_images),
        (*late_b_other, other_b0),
        (jax.ShapeDtypeStruct((quart, 8), jnp.float32), quarter_f32),
    )
    row_a, columns = after(row_a, columns)
    operands = (mask, last_a, third_a, row_a)
    (late_a,) = local_call(late_left_kernel, operands, (quarter_bf16,), held=(0, 1, 2, 3))
    late_a_other = core_swap(late_a)
    (stats_a,) = local_call(
        functools.partial(left_stats_kernel, batch_images), operands, (row_out,), held=(0, 1, 2, 3)
    )
    stats_a_other = core_swap(stats_a)

    terms, across, e_left, vec_own = local_call(
        functools.partial(partner_kernel, batch_images, 0),
        (late_a, stats_a, zero_own, partner_own, *late_b_other, columns),
        (
            jax.ShapeDtypeStruct((rows + 16, quart), jnp.float32),
            across_shape,
            quarter_bf16,
            row_out,
        ),
        [low(rows + 16, quart)],
        2 * gemm,
        room=12,
    )
    partial_right, e_right, vec_other = local_call(
        functools.partial(partner_kernel, batch_images, 1),
        (late_a_other, stats_a_other, zero_other, partner_other, *late_b_other)
        + (columns, terms, across, vec_own, xhat_other),
        (quarter_bf16, quarter_bf16, row_out),
        [low(rows + 16, quart)],
        2 * gemm,
        room=12,
    )
    from_x = x_swap(partial_right)
    right_own, left_own, *partials_left, mine, loss = local_call(
        functools.partial(own_kernel, batch_images),
        (flags, *late_b, *late_b_other, stats_a, stats_a_other)
        + (late_a, late_a_other, left_outputs, other_a0, zero_own, zero_other, own_all)
        + (right_outputs, other_b0, e_left, e_right)
        + (partner_own, partner_other)
        + (vec_own, vec_other),
        (
            quarter_f32,
            quarter_f32,
            half_block,
            half_block,
            jax.ShapeDtypeStruct((width, half), jnp.float32),
            one_out,
        ),
        [
            low(rows + 16, half),
            low(rows + 16, half),
            low(quart, half),
            pltpu.VMEM((quart, width), jnp.float32),
            pltpu.VMEM((quart, width), jnp.float32),
        ],
        8 * gemm,
        room=20,
    )
    from_core = [core_swap(x) for x in partials_left]
    core_loss = core_swap(loss)
    (loss,) = local_call(add_kernel, (loss, core_loss), (one_out,))
    x_loss = x_swap(loss)
    (left_gradient,) = local_call(left_final_kernel, (left_own, *from_core), (quarter_bf16,))
    right_own, left_gradient = after(right_own, left_gradient)
    (right_gradient,) = local_call(right_final_kernel, (right_own, from_x, *late_b), (quarter_bf16,))
    right_gradient, x_loss = after(right_gradient, x_loss)
    (loss,) = local_call(
        functools.partial(loss_kernel, feats),
        (loss, x_loss),
        (jax.ShapeDtypeStruct((1,), jnp.float32),),
    )
    return (left_gradient, right_gradient, mine[None, :, :], loss)


def solution(mesh):
    per_device = gathered_device if mesh.shape["dp"] == 4 else reduced_device
    return jax.shard_map(
        per_device,
        mesh=mesh,
        in_specs=(P(("groups", "dp"), "tile"), P(("groups", "dp"), "tile")),
        out_specs=(
            P(("groups", "dp"), "tile"),
            P(("groups", "dp"), "tile"),
            P(("groups", "tile"), "dp", None),
            P("groups"),
        ),
        check_vma=False,
    )
```
